32 devices in a mesh: seq: 8 (over z, y), ch: 4 (over x, core).
Axes of the slice: x: 2, y: 2, z: 4, core: 2. Of those that a mesh axis runs over, the one named last changes fastest.
Arguments:
- stream: bfloat16 [2048, 1536], P('seq'), may hold values from -6 to 6
- doc_bounds: int32 [2], replicated, may hold values from 1 to 2047, as said below
- norm_gains: float32 [2, 1536], replicated, may hold values from 0.5 to 1.5
- w_in: bfloat16 [1536, 2, 3072], P(None, None, 'ch'), may hold values from -0.15625 to 0.15625
- chan_vectors: float32 [7, 3072], P(None, 'ch'), may hold values from -7 to 2
- decay_logs: float32 [16, 3072], P(None, 'ch'), may hold values from -14 to 4
- w_x: bfloat16 [3072, 128], P('ch'), may hold values from -0.109375 to 0.109375
- small_gains: float32 [128], replicated, may hold values from 0.5 to 1.5
- w_dt: bfloat16 [96, 3072], P(None, 'ch'), may hold values from -0.625 to 0.625
- w_out: bfloat16 [3072, 1536], P('ch'), may hold values from -0.0546875 to 0.0546875
- w_gate_up: bfloat16 [1536, 2, 4096], P(None, None, 'ch'), may hold values from -0.15625 to 0.15625
- w_down: bfloat16 [4096, 1536], P('ch'), may hold values from -0.09375 to 0.09375
- cotangent: bfloat16 [2048, 1536], P('seq'), may hold values from -6 to 6
Outputs:
- out: bfloat16 [2048, 1536], P('seq')
- stream_grad: float32 [2048, 1536], P('seq')
- norm_gains_grad: float32 [2, 1536], P(None, 'seq')
- w_in_grad: float32 [1536, 2, 3072], P('seq', None, 'ch')
- chan_vectors_grad: float32 [7, 3072], P(None, ('ch', 'seq'))
- decay_logs_grad: float32 [16, 3072], P(None, ('ch', 'seq'))
- w_x_grad: float32 [3072, 128], P(('ch', 'seq'))
- small_gains_grad: float32 [128], P('seq')
- w_dt_grad: float32 [96, 3072], P(None, ('ch', 'seq'))
- w_out_grad: float32 [3072, 1536], P(('ch', 'seq'))
- w_gate_up_grad: float32 [1536, 2, 4096], P('seq', None, 'ch')
- w_down_grad: float32 [4096, 1536], P(('ch', 'seq'))
- stream_rms: float32 [3], replicated
The draws below stay inside these ranges and needn't reach their ends.
Inputs may be any that keep to these rules, and one draw needn't show every extreme that they name: doc_bounds[0] lies among the first 256 tokens and doc_bounds[1] among the last 256, so the second document runs from the first index of seq to the last.
All inputs are finite; a program needn't handle non-finite values.
Results may differ from the reference program's by a relative error of at most 0.022.
Values may be sent and summed in bfloat16 or wider, within the bound.
A program may use at most 192 MiB of HBM per device.

```python
import jax
import jax.numpy as jnp
from jax import lax

D = 1536
E = 3072
N = 16
R = 96
F = 4096
TOK_DEV = 256
TOKENS = 2048


def bias_row(key):
    return jax.random.uniform(jax.random.fold_in(key, 501), (E,), jnp.float32, -7.0, -4.0)


def draw_doc_bounds(key, part):
    first_key, second_key = jax.random.split(jax.random.fold_in(key, 511))
    first_bound = jax.random.randint(first_key, (), 1, TOK_DEV)
    second_bound = jax.random.randint(second_key, (), TOKENS - TOK_DEV + 1, TOKENS)
    return jnp.stack([first_bound, second_bound]).astype(jnp.int32)


def draw_chan_vectors(key, part):
    subkeys = jax.random.split(jax.random.fold_in(key, 502), 3)
    kernel = jnp.clip(0.5 * jax.random.normal(subkeys[0], (4, E), jnp.float32), -2.0, 2.0)
    skip_row = jax.random.uniform(subkeys[2], (1, E), jnp.float32, 0.5, 1.5)
    conv_bias = jax.random.uniform(subkeys[1], (1, E), jnp.float32, -0.5, 0.5)
    return jnp.concatenate([kernel, conv_bias, bias_row(key)[None], skip_row], 0)


def draw_decay_logs(key, part):
    subkeys = jax.random.split(jax.random.fold_in(key, 503), 3)
    mean_step = jnp.exp(bias_row(key) + 0.5)
    fast_share = 0.5
    is_fast = (jax.random.uniform(subkeys[0], (1, E), jnp.float32) < fast_share).astype(jnp.float32)
    fast_rate = jnp.exp(jax.random.uniform(subkeys[1], (N, E), jnp.float32, -0.7, 0.7)) / 40.0
    slow_rate = jnp.exp(jax.random.uniform(subkeys[2], (N, E), jnp.float32, -1.2, 0.7)) / TOKENS
    per_token = is_fast * fast_rate + (1.0 - is_fast) * slow_rate
    return jnp.clip(jnp.log(per_token / mean_step[None]), -14.0, 4.0)


def block_scale(rng, extent, cuts, low, largest):
    def one(dim, blocks):
        heights = jax.random.uniform(jax.random.fold_in(jax.random.fold_in(rng, 6), dim), (blocks,), jnp.float32, low / len(cuts), largest / len(cuts))
        return jnp.repeat(jnp.exp(heights), extent[dim] // blocks).reshape((-1,) + (1,) * (len(extent) - dim - 1))

    gain = one(*cuts[0])
    for cut in cuts[1:]:
        gain = gain * one(*cut)
    return gain


def scatter_about(own_key, shape, scale, reach, pieces=(), kind=jnp.bfloat16):
    entries = jax.random.normal(own_key, shape, jnp.float32) * scale
    if len(pieces) > 0:
        entries = block_scale(own_key, shape, pieces, -0.22, 0.18) * entries
    return jnp.clip(entries, min=-reach, max=reach).astype(kind)


def setup_inputs(seed: int = 0) -> dict:
    keys = jax.random.split(jax.random.key(seed), 14)
    stream = scatter_about(keys[0], (TOKENS, D), 1.0, 6.0, ((0, 8),))
    doc_bounds = draw_doc_bounds(jax.random.fold_in(keys[13], 71), 0)
    norm_gains = jnp.clip(1.0 + 0.1 * jax.random.normal(keys[2], (2, D), jnp.float32), 0.5, 1.5)
    w_in = scatter_about(keys[3], (D, 2, E), D ** -0.5, 0.15625, ((2, 4),))
    chan_vectors = draw_chan_vectors(jax.random.fold_in(keys[13], 71), 0)
    decay_logs = draw_decay_logs(jax.random.fold_in(keys[13], 71), 0)
    w_x = scatter_about(keys[6], (E, R + 2 * N), E ** -0.5, 0.109375, ((0, 4),))
    small_gains = jnp.clip(1.0 + 0.1 * jax.random.normal(keys[7], (R + 2 * N,), jnp.float32), 0.5, 1.5)
    w_dt = scatter_about(keys[8], (R, E), R ** -0.5, 0.625, ((1, 4),))
    w_out = scatter_about(keys[9], (E, D), (E * 4) ** -0.5, 0.0546875, ((0, 4),))
    w_gate_up = scatter_about(keys[10], (D, 2, F), D ** -0.5, 0.15625, ((2, 4),))
    w_down = scatter_about(keys[11], (F, D), F ** -0.5, 0.09375, ((0, 4),))
    cotangent = scatter_about(keys[12], (TOKENS, D), 1.0, 6.0, ((0, 8),))
    return {"stream": stream, "doc_bounds": doc_bounds, "norm_gains": norm_gains, "w_in": w_in, "chan_vectors": chan_vectors, "decay_logs": decay_logs, "w_x": w_x, "small_gains": small_gains, "w_dt": w_dt, "w_out": w_out, "w_gate_up": w_gate_up, "w_down": w_down, "cotangent": cotangent}


HIGHEST = lax.Precision.HIGHEST

@jax.custom_vjp
def low(v):
    return lax.optimization_barrier(v.astype(jnp.bfloat16)).astype(jnp.float32)

@jax.custom_vjp
def low_back(v):
    return v

def low_keep(v):
    return (low(v), None)

def low_pass(kept, grad):
    return (grad,)

def back_keep(v):
    return (v, None)

def back_low(kept, grad):
    return (low(grad),)
low.defvjp(low_keep, low_pass)
low_back.defvjp(back_keep, back_low)

def rms_gain(values, gain_row):
    return values * lax.rsqrt(lax.optimization_barrier(jnp.mean(values * values, axis=-1, keepdims=True)) + 1e-06) * gain_row

def rms_floor(values, gain_row):
    return values * lax.rsqrt(jnp.maximum(lax.optimization_barrier(jnp.mean(values * values, axis=-1, keepdims=True)), 0.1)) * gain_row

def norm_three(raw_proj, gains_small, step_rank):
    state_width = (raw_proj.shape[1] - step_rank) // 2
    step_norm = rms_gain(raw_proj[:, :step_rank], gains_small[:step_rank])
    input_norm = rms_floor(raw_proj[:, step_rank:step_rank + state_width], gains_small[step_rank:step_rank + state_width])
    output_norm = rms_floor(raw_proj[:, step_rank + state_width:], gains_small[step_rank + state_width:])
    return (step_norm, input_norm, output_norm)

def doc_number(places, bounds):
    return (places >= bounds[0]).astype(jnp.int32) + (places >= bounds[1]).astype(jnp.int32)

def conv_masks(places, bounds):
    own_doc = doc_number(places, bounds)
    mask_rows = []
    for offset in range(4):
        source = places - (3 - offset)
        mask_rows.append(((source >= 0) & (doc_number(source, bounds) == own_doc)).astype(jnp.float32))
    return jnp.stack(mask_rows, 0)

def conv_silu(extended, kernel, tap_masks):
    length = tap_masks.shape[1]
    summed = kernel[4]
    for offset in range(4):
        summed = summed + kernel[offset] * extended[offset:offset + length] * tap_masks[offset][:, None]
    return jax.nn.silu(summed)

def gating(scan_out, gate_pre):
    return scan_out * jax.nn.silu(gate_pre)

def swiglu(gate_up):
    return jax.nn.silu(gate_up[:, 0]) * gate_up[:, 1]

def per_token(carry_pair, inputs_row):
    carry_state, decay_rate = carry_pair
    step_row, input_row, output_row, drive_row, keep_row = inputs_row
    carry_state = jnp.exp(step_row[None, :] * decay_rate) * keep_row * carry_state + input_row[:, None] * drive_row[None, :]
    return ((carry_state, decay_rate), lax.optimization_barrier(jnp.sum(output_row[:, None] * carry_state, axis=0)))

def scan_block(carry_pair, block_inputs):
    return lax.scan(per_token, carry_pair, block_inputs)

def forward(stream_in, norm_gains, w_in, chan_vectors, decay_logs, w_x, small_gains, w_dt, w_out, w_gate_up, w_down, tap_masks, keep_mask):
    normed_one = low(rms_gain(stream_in, norm_gains[0]))
    in_proj = low_back(low(jnp.einsum('td,dke->tke', normed_one, w_in, precision=HIGHEST)))
    conv_in = in_proj[:, 0]
    gate_pre = in_proj[:, 1]
    extended = jnp.concatenate([jnp.zeros((3, E), jnp.float32), conv_in], 0)
    conv_out = low(conv_silu(extended, chan_vectors[:5], tap_masks))
    raw_proj = low_back(jnp.dot(conv_out, w_x, precision=HIGHEST))
    step_norm, input_norm, output_norm = norm_three(raw_proj, small_gains, R)
    step_pre = low_back(jnp.dot(low(step_norm), w_dt, precision=HIGHEST) + chan_vectors[5])
    step_size = jax.nn.softplus(step_pre)
    decay_rate = -jnp.exp(decay_logs)
    drive_term = step_size * conv_out
    block_len = min(128, TOKENS)
    count_blocks = TOKENS // block_len

    def blocked(values):
        return values.reshape((count_blocks, block_len) + values.shape[1:])
    _, scanned = lax.scan(jax.checkpoint(scan_block), (jnp.zeros((N, E), jnp.float32), decay_rate), (blocked(step_size), blocked(input_norm), blocked(output_norm), blocked(drive_term), blocked(keep_mask)))
    scan_out = scanned.reshape(TOKENS, E) + chan_vectors[6] * conv_out
    gated_out = low(gating(scan_out, gate_pre))
    mixer_out = low_back(jnp.dot(gated_out, w_out, precision=HIGHEST))
    middle = stream_in + mixer_out
    normed_two = low(rms_gain(middle, norm_gains[1]))
    gate_up = low_back(jnp.einsum('td,dkf->tkf', normed_two, w_gate_up, precision=HIGHEST))
    hidden_act = low(swiglu(gate_up))
    feed_out = low_back(jnp.dot(hidden_act, w_down, precision=HIGHEST))
    return (middle + feed_out, mixer_out, feed_out)

def reference(stream, doc_bounds, norm_gains, w_in, chan_vectors, decay_logs, w_x, small_gains, w_dt, w_out, w_gate_up, w_down, cotangent):
    places = jnp.arange(TOKENS, dtype=jnp.int32)
    tap_masks = conv_masks(places, doc_bounds)
    keep_mask = 1.0 - ((places == doc_bounds[0]) | (places == doc_bounds[1])).astype(jnp.float32)
    params = (stream.astype(jnp.float32), norm_gains, w_in.astype(jnp.float32), chan_vectors, decay_logs, w_x.astype(jnp.float32), small_gains, w_dt.astype(jnp.float32), w_out.astype(jnp.float32), w_gate_up.astype(jnp.float32), w_down.astype(jnp.float32))

    def closed(*params_in):
        return forward(*params_in, tap_masks, keep_mask)
    (result, mixer_out, feed_out), pullback = jax.vjp(closed, *params)
    gradients = pullback((cotangent.astype(jnp.float32), jnp.zeros_like(mixer_out), jnp.zeros_like(feed_out)))
    total_cells = TOKENS * D
    rms_values = jnp.sqrt(jnp.stack([jnp.sum(result * result), jnp.sum(mixer_out * mixer_out), jnp.sum(feed_out * feed_out)]) / total_cells)
    return (result.astype(jnp.bfloat16), gradients[0], gradients[1], gradients[2], gradients[3], gradients[4], gradients[5], gradients[6], gradients[7], gradients[8], gradients[9], gradients[10], rms_values)
```

```python
import functools
import math

import jax
import jax.numpy as jnp
from jax import lax
from jax.experimental import pallas as pl
from jax.experimental.pallas import tpu as pltpu
from jax.sharding import PartitionSpec as P

f32 = jnp.float32
bf16 = jnp.bfloat16
LOG2E = math.log2(math.e)
LN2 = math.log(2.0)
RESET = 1e30
UNROLL = 8
LANES = 256
VMEM = pl.BlockSpec(memory_space=pltpu.VMEM)


def shape_of(*dims, dtype=f32):
    return jax.ShapeDtypeStruct(dims, dtype)


def cost(us):
    return pl.CostEstimate(flops=int(us * 1e9), bytes_accessed=int(us * 1e6), transcendentals=0)


def widened(column, width):
    return jnp.concatenate([column] * (width // 128), 1)


def folded(values):
    total = values[:, :128]
    for part in range(1, values.shape[1] // 128):
        total = total + values[:, part * 128 : (part + 1) * 128]
    return total


def ahead_end_kernel(step, drive, into, rate, end):
    tokens, width = step.shape
    rates = rate[...]

    def body(index, state):
        first = pl.multiple_of(index * UNROLL, UNROLL)
        steps = step[pl.ds(first, UNROLL), :]
        drives = drive[pl.ds(first, UNROLL), :]
        for k in range(UNROLL):
            decay = jnp.exp2(steps[k : k + 1] * rates)
            state = decay * state + widened(into[first + k], width) * drives[k : k + 1]
        return state

    end[...] = lax.fori_loop(0, tokens // UNROLL, body, jnp.zeros_like(rates))


def ahead_kernel(step, drive, into, out_of, rate, start, scanned, before, end):
    tokens, width = step.shape
    rates = rate[...]

    def body(index, state):
        first = pl.multiple_of(index * UNROLL, UNROLL)
        steps = step[pl.ds(first, UNROLL), :]
        drives = drive[pl.ds(first, UNROLL), :]
        rows = []
        for k in range(UNROLL):
            before[first + k] = state
            decay = jnp.exp2(steps[k : k + 1] * rates)
            state = decay * state + widened(into[first + k], width) * drives[k : k + 1]
            rows.append(
                jnp.sum(widened(out_of[first + k], width) * state, axis=0, keepdims=True)
            )
        scanned[pl.ds(first, UNROLL), :] = jnp.concatenate(rows, 0)
        return state

    end[...] = lax.fori_loop(0, tokens // UNROLL, body, start[...])


def back_end_kernel(step, grad, out_of, rate, end):
    tokens, width = step.shape
    rates = rate[...]

    def body(index, carried):
        first = pl.multiple_of(tokens - UNROLL - index * UNROLL, UNROLL)
        steps = step[pl.ds(first, UNROLL), :]
        grads = grad[pl.ds(first, UNROLL), :]
        for k in reversed(range(UNROLL)):
            decay = jnp.exp2(steps[k : k + 1] * rates)
            carried = decay * (widened(out_of[first + k], width) * grads[k : k + 1] + carried)
        return carried

    end[...] = lax.fori_loop(0, tokens // UNROLL, body, jnp.zeros_like(rates))


def back_kernel(
    step, drive, grad, into, out_of, rate, before, end, start,
    decay_rows, push_rows, into_wide, out_wide, rate_sum,
):
    tokens, width = step.shape
    rates = rate[...]

    @pl.when(pl.program_id(0) == 0)
    def _():
        into_wide[...] = jnp.zeros_like(into_wide)
        out_wide[...] = jnp.zeros_like(out_wide)

    def body(index, carry):
        carried, state, total = carry
        first = pl.multiple_of(tokens - UNROLL - index * UNROLL, UNROLL)
        steps = step[pl.ds(first, UNROLL), :]
        drives = drive[pl.ds(first, UNROLL), :]
        grads = grad[pl.ds(first, UNROLL), :]
        decay_list, push_list = [None] * UNROLL, [None] * UNROLL
        for k in reversed(range(UNROLL)):
            place = first + k
            grad_row = grads[k : k + 1]
            decay = jnp.exp2(steps[k : k + 1] * rates)
            adjoint = widened(out_of[place], width) * grad_row + carried
            carried = decay * adjoint
            out_wide[place] = out_wide[place] + folded(state * grad_row)
            into_wide[place] = into_wide[place] + folded(adjoint * drives[k : k + 1])
            state = before[place]
            share = carried * state
            total = total + share * steps[k : k + 1]
            decay_list[k] = jnp.sum(share * rates, axis=0, keepdims=True)
            push_list[k] = jnp.sum(widened(into[place], width) * adjoint, axis=0, keepdims=True)
        decay_rows[pl.ds(first, UNROLL), :] = jnp.concatenate(decay_list, 0)
        push_rows[pl.ds(first, UNROLL), :] = jnp.concatenate(push_list, 0)
        return (carried, state, total)

    _, _, total = lax.fori_loop(
        0, tokens // UNROLL, body, (start[...], end[...], jnp.zeros_like(rates))
    )
    rate_sum[...] = total


def scan_specs(tokens, states):
    return (
        pl.BlockSpec((tokens, LANES), lambda j: (0, j)),
        pl.BlockSpec((states, LANES), lambda j: (0, j)),
        pl.BlockSpec((tokens, states, 128), lambda j: (0, 0, 0)),
        pl.BlockSpec((tokens, states, LANES), lambda j: (0, 0, j)),
    )


def scan_call(kernel, name, us, channels, in_specs, out_specs, out_shape):
    return pl.pallas_call(
        kernel,
        grid=(channels // LANES,),
        in_specs=in_specs,
        out_specs=out_specs,
        out_shape=out_shape,
        compiler_params=pltpu.CompilerParams(vmem_limit_bytes=48 * 2**20),
        cost_estimate=cost(us),
        name=name,
    )


def ahead_end(step, drive, into, rate):
    (tokens, channels), states = step.shape, rate.shape[0]
    row, st, col, _ = scan_specs(tokens, states)
    return scan_call(
        ahead_end_kernel, "ahead_end", 5, channels, [row, row, col, st], st,
        shape_of(states, channels),
    )(step, drive, into, rate)


def ahead(step, drive, into, out_of, rate, start):
    (tokens, channels), states = step.shape, rate.shape[0]
    row, st, col, hist = scan_specs(tokens, states)
    return scan_call(
        ahead_kernel, "ahead", 10, channels, [row, row, col, col, st, st], [row, hist, st],
        [shape_of(tokens, channels), shape_of(tokens, states, channels), shape_of(states, channels)],
    )(step, drive, into, out_of, rate, start)


def back_end(step, grad, out_of, rate):
    (tokens, channels), states = step.shape, rate.shape[0]
    row, st, col, _ = scan_specs(tokens, states)
    return scan_call(
        back_end_kernel, "back_end", 5, channels, [row, row, col, st], st,
        shape_of(states, channels),
    )(step, grad, out_of, rate)


def back(step, drive, grad, into, out_of, rate, before, end, start):
    (tokens, channels), states = step.shape, rate.shape[0]
    row, st, col, hist = scan_specs(tokens, states)
    wide = shape_of(tokens, states, 128)
    rows = shape_of(tokens, channels)
    return scan_call(
        back_kernel, "back", 16, channels,
        [row, row, row, col, col, st, hist, st, st], [row, row, col, col, st],
        [rows, rows, wide, wide, shape_of(states, channels)],
    )(step, drive, grad, into, out_of, rate, before, end, start)


def met(axis, partners):
    barrier = pltpu.get_barrier_semaphore()
    for partner in partners:
        pl.semaphore_signal(
            barrier, inc=1, device_id={axis: partner}, device_id_type=pl.DeviceIdType.MESH
        )
    pl.semaphore_wait(barrier, len(partners))


def sent(source, target, sends, receives, slot, axis, partner):
    copy = pltpu.make_async_remote_copy(
        src_ref=source,
        dst_ref=target,
        send_sem=sends.at[slot],
        recv_sem=receives.at[slot],
        device_id={axis: partner},
        device_id_type=pl.DeviceIdType.MESH,
    )
    copy.start()
    return copy


def bits_of(count):
    return [1 << k for k in range(count.bit_length() - 1)]


def flipped(me, bit):
    mine = lax.rem(me // bit, 2)
    return mine, me + bit - 2 * bit * mine


def exchange_params(ident):
    return pltpu.CompilerParams(
        collective_id=ident, has_side_effects=True, vmem_limit_bytes=32 * 2**20
    )


def small_sum_kernel(axis, bits, value, total, moving, landed, sends, receives):
    me = lax.axis_index(axis)
    met(axis, [flipped(me, bit)[1] for bit in bits])
    moving[0] = value[...]
    for k, bit in enumerate(bits):
        _, partner = flipped(me, bit)
        copy = sent(moving.at[k], landed.at[k], sends, receives, k, axis, partner)
        copy.wait()
        if k + 1 < len(bits):
            moving[k + 1] = moving[k] + landed[k]
        else:
            total[...] = moving[k] + landed[k]


def small_sum(value, axis, count, ident, name):
    bits = bits_of(count)
    slots = pltpu.VMEM((len(bits),) + value.shape, f32)
    return pl.pallas_call(
        functools.partial(small_sum_kernel, axis, bits),
        out_shape=shape_of(*value.shape),
        in_specs=[VMEM],
        out_specs=VMEM,
        scratch_shapes=[slots, slots] + [pltpu.SemaphoreType.DMA((len(bits),))] * 2,
        compiler_params=exchange_params(ident),
        cost_estimate=cost(7),
        name=name,
    )(value)


def four_sum_kernel(value, total, first, second, moving, sends, receives):
    me = lax.axis_index("ch")
    low, across = flipped(me, 1)
    high, along = flipped(me, 2)
    met("ch", [across, along])
    sent(value.at[:, 1 - low], first, sends, receives, 0, "ch", across).wait()
    moving[...] = (
        value[1 - high, low].astype(f32) + first[1 - high].astype(f32)
    ).astype(bf16)
    copy = sent(moving, second, sends, receives, 1, "ch", along)
    kept = value[high, low].astype(f32) + first[high].astype(f32)
    copy.wait()
    total[high, low] = (kept + second[...].astype(f32)).astype(bf16)
    sent(total.at[high, low], total.at[high, low], sends, receives, 2, "ch", along).wait()
    sent(total.at[:, low], total.at[:, low], sends, receives, 3, "ch", across).wait()


def four_sum(value, ident, name):
    rows, columns = value.shape
    part = rows // 4
    result = pl.pallas_call(
        four_sum_kernel,
        out_shape=shape_of(2, 2, part, columns, dtype=bf16),
        in_specs=[VMEM],
        out_specs=VMEM,
        scratch_shapes=[
            pltpu.VMEM((2, part, columns), bf16),
            pltpu.VMEM((part, columns), bf16),
            pltpu.VMEM((part, columns), bf16),
            pltpu.SemaphoreType.DMA((4,)),
            pltpu.SemaphoreType.DMA((4,)),
        ],
        compiler_params=exchange_params(ident),
        cost_estimate=cost(14),
        name=name,
    )(value.reshape(2, 2, part, columns))
    return result.reshape(rows, columns)


def chain_kernel(forward, bits, state, steps, rate, arriving, moving, landed, sends, receives):
    me = lax.axis_index("seq")
    states = state.shape[0]
    met("seq", [flipped(me, bit)[1] for bit in bits])
    rates = rate[...]
    all_state, all_steps = state[...], steps[...]
    mine_state, mine_steps = jnp.zeros_like(all_state), jnp.zeros_like(all_steps)
    for k, bit in enumerate(bits):
        mine, partner = flipped(me, bit)
        moving[k, :states] = all_state
        moving[k, states:] = all_steps
        sent(moving.at[k], landed.at[k], sends, receives, k, "seq", partner).wait()
        other_state, other_steps = landed[k, :states], landed[k, states:]
        earlier = (mine == 1) if forward else (mine == 0)
        through = jnp.exp2(rates * mine_steps[:1])
        mine_state = jnp.where(earlier, mine_state + through * other_state, mine_state)
        mine_steps = jnp.where(earlier, mine_steps + other_steps, mine_steps)
        after = jnp.exp2(rates * all_steps[:1]) * other_state + all_state
        ahead_of = jnp.exp2(rates * other_steps[:1]) * all_state + other_state
        all_state = jnp.where(earlier, after, ahead_of)
        all_steps = all_steps + other_steps
    arriving[...] = mine_state


def chain(state, step_total, rate, forward, count, ident, name):
    bits = bits_of(count)
    states, channels = state.shape
    slots = pltpu.VMEM((len(bits), states + 8, channels), f32)
    return pl.pallas_call(
        functools.partial(chain_kernel, forward, bits),
        out_shape=shape_of(states, channels),
        in_specs=[VMEM] * 3,
        out_specs=VMEM,
        scratch_shapes=[slots, slots] + [pltpu.SemaphoreType.DMA((len(bits),))] * 2,
        compiler_params=exchange_params(ident),
        cost_estimate=cost(14),
        name=name,
    )(state, step_total, rate)


def last_sums_kernel(bits, parts, flat, own, flat_total, *rest):
    me = lax.axis_index("seq")
    levels = len(bits)
    works, rest = rest[:levels], rest[levels:]
    lows, rest = rest[:levels], rest[levels:]
    lands, rest = rest[:levels], rest[levels:]
    moving, landed, sends, receives, flat_sends, flat_receives = rest
    met("seq", [flipped(me, bit)[1] for bit in bits])
    moving[0] = flat[...]
    for k, bit in enumerate(bits):
        mine, partner = flipped(me, bit)
        source = parts if k == 0 else works[k - 1]
        lows[k][...] = source[:, 1 - mine].astype(bf16)
        copy = sent(lows[k], lands[k], sends, receives, k, "seq", partner)
        flat_copy = sent(moving.at[k], landed.at[k], flat_sends, flat_receives, k, "seq", partner)
        copy.wait()
        summed = source[:, mine] + lands[k][...].astype(f32)
        if k + 1 < levels:
            works[k][...] = summed.reshape(works[k].shape)
        else:
            own[...] = summed.reshape(own.shape)
        flat_copy.wait()
        if k + 1 < levels:
            moving[k + 1] = moving[k] + landed[k]
        else:
            flat_total[...] = moving[k] + landed[k]


def last_sums(parts, flat, count, ident, name):
    bits = bits_of(count)
    levels = len(bits)
    rows, columns = parts.shape[0] // count, parts.shape[1]
    halves = [count >> (k + 1) for k in range(levels)]
    works = [pltpu.VMEM((max(half // 2, 1), 2 if half > 1 else 1, rows, columns), f32) for half in halves]
    lows = [pltpu.VMEM((half, rows, columns), bf16) for half in halves]
    slots = pltpu.VMEM((levels,) + flat.shape, f32)
    sems = [pltpu.SemaphoreType.DMA((levels,))] * 4
    return pl.pallas_call(
        functools.partial(last_sums_kernel, bits),
        out_shape=[shape_of(rows, columns), shape_of(*flat.shape)],
        in_specs=[VMEM] * 2,
        out_specs=[VMEM] * 2,
        scratch_shapes=works + lows + lows + [slots, slots] + sems,
        compiler_params=exchange_params(ident),
        cost_estimate=cost(20),
        name=name,
    )(parts.reshape(count // 2, 2, rows, columns), flat)


def grads_scattered(partial_grad, count):
    rows, columns = partial_grad.shape[0] // count, partial_grad.shape[1]
    me = lax.axis_index("seq")
    held = partial_grad
    left = count
    for bit in bits_of(count):
        left //= 2
        held = held.reshape(left, 2, rows, columns)
        mine = (me // bit) % 2
        away = lax.dynamic_index_in_dim(held, 1 - mine, 1, keepdims=False).astype(bf16)
        kept = lax.dynamic_index_in_dim(held, mine, 1, keepdims=False)
        came = lax.ppermute(away, "seq", [(s, s ^ bit) for s in range(count)])
        held = kept.astype(f32) + came.astype(f32)
    return held.reshape(rows, columns)


def passed_along(value, axis, steps):
    count = lax.axis_size(axis)
    leading, last = (max(0, -steps), min(count, count - steps))
    return lax.ppermute(value, axis, [(source, source + steps) for source in range(leading, last)])


def rms_gain(values, gain_row):
    return values * lax.rsqrt(jnp.mean(values * values, axis=-1, keepdims=True) + 1e-06) * gain_row


def rms_floor(values, gain_row):
    return (
        values
        * lax.rsqrt(jnp.maximum(jnp.mean(values * values, axis=-1, keepdims=True), 0.1))
        * gain_row
    )


def norm_three(raw_proj, gains_small, step_rank):
    state_width = (raw_proj.shape[1] - step_rank) // 2
    step_norm = rms_gain(raw_proj[:, :step_rank], gains_small[:step_rank])
    input_norm = rms_floor(
        raw_proj[:, step_rank : step_rank + state_width],
        gains_small[step_rank : step_rank + state_width],
    )
    output_norm = rms_floor(
        raw_proj[:, step_rank + state_width :], gains_small[step_rank + state_width :]
    )
    return (step_norm, input_norm, output_norm)


def doc_number(places, bounds):
    return (places >= bounds[0]).astype(jnp.int32) + (places >= bounds[1]).astype(jnp.int32)


def conv_masks(places, bounds):
    own_doc = doc_number(places, bounds)
    mask_rows = []
    for offset in range(4):
        source = places - (3 - offset)
        mask_rows.append(((source >= 0) & (doc_number(source, bounds) == own_doc)).astype(f32))
    return jnp.stack(mask_rows, 0)


def conv_silu(extended, kernel, tap_masks):
    length = tap_masks.shape[1]
    summed = kernel[4]
    for offset in range(4):
        summed = (
            summed
            + kernel[offset] * extended[offset : offset + length] * tap_masks[offset][:, None]
        )
    return jax.nn.silu(summed)


def gating(scan_out, gate_pre):
    return scan_out * jax.nn.silu(gate_pre)


def swiglu(gate_up):
    return jax.nn.silu(gate_up[:, 0]) * gate_up[:, 1]


def local(
    seq_count,
    ch_count,
    stream,
    doc_bounds,
    norm_gains,
    w_in,
    chan_vectors,
    decay_logs,
    w_x,
    small_gains,
    w_dt,
    w_out,
    w_gate_up,
    w_down,
    cotangent,
):
    tok_rows, width = stream.shape
    step_rank = w_dt.shape[0]
    states, channels = decay_logs.shape
    first_row = lax.axis_index("seq") * tok_rows
    places = first_row + jnp.arange(tok_rows, dtype=jnp.int32)
    tap_masks = conv_masks(places, doc_bounds)
    resets = ((places == doc_bounds[0]) | (places == doc_bounds[1])).astype(f32) * RESET

    stream_in = stream.astype(f32)
    normed_one, norm_one_back = jax.vjp(rms_gain, stream_in, norm_gains[0])
    normed_low = normed_one.astype(bf16)
    in_proj = jnp.einsum("td,dke->tke", normed_low, w_in, preferred_element_type=f32).astype(bf16)
    conv_in = in_proj[:, 0]
    gate_pre = in_proj[:, 1].astype(f32)
    rim_rows = passed_along(conv_in[tok_rows - 3 :], "seq", 1)
    extended = jnp.concatenate([rim_rows, conv_in], 0).astype(f32)
    conv_out, conv_back = jax.vjp(
        functools.partial(conv_silu, tap_masks=tap_masks), extended, chan_vectors[:5]
    )
    conv_low = conv_out.astype(bf16)
    conv_used = conv_low.astype(f32)
    raw_proj = small_sum(
        jnp.dot(conv_low, w_x, preferred_element_type=f32), "ch", ch_count, 0, "raw_sum"
    )
    (step_norm, input_norm, output_norm), norm_three_back = jax.vjp(
        functools.partial(norm_three, step_rank=step_rank), raw_proj, small_gains
    )
    step_low = step_norm.astype(bf16)
    step_pre = jnp.dot(step_low, w_dt, preferred_element_type=f32) + chan_vectors[5]
    step_size = jax.nn.softplus(step_pre)
    step_reset = step_size + resets[:, None]
    decay_rate = -jnp.exp(decay_logs)
    rate_two = decay_rate * LOG2E
    drive_term = step_size * conv_used
    into = jnp.broadcast_to(input_norm[:, :, None], (tok_rows, states, 128))
    out_of = jnp.broadcast_to(output_norm[:, :, None], (tok_rows, states, 128))
    step_total = jnp.broadcast_to(jnp.sum(step_reset, axis=0)[None], (8, channels))

    end_state = ahead_end(step_reset, drive_term, into, rate_two)
    incoming = chain(end_state, step_total, rate_two, True, seq_count, 1, "chain_ahead")
    scanned, before, last_state = ahead(
        step_reset, drive_term, into, out_of, rate_two, incoming
    )
    scan_out = scanned + chan_vectors[6] * conv_used
    gated_out, gate_back = jax.vjp(gating, scan_out, gate_pre)
    gated_low = gated_out.astype(bf16)
    mixer_out = four_sum(
        jnp.dot(gated_low, w_out, preferred_element_type=f32).astype(bf16), 2, "mixer_sum"
    ).astype(f32)
    middle = stream_in + mixer_out
    normed_two, norm_two_back = jax.vjp(rms_gain, middle, norm_gains[1])
    normed_two_low = normed_two.astype(bf16)
    gate_up = jnp.einsum("td,dkf->tkf", normed_two_low, w_gate_up, preferred_element_type=f32)
    hidden_act, act_back = jax.vjp(swiglu, gate_up)
    hidden_low = hidden_act.astype(bf16)

    grad_out = cotangent.astype(f32)
    hidden_grad = jnp.einsum("td,fd->tf", cotangent, w_down, preferred_element_type=f32)
    (gate_up_grad,) = act_back(hidden_grad)
    gate_up_low = gate_up_grad.astype(bf16)
    normed_two_part = jnp.einsum(
        "tkf,dkf->td", gate_up_low, w_gate_up, preferred_element_type=f32
    )
    normed_two_grad = four_sum(normed_two_part.astype(bf16), 3, "normed_two_sum").astype(f32)
    grad_gate_up = jnp.dot(
        normed_two_low.T, gate_up_low.reshape(tok_rows, -1), preferred_element_type=f32
    )
    grad_down = jnp.dot(hidden_low.T, cotangent, preferred_element_type=f32)
    gate_up_part = grads_scattered(grad_gate_up, seq_count)
    down_part = grads_scattered(grad_down, seq_count)
    middle_part, gain_two_grad = norm_two_back(normed_two_grad)
    middle_grad = grad_out + middle_part
    middle_low = middle_grad.astype(bf16)
    gated_grad = jnp.einsum("td,ed->te", middle_low, w_out, preferred_element_type=f32)
    scan_grad, gate_pre_grad = gate_back(gated_grad)
    grad_out_proj = jnp.dot(gated_low.T, middle_low, preferred_element_type=f32)
    out_part = grads_scattered(grad_out_proj, seq_count)
    gate_pre_low = gate_pre_grad.astype(bf16)
    gate_in_part = grads_scattered(
        jnp.dot(normed_low.T, gate_pre_low, preferred_element_type=f32), seq_count
    )

    left_total = back_end(step_reset, scan_grad, out_of, rate_two)
    returning = chain(left_total, step_total, rate_two, False, seq_count, 4, "chain_back")
    decay_rows, push_rows, into_wide, out_wide, rate_sum = back(
        step_reset, drive_term, scan_grad, into, out_of, rate_two, before, last_state, returning
    )

    feed_part = jnp.dot(hidden_low, w_down, preferred_element_type=f32)
    feed_out = four_sum(feed_part.astype(bf16), 5, "feed_sum").astype(f32)
    result = middle + feed_out
    squares = jnp.stack(
        [jnp.sum(result * result), jnp.sum(mixer_out * mixer_out), jnp.sum(feed_out * feed_out)]
    )
    out_rows_all = result.astype(bf16)

    step_grads = LN2 * decay_rows + push_rows * conv_used
    conv_total = push_rows * step_size + chan_vectors[6] * scan_grad
    skip_grad = jnp.sum(scan_grad * conv_used, axis=0)
    step_pre_low = (step_grads * jax.nn.sigmoid(step_pre)).astype(bf16)
    bias_grad = jnp.sum(step_pre_low.astype(f32), axis=0)
    step_norm_part = jnp.einsum("te,re->tr", step_pre_low, w_dt, preferred_element_type=f32)
    norm_grads = small_sum(
        jnp.concatenate(
            [step_norm_part, jnp.sum(into_wide, axis=-1), jnp.sum(out_wide, axis=-1)], 1
        ),
        "ch",
        ch_count,
        6,
        "norm_grads_sum",
    )
    raw_grad, small_grad = norm_three_back(
        (
            norm_grads[:, :step_rank],
            norm_grads[:, step_rank : step_rank + states],
            norm_grads[:, step_rank + states :],
        )
    )
    raw_low = raw_grad.astype(bf16)
    conv_total = conv_total + jnp.einsum("tk,ek->te", raw_low, w_x, preferred_element_type=f32)
    extended_grad, kernel_grad = conv_back(conv_total)
    edge_grad = passed_along(extended_grad[:3], "seq", -1)
    conv_in_grad = extended_grad[3:].at[tok_rows - 3 :].add(edge_grad)
    conv_in_low = conv_in_grad.astype(bf16)
    conv_in_part = grads_scattered(
        jnp.dot(normed_low.T, conv_in_low, preferred_element_type=f32), seq_count
    )
    normed_one_part = jnp.einsum(
        "tke,dke->td",
        jnp.stack([conv_in_low, gate_pre_low], 1),
        w_in,
        preferred_element_type=f32,
    )
    normed_one_grad = four_sum(normed_one_part.astype(bf16), 7, "normed_one_sum").astype(f32)
    stream_part, gain_one_grad = norm_one_back(normed_one_grad)
    stream_grad = middle_grad + stream_part

    grad_x = jnp.dot(conv_low.T, raw_low, preferred_element_type=f32)
    grad_dt = jnp.dot(step_pre_low.T, step_low, preferred_element_type=f32)
    small_rows = jnp.concatenate(
        [rate_sum * decay_rate, kernel_grad, bias_grad[None], skip_grad[None]], 0
    )
    narrow = step_rank + grad_x.shape[1] + small_rows.shape[0]
    padding = -narrow % 128
    columns_all = jnp.concatenate(
        [grad_x, grad_dt, small_rows.T, jnp.zeros((channels, padding), f32)], 1
    )

    def as_row(values):
        return jnp.pad(values, (0, width - values.shape[0]))[None]

    flat = jnp.concatenate(
        [
            gain_one_grad[None],
            gain_two_grad[None],
            as_row(small_grad),
            as_row(squares),
            jnp.zeros((4, width), f32),
        ],
        0,
    )
    own, flat_total = last_sums(columns_all, flat, seq_count, 8, "last_sums")
    at = grad_x.shape[1]
    x_part = own[:, :at]
    dt_part = own[:, at : at + step_rank].T
    at += step_rank
    decay_out = own[:, at : at + states].T
    at += states
    chan_part = own[:, at : at + 7].T
    me = lax.axis_index("seq")
    gains_part = lax.dynamic_slice_in_dim(
        flat_total[:2], me * (width // seq_count), width // seq_count, 1
    )
    small_width = small_gains.shape[0] // seq_count
    small_part = lax.dynamic_slice_in_dim(flat_total[2], me * small_width, small_width, 0)
    rms_values = jnp.sqrt(flat_total[3, :3] / (tok_rows * seq_count * width))
    in_part = jnp.stack([conv_in_part, gate_in_part], 1)
    return (
        out_rows_all,
        stream_grad,
        gains_part,
        in_part,
        chan_part,
        decay_out,
        x_part,
        small_part,
        dt_part,
        out_part,
        gate_up_part.reshape(gate_up_part.shape[0], 2, -1),
        down_part,
        rms_values,
    )


def solution(mesh):
    in_specs = (
        P("seq", None),
        P(),
        P(),
        P(None, None, "ch"),
        P(None, "ch"),
        P(None, "ch"),
        P("ch", None),
        P(),
        P(None, "ch"),
        P("ch", None),
        P(None, None, "ch"),
        P("ch", None),
        P("seq", None),
    )
    out_specs = (
        P("seq", None),
        P("seq", None),
        P(None, "seq"),
        P("seq", None, "ch"),
        P(None, ("ch", "seq")),
        P(None, ("ch", "seq")),
        P(("ch", "seq"), None),
        P("seq"),
        P(None, ("ch", "seq")),
        P(("ch", "seq"), None),
        P("seq", None, "ch"),
        P(("ch", "seq"), None),
        P(),
    )
    return jax.shard_map(
        functools.partial(local, mesh.shape["seq"], mesh.shape["ch"]),
        mesh=mesh,
        in_specs=in_specs,
        out_specs=out_specs,
        check_vma=False,
    )
```

```python
import functools
import math

import jax
import jax.numpy as jnp
from jax import lax
from jax.experimental import pallas as pl
from jax.experimental.pallas import tpu as pltpu
from jax.sharding import PartitionSpec as P

f32 = jnp.float32
bf16 = jnp.bfloat16
LOG2E = math.log2(math.e)
LN2 = math.log(2.0)
RESET = 1e30
UNROLL = 8
LANES = 256
VMEM = pl.BlockSpec(memory_space=pltpu.VMEM)


def shape_of(*dims, dtype=f32):
    return jax.ShapeDtypeStruct(dims, dtype)


def cost(us):
    return pl.CostEstimate(flops=int(us * 1e9), bytes_accessed=int(us * 1e6), transcendentals=0)


def widened(column, width):
    return jnp.concatenate([column] * (width // 128), 1)


def folded(values):
    total = values[:, :128]
    for part in range(1, values.shape[1] // 128):
        total = total + values[:, part * 128 : (part + 1) * 128]
    return total


def ahead_end_kernel(step, drive, into, rate, end):
    tokens, width = step.shape
    rates = rate[...]

    def body(index, state):
        first = pl.multiple_of(index * UNROLL, UNROLL)
        steps = step[pl.ds(first, UNROLL), :]
        drives = drive[pl.ds(first, UNROLL), :]
        for k in range(UNROLL):
            decay = jnp.exp2(steps[k : k + 1] * rates)
            state = decay * state + widened(into[first + k], width) * drives[k : k + 1]
        return state

    end[...] = lax.fori_loop(0, tokens // UNROLL, body, jnp.zeros_like(rates))


def ahead_kernel(step, drive, into, out_of, rate, start, scanned, before, end):
    tokens, width = step.shape
    rates = rate[...]

    def body(index, state):
        first = pl.multiple_of(index * UNROLL, UNROLL)
        steps = step[pl.ds(first, UNROLL), :]
        drives = drive[pl.ds(first, UNROLL), :]
        rows = []
        for k in range(UNROLL):
            before[first + k] = state
            decay = jnp.exp2(steps[k : k + 1] * rates)
            state = decay * state + widened(into[first + k], width) * drives[k : k + 1]
            rows.append(
                jnp.sum(widened(out_of[first + k], width) * state, axis=0, keepdims=True)
            )
        scanned[pl.ds(first, UNROLL), :] = jnp.concatenate(rows, 0)
        return state

    end[...] = lax.fori_loop(0, tokens // UNROLL, body, start[...])


def back_end_kernel(step, grad, out_of, rate, end):
    tokens, width = step.shape
    rates = rate[...]

    def body(index, carried):
        first = pl.multiple_of(tokens - UNROLL - index * UNROLL, UNROLL)
        steps = step[pl.ds(first, UNROLL), :]
        grads = grad[pl.ds(first, UNROLL), :]
        for k in reversed(range(UNROLL)):
            decay = jnp.exp2(steps[k : k + 1] * rates)
            carried = decay * (widened(out_of[first + k], width) * grads[k : k + 1] + carried)
        return carried

    end[...] = lax.fori_loop(0, tokens // UNROLL, body, jnp.zeros_like(rates))


def back_kernel(
    step, drive, grad, into, out_of, rate, before, end, start,
    decay_rows, push_rows, into_wide, out_wide, rate_sum,
):
    tokens, width = step.shape
    rates = rate[...]

    @pl.when(pl.program_id(0) == 0)
    def _():
        into_wide[...] = jnp.zeros_like(into_wide)
        out_wide[...] = jnp.zeros_like(out_wide)

    def body(index, carry):
        carried, state, total = carry
        first = pl.multiple_of(tokens - UNROLL - index * UNROLL, UNROLL)
        steps = step[pl.ds(first, UNROLL), :]
        drives = drive[pl.ds(first, UNROLL), :]
        grads = grad[pl.ds(first, UNROLL), :]
        decay_list, push_list = [None] * UNROLL, [None] * UNROLL
        for k in reversed(range(UNROLL)):
            place = first + k
            grad_row = grads[k : k + 1]
            decay = jnp.exp2(steps[k : k + 1] * rates)
            adjoint = widened(out_of[place], width) * grad_row + carried
            carried = decay * adjoint
            out_wide[place] = out_wide[place] + folded(state * grad_row)
            into_wide[place] = into_wide[place] + folded(adjoint * drives[k : k + 1])
            state = before[place]
            share = carried * state
            total = total + share * steps[k : k + 1]
            decay_list[k] = jnp.sum(share * rates, axis=0, keepdims=True)
            push_list[k] = jnp.sum(widened(into[place], width) * adjoint, axis=0, keepdims=True)
        decay_rows[pl.ds(first, UNROLL), :] = jnp.concatenate(decay_list, 0)
        push_rows[pl.ds(first, UNROLL), :] = jnp.concatenate(push_list, 0)
        return (carried, state, total)

    _, _, total = lax.fori_loop(
        0, tokens // UNROLL, body, (start[...], end[...], jnp.zeros_like(rates))
    )
    rate_sum[...] = total


def scan_specs(tokens, states):
    return (
        pl.BlockSpec((tokens, LANES), lambda j: (0, j)),
        pl.BlockSpec((states, LANES), lambda j: (0, j)),
        pl.BlockSpec((tokens, states, 128), lambda j: (0, 0, 0)),
        pl.BlockSpec((tokens, states, LANES), lambda j: (0, 0, j)),
    )


def scan_call(kernel, name, us, channels, in_specs, out_specs, out_shape):
    return pl.pallas_call(
        kernel,
        grid=(channels // LANES,),
        in_specs=in_specs,
        out_specs=out_specs,
        out_shape=out_shape,
        compiler_params=pltpu.CompilerParams(vmem_limit_bytes=48 * 2**20),
        cost_estimate=cost(us),
        name=name,
    )


def ahead_end(step, drive, into, rate):
    (tokens, channels), states = step.shape, rate.shape[0]
    row, st, col, _ = scan_specs(tokens, states)
    return scan_call(
        ahead_end_kernel, "ahead_end", 5, channels, [row, row, col, st], st,
        shape_of(states, channels),
    )(step, drive, into, rate)


def ahead(step, drive, into, out_of, rate, start):
    (tokens, channels), states = step.shape, rate.shape[0]
    row, st, col, hist = scan_specs(tokens, states)
    return scan_call(
        ahead_kernel, "ahead", 10, channels, [row, row, col, col, st, st], [row, hist, st],
        [shape_of(tokens, channels), shape_of(tokens, states, channels), shape_of(states, channels)],
    )(step, drive, into, out_of, rate, start)


def back_end(step, grad, out_of, rate, ties=()):
    (tokens, channels), states = step.shape, rate.shape[0]
    row, st, col, _ = scan_specs(tokens, states)
    return scan_call(
        tied(back_end_kernel, 4, len(ties)), "back_end", 5, channels,
        [row, row, col, st] + [ANY] * len(ties), st, shape_of(states, channels),
    )(step, grad, out_of, rate, *ties)


def back(step, drive, grad, into, out_of, rate, before, end, start):
    (tokens, channels), states = step.shape, rate.shape[0]
    row, st, col, hist = scan_specs(tokens, states)
    wide = shape_of(tokens, states, 128)
    rows = shape_of(tokens, channels)
    return scan_call(
        back_kernel, "back", 16, channels,
        [row, row, row, col, col, st, hist, st, st], [row, row, col, col, st],
        [rows, rows, wide, wide, shape_of(states, channels)],
    )(step, drive, grad, into, out_of, rate, before, end, start)


ANY = pl.BlockSpec(memory_space=pl.ANY)


def tied(kernel, ins, ties):
    def body(*refs):
        return kernel(*refs[:ins], *refs[ins + ties :])

    return body


def met(axis, partners):
    barrier = pltpu.get_barrier_semaphore()
    for partner in partners:
        pl.semaphore_signal(
            barrier, inc=1, device_id={axis: partner}, device_id_type=pl.DeviceIdType.MESH
        )
    pl.semaphore_wait(barrier, len(partners))


def sent(source, target, sends, receives, slot, axis, partner):
    copy = pltpu.make_async_remote_copy(
        src_ref=source,
        dst_ref=target,
        send_sem=sends.at[slot],
        recv_sem=receives.at[slot],
        device_id={axis: partner},
        device_id_type=pl.DeviceIdType.MESH,
    )
    copy.start()
    return copy


def bits_of(count):
    return [1 << k for k in range(count.bit_length() - 1)]


def flipped(me, bit):
    mine = lax.rem(me // bit, 2)
    return mine, me + bit - 2 * bit * mine


def exchange_params(ident):
    return pltpu.CompilerParams(
        collective_id=ident, has_side_effects=True, vmem_limit_bytes=32 * 2**20
    )


def small_sum_kernel(axis, bits, value, total, moving, landed, sends, receives):
    me = lax.axis_index(axis)
    met(axis, [flipped(me, bit)[1] for bit in bits])
    moving[0] = value[...]
    for k, bit in enumerate(bits):
        _, partner = flipped(me, bit)
        copy = sent(moving.at[k], landed.at[k], sends, receives, k, axis, partner)
        copy.wait()
        if k + 1 < len(bits):
            moving[k + 1] = moving[k] + landed[k]
        else:
            total[...] = moving[k] + landed[k]


def small_sum(value, axis, count, ident, name, ties=()):
    bits = bits_of(count)
    slots = pltpu.VMEM((len(bits),) + value.shape, f32)
    return pl.pallas_call(
        tied(functools.partial(small_sum_kernel, axis, bits), 1, len(ties)),
        out_shape=shape_of(*value.shape),
        in_specs=[VMEM] + [ANY] * len(ties),
        out_specs=VMEM,
        scratch_shapes=[slots, slots] + [pltpu.SemaphoreType.DMA((len(bits),))] * 2,
        compiler_params=exchange_params(ident),
        cost_estimate=cost(7),
        name=name,
    )(value, *ties)


def four_sum_kernel(value, total, first, second, moving, sends, receives):
    me = lax.axis_index("ch")
    low, across = flipped(me, 1)
    high, along = flipped(me, 2)
    met("ch", [across, along])
    sent(value.at[:, 1 - low], first, sends, receives, 0, "ch", across).wait()
    moving[...] = (
        value[1 - high, low].astype(f32) + first[1 - high].astype(f32)
    ).astype(bf16)
    copy = sent(moving, second, sends, receives, 1, "ch", along)
    kept = value[high, low].astype(f32) + first[high].astype(f32)
    copy.wait()
    total[high, low] = (kept + second[...].astype(f32)).astype(bf16)
    sent(total.at[high, low], total.at[high, low], sends, receives, 2, "ch", along).wait()
    sent(total.at[:, low], total.at[:, low], sends, receives, 3, "ch", across).wait()


def four_sum(value, ident, name, ties=()):
    rows, columns = value.shape
    part = rows // 4
    result = pl.pallas_call(
        tied(four_sum_kernel, 1, len(ties)),
        out_shape=shape_of(2, 2, part, columns, dtype=bf16),
        in_specs=[VMEM] + [ANY] * len(ties),
        out_specs=VMEM,
        scratch_shapes=[
            pltpu.VMEM((2, part, columns), bf16),
            pltpu.VMEM((part, columns), bf16),
            pltpu.VMEM((part, columns), bf16),
            pltpu.SemaphoreType.DMA((4,)),
            pltpu.SemaphoreType.DMA((4,)),
        ],
        compiler_params=exchange_params(ident),
        cost_estimate=cost(14),
        name=name,
    )(value.reshape(2, 2, part, columns), *ties)
    return result.reshape(rows, columns)


def chain_kernel(forward, bits, state, steps, rate, arriving, moving, landed, sends, receives):
    me = lax.axis_index("seq")
    states = state.shape[0]
    met("seq", [flipped(me, bit)[1] for bit in bits])
    rates = rate[...]
    all_state, all_steps = state[...], steps[...]
    mine_state, mine_steps = jnp.zeros_like(all_state), jnp.zeros_like(all_steps)
    for k, bit in enumerate(bits):
        mine, partner = flipped(me, bit)
        moving[k, :states] = all_state
        moving[k, states:] = all_steps
        sent(moving.at[k], landed.at[k], sends, receives, k, "seq", partner).wait()
        other_state, other_steps = landed[k, :states], landed[k, states:]
        earlier = (mine == 1) if forward else (mine == 0)
        through = jnp.exp2(rates * mine_steps[:1])
        mine_state = jnp.where(earlier, mine_state + through * other_state, mine_state)
        mine_steps = jnp.where(earlier, mine_steps + other_steps, mine_steps)
        after = jnp.exp2(rates * all_steps[:1]) * other_state + all_state
        ahead_of = jnp.exp2(rates * other_steps[:1]) * all_state + other_state
        all_state = jnp.where(earlier, after, ahead_of)
        all_steps = all_steps + other_steps
    arriving[...] = mine_state


def chain(state, step_total, rate, forward, count, ident, name):
    bits = bits_of(count)
    states, channels = state.shape
    slots = pltpu.VMEM((len(bits), states + 8, channels), f32)
    return pl.pallas_call(
        functools.partial(chain_kernel, forward, bits),
        out_shape=shape_of(states, channels),
        in_specs=[VMEM] * 3,
        out_specs=VMEM,
        scratch_shapes=[slots, slots] + [pltpu.SemaphoreType.DMA((len(bits),))] * 2,
        compiler_params=exchange_params(ident),
        cost_estimate=cost(14),
        name=name,
    )(state, step_total, rate)


def last_sums_kernel(bits, parts, flat, own, flat_total, *rest):
    me = lax.axis_index("seq")
    levels = len(bits)
    works, rest = rest[:levels], rest[levels:]
    lows, rest = rest[:levels], rest[levels:]
    lands, rest = rest[:levels], rest[levels:]
    moving, landed, sends, receives, flat_sends, flat_receives = rest
    met("seq", [flipped(me, bit)[1] for bit in bits])
    moving[0] = flat[...]
    for k, bit in enumerate(bits):
        mine, partner = flipped(me, bit)
        source = parts if k == 0 else works[k - 1]
        lows[k][...] = source[:, 1 - mine].astype(bf16)
        copy = sent(lows[k], lands[k], sends, receives, k, "seq", partner)
        flat_copy = sent(moving.at[k], landed.at[k], flat_sends, flat_receives, k, "seq", partner)
        copy.wait()
        summed = source[:, mine] + lands[k][...].astype(f32)
        if k + 1 < levels:
            works[k][...] = summed.reshape(works[k].shape)
        else:
            own[...] = summed.reshape(own.shape)
        flat_copy.wait()
        if k + 1 < levels:
            moving[k + 1] = moving[k] + landed[k]
        else:
            flat_total[...] = moving[k] + landed[k]


def last_sums(parts, flat, count, ident, name, ties=()):
    bits = bits_of(count)
    levels = len(bits)
    rows, columns = parts.shape[0] // count, parts.shape[1]
    halves = [count >> (k + 1) for k in range(levels)]
    works = [pltpu.VMEM((max(half // 2, 1), 2 if half > 1 else 1, rows, columns), f32) for half in halves]
    lows = [pltpu.VMEM((half, rows, columns), bf16) for half in halves]
    slots = pltpu.VMEM((levels,) + flat.shape, f32)
    sems = [pltpu.SemaphoreType.DMA((levels,))] * 4
    return pl.pallas_call(
        tied(functools.partial(last_sums_kernel, bits), 2, len(ties)),
        out_shape=[shape_of(rows, columns), shape_of(*flat.shape)],
        in_specs=[VMEM] * 2 + [ANY] * len(ties),
        out_specs=[VMEM] * 2,
        scratch_shapes=works + lows + lows + [slots, slots] + sems,
        compiler_params=exchange_params(ident),
        cost_estimate=cost(20),
        name=name,
    )(parts.reshape(count // 2, 2, rows, columns), flat, *ties)


def swapped(value, bit, count):
    return lax.ppermute(value, "seq", [(s, s ^ bit) for s in range(count)])


def side(columns, mine, count):
    rows, width = columns.shape
    part = width // count
    blocks = [columns[:, k * part : (k + 1) * part] for k in range(count)]
    return jnp.where(
        mine == 0, jnp.concatenate(blocks[::2], 1), jnp.concatenate(blocks[1::2], 1)
    )


class Scattered:
    def __init__(self, half, count):
        self.count = count
        self.bits = bits_of(count)[1:]
        self.held = half
        self.left = count // 2
        self.step = 0

    def go(self):
        bit = self.bits[self.step]
        self.step += 1
        self.left //= 2
        rows = self.held.reshape(-1, self.held.shape[-1]).shape[0] // (2 * self.left)
        held = self.held.reshape(self.left, 2, rows, self.held.shape[-1])
        mine = (lax.axis_index("seq") // bit) % 2
        self.away = lax.dynamic_index_in_dim(held, 1 - mine, 1, keepdims=False).astype(bf16)
        self.kept = lax.dynamic_index_in_dim(held, mine, 1, keepdims=False)
        self.came = swapped(self.away, bit, self.count)
        self.held = self.kept.astype(f32) + self.came.astype(f32)
        return self.away

    def rest(self):
        while self.step < len(self.bits):
            self.go()
        return self.held.reshape(-1, self.held.shape[-1])


def paired(own_left, own_right, came_left, came_right, count):
    half = jnp.dot(own_left.T, own_right, preferred_element_type=f32) + jnp.dot(
        came_left.T, came_right, preferred_element_type=f32
    )
    return Scattered(half, count)


CHUNK = 32


def sigmoid(values):
    return 1.0 / (1.0 + jnp.exp(-values))


def softplus(values):
    return jnp.maximum(values, 0.0) + jnp.log1p(jnp.exp(-jnp.abs(values)))


def row_doc(places, bounds):
    return (places >= bounds[0]).astype(jnp.int32) + (places >= bounds[1]).astype(jnp.int32)


def tap_mask(places, bounds, offset):
    source = places - offset
    same = row_doc(source, bounds) == row_doc(places, bounds)
    return jnp.where((source >= 0) & same, 1.0, 0.0)


def mean_square(values):
    return jnp.mean(values * values, axis=-1, keepdims=True)


def three_norms(raw, gains, rank, states):
    low, mid, high = raw[:, :rank], raw[:, rank : rank + states], raw[:, rank + states :]
    low_scale = lax.rsqrt(mean_square(low) + 1e-06)
    mid_scale = lax.rsqrt(jnp.maximum(mean_square(mid), 0.1))
    high_scale = lax.rsqrt(jnp.maximum(mean_square(high), 0.1))
    return (
        low * low_scale * gains[:, :rank],
        mid * mid_scale * gains[:, rank : rank + states],
        high * high_scale * gains[:, rank + states :],
    )


def widen(values, wide, first, count):
    states = values.shape[1]
    eye = (
        lax.broadcasted_iota(jnp.int32, (states, states), 0)
        == lax.broadcasted_iota(jnp.int32, (states, states), 1)
    ).astype(f32)
    spread = jnp.sum(values[:, None, :] * eye[None], axis=-1, keepdims=True)
    wide[pl.ds(first, count)] = jnp.broadcast_to(spread, (count, states, 128))


def greeted(axis_partners):
    barrier = pltpu.get_barrier_semaphore()
    for axis, partner in axis_partners:
        pl.semaphore_signal(
            barrier, inc=1, device_id={axis: partner}, device_id_type=pl.DeviceIdType.MESH
        )
    pl.semaphore_wait(barrier, len(axis_partners))


def chained(forward, bits, state, steps, rates, moving, landed, sends, receives, base):
    me = lax.axis_index("seq")
    states = state.shape[0]
    all_state, all_steps = state, steps
    mine_state, mine_steps = jnp.zeros_like(all_state), jnp.zeros_like(all_steps)
    for k, bit in enumerate(bits):
        mine, partner = flipped(me, bit)
        moving[k, :states] = all_state
        moving[k, states:] = all_steps
        sent(moving.at[k], landed.at[k], sends, receives, base + k, "seq", partner).wait()
        other_state, other_steps = landed[k, :states], landed[k, states:]
        earlier = (mine == 1) if forward else (mine == 0)
        through = jnp.exp2(rates * mine_steps[:1])
        mine_state = jnp.where(earlier, mine_state + through * other_state, mine_state)
        mine_steps = jnp.where(earlier, mine_steps + other_steps, mine_steps)
        after = jnp.exp2(rates * all_steps[:1]) * other_state + all_state
        ahead_of = jnp.exp2(rates * other_steps[:1]) * all_state + other_state
        all_state = jnp.where(earlier, after, ahead_of)
        all_steps = all_steps + other_steps
    return mine_state


def forward_kernel(
    bits, bounds, proj, chan, logs, w_x, gains, w_dt, w_out,
    halo, pre_out, low_out, raw_out, step_pre_out, into, out_of, scan_out, gated_out, last_state,
    mixer, hist_out,
    extended, raw_move, raw_land, step, drive, starts, moving, landed, part, first_land,
    second_move, second_land, hist, sends, receives, hist_sem,
):
    tokens, channels = proj.shape[1:]
    rank, states = w_dt.shape[0], logs.shape[0]
    chunks = tokens // CHUNK
    ch_me, me = lax.axis_index("ch"), lax.axis_index("seq")
    seq_count = 1 << len(bits)
    low, across = flipped(ch_me, 1)
    high, along = flipped(ch_me, 2)
    following, previous = lax.rem(me + 1, seq_count), lax.rem(me + seq_count - 1, seq_count)
    greeted(
        [("ch", across), ("ch", along), ("seq", following), ("seq", previous)]
        + [("seq", flipped(me, bit)[1]) for bit in bits]
    )
    halo_copy = sent(
        proj.at[0, pl.ds(tokens - 16, 16)], halo, sends, receives, 0, "seq", following
    )
    rates = -jnp.exp(logs[...]) * LOG2E
    halo_copy.wait()
    extended[0:16] = halo[...].astype(f32)

    def spread(index, _):
        first = pl.multiple_of(index * CHUNK, CHUNK)
        extended[pl.ds(first + 16, CHUNK)] = proj[0, pl.ds(first, CHUNK)].astype(f32)
        return 0

    lax.fori_loop(0, chunks, spread, 0)

    def convolved(index, _):
        first = pl.multiple_of(index * CHUNK, CHUNK)
        places = me * tokens + first + lax.broadcasted_iota(jnp.int32, (CHUNK, 128), 0)
        window = extended[pl.ds(first, CHUNK + 16)]
        summed = chan[4:5]
        for k in range(4):
            mask = widened(tap_mask(places, bounds, 3 - k), channels)
            summed = summed + chan[k : k + 1] * window[13 + k : 13 + k + CHUNK] * mask
        pre_out[pl.ds(first, CHUNK)] = summed
        low_out[pl.ds(first, CHUNK)] = (summed * sigmoid(summed)).astype(bf16)
        return 0

    lax.fori_loop(0, chunks, convolved, 0)
    raw_move[0] = jnp.dot(low_out[...], w_x[...], preferred_element_type=f32)
    sent(raw_move.at[0], raw_land.at[0], sends, receives, 1, "ch", across).wait()
    raw_move[1] = raw_move[0] + raw_land[0]
    sent(raw_move.at[1], raw_land.at[1], sends, receives, 2, "ch", along).wait()

    def stepped(index, total):
        first = pl.multiple_of(index * CHUNK, CHUNK)
        rows = pl.ds(first, CHUNK)
        raw = raw_move[1, rows] + raw_land[1, rows]
        raw_out[rows] = raw
        step_norm, input_norm, output_norm = three_norms(raw, gains[...], rank, states)
        widen(input_norm, into, first, CHUNK)
        widen(output_norm, out_of, first, CHUNK)
        pre = (
            jnp.dot(step_norm.astype(bf16), w_dt[...], preferred_element_type=f32) + chan[5:6]
        )
        step_pre_out[rows] = pre
        size = softplus(pre)
        drive[rows] = size * low_out[rows].astype(f32)
        places = me * tokens + first + lax.broadcasted_iota(jnp.int32, (CHUNK, 128), 0)
        resets = jnp.where((places == bounds[0]) | (places == bounds[1]), RESET, 0.0)
        size = size + widened(resets, channels)
        step[rows] = size
        return total + jnp.sum(size, axis=0, keepdims=True)

    total = lax.fori_loop(0, chunks, stepped, jnp.zeros((1, channels), f32))
    blocks = [slice(j, j + LANES) for j in range(0, channels, LANES)]
    for lanes in blocks:
        block_rates = rates[:, lanes]

        def ended(index, state, lanes=lanes, block_rates=block_rates):
            first = pl.multiple_of(index * UNROLL, UNROLL)
            steps, drives = step[pl.ds(first, UNROLL), lanes], drive[pl.ds(first, UNROLL), lanes]
            for k in range(UNROLL):
                decay = jnp.exp2(steps[k : k + 1] * block_rates)
                state = decay * state + widened(into[first + k], LANES) * drives[k : k + 1]
            return state

        starts[:, lanes] = lax.fori_loop(
            0, tokens // UNROLL, ended, jnp.zeros((states, LANES), f32)
        )
    starts[...] = chained(
        True, bits, starts[...], jnp.broadcast_to(total, (8, channels)), rates, moving, landed,
        sends, receives, 7,
    )
    hist_copies = []
    for number, lanes in enumerate(blocks):
        block_rates = rates[:, lanes]
        skip = chan[6:7, lanes]

        def walked(index, state, lanes=lanes, block_rates=block_rates, skip=skip):
            first = pl.multiple_of(index * UNROLL, UNROLL)
            steps, drives = step[pl.ds(first, UNROLL), lanes], drive[pl.ds(first, UNROLL), lanes]
            rows = []
            for k in range(UNROLL):
                hist[first + k, :, lanes] = state
                decay = jnp.exp2(steps[k : k + 1] * block_rates)
                state = decay * state + widened(into[first + k], LANES) * drives[k : k + 1]
                rows.append(
                    jnp.sum(widened(out_of[first + k], LANES) * state, axis=0, keepdims=True)
                )
            scan_out[pl.ds(first, UNROLL), lanes] = jnp.concatenate(rows, 0)
            return state

        last_state[:, lanes] = lax.fori_loop(0, tokens // UNROLL, walked, starts[:, lanes])
        copy = pltpu.make_async_copy(
            hist.at[:, :, lanes], hist_out.at[:, :, lanes], hist_sem.at[number]
        )
        copy.start()
        hist_copies.append(copy)

    def gate(index, _):
        first = pl.multiple_of(index * CHUNK, CHUNK)
        rows = pl.ds(first, CHUNK)
        scanned = scan_out[rows] + chan[6:7] * low_out[rows].astype(f32)
        scan_out[rows] = scanned
        gate_pre = proj[1, rows].astype(f32)
        gated_out[rows] = (scanned * gate_pre * sigmoid(gate_pre)).astype(bf16)
        return 0

    lax.fori_loop(0, chunks, gate, 0)
    quarter = tokens // 4
    width = w_out.shape[1]

    def mixed(index, _):
        first = pl.multiple_of(index * 512, 512)
        product = jnp.dot(
            gated_out[...], w_out[:, pl.ds(first, 512)], preferred_element_type=f32
        ).astype(bf16)
        for k in range(4):
            part[k // 2, k % 2, :, pl.ds(first, 512)] = product[k * quarter : (k + 1) * quarter]
        return 0

    lax.fori_loop(0, width // 512, mixed, 0)
    four_summed(
        part, mixer, first_land, second_land, second_move, sends, receives, 3, low, across, high,
        along,
    )
    for copy in hist_copies:
        copy.wait()


def four_summed(
    value, total, first, second, moving, sends, receives, base, low, across, high, along
):
    sent(value.at[:, 1 - low], first, sends, receives, base, "ch", across).wait()
    moving[...] = (
        value[1 - high, low].astype(f32) + first[1 - high].astype(f32)
    ).astype(bf16)
    copy = sent(moving, second, sends, receives, base + 1, "ch", along)
    kept = value[high, low].astype(f32) + first[high].astype(f32)
    copy.wait()
    total[high, low] = (kept + second[...].astype(f32)).astype(bf16)
    own = total.at[high, low]
    sent(own, own, sends, receives, base + 2, "ch", along).wait()
    both = total.at[:, low]
    sent(both, both, sends, receives, base + 3, "ch", across).wait()


def mixer_forward(bounds, proj, chan, logs, w_x, gains, w_dt, w_out, count, ident):
    bits = bits_of(count)
    _, tokens, channels = proj.shape
    states, rank, width = logs.shape[0], w_dt.shape[0], w_out.shape[1]
    quarter, narrow = tokens // 4, w_x.shape[1]
    rows = shape_of(tokens, channels)
    low_rows = shape_of(tokens, channels, dtype=bf16)
    wide = shape_of(tokens, states, 128)
    slots = pltpu.VMEM((len(bits), states + 8, channels), f32)
    raws = pltpu.VMEM((2, tokens, narrow), f32)
    out = pl.pallas_call(
        functools.partial(forward_kernel, bits),
        out_shape=[
            shape_of(16, channels, dtype=bf16), rows, low_rows, shape_of(tokens, narrow), rows,
            wide, wide, rows, low_rows, shape_of(states, channels),
            shape_of(2, 2, quarter, width, dtype=bf16), shape_of(tokens, states, channels),
        ],
        in_specs=[pl.BlockSpec(memory_space=pltpu.SMEM)] + [VMEM] * 7,
        out_specs=[VMEM] * 11 + [ANY],
        scratch_shapes=[
            pltpu.VMEM((tokens + 16, channels), f32), raws, raws,
            pltpu.VMEM((tokens, channels), f32), pltpu.VMEM((tokens, channels), f32),
            pltpu.VMEM((states, channels), f32), slots, slots,
            pltpu.VMEM((2, 2, quarter, width), bf16), pltpu.VMEM((2, quarter, width), bf16),
            pltpu.VMEM((quarter, width), bf16), pltpu.VMEM((quarter, width), bf16),
            pltpu.VMEM((tokens, states, channels), f32),
            pltpu.SemaphoreType.DMA((7 + len(bits),)), pltpu.SemaphoreType.DMA((7 + len(bits),)),
            pltpu.SemaphoreType.DMA((channels // LANES,)),
        ],
        compiler_params=pltpu.CompilerParams(
            collective_id=ident, has_side_effects=True, vmem_limit_bytes=56 * 2**20
        ),
        cost_estimate=cost(6),
        name="mixer_forward",
    )(bounds, proj, chan, logs, w_x, gains, w_dt, w_out)
    out = list(out)
    out[10] = out[10].reshape(tokens, width)
    return out


def passed_along(value, axis, steps):
    count = lax.axis_size(axis)
    leading, last = (max(0, -steps), min(count, count - steps))
    return lax.ppermute(value, axis, [(source, source + steps) for source in range(leading, last)])


def rms_gain(values, gain_row):
    return values * lax.rsqrt(jnp.mean(values * values, axis=-1, keepdims=True) + 1e-06) * gain_row


def rms_floor(values, gain_row):
    return (
        values
        * lax.rsqrt(jnp.maximum(jnp.mean(values * values, axis=-1, keepdims=True), 0.1))
        * gain_row
    )


def norm_three(raw_proj, gains_small, step_rank):
    state_width = (raw_proj.shape[1] - step_rank) // 2
    step_norm = rms_gain(raw_proj[:, :step_rank], gains_small[:step_rank])
    input_norm = rms_floor(
        raw_proj[:, step_rank : step_rank + state_width],
        gains_small[step_rank : step_rank + state_width],
    )
    output_norm = rms_floor(
        raw_proj[:, step_rank + state_width :], gains_small[step_rank + state_width :]
    )
    return (step_norm, input_norm, output_norm)


def doc_number(places, bounds):
    return (places >= bounds[0]).astype(jnp.int32) + (places >= bounds[1]).astype(jnp.int32)


def conv_masks(places, bounds):
    own_doc = doc_number(places, bounds)
    mask_rows = []
    for offset in range(4):
        source = places - (3 - offset)
        mask_rows.append(((source >= 0) & (doc_number(source, bounds) == own_doc)).astype(f32))
    return jnp.stack(mask_rows, 0)


def conv_silu(extended, kernel, tap_masks):
    length = tap_masks.shape[1]
    summed = kernel[4]
    for offset in range(4):
        summed = (
            summed
            + kernel[offset] * extended[offset : offset + length] * tap_masks[offset][:, None]
        )
    return jax.nn.silu(summed)


def gating(scan_out, gate_pre):
    return scan_out * jax.nn.silu(gate_pre)


def swiglu(gate_up):
    return jax.nn.silu(gate_up[:, 0]) * gate_up[:, 1]


def local(
    seq_count,
    ch_count,
    stream,
    doc_bounds,
    norm_gains,
    w_in,
    chan_vectors,
    decay_logs,
    w_x,
    small_gains,
    w_dt,
    w_out,
    w_gate_up,
    w_down,
    cotangent,
):
    tok_rows, width = stream.shape
    step_rank = w_dt.shape[0]
    states, channels = decay_logs.shape
    first_row = lax.axis_index("seq") * tok_rows
    places = first_row + jnp.arange(tok_rows, dtype=jnp.int32)
    tap_masks = conv_masks(places, doc_bounds)
    resets = ((places == doc_bounds[0]) | (places == doc_bounds[1])).astype(f32) * RESET

    stream_in = stream.astype(f32)
    normed_one, norm_one_back = jax.vjp(rms_gain, stream_in, norm_gains[0])
    normed_low = normed_one.astype(bf16)
    in_proj = jnp.einsum("td,dke->kte", normed_low, w_in, preferred_element_type=f32).astype(bf16)
    (
        halo, pre_conv, conv_low, raw_proj, step_pre, into, out_of, scan_out, gated_low,
        last_state, mixer_low, before,
    ) = mixer_forward(
        doc_bounds, in_proj, chan_vectors, decay_logs, w_x, small_gains[None], w_dt, w_out,
        seq_count, 1,
    )
    gate_pre = in_proj[1].astype(f32)
    extended = jnp.concatenate([halo[13:], in_proj[0]], 0).astype(f32)
    _, conv_back = jax.vjp(
        functools.partial(conv_silu, tap_masks=tap_masks), extended, chan_vectors[:5]
    )
    conv_used = conv_low.astype(f32)
    (step_norm, input_norm, output_norm), norm_three_back = jax.vjp(
        functools.partial(norm_three, step_rank=step_rank), raw_proj, small_gains
    )
    step_low = step_norm.astype(bf16)
    step_size = jax.nn.softplus(step_pre)
    step_reset = step_size + resets[:, None]
    decay_rate = -jnp.exp(decay_logs)
    rate_two = decay_rate * LOG2E
    drive_term = step_size * conv_used
    step_total = jnp.broadcast_to(jnp.sum(step_reset, axis=0)[None], (8, channels))
    _, gate_back = jax.vjp(gating, scan_out, gate_pre)
    mixer_out = mixer_low.astype(f32)
    middle = stream_in + mixer_out
    normed_two, norm_two_back = jax.vjp(rms_gain, middle, norm_gains[1])
    normed_two_low = normed_two.astype(bf16)
    gate_up = jnp.einsum("td,dkf->tkf", normed_two_low, w_gate_up, preferred_element_type=f32)
    hidden_act, act_back = jax.vjp(swiglu, gate_up)
    hidden_low = hidden_act.astype(bf16)

    grad_out = cotangent.astype(f32)
    mine = lax.axis_index("seq") % 2
    sides = functools.partial(side, count=seq_count)
    pair = functools.partial(swapped, bit=1, count=seq_count)
    one_own, one_came = sides(normed_low, mine), pair(sides(normed_low, 1 - mine))
    two_own, two_came = sides(normed_two_low, mine), pair(sides(normed_two_low, 1 - mine))
    gated_own, gated_came = sides(gated_low, mine), pair(sides(gated_low, 1 - mine))
    hidden_own, hidden_came = sides(hidden_low, mine), pair(sides(hidden_low, 1 - mine))
    cotangent_came = pair(cotangent)
    hidden_grad = jnp.einsum("td,fd->tf", cotangent, w_down, preferred_element_type=f32)
    (gate_up_grad,) = act_back(hidden_grad)
    gate_up_low = gate_up_grad.astype(bf16)
    normed_two_part = jnp.einsum(
        "tkf,dkf->td", gate_up_low, w_gate_up, preferred_element_type=f32
    )
    gate_up_flat = gate_up_low.reshape(tok_rows, -1)
    gate_up_came = pair(gate_up_flat)
    down_sum = paired(hidden_own, cotangent, hidden_came, cotangent_came, seq_count)
    down_away = down_sum.go()
    normed_two_grad = four_sum(
        normed_two_part.astype(bf16), 3, "normed_two_sum", ties=[down_away]
    ).astype(f32)
    gate_up_sum = paired(two_own, gate_up_flat, two_came, gate_up_came, seq_count)
    gate_up_away = gate_up_sum.go()
    middle_part, gain_two_grad = norm_two_back(normed_two_grad)
    middle_grad = grad_out + middle_part
    middle_low = middle_grad.astype(bf16)
    middle_came = pair(middle_low)
    gated_grad = jnp.einsum("td,ed->te", middle_low, w_out, preferred_element_type=f32)
    scan_grad, gate_pre_grad = gate_back(gated_grad)
    gate_pre_low = gate_pre_grad.astype(bf16)
    gate_pre_came = pair(gate_pre_low)

    left_total = back_end(
        step_reset, scan_grad, out_of, rate_two, ties=[gate_up_away, gate_pre_low]
    )
    returning = chain(left_total, step_total, rate_two, False, seq_count, 4, "chain_back")
    decay_rows, push_rows, into_wide, out_wide, rate_sum = back(
        step_reset, drive_term, scan_grad, into, out_of, rate_two, before, last_state, returning
    )

    out_sum = paired(gated_own, middle_low, gated_came, middle_came, seq_count)
    out_away = out_sum.go()
    gate_in_sum = paired(one_own, gate_pre_low, one_came, gate_pre_came, seq_count)
    gate_in_away = gate_in_sum.go()
    gate_up_next = gate_up_sum.go()
    down_next = down_sum.go()
    step_grads = LN2 * decay_rows + push_rows * conv_used
    conv_total = push_rows * step_size + chan_vectors[6] * scan_grad
    skip_grad = jnp.sum(scan_grad * conv_used, axis=0)
    step_pre_low = (step_grads * jax.nn.sigmoid(step_pre)).astype(bf16)
    bias_grad = jnp.sum(step_pre_low.astype(f32), axis=0)
    step_norm_part = jnp.einsum("te,re->tr", step_pre_low, w_dt, preferred_element_type=f32)
    norm_grads = small_sum(
        jnp.concatenate(
            [step_norm_part, jnp.sum(into_wide, axis=-1), jnp.sum(out_wide, axis=-1)], 1
        ),
        "ch",
        ch_count,
        6,
        "norm_grads_sum",
        ties=[out_away, gate_in_away, gate_up_next, down_next],
    )
    raw_grad, small_grad = norm_three_back(
        (
            norm_grads[:, :step_rank],
            norm_grads[:, step_rank : step_rank + states],
            norm_grads[:, step_rank + states :],
        )
    )
    raw_low = raw_grad.astype(bf16)
    conv_total = conv_total + jnp.einsum("tk,ek->te", raw_low, w_x, preferred_element_type=f32)
    extended_grad, kernel_grad = conv_back(conv_total)
    edge_grad = passed_along(extended_grad[:3], "seq", -1)
    conv_in_grad = extended_grad[3:].at[tok_rows - 3 :].add(edge_grad)
    conv_in_low = conv_in_grad.astype(bf16)
    conv_in_came = pair(conv_in_low)
    out_next = out_sum.go()
    gate_in_next = gate_in_sum.go()
    normed_one_part = jnp.einsum(
        "tke,dke->td",
        jnp.stack([conv_in_low, gate_pre_low], 1),
        w_in,
        preferred_element_type=f32,
    )
    normed_one_grad = four_sum(
        normed_one_part.astype(bf16), 7, "normed_one_sum", ties=[out_next, gate_in_next]
    ).astype(f32)
    conv_in_sum = paired(one_own, conv_in_low, one_came, conv_in_came, seq_count)
    conv_in_away = conv_in_sum.go()

    feed_part = jnp.dot(hidden_low, w_down, preferred_element_type=f32)
    feed_out = four_sum(feed_part.astype(bf16), 5, "feed_sum", ties=[conv_in_away]).astype(f32)
    result = middle + feed_out
    squares = jnp.stack(
        [jnp.sum(result * result), jnp.sum(mixer_out * mixer_out), jnp.sum(feed_out * feed_out)]
    )
    out_rows_all = result.astype(bf16)
    stream_part, gain_one_grad = norm_one_back(normed_one_grad)
    stream_grad = middle_grad + stream_part

    grad_x = jnp.dot(conv_low.T, raw_low, preferred_element_type=f32)
    grad_dt = jnp.dot(step_pre_low.T, step_low, preferred_element_type=f32)
    small_rows = jnp.concatenate(
        [rate_sum * decay_rate, kernel_grad, bias_grad[None], skip_grad[None]], 0
    )
    narrow = step_rank + grad_x.shape[1] + small_rows.shape[0]
    padding = -narrow % 128
    columns_all = jnp.concatenate(
        [grad_x, grad_dt, small_rows.T, jnp.zeros((channels, padding), f32)], 1
    )

    def as_row(values):
        return jnp.pad(values, (0, width - values.shape[0]))[None]

    flat = jnp.concatenate(
        [
            gain_one_grad[None],
            gain_two_grad[None],
            as_row(small_grad),
            as_row(squares),
            jnp.zeros((4, width), f32),
        ],
        0,
    )
    conv_in_next = conv_in_sum.go()
    own, flat_total = last_sums(
        columns_all, flat, seq_count, 8, "last_sums", ties=[conv_in_next]
    )
    conv_in_part, gate_in_part = conv_in_sum.rest(), gate_in_sum.rest()
    out_part, gate_up_part, down_part = out_sum.rest(), gate_up_sum.rest(), down_sum.rest()
    at = grad_x.shape[1]
    x_part = own[:, :at]
    dt_part = own[:, at : at + step_rank].T
    at += step_rank
    decay_out = own[:, at : at + states].T
    at += states
    chan_part = own[:, at : at + 7].T
    me = lax.axis_index("seq")
    gains_part = lax.dynamic_slice_in_dim(
        flat_total[:2], me * (width // seq_count), width // seq_count, 1
    )
    small_width = small_gains.shape[0] // seq_count
    small_part = lax.dynamic_slice_in_dim(flat_total[2], me * small_width, small_width, 0)
    rms_values = jnp.sqrt(flat_total[3, :3] / (tok_rows * seq_count * width))
    in_part = jnp.stack([conv_in_part, gate_in_part], 1)
    return (
        out_rows_all,
        stream_grad,
        gains_part,
        in_part,
        chan_part,
        decay_out,
        x_part,
        small_part,
        dt_part,
        out_part,
        gate_up_part.reshape(gate_up_part.shape[0], 2, -1),
        down_part,
        rms_values,
    )


def solution(mesh):
    in_specs = (
        P("seq", None),
        P(),
        P(),
        P(None, None, "ch"),
        P(None, "ch"),
        P(None, "ch"),
        P("ch", None),
        P(),
        P(None, "ch"),
        P("ch", None),
        P(None, None, "ch"),
        P("ch", None),
        P("seq", None),
    )
    out_specs = (
        P("seq", None),
        P("seq", None),
        P(None, "seq"),
        P("seq", None, "ch"),
        P(None, ("ch", "seq")),
        P(None, ("ch", "seq")),
        P(("ch", "seq"), None),
        P("seq"),
        P(None, ("ch", "seq")),
        P(("ch", "seq"), None),
        P("seq", None, "ch"),
        P(("ch", "seq"), None),
        P(),
    )
    return jax.shard_map(
        functools.partial(local, mesh.shape["seq"], mesh.shape["ch"]),
        mesh=mesh,
        in_specs=in_specs,
        out_specs=out_specs,
        check_vma=False,
    )
```

```python
import functools
import math
import types

import jax
import jax.numpy as jnp
from jax import lax
from jax.experimental import pallas as pl
from jax.experimental.pallas import tpu as pltpu
from jax.sharding import PartitionSpec as P

f32 = jnp.float32
bf16 = jnp.bfloat16
LOG2E = math.log2(math.e)
LN2 = math.log(2.0)
RESET = 1e30
UNROLL = 8
LANES = 256
VMEM = pl.BlockSpec(memory_space=pltpu.VMEM)


def shape_of(*dims, dtype=f32):
    return jax.ShapeDtypeStruct(dims, dtype)


def cost(us):
    return pl.CostEstimate(flops=int(us * 1e9), bytes_accessed=int(us * 1e6), transcendentals=0)


def widened(column, width):
    return jnp.concatenate([column] * (width // 128), 1)


ANY = pl.BlockSpec(memory_space=pl.ANY)


def sent(source, target, sends, receives, slot, axis, partner):
    copy = pltpu.make_async_remote_copy(
        src_ref=source,
        dst_ref=target,
        send_sem=sends.at[slot],
        recv_sem=receives.at[slot],
        device_id={axis: partner},
        device_id_type=pl.DeviceIdType.MESH,
    )
    copy.start()
    return copy


def bits_of(count):
    return [1 << k for k in range(count.bit_length() - 1)]


def flipped(me, bit):
    mine = lax.rem(me // bit, 2)
    return mine, me + bit - 2 * bit * mine


CHUNK = 32


def sigmoid(values):
    return 1.0 / (1.0 + jnp.exp(-values))


def softplus(values):
    return jnp.maximum(values, 0.0) + jnp.log1p(jnp.exp(-jnp.abs(values)))


def row_doc(places, bounds):
    return (places >= bounds[0]).astype(jnp.int32) + (places >= bounds[1]).astype(jnp.int32)


def tap_mask(places, bounds, offset):
    source = places - offset
    same = row_doc(source, bounds) == row_doc(places, bounds)
    return jnp.where((source >= 0) & same, 1.0, 0.0)


def mean_square(values):
    return jnp.mean(values * values, axis=-1, keepdims=True)


def three_norms(raw, gains, rank, states):
    low, mid, high = raw[:, :rank], raw[:, rank : rank + states], raw[:, rank + states :]
    low_scale = lax.rsqrt(mean_square(low) + 1e-06)
    mid_scale = lax.rsqrt(jnp.maximum(mean_square(mid), 0.1))
    high_scale = lax.rsqrt(jnp.maximum(mean_square(high), 0.1))
    return (
        low * low_scale * gains[:, :rank],
        mid * mid_scale * gains[:, rank : rank + states],
        high * high_scale * gains[:, rank + states :],
    )


def widen(values, wide, first, count):
    states = values.shape[1]
    eye = (
        lax.broadcasted_iota(jnp.int32, (states, states), 0)
        == lax.broadcasted_iota(jnp.int32, (states, states), 1)
    ).astype(f32)
    spread = jnp.sum(values[:, None, :] * eye[None], axis=-1, keepdims=True)
    wide[pl.ds(first, count)] = jnp.broadcast_to(spread, (count, states, 128))


def greeted(axis_partners):
    barrier = pltpu.get_barrier_semaphore()
    for axis, partner in axis_partners:
        pl.semaphore_signal(
            barrier, inc=1, device_id={axis: partner}, device_id_type=pl.DeviceIdType.MESH
        )
    pl.semaphore_wait(barrier, len(axis_partners))


def chained(forward, bits, state, steps, rates, moving, landed, sends, receives, base):
    me = lax.axis_index("seq")
    states = state.shape[0]
    all_state, all_steps = state, steps
    mine_state, mine_steps = jnp.zeros_like(all_state), jnp.zeros_like(all_steps)
    for k, bit in enumerate(bits):
        mine, partner = flipped(me, bit)
        moving[k, :states] = all_state
        moving[k, states:] = all_steps
        sent(moving.at[k], landed.at[k], sends, receives, base + k, "seq", partner).wait()
        other_state, other_steps = landed[k, :states], landed[k, states:]
        earlier = (mine == 1) if forward else (mine == 0)
        through = jnp.exp2(rates * mine_steps[:1])
        mine_state = jnp.where(earlier, mine_state + through * other_state, mine_state)
        mine_steps = jnp.where(earlier, mine_steps + other_steps, mine_steps)
        after = jnp.exp2(rates * all_steps[:1]) * other_state + all_state
        ahead_of = jnp.exp2(rates * other_steps[:1]) * all_state + other_state
        all_state = jnp.where(earlier, after, ahead_of)
        all_steps = all_steps + other_steps
    return mine_state


def forward_kernel(
    bits, bounds, proj, chan, logs, w_x, gains, w_dt, w_out, one_in, cot,
    halo, pre_out, low_out, raw_out, step_pre_out, into, out_of, scan_out, gated_out, last_state,
    mixer, hist_out, one_came, cot_came,
    extended, raw_move, raw_land, step, drive, starts, moving, landed, part, first_land,
    second_move, second_land, hist, sends, receives, hist_sem, shared_sends, shared_receives,
):
    tokens, channels = low_out.shape
    rank, states = w_dt.shape[0], logs.shape[0]
    chunks = tokens // CHUNK
    ch_me, me = lax.axis_index("ch"), lax.axis_index("seq")
    seq_count = 1 << len(bits)
    low, across = flipped(ch_me, 1)
    high, along = flipped(ch_me, 2)
    following, previous = lax.rem(me + 1, seq_count), lax.rem(me + seq_count - 1, seq_count)
    greeted(
        [("ch", across), ("ch", along), ("seq", following), ("seq", previous)]
        + [("seq", flipped(me, bit)[1]) for bit in bits]
    )
    halo_copy = sent(
        proj.at[pl.ds(tokens - 16, 16), pl.ds(0, channels)], halo, sends, receives, 0, "seq",
        following,
    )
    mine, pair = flipped(me, bits[0])
    half = one_in.shape[0] // 2
    some = pl.ds(low * half, half)
    at = pl.ds(pl.multiple_of(low * (tokens // 2), tokens // 2), tokens // 2)
    shared = [
        (one_in.at[some, 1 - mine], one_came.at[some]),
        (cot.at[at], cot_came.at[at]),
    ]
    shared_copies = [
        sent(source, target, shared_sends, shared_receives, k, "seq", pair)
        for k, (source, target) in enumerate(shared)
    ]
    rates = -jnp.exp(logs[...]) * LOG2E
    halo_copy.wait()
    extended[0:16] = halo[...].astype(f32)

    def spread(index, _):
        first = pl.multiple_of(index * CHUNK, CHUNK)
        extended[pl.ds(first + 16, CHUNK)] = proj[pl.ds(first, CHUNK), :channels].astype(f32)
        return 0

    lax.fori_loop(0, chunks, spread, 0)

    def convolved(index, _):
        first = pl.multiple_of(index * CHUNK, CHUNK)
        places = me * tokens + first + lax.broadcasted_iota(jnp.int32, (CHUNK, 128), 0)
        window = extended[pl.ds(first, CHUNK + 16)]
        summed = chan[4:5]
        for k in range(4):
            mask = widened(tap_mask(places, bounds, 3 - k), channels)
            summed = summed + chan[k : k + 1] * window[13 + k : 13 + k + CHUNK] * mask
        pre_out[pl.ds(first, CHUNK)] = summed
        low_out[pl.ds(first, CHUNK)] = (summed * sigmoid(summed)).astype(bf16)
        return 0

    lax.fori_loop(0, chunks, convolved, 0)
    raw_move[0] = jnp.dot(low_out[...], w_x[...], preferred_element_type=f32)
    sent(raw_move.at[0], raw_land.at[0], sends, receives, 1, "ch", across).wait()
    raw_move[1] = raw_move[0] + raw_land[0]
    sent(raw_move.at[1], raw_land.at[1], sends, receives, 2, "ch", along).wait()

    def stepped(index, total):
        first = pl.multiple_of(index * CHUNK, CHUNK)
        rows = pl.ds(first, CHUNK)
        raw = raw_move[1, rows] + raw_land[1, rows]
        raw_out[rows] = raw
        step_norm, input_norm, output_norm = three_norms(raw, gains[...], rank, states)
        widen(input_norm, into, first, CHUNK)
        widen(output_norm, out_of, first, CHUNK)
        pre = (
            jnp.dot(step_norm.astype(bf16), w_dt[...], preferred_element_type=f32) + chan[5:6]
        )
        step_pre_out[rows] = pre
        size = softplus(pre)
        drive[rows] = size * low_out[rows].astype(f32)
        places = me * tokens + first + lax.broadcasted_iota(jnp.int32, (CHUNK, 128), 0)
        resets = jnp.where((places == bounds[0]) | (places == bounds[1]), RESET, 0.0)
        size = size + widened(resets, channels)
        step[rows] = size
        return total + jnp.sum(size, axis=0, keepdims=True)

    total = lax.fori_loop(0, chunks, stepped, jnp.zeros((1, channels), f32))
    blocks = [slice(j, j + LANES) for j in range(0, channels, LANES)]
    for lanes in blocks:
        block_rates = rates[:, lanes]

        def ended(index, state, lanes=lanes, block_rates=block_rates):
            first = pl.multiple_of(index * UNROLL, UNROLL)
            steps, drives = step[pl.ds(first, UNROLL), lanes], drive[pl.ds(first, UNROLL), lanes]
            for k in range(UNROLL):
                decay = jnp.exp2(steps[k : k + 1] * block_rates)
                state = decay * state + widened(into[first + k], LANES) * drives[k : k + 1]
            return state

        starts[:, lanes] = lax.fori_loop(
            0, tokens // UNROLL, ended, jnp.zeros((states, LANES), f32)
        )
    starts[...] = chained(
        True, bits, starts[...], jnp.broadcast_to(total, (8, channels)), rates, moving, landed,
        sends, receives, 7,
    )
    hist_copies = []
    for number, lanes in enumerate(blocks):
        block_rates = rates[:, lanes]
        skip = chan[6:7, lanes]

        def walked(index, state, lanes=lanes, block_rates=block_rates, skip=skip):
            first = pl.multiple_of(index * UNROLL, UNROLL)
            steps, drives = step[pl.ds(first, UNROLL), lanes], drive[pl.ds(first, UNROLL), lanes]
            rows = []
            for k in range(UNROLL):
                hist[first + k, :, lanes] = state
                decay = jnp.exp2(steps[k : k + 1] * block_rates)
                state = decay * state + widened(into[first + k], LANES) * drives[k : k + 1]
                rows.append(
                    jnp.sum(widened(out_of[first + k], LANES) * state, axis=0, keepdims=True)
                )
            scan_out[pl.ds(first, UNROLL), lanes] = jnp.concatenate(rows, 0)
            return state

        last_state[:, lanes] = lax.fori_loop(0, tokens // UNROLL, walked, starts[:, lanes])
        copy = pltpu.make_async_copy(
            hist.at[:, :, lanes], hist_out.at[:, :, lanes], hist_sem.at[number]
        )
        copy.start()
        hist_copies.append(copy)

    def gate(index, _):
        first = pl.multiple_of(index * CHUNK, CHUNK)
        rows = pl.ds(first, CHUNK)
        scanned = scan_out[rows] + chan[6:7] * low_out[rows].astype(f32)
        scan_out[rows] = scanned
        gate_pre = proj[rows, channels:].astype(f32)
        gated_out[rows] = (scanned * gate_pre * sigmoid(gate_pre)).astype(bf16)
        return 0

    lax.fori_loop(0, chunks, gate, 0)
    quarter = tokens // 4
    width = w_out.shape[1]
    for k, (_, target) in enumerate(shared):
        shared_copies[k].wait()
        shared_copies[k] = sent(
            target, target, shared_sends, shared_receives, 2 + k, "ch", across
        )

    def mixed(index, _):
        first = pl.multiple_of(index * 512, 512)
        product = jnp.dot(
            gated_out[...], w_out[:, pl.ds(first, 512)], preferred_element_type=f32
        ).astype(bf16)
        for k in range(4):
            part[k // 2, k % 2, :, pl.ds(first, 512)] = product[k * quarter : (k + 1) * quarter]
        return 0

    lax.fori_loop(0, width // 512, mixed, 0)
    four_summed(
        part, mixer, first_land, second_land, second_move, sends, receives, 3, low, across, high,
        along,
    )
    for copy in hist_copies + shared_copies:
        copy.wait()


def four_summed(
    value, total, first, second, moving, sends, receives, base, low, across, high, along
):
    sent(value.at[:, 1 - low], first, sends, receives, base, "ch", across).wait()
    moving[...] = (
        value[1 - high, low].astype(f32) + first[1 - high].astype(f32)
    ).astype(bf16)
    copy = sent(moving, second, sends, receives, base + 1, "ch", along)
    kept = value[high, low].astype(f32) + first[high].astype(f32)
    copy.wait()
    total[high, low] = (kept + second[...].astype(f32)).astype(bf16)
    own = total.at[high, low]
    sent(own, own, sends, receives, base + 2, "ch", along).wait()
    both = total.at[:, low]
    sent(both, both, sends, receives, base + 3, "ch", across).wait()


def mixer_forward(bounds, proj, chan, logs, w_x, gains, w_dt, w_out, one_in, cot, count, ident):
    bits = bits_of(count)
    tokens, channels = proj.shape[0], proj.shape[1] // 2
    states, rank, width = logs.shape[0], w_dt.shape[0], w_out.shape[1]
    quarter, narrow = tokens // 4, w_x.shape[1]
    rows = shape_of(tokens, channels)
    low_rows = shape_of(tokens, channels, dtype=bf16)
    wide = shape_of(tokens, states, 128)
    slots = pltpu.VMEM((len(bits), states + 8, channels), f32)
    raws = pltpu.VMEM((2, tokens, narrow), f32)
    out = pl.pallas_call(
        functools.partial(forward_kernel, bits),
        out_shape=[
            shape_of(16, channels, dtype=bf16), rows, low_rows, shape_of(tokens, narrow), rows,
            wide, wide, rows, low_rows, shape_of(states, channels),
            shape_of(2, 2, quarter, width, dtype=bf16), shape_of(tokens, states, channels),
            shape_of(one_in.shape[0], *one_in.shape[2:], dtype=bf16),
            shape_of(tokens, width, dtype=bf16),
        ],
        in_specs=[pl.BlockSpec(memory_space=pltpu.SMEM)] + [VMEM] * 7 + [ANY] * 2,
        out_specs=[VMEM] * 11 + [ANY] * 3,
        scratch_shapes=[
            pltpu.VMEM((tokens + 16, channels), f32), raws, raws,
            pltpu.VMEM((tokens, channels), f32), pltpu.VMEM((tokens, channels), f32),
            pltpu.VMEM((states, channels), f32), slots, slots,
            pltpu.VMEM((2, 2, quarter, width), bf16), pltpu.VMEM((2, quarter, width), bf16),
            pltpu.VMEM((quarter, width), bf16), pltpu.VMEM((quarter, width), bf16),
            pltpu.VMEM((tokens, states, channels), f32),
            pltpu.SemaphoreType.DMA((7 + len(bits),)), pltpu.SemaphoreType.DMA((7 + len(bits),)),
            pltpu.SemaphoreType.DMA((channels // LANES,)),
            pltpu.SemaphoreType.DMA((4,)), pltpu.SemaphoreType.DMA((4,)),
        ],
        compiler_params=pltpu.CompilerParams(
            collective_id=ident, has_side_effects=True, vmem_limit_bytes=56 * 2**20
        ),
        cost_estimate=cost(6),
        name="mixer_forward",
    )(bounds, proj, chan, logs, w_x, gains, w_dt, w_out, one_in, cot)
    return out


class Unit:
    def __init__(self, name, left, right, columns, refs, sends, receives, slot, bits, ready):
        self.name, self.left, self.right, self.columns = name, left, right, columns
        self.away, self.land, self.kept = refs
        self.sends, self.receives, self.slot, self.bits = sends, receives, slot, bits
        self.ready = ready
        self.stage = 0
        self.copy = None

    def next(self):
        stage, me = self.stage, lax.axis_index("seq")
        self.stage += 1
        left_over = stage == len(self.bits)
        if stage == 0:
            for wait in self.ready:
                wait()
            mine, partner = flipped(me, self.bits[0])
            self.make(1 - mine, self.away[0])
            self.copy = self.start(0, partner)
            self.make(mine, self.kept)
            return
        self.copy.wait()
        count = self.land[stage - 1].shape[0]
        rows = self.kept.shape[1]
        part = 32 if rows % 32 == 0 else rows
        parts = rows // part

        def total(index, at):
            return self.kept[index, at] + self.land[stage - 1][index, at].astype(f32)

        if left_over:

            def finish(step, _):
                at = pl.ds(pl.multiple_of(step * part, part), part)
                self.kept[0, at] = total(0, at)
                return 0

            lax.fori_loop(0, parts, finish, 0)
            return
        mine, partner = flipped(me, self.bits[stage])

        def send(step, _):
            index = lax.div(step, parts)
            at = pl.ds(pl.multiple_of(lax.rem(step, parts) * part, part), part)
            self.away[stage][index, at] = total(2 * index + 1 - mine, at).astype(bf16)
            return 0

        lax.fori_loop(0, (count // 2) * parts, send, 0)
        self.copy = self.start(stage, partner)

        def keep(step, _):
            index = lax.div(step, parts)
            at = pl.ds(pl.multiple_of(lax.rem(step, parts) * part, part), part)
            self.kept[index, at] = total(2 * index + mine, at)
            return 0

        lax.fori_loop(0, (count // 2) * parts, keep, 0)

    def start(self, stage, partner):
        return sent(
            self.away[stage], self.land[stage], self.sends, self.receives, self.slot + stage,
            "seq", partner,
        )

    def make(self, side, target):
        first, width = self.columns
        tile = 512 if width % 512 == 0 else 256
        tiles = width // tile

        def block(step, _):
            index = lax.div(step, tiles)
            column = pl.multiple_of(lax.rem(step, tiles) * tile, tile)
            product = jnp.dot(
                self.left[2 * index + side],
                self.right[:, pl.ds(first + column, tile)],
                preferred_element_type=f32,
            )
            target[index, :, pl.ds(column, tile)] = product.astype(target.dtype)
            return 0

        lax.fori_loop(0, target.shape[0] * tiles, block, 0)


def norm_back(values, scale, gains, grad, free=True):
    weighted = gains * grad
    result = scale * weighted
    inner = jnp.mean(values * weighted, axis=-1, keepdims=True)
    return result - jnp.where(free, 1.0, 0.0) * values * (scale * scale * scale) * inner, (
        grad * values * scale
    )


def silu_slope(values):
    part = sigmoid(values)
    return part * (1.0 + values * (1.0 - part))


def narrowed(wide, first, count):
    states = wide.shape[1]
    eye = (
        lax.broadcasted_iota(jnp.int32, (states, states), 0)
        == lax.broadcasted_iota(jnp.int32, (states, states), 1)
    ).astype(f32)
    sums = jnp.sum(wide[pl.ds(first, count)], axis=-1, keepdims=True)
    return jnp.sum(sums * eye[None], axis=1)


def dot_rows(left, right):
    return lax.dot_general(left, right, (((1,), (1,)), ((), ())), preferred_element_type=f32)


def backward_kernel(bits, names, *refs):
    r = types.SimpleNamespace(**dict(zip(names, refs)))
    tokens, width = r.stream.shape
    channels, rank, states = r.low.shape[1], r.w_dt.shape[0], r.logs.shape[0]
    quarter, chunks = tokens // 4, tokens // CHUNK
    ch_me, me = lax.axis_index("ch"), lax.axis_index("seq")
    seq_count = 1 << len(bits)
    low, across = flipped(ch_me, 1)
    high, along = flipped(ch_me, 2)
    mine, pair = flipped(me, bits[0])
    following, previous = lax.rem(me + 1, seq_count), lax.rem(me + seq_count - 1, seq_count)
    loads = {}

    def load(name, source, target):
        copy = pltpu.make_async_copy(source, target, r.load_sems.at[len(loads)])
        copy.start()
        loads[name] = copy

    def have(*wanted):
        for name in wanted:
            if name in loads and loads[name] is not None:
                loads[name].wait()
                loads[name] = None

    own, other = pl.ds(0, tokens), pl.ds(tokens, tokens)
    half = r.left_two.shape[0]
    hid = r.right_two.shape[1] // 2
    load("hidden", r.hidden_in.at[:, mine], r.left_hidden.at[:, :, own])
    load("cot", r.cot, r.right_down.at[own])
    load("cot_came", r.cot_came, r.right_down.at[other])
    load("two_right", r.gate_up_in, r.right_two.at[own])
    load("two", r.two_in.at[:, mine], r.left_two.at[:, :, own])
    load("mixer", r.mixer_in, r.mixer)
    load("w_out", r.w_out, r.weights)
    load("one", r.one_in.at[:, mine], r.left_one.at[:, :, own])
    load("one_came", r.one_came, r.left_one.at[:, :, other])
    load("gated", r.gated_in.at[:, mine], r.left_gated.at[:, :, own])
    load("scan_out", r.scan_in, r.scan)
    load("into", r.into_in, r.into)
    load("out_of", r.out_of_in, r.out_of)
    blocks = [slice(j, j + 128) for j in range(0, channels, 128)]
    load("hist0", r.hist_in.at[:, :, blocks[0]], r.hist.at[0])
    load("hist1", r.hist_in.at[:, :, blocks[1]], r.hist.at[1])

    greeted(
        [("ch", across), ("ch", along), ("seq", following), ("seq", previous)]
        + [("seq", flipped(me, bit)[1]) for bit in bits]
    )
    pair_copies, shared_copies = {}, {}

    def swap(name, source, target):
        slot = len(pair_copies)
        pair_copies[name] = sent(
            source, target, r.pair_sends, r.pair_receives, slot, "seq", pair
        )

    def came(name):
        return lambda: (pair_copies[name].wait(), pair_copies.__setitem__(name, Done))

    def swap_shared(name, source, target):
        slot = len(shared_copies)
        copy = sent(source, target, r.shared_sends, r.shared_receives, 2 * slot, "seq", pair)
        shared_copies[name] = (copy, target, 2 * slot + 1)

    def came_shared(name):
        def wait():
            copy, target, slot = shared_copies[name]
            copy.wait()
            sent(target, target, r.shared_sends, r.shared_receives, slot, "ch", across).wait()

        return wait

    n_bits = len(bits) - 1

    def unit(name, left, right, columns, slot, ready):
        refs = (
            [getattr(r, f"{name}_away").at[pl.ds(0, half >> (k + 1))] for k in range(n_bits)],
            [getattr(r, f"{name}_land{k}") for k in range(n_bits)],
            getattr(r, f"{name}_kept"),
        )
        return Unit(
            name, left, right, columns, refs, r.unit_sends, r.unit_receives, slot * n_bits,
            bits[1:], ready,
        )

    down = unit("down", r.left_hidden, r.right_down, (0, width), 0,
                [lambda: have("hidden", "cot", "cot_came"), came("hidden")])
    gate = unit("gate", r.left_two, r.right_two, (0, hid), 1,
                [lambda: have("two", "two_right"), came_shared("two"), came("gate")])
    up = unit("up", r.left_two, r.right_two, (hid, hid), 2, [came("up")])
    out = unit("out", r.left_gated, r.right_out, (0, width), 3,
               [lambda: have("gated"), came("gated"), came_shared("mixer")])
    gin = unit("gin", r.left_one, r.right_in, (channels, channels), 4,
               [lambda: have("one", "one_came"), came("gin")])
    cin = unit("cin", r.left_one, r.right_in, (0, channels), 5, [came("cin")])
    queue = [down, gate, up, down, gate, None, None, up, out, gin, out, gin, down, gate, up]
    if n_bits > 2:
        queue += [down, gate, up, out, gin] * (n_bits - 2)
    results = {"down": r.down_out, "gate": r.gate_out, "up": r.up_out, "out": r.out_out,
               "gin": r.gin_out, "cin": r.cin_out}
    written = []

    def step():
        if queue:
            item = queue.pop(0)
            if item is not None:
                advance(item)

    def advance(item):
        if item.stage > n_bits:
            return
        item.next()
        if item.stage == n_bits + 1:
            copy = pltpu.make_async_copy(
                item.kept.at[0], results[item.name], r.write_sems.at[len(written)]
            )
            copy.start()
            written.append(copy)

    swap("hidden", r.hidden_in.at[:, 1 - mine], r.left_hidden.at[:, :, other])
    some = pl.ds(low * (half // 2), half // 2)
    swap_shared("two", r.two_in.at[some, 1 - mine], r.left_two.at[some, :, other])
    swap("gate", r.gate_up_in.at[:, pl.ds(0, hid)], r.right_two.at[other, pl.ds(0, hid)])
    swap("up", r.gate_up_in.at[:, pl.ds(hid, hid)], r.right_two.at[other, pl.ds(hid, hid)])
    swap("gated", r.gated_in.at[:, 1 - mine], r.left_gated.at[:, :, other])

    sums = (r.first_land, r.second_land, r.second_move, r.sum_sends, r.sum_receives)

    def summed(value, base, fillers):
        first, second, moving, sends, receives = sums
        copy = sent(value.at[:, 1 - low], first, sends, receives, base, "ch", across)
        fillers[0]()
        copy.wait()
        moving[...] = (
            value[1 - high, low].astype(f32) + first[1 - high].astype(f32)
        ).astype(bf16)
        copy = sent(moving, second, sends, receives, base + 1, "ch", along)
        fillers[1]()
        copy.wait()
        r.total[high, low] = (
            value[high, low].astype(f32) + first[high].astype(f32) + second[...].astype(f32)
        ).astype(bf16)
        part = r.total.at[high, low]
        copy = sent(part, part, sends, receives, base + 2, "ch", along)
        fillers[2]()
        copy.wait()
        both = r.total.at[:, low]
        copy = sent(both, both, sends, receives, base + 3, "ch", across)
        fillers[3]()
        copy.wait()

    def idle():
        return None

    rates = -jnp.exp(r.logs[...]) * LOG2E

    def places_of(first, count):
        return me * tokens + first + lax.broadcasted_iota(jnp.int32, (count, 128), 0)

    def resteps():
        def body(index, total):
            first = pl.multiple_of(index * CHUNK, CHUNK)
            rows = pl.ds(first, CHUNK)
            size = softplus(r.step_pre[rows])
            r.drive[rows] = size * r.low[rows].astype(f32)
            places = places_of(first, CHUNK)
            resets = jnp.where((places == r.bounds[0]) | (places == r.bounds[1]), RESET, 0.0)
            size = size + widened(resets, channels)
            r.step[rows] = size
            return total + jnp.sum(size, axis=0, keepdims=True)

        r.step_sum[...] = jnp.broadcast_to(
            lax.fori_loop(0, chunks, body, jnp.zeros((1, channels), f32)), (8, channels)
        )

    load("part", r.two_part, r.part)
    have("part")
    summed(r.part, 0, [resteps, step, idle, idle])
    load("feed", r.feed_part, r.part)
    have("mixer", "cot")

    def quarter_rows(index):
        per = quarter // CHUNK
        part = lax.div(index, per)
        at = pl.ds(pl.multiple_of(lax.rem(index, per) * CHUNK, CHUNK), CHUNK)
        return lax.div(part, 2), lax.rem(part, 2), at

    def norm_two(index, total):
        first = pl.multiple_of(index * CHUNK, CHUNK)
        rows = pl.ds(first, CHUNK)
        a, b, at = quarter_rows(index)
        middle = r.stream[rows].astype(f32) + r.mixer[a, b, at].astype(f32)
        scale = lax.rsqrt(mean_square(middle) + 1e-06)
        back, gain = norm_back(middle, scale, r.gains[1:2], r.total[a, b, at].astype(f32))
        grad = r.right_down[rows].astype(f32) + back
        r.stream_grad[rows] = grad
        r.right_out[rows] = grad.astype(bf16)
        return total + jnp.sum(gain, axis=0, keepdims=True)

    gain_two = lax.fori_loop(0, chunks, norm_two, jnp.zeros((1, width), f32))
    r.flat_move[0] = jnp.zeros_like(r.flat_move[0])
    r.flat_move[0, 1:2] = gain_two
    first = pl.multiple_of(low * (tokens // 2), tokens // 2)
    swap_shared(
        "mixer",
        r.right_out.at[pl.ds(first, tokens // 2)],
        r.right_out.at[pl.ds(tokens + first, tokens // 2)],
    )
    have("w_out", "scan_out")

    skips = []
    for j in range(0, channels, 256):
        lanes = slice(j, j + 256)
        gated_grad = dot_rows(r.right_out[own], r.weights[pl.ds(j, 256)])
        gate_pre = r.proj[:, channels + j : channels + j + 256].astype(f32)
        part = sigmoid(gate_pre)
        slope = part * (1.0 + gate_pre * (1.0 - part))
        r.right_in[own, channels + j : channels + j + 256] = (
            gated_grad * r.scan[:, lanes] * slope
        ).astype(bf16)
        grad = gated_grad * gate_pre * part
        r.scan[:, lanes] = grad
        skips.append(jnp.sum(grad * r.low[:, lanes].astype(f32), axis=0, keepdims=True))
    skip_grad = jnp.concatenate(skips, 1)
    swap("gin", r.right_in.at[own, pl.ds(channels, channels)],
         r.right_in.at[other, pl.ds(channels, channels)])
    load("w_in0", r.w_in.at[pl.ds(0, channels)], r.weights)
    have("into", "out_of")
    for j in range(0, channels, LANES):
        lanes = slice(j, j + LANES)

        def ended(index, carried, lanes=lanes, block_rates=rates[:, j : j + LANES]):
            first = pl.multiple_of(tokens - UNROLL - index * UNROLL, UNROLL)
            steps, grads = r.step[pl.ds(first, UNROLL), lanes], r.scan[pl.ds(first, UNROLL), lanes]
            for k in reversed(range(UNROLL)):
                decay = jnp.exp2(steps[k : k + 1] * block_rates)
                carried = decay * (widened(r.out_of[first + k], LANES) * grads[k : k + 1] + carried)
            return carried

        r.starts[:, lanes] = lax.fori_loop(
            0, tokens // UNROLL, ended, jnp.zeros((states, LANES), f32)
        )

    all_state, all_steps = r.starts[...], r.step_sum[...]
    mine_state, mine_steps = jnp.zeros_like(all_state), jnp.zeros_like(all_steps)
    for k, bit in enumerate(bits):
        side, partner = flipped(me, bit)
        r.chain_move[k, :states] = all_state
        r.chain_move[k, states:] = all_steps
        copy = sent(r.chain_move.at[k], r.chain_land.at[k], r.chain_sends, r.chain_receives, k,
                    "seq", partner)
        if k == 0:
            step()
        copy.wait()
        other_state, other_steps = r.chain_land[k, :states], r.chain_land[k, states:]
        earlier = side == 0
        through = jnp.exp2(rates * mine_steps[:1])
        mine_state = jnp.where(earlier, mine_state + through * other_state, mine_state)
        mine_steps = jnp.where(earlier, mine_steps + other_steps, mine_steps)
        after = jnp.exp2(rates * all_steps[:1]) * other_state + all_state
        ahead_of = jnp.exp2(rates * other_steps[:1]) * all_state + other_state
        all_state = jnp.where(earlier, after, ahead_of)
        all_steps = all_steps + other_steps
    r.starts[...] = mine_state
    step()

    r.into_wide[...] = jnp.zeros_like(r.into_wide)
    r.out_wide[...] = jnp.zeros_like(r.out_wide)
    for number, lanes in enumerate(blocks):
        have(f"hist{number}")
        hist = r.hist.at[number % 2]
        block_rates = rates[:, lanes]

        def walked(index, carry, lanes=lanes, block_rates=block_rates, hist=hist):
            carried, state, total = carry
            first = pl.multiple_of(tokens - UNROLL - index * UNROLL, UNROLL)
            some = pl.ds(first, UNROLL)
            steps, drives, grads = r.step[some, lanes], r.drive[some, lanes], r.scan[some, lanes]
            decay_list, push_list = [None] * UNROLL, [None] * UNROLL
            for k in reversed(range(UNROLL)):
                place = first + k
                grad_row = grads[k : k + 1]
                decay = jnp.exp2(steps[k : k + 1] * block_rates)
                adjoint = r.out_of[place] * grad_row + carried
                carried = decay * adjoint
                r.out_wide[place] = r.out_wide[place] + state * grad_row
                r.into_wide[place] = r.into_wide[place] + adjoint * drives[k : k + 1]
                state = hist[place]
                share = carried * state
                total = total + share * steps[k : k + 1]
                decay_list[k] = jnp.sum(share * block_rates, axis=0, keepdims=True)
                push_list[k] = jnp.sum(r.into[place] * adjoint, axis=0, keepdims=True)
            r.decay_rows[some, :] = jnp.concatenate(decay_list, 0)
            r.push[some, lanes] = jnp.concatenate(push_list, 0)
            return (carried, state, total)

        _, _, total = lax.fori_loop(
            0,
            tokens // UNROLL,
            walked,
            (r.starts[:, lanes], r.last_state[:, lanes], jnp.zeros((states, 128), f32)),
        )
        r.rate_sum[:, lanes] = total * (rates[:, lanes] * LN2)

        def gathered(index, _, lanes=lanes):
            rows = pl.ds(pl.multiple_of(index * CHUNK, CHUNK), CHUNK)
            used, pushed = r.low[rows, lanes].astype(f32), r.push[rows, lanes]
            pre = r.step_pre[rows, lanes]
            grad = (LN2 * r.decay_rows[rows] + pushed * used) * sigmoid(pre)
            r.step_low_grad[rows, lanes] = grad.astype(bf16)
            r.push[rows, lanes] = pushed * softplus(pre) + r.chan[6:7, lanes] * r.scan[rows, lanes]
            return 0

        lax.fori_loop(0, chunks, gathered, 0)
        if number + 2 < len(blocks):
            load(f"hist{number + 2}", r.hist_in.at[:, :, blocks[number + 2]], r.hist.at[number % 2])
        step()

    def norm_grads(index, _):
        first = pl.multiple_of(index * CHUNK, CHUNK)
        rows = pl.ds(first, CHUNK)
        low_part = dot_rows(r.step_low_grad[rows], r.w_dt[...])
        r.raw_move[0, rows] = jnp.concatenate(
            [low_part, narrowed(r.into_wide, first, CHUNK), narrowed(r.out_wide, first, CHUNK)], 1
        )
        return 0

    lax.fori_loop(0, chunks, norm_grads, 0)
    copy = sent(r.raw_move.at[0], r.raw_land.at[0], r.raw_sends, r.raw_receives, 0, "ch", across)
    step()
    copy.wait()
    r.raw_move[1] = r.raw_move[0] + r.raw_land[0]
    copy = sent(r.raw_move.at[1], r.raw_land.at[1], r.raw_sends, r.raw_receives, 1, "ch", along)
    step()
    copy.wait()

    def raw_back(index, total):
        rows = pl.ds(pl.multiple_of(index * CHUNK, CHUNK), CHUNK)
        grads, raw = r.raw_move[1, rows] + r.raw_land[1, rows], r.raw[rows]
        gains = r.small_gains[...]
        values, sums_to = [], []
        for start, stop, floor in ((0, rank, None), (rank, rank + states, 0.1),
                                   (rank + states, rank + 2 * states, 0.1)):
            value = raw[:, start:stop]
            square = mean_square(value)
            if floor is None:
                scale, free = lax.rsqrt(square + 1e-06), True
            else:
                scale, free = lax.rsqrt(jnp.maximum(square, floor)), square > floor
            back, gain = norm_back(value, scale, gains[:, start:stop], grads[:, start:stop], free)
            values.append(back)
            sums_to.append(jnp.sum(gain, axis=0, keepdims=True))
        norm = raw[:, :rank] * lax.rsqrt(mean_square(raw[:, :rank]) + 1e-06) * gains[:, :rank]
        r.raw_low[rows] = jnp.concatenate(values, 1).astype(bf16)
        r.step_low[rows] = norm.astype(bf16)
        return total + jnp.concatenate(sums_to, 1)

    small = lax.fori_loop(0, chunks, raw_back, jnp.zeros((1, rank + 2 * states), f32))
    r.flat_move[0, 2:3, : rank + 2 * states] = small

    def conv_back(index, total):
        first = pl.multiple_of(index * CHUNK, CHUNK)
        rows = pl.ds(first, CHUNK)
        grad = r.push[rows] + dot_rows(r.raw_low[rows], r.w_x[...])
        grad = grad * silu_slope(r.pre[rows])
        r.grad_pre[rows] = grad
        return total + jnp.sum(grad, axis=0, keepdims=True)

    tap_bias = lax.fori_loop(0, chunks, conv_back, jnp.zeros((1, channels), f32))
    copy = sent(r.grad_pre.at[pl.ds(0, 8)], r.grad_pre.at[pl.ds(tokens, 8)], r.raw_sends,
                r.raw_receives, 2, "seq", previous)
    r.extended[0:16] = r.halo[...].astype(f32)

    def extend(index, _):
        first = pl.multiple_of(index * CHUNK, CHUNK)
        r.extended[pl.ds(first + 16, CHUNK)] = r.proj[pl.ds(first, CHUNK), :channels].astype(f32)
        return 0

    lax.fori_loop(0, chunks, extend, 0)

    def taps(index, totals):
        first = pl.multiple_of(index * CHUNK, CHUNK)
        places = places_of(first, CHUNK)
        window = r.extended[pl.ds(first, CHUNK + 16)]
        grad = r.grad_pre[pl.ds(first, CHUNK)]
        return tuple(
            totals[k]
            + jnp.sum(
                grad
                * widened(tap_mask(places, r.bounds, 3 - k), channels)
                * window[13 + k : 13 + k + CHUNK],
                axis=0,
                keepdims=True,
            )
            for k in range(4)
        )

    tap_grads = lax.fori_loop(
        0, chunks, taps, tuple(jnp.zeros((1, channels), f32) for _ in range(4))
    )
    copy.wait()

    def conv_in_back(index, _):
        first = pl.multiple_of(index * CHUNK, CHUNK)
        window = r.grad_pre[pl.ds(first, CHUNK + 8)]
        grad = jnp.zeros((CHUNK, channels), f32)
        for k in range(4):
            places = places_of(first + 3 - k, CHUNK)
            mask = jnp.where(
                places < seq_count * tokens, tap_mask(places, r.bounds, 3 - k), 0.0
            )
            grad = grad + r.chan[k : k + 1] * widened(mask, channels) * window[3 - k : 3 - k + CHUNK]
        r.right_in[pl.ds(first, CHUNK), :channels] = grad.astype(bf16)
        return 0

    lax.fori_loop(0, chunks, conv_in_back, 0)
    swap("cin", r.right_in.at[own, pl.ds(0, channels)], r.right_in.at[other, pl.ds(0, channels)])

    have("feed")
    summed(r.part, 4, [idle, step, step, idle])

    def results_of(index, totals):
        rows = pl.ds(pl.multiple_of(index * CHUNK, CHUNK), CHUNK)
        a, b, at = quarter_rows(index)
        mixed, feed = r.mixer[a, b, at].astype(f32), r.total[a, b, at].astype(f32)
        result = r.stream[rows].astype(f32) + mixed + feed
        r.out_rows[rows] = result.astype(bf16)
        return tuple(
            total + jnp.sum(v * v, axis=0, keepdims=True)
            for total, v in zip(totals, (result, mixed, feed))
        )

    squares = lax.fori_loop(
        0, chunks, results_of, tuple(jnp.zeros((1, width), f32) for _ in range(3))
    )
    for number, total in enumerate(squares):
        r.flat_move[0, 3 + number : 4 + number] = total

    have("w_in0")
    for number in range(width // channels):

        def one_part(index, _, first=number * channels):
            at = pl.multiple_of(index * 256, 256)
            product = dot_rows(r.right_in[own], r.weights[pl.ds(at, 256)]).astype(bf16)
            for k in range(4):
                r.part[k // 2, k % 2, :, pl.ds(first + at, 256)] = product[
                    k * quarter : (k + 1) * quarter
                ]
            return 0

        lax.fori_loop(0, channels // 256, one_part, 0)
        if (number + 1) * channels < width:
            load(f"w_in{number + 1}", r.w_in.at[pl.ds((number + 1) * channels, channels)], r.weights)
            have(f"w_in{number + 1}")
    queue[:] = [cin, *queue, out, gin, cin, cin]

    def small_columns():
        narrow = r.w_x.shape[1]
        pack = r.step
        pack[0:narrow] = lax.dot_general(
            r.raw_low[...], r.low[...], (((0,), (0,)), ((), ())), preferred_element_type=f32
        )
        pack[narrow : narrow + rank] = lax.dot_general(
            r.step_low[...], r.step_low_grad[...], (((0,), (0,)), ((), ())),
            preferred_element_type=f32,
        )
        at = narrow + rank
        pack[at : at + states] = r.rate_sum[...]
        at += states
        bias = jnp.sum(r.step_low_grad[...].astype(f32), axis=0, keepdims=True)
        pack[at : at + 8] = jnp.concatenate(
            [*tap_grads, tap_bias, bias, skip_grad, jnp.zeros((1, channels), f32)], 0
        )
        at += 8
        pack[at:] = jnp.zeros((pack.shape[0] - at, channels), f32)
        turned = pack[...].T
        r.small_work0[...] = turned.reshape(r.small_work0.shape)

    summed(r.part, 8, [step, small_columns, step, idle])

    def norm_one(index, total):
        rows = pl.ds(pl.multiple_of(index * CHUNK, CHUNK), CHUNK)
        a, b, at = quarter_rows(index)
        value = r.stream[rows].astype(f32)
        scale = lax.rsqrt(mean_square(value) + 1e-06)
        back, gain = norm_back(value, scale, r.gains[0:1], r.total[a, b, at].astype(f32))
        r.stream_grad[rows] = r.stream_grad[rows] + back
        return total + jnp.sum(gain, axis=0, keepdims=True)

    r.flat_move[0, 0:1] = lax.fori_loop(0, chunks, norm_one, jnp.zeros((1, width), f32))

    for k, bit in enumerate(bits):
        side, partner = flipped(me, bit)
        work = getattr(r, f"small_work{k}")
        away, land = getattr(r, f"small_away{k}"), getattr(r, f"small_land{k}")
        away[...] = work[:, 1 - side].astype(bf16)
        copy = sent(away, land, r.last_sends, r.last_receives, 2 * k, "seq", partner)
        flat = sent(r.flat_move.at[k], r.flat_land.at[k], r.last_sends, r.last_receives, 2 * k + 1,
                    "seq", partner)
        step()
        copy.wait()
        total = work[:, side] + land[...].astype(f32)
        flat.wait()
        if k + 1 < len(bits):
            target = getattr(r, f"small_work{k + 1}")
            target[...] = total.reshape(target.shape)
            r.flat_move[k + 1] = r.flat_move[k] + r.flat_land[k]
        else:
            r.small_out[...] = total.reshape(r.small_out.shape)
            r.flat_out[...] = r.flat_move[k] + r.flat_land[k]
    while queue:
        step()
    pending = [down, gate, up, out, gin, cin]
    while any(item.stage <= n_bits for item in pending):
        for item in pending:
            advance(item)
    for copy in written:
        copy.wait()


class Done:
    @staticmethod
    def wait():
        return None


def backward(ins, hbm_ins, count, ident):
    bits = bits_of(count)
    n_bits = len(bits) - 1
    tokens, width = ins["stream"].shape
    channels, rank, states = ins["low"].shape[1], ins["w_dt"].shape[0], ins["logs"].shape[0]
    hid = hbm_ins["gate_up_in"].shape[1] // 2
    narrow = ins["w_x"].shape[1]
    half, quarter = count // 2, tokens // 4
    rows_in, rows_out, rows_down = width // count, channels // count, hid // count
    rows = pltpu.VMEM((tokens, channels), f32)

    def low(*dims):
        return pltpu.VMEM(dims, bf16)

    def full(*dims):
        return pltpu.VMEM(dims, f32)

    outs = {
        "stream_grad": (shape_of(tokens, width), VMEM),
        "out_rows": (shape_of(tokens, width, dtype=bf16), VMEM),
        "small_out": (shape_of(rows_out, tokens), VMEM),
        "flat_out": (shape_of(8, width), VMEM),
        "down_out": (shape_of(rows_down, width), ANY),
        "gate_out": (shape_of(rows_in, hid), ANY),
        "up_out": (shape_of(rows_in, hid), ANY),
        "out_out": (shape_of(rows_out, width), ANY),
        "gin_out": (shape_of(rows_in, channels), ANY),
        "cin_out": (shape_of(rows_in, channels), ANY),
    }
    scratch = {
        "left_hidden": low(half, rows_down, 2 * tokens),
        "left_two": low(half, rows_in, 2 * tokens),
        "left_one": low(half, rows_in, 2 * tokens),
        "left_gated": low(half, rows_out, 2 * tokens),
        "right_down": low(2 * tokens, width),
        "right_two": low(2 * tokens, 2 * hid),
        "right_out": low(2 * tokens, width),
        "right_in": low(2 * tokens, 2 * channels),
        "mixer": low(2, 2, quarter, width),
        "weights": low(channels, width),
        "scan": rows, "step": rows, "drive": rows, "push": rows,
        "decay_rows": full(tokens, 128),
        "into": full(tokens, states, 128), "out_of": full(tokens, states, 128),
        "into_wide": full(tokens, states, 128), "out_wide": full(tokens, states, 128),
        "hist": full(2, tokens, states, 128),
        "step_sum": full(8, channels), "starts": full(states, channels),
        "rate_sum": full(states, channels),
        "step_low_grad": low(tokens, channels),
        "chain_move": full(len(bits), states + 8, channels),
        "chain_land": full(len(bits), states + 8, channels),
        "part": low(2, 2, quarter, width), "total": low(2, 2, quarter, width),
        "first_land": low(2, quarter, width), "second_land": low(quarter, width),
        "second_move": low(quarter, width),
        "raw_move": full(2, tokens, narrow), "raw_land": full(2, tokens, narrow),
        "raw_low": low(tokens, narrow), "step_low": low(tokens, rank),
        "grad_pre": full(tokens + 8, channels), "extended": full(tokens + 16, channels),
        "flat_move": full(len(bits), 8, width), "flat_land": full(len(bits), 8, width),
    }
    for k in range(len(bits)):
        size = count >> (k + 1)
        scratch[f"small_work{k}"] = full(size, 2, rows_out, tokens)
        scratch[f"small_away{k}"] = low(size, rows_out, tokens)
        scratch[f"small_land{k}"] = low(size, rows_out, tokens)
    units = {
        "down": (rows_down, width), "gate": (rows_in, hid), "up": (rows_in, hid),
        "out": (rows_out, width), "gin": (rows_in, channels), "cin": (rows_in, channels),
    }
    for name, (part, columns) in units.items():
        scratch[f"{name}_away"] = low(half // 2, part, columns)
        for k in range(n_bits):
            scratch[f"{name}_land{k}"] = low(half >> (k + 1), part, columns)
        scratch[f"{name}_kept"] = full(half // 2, part, columns)

    def sems(size):
        return pltpu.SemaphoreType.DMA((size,))

    scratch |= {
        "load_sems": sems(40), "write_sems": sems(6),
        "pair_sends": sems(8), "pair_receives": sems(8),
        "shared_sends": sems(4), "shared_receives": sems(4),
        "unit_sends": sems(6 * n_bits), "unit_receives": sems(6 * n_bits),
        "sum_sends": sems(12), "sum_receives": sems(12),
        "chain_sends": sems(len(bits)), "chain_receives": sems(len(bits)),
        "raw_sends": sems(3), "raw_receives": sems(3),
        "last_sends": sems(2 * len(bits)), "last_receives": sems(2 * len(bits)),
    }
    names = [*ins, *hbm_ins, *outs, *scratch]
    made = pl.pallas_call(
        functools.partial(backward_kernel, bits, names),
        out_shape=[shape for shape, _ in outs.values()],
        in_specs=[
            pl.BlockSpec(memory_space=pltpu.SMEM) if name == "bounds" else VMEM for name in ins
        ]
        + [ANY] * len(hbm_ins),
        out_specs=[spec for _, spec in outs.values()],
        scratch_shapes=list(scratch.values()),
        compiler_params=pltpu.CompilerParams(
            collective_id=ident, has_side_effects=True, vmem_limit_bytes=63 * 2**20
        ),
        name="block_backward",
    )(*ins.values(), *hbm_ins.values())
    return dict(zip(outs, made))


def rms_gain(values, gain_row):
    return values * lax.rsqrt(jnp.mean(values * values, axis=-1, keepdims=True) + 1e-06) * gain_row


def swiglu(gate_up):
    return jax.nn.silu(gate_up[:, 0]) * gate_up[:, 1]


def local(
    seq_count,
    stream,
    doc_bounds,
    norm_gains,
    w_in,
    chan_vectors,
    decay_logs,
    w_x,
    small_gains,
    w_dt,
    w_out,
    w_gate_up,
    w_down,
    cotangent,
):
    tokens, width = stream.shape
    rank, (states, channels) = w_dt.shape[0], decay_logs.shape

    def turned(values):
        return values.T.reshape(seq_count // 2, 2, values.shape[1] // seq_count, tokens)

    stream_in = stream.astype(f32)
    normed_low = rms_gain(stream_in, norm_gains[0]).astype(bf16)
    w_in_flat = w_in.reshape(width, 2 * channels)
    in_proj = jnp.dot(normed_low, w_in_flat, preferred_element_type=f32).astype(bf16)
    one_in = turned(normed_low)
    (
        halo, pre_conv, conv_low, raw_proj, step_pre, into, out_of, scan_out, gated_low,
        last_state, mixer_low, before, one_came, cot_came,
    ) = mixer_forward(
        doc_bounds, in_proj, chan_vectors, decay_logs, w_x, small_gains[None], w_dt, w_out,
        one_in, cotangent, seq_count, 1,
    )
    middle = stream_in + mixer_low.reshape(tokens, width).astype(f32)
    normed_two_low = rms_gain(middle, norm_gains[1]).astype(bf16)
    gate_up = jnp.einsum("td,dkf->tkf", normed_two_low, w_gate_up, preferred_element_type=f32)
    hidden_act, act_back = jax.vjp(swiglu, gate_up)
    hidden_low = hidden_act.astype(bf16)
    hidden_grad = jnp.einsum("td,fd->tf", cotangent, w_down, preferred_element_type=f32)
    (gate_up_grad,) = act_back(hidden_grad)
    gate_up_low = gate_up_grad.astype(bf16)
    normed_two_part = jnp.einsum("tkf,dkf->td", gate_up_low, w_gate_up, preferred_element_type=f32)
    feed_part = jnp.dot(hidden_low, w_down, preferred_element_type=f32)

    def quartered(values):
        return values.astype(bf16).reshape(2, 2, tokens // 4, width)

    made = backward(
        {
            "bounds": doc_bounds, "stream": stream, "gains": norm_gains, "proj": in_proj,
            "halo": halo, "pre": pre_conv, "low": conv_low, "raw": raw_proj,
            "step_pre": step_pre, "last_state": last_state, "chan": chan_vectors,
            "logs": decay_logs, "w_x": w_x, "w_dt": w_dt, "small_gains": small_gains[None],
        },
        {
            "two_part": quartered(normed_two_part), "feed_part": quartered(feed_part),
            "mixer_in": mixer_low, "cot": cotangent, "cot_came": cot_came,
            "gate_up_in": gate_up_low.reshape(tokens, -1), "two_in": turned(normed_two_low),
            "hidden_in": turned(hidden_low), "gated_in": turned(gated_low), "one_in": one_in,
            "one_came": one_came, "w_out": w_out, "w_in": w_in_flat, "scan_in": scan_out,
            "into_in": into, "out_of_in": out_of, "hist_in": before,
        },
        seq_count,
        2,
    )
    small, flat = made["small_out"], made["flat_out"]
    at = w_x.shape[1]
    x_part, small = small[:, :at], small[:, at:].T
    dt_part, decay_out = small[:rank], small[rank : rank + states]
    chan_part = small[rank + states : rank + states + 7]
    me = lax.axis_index("seq")
    gain_width = width // seq_count
    gains_part = lax.dynamic_slice_in_dim(flat[:2], me * gain_width, gain_width, 1)
    small_width = small_gains.shape[0] // seq_count
    small_part = lax.dynamic_slice_in_dim(flat[2], me * small_width, small_width, 0)
    rms_values = jnp.sqrt(jnp.sum(flat[3:6], axis=1) / (tokens * seq_count * width))
    return (
        made["out_rows"],
        made["stream_grad"],
        gains_part,
        jnp.stack([made["cin_out"], made["gin_out"]], 1),
        chan_part,
        decay_out,
        x_part,
        small_part,
        dt_part,
        made["out_out"],
        jnp.stack([made["gate_out"], made["up_out"]], 1),
        made["down_out"],
        rms_values,
    )


def solution(mesh):
    in_specs = (
        P("seq", None),
        P(),
        P(),
        P(None, None, "ch"),
        P(None, "ch"),
        P(None, "ch"),
        P("ch", None),
        P(),
        P(None, "ch"),
        P("ch", None),
        P(None, None, "ch"),
        P("ch", None),
        P("seq", None),
    )
    out_specs = (
        P("seq", None),
        P("seq", None),
        P(None, "seq"),
        P("seq", None, "ch"),
        P(None, ("ch", "seq")),
        P(None, ("ch", "seq")),
        P(("ch", "seq"), None),
        P("seq"),
        P(None, ("ch", "seq")),
        P(("ch", "seq"), None),
        P("seq", None, "ch"),
        P(("ch", "seq"), None),
        P(),
    )
    return jax.shard_map(
        functools.partial(local, mesh.shape["seq"]),
        mesh=mesh,
        in_specs=in_specs,
        out_specs=out_specs,
        check_vma=False,
    )
```

```python
import functools
import math
import types

import jax
import jax.numpy as jnp
from jax import lax
from jax.experimental import pallas as pl
from jax.experimental.pallas import tpu as pltpu
from jax.sharding import PartitionSpec as P

f32 = jnp.float32
bf16 = jnp.bfloat16
LOG2E = math.log2(math.e)
LN2 = math.log(2.0)
RESET = 1e30
UNROLL = 8
LANES = 256
VMEM = pl.BlockSpec(memory_space=pltpu.VMEM)


def shape_of(*dims, dtype=f32):
    return jax.ShapeDtypeStruct(dims, dtype)


def cost(us):
    return pl.CostEstimate(flops=int(us * 1e9), bytes_accessed=int(us * 1e6), transcendentals=0)


def widened(column, width):
    return jnp.concatenate([column] * (width // 128), 1)


ANY = pl.BlockSpec(memory_space=pl.ANY)


def sent(source, target, sends, receives, slot, axis, partner):
    copy = pltpu.make_async_remote_copy(
        src_ref=source,
        dst_ref=target,
        send_sem=sends.at[slot],
        recv_sem=receives.at[slot],
        device_id={axis: partner},
        device_id_type=pl.DeviceIdType.MESH,
    )
    copy.start()
    return copy


def bits_of(count):
    return [1 << k for k in range(count.bit_length() - 1)]


def flipped(me, bit):
    mine = lax.rem(me // bit, 2)
    return mine, me + bit - 2 * bit * mine


CHUNK = 32


def sigmoid(values):
    return 1.0 / (1.0 + jnp.exp(-values))


def softplus(values):
    return jnp.maximum(values, 0.0) + jnp.log1p(jnp.exp(-jnp.abs(values)))


def row_doc(places, bounds):
    return (places >= bounds[0]).astype(jnp.int32) + (places >= bounds[1]).astype(jnp.int32)


def tap_mask(places, bounds, offset):
    source = places - offset
    same = row_doc(source, bounds) == row_doc(places, bounds)
    return jnp.where((source >= 0) & same, 1.0, 0.0)


def mean_square(values):
    return jnp.mean(values * values, axis=-1, keepdims=True)


def three_norms(raw, gains, rank, states):
    low, mid, high = raw[:, :rank], raw[:, rank : rank + states], raw[:, rank + states :]
    low_scale = lax.rsqrt(mean_square(low) + 1e-06)
    mid_scale = lax.rsqrt(jnp.maximum(mean_square(mid), 0.1))
    high_scale = lax.rsqrt(jnp.maximum(mean_square(high), 0.1))
    return (
        low * low_scale * gains[:, :rank],
        mid * mid_scale * gains[:, rank : rank + states],
        high * high_scale * gains[:, rank + states :],
    )


def widen(values, wide, first, count):
    states = values.shape[1]
    eye = (
        lax.broadcasted_iota(jnp.int32, (states, states), 0)
        == lax.broadcasted_iota(jnp.int32, (states, states), 1)
    ).astype(f32)
    spread = jnp.sum(values[:, None, :] * eye[None], axis=-1, keepdims=True)
    wide[pl.ds(first, count)] = jnp.broadcast_to(spread, (count, states, 128))


def greeted(axis_partners):
    barrier = pltpu.get_barrier_semaphore()
    for axis, partner in axis_partners:
        pl.semaphore_signal(
            barrier, inc=1, device_id={axis: partner}, device_id_type=pl.DeviceIdType.MESH
        )
    pl.semaphore_wait(barrier, len(axis_partners))


def chained(forward, bits, state, steps, rates, moving, landed, sends, receives, base):
    me = lax.axis_index("seq")
    states = state.shape[0]
    all_state, all_steps = state, steps
    mine_state, mine_steps = jnp.zeros_like(all_state), jnp.zeros_like(all_steps)
    for k, bit in enumerate(bits):
        mine, partner = flipped(me, bit)
        moving[k, :states] = all_state
        moving[k, states:] = all_steps
        sent(moving.at[k], landed.at[k], sends, receives, base + k, "seq", partner).wait()
        other_state, other_steps = landed[k, :states], landed[k, states:]
        earlier = (mine == 1) if forward else (mine == 0)
        through = jnp.exp2(rates * mine_steps[:1])
        mine_state = jnp.where(earlier, mine_state + through * other_state, mine_state)
        mine_steps = jnp.where(earlier, mine_steps + other_steps, mine_steps)
        after = jnp.exp2(rates * all_steps[:1]) * other_state + all_state
        ahead_of = jnp.exp2(rates * other_steps[:1]) * all_state + other_state
        all_state = jnp.where(earlier, after, ahead_of)
        all_steps = all_steps + other_steps
    return mine_state


def forward_kernel(
    bits, bounds, proj, chan, logs, w_x, gains, w_dt, w_out, one_in, cot,
    halo, pre_out, low_out, raw_out, step_pre_out, into, out_of, scan_out, gated_out, last_state,
    mixer, hist_out, one_came, cot_came,
    extended, raw_move, raw_land, step, drive, starts, moving, landed, part, first_land,
    second_move, second_land, hist, sends, receives, hist_sem, shared_sends, shared_receives,
):
    tokens, channels = low_out.shape
    rank, states = w_dt.shape[0], logs.shape[0]
    chunks = tokens // CHUNK
    ch_me, me = lax.axis_index("ch"), lax.axis_index("seq")
    seq_count = 1 << len(bits)
    low, across = flipped(ch_me, 1)
    high, along = flipped(ch_me, 2)
    following, previous = lax.rem(me + 1, seq_count), lax.rem(me + seq_count - 1, seq_count)
    greeted(
        [("ch", across), ("ch", along), ("seq", following), ("seq", previous)]
        + [("seq", flipped(me, bit)[1]) for bit in bits]
    )
    halo_copy = sent(
        proj.at[pl.ds(tokens - 16, 16), pl.ds(0, channels)], halo, sends, receives, 0, "seq",
        following,
    )
    mine, pair = flipped(me, bits[1])
    half = one_in.shape[0] // 2
    some = pl.ds(low * half, half)
    at = pl.ds(pl.multiple_of(low * (tokens // 2), tokens // 2), tokens // 2)
    shared = [
        (one_in.at[some, 1 - mine], one_came.at[some]),
        (cot.at[at], cot_came.at[at]),
    ]
    shared_copies = [
        sent(source, target, shared_sends, shared_receives, k, "seq", pair)
        for k, (source, target) in enumerate(shared)
    ]
    rates = -jnp.exp(logs[...]) * LOG2E
    halo_copy.wait()
    extended[0:16] = halo[...].astype(f32)

    def spread(index, _):
        first = pl.multiple_of(index * CHUNK, CHUNK)
        extended[pl.ds(first + 16, CHUNK)] = proj[pl.ds(first, CHUNK), :channels].astype(f32)
        return 0

    lax.fori_loop(0, chunks, spread, 0)

    def convolved(index, _):
        first = pl.multiple_of(index * CHUNK, CHUNK)
        places = me * tokens + first + lax.broadcasted_iota(jnp.int32, (CHUNK, 128), 0)
        window = extended[pl.ds(first, CHUNK + 16)]
        summed = chan[4:5]
        for k in range(4):
            mask = widened(tap_mask(places, bounds, 3 - k), channels)
            summed = summed + chan[k : k + 1] * window[13 + k : 13 + k + CHUNK] * mask
        pre_out[pl.ds(first, CHUNK)] = summed
        low_out[pl.ds(first, CHUNK)] = (summed * sigmoid(summed)).astype(bf16)
        return 0

    lax.fori_loop(0, chunks, convolved, 0)
    raw_move[0] = jnp.dot(low_out[...], w_x[...], preferred_element_type=f32)
    sent(raw_move.at[0], raw_land.at[0], sends, receives, 1, "ch", across).wait()
    raw_move[1] = raw_move[0] + raw_land[0]
    sent(raw_move.at[1], raw_land.at[1], sends, receives, 2, "ch", along).wait()

    def stepped(index, total):
        first = pl.multiple_of(index * CHUNK, CHUNK)
        rows = pl.ds(first, CHUNK)
        raw = raw_move[1, rows] + raw_land[1, rows]
        raw_out[rows] = raw
        step_norm, input_norm, output_norm = three_norms(raw, gains[...], rank, states)
        widen(input_norm, into, first, CHUNK)
        widen(output_norm, out_of, first, CHUNK)
        pre = (
            jnp.dot(step_norm.astype(bf16), w_dt[...], preferred_element_type=f32) + chan[5:6]
        )
        step_pre_out[rows] = pre
        size = softplus(pre)
        drive[rows] = size * low_out[rows].astype(f32)
        places = me * tokens + first + lax.broadcasted_iota(jnp.int32, (CHUNK, 128), 0)
        resets = jnp.where((places == bounds[0]) | (places == bounds[1]), RESET, 0.0)
        size = size + widened(resets, channels)
        step[rows] = size
        return total + jnp.sum(size, axis=0, keepdims=True)

    total = lax.fori_loop(0, chunks, stepped, jnp.zeros((1, channels), f32))
    blocks = [slice(j, j + LANES) for j in range(0, channels, LANES)]
    for lanes in blocks:
        block_rates = rates[:, lanes]

        def ended(index, state, lanes=lanes, block_rates=block_rates):
            first = pl.multiple_of(index * UNROLL, UNROLL)
            steps, drives = step[pl.ds(first, UNROLL), lanes], drive[pl.ds(first, UNROLL), lanes]
            for k in range(UNROLL):
                decay = jnp.exp2(steps[k : k + 1] * block_rates)
                state = decay * state + widened(into[first + k], LANES) * drives[k : k + 1]
            return state

        starts[:, lanes] = lax.fori_loop(
            0, tokens // UNROLL, ended, jnp.zeros((states, LANES), f32)
        )
    starts[...] = chained(
        True, bits, starts[...], jnp.broadcast_to(total, (8, channels)), rates, moving, landed,
        sends, receives, 7,
    )
    hist_copies = []
    for number, lanes in enumerate(blocks):
        block_rates = rates[:, lanes]
        skip = chan[6:7, lanes]

        def walked(index, state, lanes=lanes, block_rates=block_rates, skip=skip):
            first = pl.multiple_of(index * UNROLL, UNROLL)
            steps, drives = step[pl.ds(first, UNROLL), lanes], drive[pl.ds(first, UNROLL), lanes]
            rows = []
            for k in range(UNROLL):
                hist[first + k, :, lanes] = state
                decay = jnp.exp2(steps[k : k + 1] * block_rates)
                state = decay * state + widened(into[first + k], LANES) * drives[k : k + 1]
                rows.append(
                    jnp.sum(widened(out_of[first + k], LANES) * state, axis=0, keepdims=True)
                )
            scan_out[pl.ds(first, UNROLL), lanes] = jnp.concatenate(rows, 0)
            return state

        last_state[:, lanes] = lax.fori_loop(0, tokens // UNROLL, walked, starts[:, lanes])
        copy = pltpu.make_async_copy(
            hist.at[:, :, lanes], hist_out.at[:, :, lanes], hist_sem.at[number]
        )
        copy.start()
        hist_copies.append(copy)

    def gate(index, _):
        first = pl.multiple_of(index * CHUNK, CHUNK)
        rows = pl.ds(first, CHUNK)
        scanned = scan_out[rows] + chan[6:7] * low_out[rows].astype(f32)
        scan_out[rows] = scanned
        gate_pre = proj[rows, channels:].astype(f32)
        gated_out[rows] = (scanned * gate_pre * sigmoid(gate_pre)).astype(bf16)
        return 0

    lax.fori_loop(0, chunks, gate, 0)
    quarter = tokens // 4
    width = w_out.shape[1]
    for k, (_, target) in enumerate(shared):
        shared_copies[k].wait()
        shared_copies[k] = sent(
            target, target, shared_sends, shared_receives, 2 + k, "ch", across
        )

    def mixed(index, _):
        first = pl.multiple_of(index * 512, 512)
        product = jnp.dot(
            gated_out[...], w_out[:, pl.ds(first, 512)], preferred_element_type=f32
        ).astype(bf16)
        for k in range(4):
            part[k // 2, k % 2, :, pl.ds(first, 512)] = product[k * quarter : (k + 1) * quarter]
        return 0

    lax.fori_loop(0, width // 512, mixed, 0)
    four_summed(
        part, mixer, first_land, second_land, second_move, sends, receives, 3, low, across, high,
        along,
    )
    for copy in hist_copies + shared_copies:
        copy.wait()


def four_summed(
    value, total, first, second, moving, sends, receives, base, low, across, high, along
):
    sent(value.at[:, 1 - low], first, sends, receives, base, "ch", across).wait()
    moving[...] = (
        value[1 - high, low].astype(f32) + first[1 - high].astype(f32)
    ).astype(bf16)
    copy = sent(moving, second, sends, receives, base + 1, "ch", along)
    kept = value[high, low].astype(f32) + first[high].astype(f32)
    copy.wait()
    total[high, low] = (kept + second[...].astype(f32)).astype(bf16)
    own = total.at[high, low]
    sent(own, own, sends, receives, base + 2, "ch", along).wait()
    both = total.at[:, low]
    sent(both, both, sends, receives, base + 3, "ch", across).wait()


def mixer_forward(bounds, proj, chan, logs, w_x, gains, w_dt, w_out, one_in, cot, count, ident):
    bits = bits_of(count)
    tokens, channels = proj.shape[0], proj.shape[1] // 2
    states, rank, width = logs.shape[0], w_dt.shape[0], w_out.shape[1]
    quarter, narrow = tokens // 4, w_x.shape[1]
    rows = shape_of(tokens, channels)
    low_rows = shape_of(tokens, channels, dtype=bf16)
    wide = shape_of(tokens, states, 128)
    slots = pltpu.VMEM((len(bits), states + 8, channels), f32)
    raws = pltpu.VMEM((2, tokens, narrow), f32)
    out = pl.pallas_call(
        functools.partial(forward_kernel, bits),
        out_shape=[
            shape_of(16, channels, dtype=bf16), rows, low_rows, shape_of(tokens, narrow), rows,
            wide, wide, rows, low_rows, shape_of(states, channels),
            shape_of(2, 2, quarter, width, dtype=bf16), shape_of(tokens, states, channels),
            shape_of(one_in.shape[0], *one_in.shape[2:], dtype=bf16),
            shape_of(tokens, width, dtype=bf16),
        ],
        in_specs=[pl.BlockSpec(memory_space=pltpu.SMEM)] + [VMEM] * 7 + [ANY] * 2,
        out_specs=[VMEM] * 11 + [ANY] * 3,
        scratch_shapes=[
            pltpu.VMEM((tokens + 16, channels), f32), raws, raws,
            pltpu.VMEM((tokens, channels), f32), pltpu.VMEM((tokens, channels), f32),
            pltpu.VMEM((states, channels), f32), slots, slots,
            pltpu.VMEM((2, 2, quarter, width), bf16), pltpu.VMEM((2, quarter, width), bf16),
            pltpu.VMEM((quarter, width), bf16), pltpu.VMEM((quarter, width), bf16),
            pltpu.VMEM((tokens, states, channels), f32),
            pltpu.SemaphoreType.DMA((7 + len(bits),)), pltpu.SemaphoreType.DMA((7 + len(bits),)),
            pltpu.SemaphoreType.DMA((channels // LANES,)),
            pltpu.SemaphoreType.DMA((4,)), pltpu.SemaphoreType.DMA((4,)),
        ],
        compiler_params=pltpu.CompilerParams(
            collective_id=ident, has_side_effects=True, vmem_limit_bytes=56 * 2**20
        ),
        cost_estimate=cost(6),
        name="mixer_forward",
    )(bounds, proj, chan, logs, w_x, gains, w_dt, w_out, one_in, cot)
    return out


class Unit:
    def __init__(self, left, right, columns, refs, sends, receives, slot, bits, result):
        self.left, self.right, self.columns = left, right, columns
        away, *self.land, self.kept = refs
        self.away = [away.at[pl.ds(0, land.shape[0])] for land in self.land]
        self.sends, self.receives, self.slot, self.bits = sends, receives, slot, bits
        self.result = result
        self.stage = 0
        self.copy = None

    def made(self, *needed):
        for item in needed:
            item.wait()
        mine, partner = flipped(lax.axis_index("seq"), self.bits[0])
        self.make(1 - mine, self.away[0])
        self.stage = 1
        self.go = lambda: self.begin(partner, mine)
        return self

    def begin(self, partner, mine):
        self.copy = self.start(0, partner)
        self.make(mine, self.kept)

    def next(self):
        stage, me = self.stage, lax.axis_index("seq")
        if stage > len(self.bits):
            return
        self.stage += 1
        left_over = stage == len(self.bits)
        self.copy.wait()
        count = self.land[stage - 1].shape[0]
        rows = self.kept.shape[1]
        part = 32 if rows % 32 == 0 else rows
        parts = rows // part

        def total(index, at):
            return self.kept[index, at] + self.land[stage - 1][index, at].astype(f32)

        if left_over:

            def finish(step, _):
                at = pl.ds(pl.multiple_of(step * part, part), part)
                self.kept[0, at] = total(0, at)
                return 0

            lax.fori_loop(0, parts, finish, 0)
            self.written = self.result(self.kept.at[0])
            return
        mine, partner = flipped(me, self.bits[stage])

        def send(step, _):
            index = lax.div(step, parts)
            at = pl.ds(pl.multiple_of(lax.rem(step, parts) * part, part), part)
            self.away[stage][index, at] = total(2 * index + 1 - mine, at).astype(bf16)
            return 0

        lax.fori_loop(0, (count // 2) * parts, send, 0)
        self.copy = self.start(stage, partner)

        def keep(step, _):
            index = lax.div(step, parts)
            at = pl.ds(pl.multiple_of(lax.rem(step, parts) * part, part), part)
            self.kept[index, at] = total(2 * index + mine, at)
            return 0

        lax.fori_loop(0, (count // 2) * parts, keep, 0)

    def start(self, stage, partner):
        return sent(
            self.away[stage], self.land[stage], self.sends, self.receives, self.slot + stage,
            "seq", partner,
        )

    def make(self, side, target):
        first, width = self.columns
        tile = 512 if width % 512 == 0 else 256
        tiles = width // tile

        def block(step, _):
            index = lax.div(step, tiles)
            column = pl.multiple_of(lax.rem(step, tiles) * tile, tile)
            product = jnp.dot(
                self.left[index, side],
                self.right[:, pl.ds(first + column, tile)],
                preferred_element_type=f32,
            )
            target[index, :, pl.ds(column, tile)] = product.astype(target.dtype)
            return 0

        lax.fori_loop(0, target.shape[0] * tiles, block, 0)


def norm_back(values, scale, gains, grad, free=True):
    weighted = gains * grad
    result = scale * weighted
    inner = jnp.mean(values * weighted, axis=-1, keepdims=True)
    return result - jnp.where(free, 1.0, 0.0) * values * (scale * scale * scale) * inner, (
        grad * values * scale
    )


def silu_slope(values):
    part = sigmoid(values)
    return part * (1.0 + values * (1.0 - part))


def narrowed(wide, first, count):
    states = wide.shape[1]
    eye = (
        lax.broadcasted_iota(jnp.int32, (states, states), 0)
        == lax.broadcasted_iota(jnp.int32, (states, states), 1)
    ).astype(f32)
    sums = jnp.sum(wide[pl.ds(first, count)], axis=-1, keepdims=True)
    return jnp.sum(sums * eye[None], axis=1)


def dot_rows(left, right):
    return lax.dot_general(left, right, (((1,), (1,)), ((), ())), preferred_element_type=f32)


class Once:
    def __init__(self, *copies, then=None):
        self.copies, self.then = copies, then

    def wait(self):
        for copy in self.copies:
            copy.wait()
        self.copies = ()
        if self.then is not None:
            after, self.then = self.then, None
            after().wait()


def named(names, refs):
    refs, found = list(refs), {}
    for name, count in names:
        taken, refs = refs[: count or 1], refs[count or 1 :]
        found[name] = taken if count else taken[0]
    return types.SimpleNamespace(**found)


def backward_kernel(bits, names, *refs):
    r = named(names, refs)
    tokens, width = r.stream.shape
    channels, rank, states = r.low.shape[1], r.w_dt.shape[0], r.logs.shape[0]
    quarter, chunks = tokens // 4, tokens // CHUNK
    ch_me, me = lax.axis_index("ch"), lax.axis_index("seq")
    seq_count = 1 << len(bits)
    low, across = flipped(ch_me, 1)
    high, along = flipped(ch_me, 2)
    pair_bit, rest_bits = bits[1], [bits[0], *bits[2:]]
    mine, pair = flipped(me, pair_bit)
    following, previous = lax.rem(me + 1, seq_count), lax.rem(me + seq_count - 1, seq_count)
    load_slots, pair_slots, shared_slots, write_slots = ([] for _ in range(4))

    def slot_of(slots):
        slots.append(0)
        return len(slots) - 1

    def load(source, target):
        copy = pltpu.make_async_copy(source, target, r.load_sems.at[slot_of(load_slots)])
        copy.start()
        return Once(copy)

    own, other = pl.ds(0, tokens), pl.ds(tokens, tokens)
    high_count = r.left_two.shape[0]
    hid = r.right_two.shape[1] // 2
    part_in = load(r.two_part, r.part)
    hidden_own = load(r.hidden_in.at[:, mine], r.left_hidden.at[:, :, :, own])
    cot_own = load(r.cot, r.right_down.at[own])
    cot_other = load(r.cot_came, r.right_down.at[other])
    gate_up_own = load(r.gate_up_in, r.right_two.at[own])
    two_own = load(r.two_in.at[:, mine], r.left_two.at[:, :, :, own])
    mixer_own = load(r.mixer_in, r.mixer)
    weights = load(r.w_out, r.weights)
    scan_own = load(r.scan_in, r.scan)
    out_of_own = load(r.out_of_in, r.out_of)
    into_own = load(r.into_in, r.into)
    one_own = load(r.one_in.at[:, mine], r.left_one.at[:, :, :, own])
    one_other = load(r.one_came, r.left_one.at[:, :, :, other])
    gated_own = load(r.gated_in.at[:, mine], r.left_gated.at[:, :, :, own])
    blocks = [slice(j, j + 128) for j in range(0, channels, 128)]
    hists = [load(r.hist_in.at[:, :, blocks[k]], r.hist.at[k]) for k in range(2)]

    greeted(
        [("ch", across), ("ch", along), ("seq", following), ("seq", previous)]
        + [("seq", flipped(me, bit)[1]) for bit in bits]
    )

    def swap(source, target):
        slot = slot_of(pair_slots)
        return Once(sent(source, target, r.pair_sends, r.pair_receives, slot, "seq", pair))

    def swap_shared(source, target):
        slot = 2 * slot_of(shared_slots)
        copy = sent(source, target, r.shared_sends, r.shared_receives, slot, "seq", pair)
        return Once(
            copy,
            then=lambda: sent(
                target, target, r.shared_sends, r.shared_receives, slot + 1, "ch", across
            ),
        )

    n_bits = len(rest_bits)

    def writer(target):
        def write(source):
            copy = pltpu.make_async_copy(source, target, r.write_sems.at[slot_of(write_slots)])
            copy.start()
            return copy

        return write

    def unit(left, right, columns, refs, slot, target):
        return Unit(
            left, right, columns, refs, r.unit_sends, r.unit_receives, slot * n_bits, rest_bits,
            writer(target),
        )

    down = unit(r.left_hidden, r.right_down, (0, width), r.down, 0, r.down_out)
    gate = unit(r.left_two, r.right_two, (0, hid), r.gate, 1, r.gate_out)
    up = unit(r.left_two, r.right_two, (hid, hid), r.up, 2, r.up_out)
    out = unit(r.left_gated, r.right_out, (0, width), r.out, 3, r.out_out)
    gin = unit(r.left_one, r.right_in, (channels, channels), r.gin, 4, r.gin_out)
    cin = unit(r.left_one, r.right_in, (0, channels), r.cin, 5, r.cin_out)

    some = pl.ds(low * (high_count // 2), high_count // 2)
    hidden_other = swap(r.hidden_in.at[:, 1 - mine], r.left_hidden.at[:, :, :, other])
    two_other = swap_shared(r.two_in.at[some, 1 - mine], r.left_two.at[some, :, :, other])
    gate_other = swap(r.gate_up_in.at[:, pl.ds(0, hid)], r.right_two.at[other, pl.ds(0, hid)])
    up_other = swap(r.gate_up_in.at[:, pl.ds(hid, hid)], r.right_two.at[other, pl.ds(hid, hid)])

    sums = (r.first_land, r.second_land, r.second_move, r.sum_sends, r.sum_receives)

    def summed(value, base):
        first, second, moving, sends, receives = sums
        copy = sent(value.at[:, 1 - low], first, sends, receives, base, "ch", across)
        yield
        copy.wait()
        moving[...] = (
            value[1 - high, low].astype(f32) + first[1 - high].astype(f32)
        ).astype(bf16)
        copy = sent(moving, second, sends, receives, base + 1, "ch", along)
        yield
        copy.wait()
        r.total[high, low] = (
            value[high, low].astype(f32) + first[high].astype(f32) + second[...].astype(f32)
        ).astype(bf16)
        part = r.total.at[high, low]
        copy = sent(part, part, sends, receives, base + 2, "ch", along)
        yield
        copy.wait()
        both = r.total.at[:, low]
        copy = sent(both, both, sends, receives, base + 3, "ch", across)
        yield
        copy.wait()
        yield

    rates = -jnp.exp(r.logs[...]) * LOG2E

    def places_of(first, count):
        return me * tokens + first + lax.broadcasted_iota(jnp.int32, (count, 128), 0)

    def resteps():
        def body(index, total):
            first = pl.multiple_of(index * CHUNK, CHUNK)
            rows = pl.ds(first, CHUNK)
            size = softplus(r.step_pre[rows])
            r.drive[rows] = size * r.low[rows].astype(f32)
            places = places_of(first, CHUNK)
            resets = jnp.where((places == r.bounds[0]) | (places == r.bounds[1]), RESET, 0.0)
            size = size + widened(resets, channels)
            r.step[rows] = size
            return total + jnp.sum(size, axis=0, keepdims=True)

        r.step_sum[...] = jnp.broadcast_to(
            lax.fori_loop(0, chunks, body, jnp.zeros((1, channels), f32)), (8, channels)
        )

    part_in.wait()
    two_sum = summed(r.part, 0)
    next(two_sum)
    resteps()
    next(two_sum)
    down.made(hidden_own, cot_own, cot_other, hidden_other).go()
    next(two_sum)
    next(two_sum)
    next(two_sum)
    part_in = load(r.feed_part, r.part)
    mixer_own.wait()

    def quarter_rows(index):
        per = quarter // CHUNK
        part = lax.div(index, per)
        at = pl.ds(pl.multiple_of(lax.rem(index, per) * CHUNK, CHUNK), CHUNK)
        return lax.div(part, 2), lax.rem(part, 2), at

    def norm_two(index, total):
        first = pl.multiple_of(index * CHUNK, CHUNK)
        rows = pl.ds(first, CHUNK)
        a, b, at = quarter_rows(index)
        middle = r.stream[rows].astype(f32) + r.mixer[a, b, at].astype(f32)
        scale = lax.rsqrt(mean_square(middle) + 1e-06)
        back, gain = norm_back(middle, scale, r.gains[1:2], r.total[a, b, at].astype(f32))
        grad = r.right_down[rows].astype(f32) + back
        r.stream_grad[rows] = grad
        r.right_out[rows] = grad.astype(bf16)
        return total + jnp.sum(gain, axis=0, keepdims=True)

    gain_two = lax.fori_loop(0, chunks, norm_two, jnp.zeros((1, width), f32))
    r.flat_move[0] = jnp.zeros_like(r.flat_move[0])
    r.flat_move[0, 1:2] = gain_two
    weights.wait()
    scan_own.wait()
    skips = []
    for j in range(0, channels, 256):
        lanes = slice(j, j + 256)
        gated_grad = dot_rows(r.right_out[own], r.weights[pl.ds(j, 256)])
        gate_pre = r.proj[:, channels + j : channels + j + 256].astype(f32)
        part = sigmoid(gate_pre)
        slope = part * (1.0 + gate_pre * (1.0 - part))
        r.right_in[own, channels + j : channels + j + 256] = (
            gated_grad * r.scan[:, lanes] * slope
        ).astype(bf16)
        grad = gated_grad * gate_pre * part
        r.scan[:, lanes] = grad
        skips.append(jnp.sum(grad * r.low[:, lanes].astype(f32), axis=0, keepdims=True))
    skip_grad = jnp.concatenate(skips, 1)
    weights = load(r.w_in.at[pl.ds(0, channels)], r.weights)
    out_of_own.wait()
    for j in range(0, channels, LANES):
        lanes = slice(j, j + LANES)

        def ended(index, carried, lanes=lanes, block_rates=rates[:, j : j + LANES]):
            first = pl.multiple_of(tokens - UNROLL - index * UNROLL, UNROLL)
            steps, grads = r.step[pl.ds(first, UNROLL), lanes], r.scan[pl.ds(first, UNROLL), lanes]
            for k in reversed(range(UNROLL)):
                decay = jnp.exp2(steps[k : k + 1] * block_rates)
                carried = decay * (widened(r.out_of[first + k], LANES) * grads[k : k + 1] + carried)
            return carried

        r.starts[:, lanes] = lax.fori_loop(
            0, tokens // UNROLL, ended, jnp.zeros((states, LANES), f32)
        )

    def handed():
        all_state, all_steps = r.starts[...], r.step_sum[...]
        mine_state, mine_steps = jnp.zeros_like(all_state), jnp.zeros_like(all_steps)
        for k, bit in enumerate(bits):
            side, partner = flipped(me, bit)
            r.chain_move[k, :states] = all_state
            r.chain_move[k, states:] = all_steps
            copy = sent(r.chain_move.at[k], r.chain_land.at[k], r.chain_sends, r.chain_receives,
                        k, "seq", partner)
            yield
            copy.wait()
            other_state, other_steps = r.chain_land[k, :states], r.chain_land[k, states:]
            earlier = side == 0
            through = jnp.exp2(rates * mine_steps[:1])
            mine_state = jnp.where(earlier, mine_state + through * other_state, mine_state)
            mine_steps = jnp.where(earlier, mine_steps + other_steps, mine_steps)
            after = jnp.exp2(rates * all_steps[:1]) * other_state + all_state
            ahead_of = jnp.exp2(rates * other_steps[:1]) * all_state + other_state
            all_state = jnp.where(earlier, after, ahead_of)
            all_steps = all_steps + other_steps
        r.starts[...] = mine_state
        yield

    chain = handed()
    next(chain)
    gate.made(two_own, gate_up_own, two_other, gate_other)
    next(chain)
    gate.go()
    next(chain)
    first = pl.multiple_of(low * (tokens // 2), tokens // 2)
    mixer_other = swap_shared(
        r.right_out.at[pl.ds(first, tokens // 2)],
        r.right_out.at[pl.ds(tokens + first, tokens // 2)],
    )
    gated_other = swap(r.gated_in.at[:, 1 - mine], r.left_gated.at[:, :, :, other])
    gin_other = swap(
        r.right_in.at[own, pl.ds(channels, channels)],
        r.right_in.at[other, pl.ds(channels, channels)],
    )
    up.made(up_other).go()
    for _ in chain:
        pass

    part_in.wait()
    feed_sum = summed(r.part, 4)
    into_own.wait()

    def results():
        totals = lax.fori_loop(
            0, chunks, results_of, tuple(jnp.zeros((1, width), f32) for _ in range(3))
        )
        for number, total in enumerate(totals):
            r.flat_move[0, 3 + number : 4 + number] = total

    between = [
        lambda: (next(feed_sum), down.next()),
        lambda: next(feed_sum),
        lambda: (next(feed_sum), gate.next()),
        lambda: (next(feed_sum), out.made(gated_own, mixer_other, gated_other).go()),
        lambda: (next(feed_sum), results()),
        lambda: gin.made(one_own, one_other, gin_other).go(),
    ]

    def results_of(index, totals):
        rows = pl.ds(pl.multiple_of(index * CHUNK, CHUNK), CHUNK)
        a, b, at = quarter_rows(index)
        mixed, feed = r.mixer[a, b, at].astype(f32), r.total[a, b, at].astype(f32)
        result = r.stream[rows].astype(f32) + mixed + feed
        r.out_rows[rows] = result.astype(bf16)
        return tuple(
            total + jnp.sum(v * v, axis=0, keepdims=True)
            for total, v in zip(totals, (result, mixed, feed))
        )

    r.into_wide[...] = jnp.zeros_like(r.into_wide)
    r.out_wide[...] = jnp.zeros_like(r.out_wide)
    for number, lanes in enumerate(blocks):
        hists[number].wait()
        hist = r.hist.at[number % 2]
        block_rates = rates[:, lanes]

        def walked(index, carry, lanes=lanes, block_rates=block_rates, hist=hist):
            carried, state, total = carry
            first = pl.multiple_of(tokens - UNROLL - index * UNROLL, UNROLL)
            some = pl.ds(first, UNROLL)
            steps, drives, grads = r.step[some, lanes], r.drive[some, lanes], r.scan[some, lanes]
            decay_list, push_list = [None] * UNROLL, [None] * UNROLL
            for k in reversed(range(UNROLL)):
                place = first + k
                grad_row = grads[k : k + 1]
                decay = jnp.exp2(steps[k : k + 1] * block_rates)
                adjoint = r.out_of[place] * grad_row + carried
                carried = decay * adjoint
                r.out_wide[place] = r.out_wide[place] + state * grad_row
                r.into_wide[place] = r.into_wide[place] + adjoint * drives[k : k + 1]
                state = hist[place]
                share = carried * state
                total = total + share * steps[k : k + 1]
                decay_list[k] = jnp.sum(share * block_rates, axis=0, keepdims=True)
                push_list[k] = jnp.sum(r.into[place] * adjoint, axis=0, keepdims=True)
            r.decay_rows[some, :] = jnp.concatenate(decay_list, 0)
            r.push[some, lanes] = jnp.concatenate(push_list, 0)
            return (carried, state, total)

        _, _, total = lax.fori_loop(
            0,
            tokens // UNROLL,
            walked,
            (r.starts[:, lanes], r.last_state[:, lanes], jnp.zeros((states, 128), f32)),
        )
        r.rate_sum[:, lanes] = total * (rates[:, lanes] * LN2)

        def gathered(index, _, lanes=lanes):
            rows = pl.ds(pl.multiple_of(index * CHUNK, CHUNK), CHUNK)
            used, pushed = r.low[rows, lanes].astype(f32), r.push[rows, lanes]
            pre = r.step_pre[rows, lanes]
            grad = (LN2 * r.decay_rows[rows] + pushed * used) * sigmoid(pre)
            r.step_low_grad[rows, lanes] = grad.astype(bf16)
            r.push[rows, lanes] = pushed * softplus(pre) + r.chan[6:7, lanes] * r.scan[rows, lanes]
            return 0

        lax.fori_loop(0, chunks, gathered, 0)
        if number + 2 < len(blocks):
            hists.append(load(r.hist_in.at[:, :, blocks[number + 2]], r.hist.at[number % 2]))
        if number < len(between):
            between[number]()
    for later in between[len(blocks) :]:
        later()

    def norm_grads(index, _):
        first = pl.multiple_of(index * CHUNK, CHUNK)
        rows = pl.ds(first, CHUNK)
        low_part = dot_rows(r.step_low_grad[rows], r.w_dt[...])
        r.raw_move[0, rows] = jnp.concatenate(
            [low_part, narrowed(r.into_wide, first, CHUNK), narrowed(r.out_wide, first, CHUNK)], 1
        )
        return 0

    lax.fori_loop(0, chunks, norm_grads, 0)
    copy = sent(r.raw_move.at[0], r.raw_land.at[0], r.raw_sends, r.raw_receives, 0, "ch", across)
    copy.wait()
    r.raw_move[1] = r.raw_move[0] + r.raw_land[0]
    copy = sent(r.raw_move.at[1], r.raw_land.at[1], r.raw_sends, r.raw_receives, 1, "ch", along)
    copy.wait()

    def raw_back(index, total):
        rows = pl.ds(pl.multiple_of(index * CHUNK, CHUNK), CHUNK)
        grads, raw = r.raw_move[1, rows] + r.raw_land[1, rows], r.raw[rows]
        gains = r.small_gains[...]
        values, sums_to = [], []
        for start, stop, floor in ((0, rank, None), (rank, rank + states, 0.1),
                                   (rank + states, rank + 2 * states, 0.1)):
            value = raw[:, start:stop]
            square = mean_square(value)
            if floor is None:
                scale, free = lax.rsqrt(square + 1e-06), True
            else:
                scale, free = lax.rsqrt(jnp.maximum(square, floor)), square > floor
            back, gain = norm_back(value, scale, gains[:, start:stop], grads[:, start:stop], free)
            values.append(back)
            sums_to.append(jnp.sum(gain, axis=0, keepdims=True))
        norm = raw[:, :rank] * lax.rsqrt(mean_square(raw[:, :rank]) + 1e-06) * gains[:, :rank]
        r.raw_low[rows] = jnp.concatenate(values, 1).astype(bf16)
        r.step_low[rows] = norm.astype(bf16)
        return total + jnp.concatenate(sums_to, 1)

    small = lax.fori_loop(0, chunks, raw_back, jnp.zeros((1, rank + 2 * states), f32))
    r.flat_move[0, 2:3, : rank + 2 * states] = small

    def conv_back(index, total):
        first = pl.multiple_of(index * CHUNK, CHUNK)
        rows = pl.ds(first, CHUNK)
        grad = r.push[rows] + dot_rows(r.raw_low[rows], r.w_x[...])
        grad = grad * silu_slope(r.pre[rows])
        r.grad_pre[rows] = grad
        return total + jnp.sum(grad, axis=0, keepdims=True)

    tap_bias = lax.fori_loop(0, chunks, conv_back, jnp.zeros((1, channels), f32))
    copy = sent(r.grad_pre.at[pl.ds(0, 8)], r.grad_pre.at[pl.ds(tokens, 8)], r.raw_sends,
                r.raw_receives, 2, "seq", previous)
    r.extended[0:16] = r.halo[...].astype(f32)

    def extend(index, _):
        first = pl.multiple_of(index * CHUNK, CHUNK)
        r.extended[pl.ds(first + 16, CHUNK)] = r.proj[pl.ds(first, CHUNK), :channels].astype(f32)
        return 0

    lax.fori_loop(0, chunks, extend, 0)

    def taps(index, totals):
        first = pl.multiple_of(index * CHUNK, CHUNK)
        places = places_of(first, CHUNK)
        window = r.extended[pl.ds(first, CHUNK + 16)]
        grad = r.grad_pre[pl.ds(first, CHUNK)]
        return tuple(
            totals[k]
            + jnp.sum(
                grad
                * widened(tap_mask(places, r.bounds, 3 - k), channels)
                * window[13 + k : 13 + k + CHUNK],
                axis=0,
                keepdims=True,
            )
            for k in range(4)
        )

    tap_grads = lax.fori_loop(
        0, chunks, taps, tuple(jnp.zeros((1, channels), f32) for _ in range(4))
    )
    copy.wait()

    def conv_in_back(index, _):
        first = pl.multiple_of(index * CHUNK, CHUNK)
        window = r.grad_pre[pl.ds(first, CHUNK + 8)]
        grad = jnp.zeros((CHUNK, channels), f32)
        for k in range(4):
            places = places_of(first + 3 - k, CHUNK)
            mask = jnp.where(
                places < seq_count * tokens, tap_mask(places, r.bounds, 3 - k), 0.0
            )
            grad = grad + r.chan[k : k + 1] * widened(mask, channels) * window[3 - k : 3 - k + CHUNK]
        r.right_in[pl.ds(first, CHUNK), :channels] = grad.astype(bf16)
        return 0

    lax.fori_loop(0, chunks, conv_in_back, 0)
    cin_other = swap(
        r.right_in.at[own, pl.ds(0, channels)], r.right_in.at[other, pl.ds(0, channels)]
    )

    for number in range(width // channels):
        weights.wait()

        def one_part(index, _, first=number * channels):
            at = pl.multiple_of(index * 256, 256)
            product = dot_rows(r.right_in[own], r.weights[pl.ds(at, 256)]).astype(bf16)
            for k in range(4):
                r.part[k // 2, k % 2, :, pl.ds(first + at, 256)] = product[
                    k * quarter : (k + 1) * quarter
                ]
            return 0

        lax.fori_loop(0, channels // 256, one_part, 0)
        if (number + 1) * channels < width:
            weights = load(r.w_in.at[pl.ds((number + 1) * channels, channels)], r.weights)
    one_sum = summed(r.part, 8)
    next(one_sum)

    def small_columns():
        narrow = r.w_x.shape[1]
        pack = r.step
        pack[0:narrow] = lax.dot_general(
            r.raw_low[...], r.low[...], (((0,), (0,)), ((), ())), preferred_element_type=f32
        )
        pack[narrow : narrow + rank] = lax.dot_general(
            r.step_low[...], r.step_low_grad[...], (((0,), (0,)), ((), ())),
            preferred_element_type=f32,
        )
        at = narrow + rank
        pack[at : at + states] = r.rate_sum[...]
        at += states
        bias = jnp.sum(r.step_low_grad[...].astype(f32), axis=0, keepdims=True)
        pack[at : at + 8] = jnp.concatenate(
            [*tap_grads, tap_bias, bias, skip_grad, jnp.zeros((1, channels), f32)], 0
        )
        at += 8
        pack[at:] = jnp.zeros((pack.shape[0] - at, channels), f32)
        turned = pack[...].T
        r.small_work[0][...] = turned.reshape(r.small_work[0].shape)

    def small_summed():
        for k, bit in enumerate(bits):
            side, partner = flipped(me, bit)
            work, away, land = r.small_work[k], r.small_away[k], r.small_land[k]
            away[...] = work[:, 1 - side].astype(bf16)
            copy = sent(away, land, r.last_sends, r.last_receives, 2 * k, "seq", partner)
            yield
            copy.wait()
            total = work[:, side] + land[...].astype(f32)
            target = r.small_work[k + 1] if k + 1 < len(bits) else r.small_out
            target[...] = total.reshape(target.shape)
        yield

    def flat_summed():
        for k, bit in enumerate(bits):
            _, partner = flipped(me, bit)
            copy = sent(r.flat_move.at[k], r.flat_land.at[k], r.last_sends, r.last_receives,
                        2 * k + 1, "seq", partner)
            yield
            copy.wait()
            target = r.flat_move.at[k + 1] if k + 1 < len(bits) else r.flat_out
            target[...] = r.flat_move[k] + r.flat_land[k]
        yield

    small_columns()
    next(one_sum)
    small_sum = small_summed()
    next(small_sum)
    up.next()
    next(one_sum)
    out.next()
    next(one_sum)
    cin.made(cin_other).go()
    next(one_sum)

    def norm_one(index, total):
        rows = pl.ds(pl.multiple_of(index * CHUNK, CHUNK), CHUNK)
        a, b, at = quarter_rows(index)
        value = r.stream[rows].astype(f32)
        scale = lax.rsqrt(mean_square(value) + 1e-06)
        back, gain = norm_back(value, scale, r.gains[0:1], r.total[a, b, at].astype(f32))
        r.stream_grad[rows] = r.stream_grad[rows] + back
        return total + jnp.sum(gain, axis=0, keepdims=True)

    r.flat_move[0, 0:1] = lax.fori_loop(0, chunks, norm_one, jnp.zeros((1, width), f32))

    flat_sum = flat_summed()
    next(flat_sum)
    next(small_sum)
    gin.next()
    down.next()
    next(flat_sum)
    gate.next()
    next(small_sum)
    up.next()
    cin.next()
    for waiting in (flat_sum, small_sum):
        for _ in waiting:
            pass
    pending = [out, gin, cin, down, gate, up]
    for _ in range(len(bits)):
        for item in pending:
            item.next()
    for item in pending:
        item.written.wait()


def backward(ins, hbm_ins, count, ident):
    bits = bits_of(count)
    n_bits = len(bits) - 1
    tokens, width = ins["stream"].shape
    channels, rank, states = ins["low"].shape[1], ins["w_dt"].shape[0], ins["logs"].shape[0]
    hid = hbm_ins["gate_up_in"].shape[1] // 2
    narrow = ins["w_x"].shape[1]
    half, quarter = count // 2, tokens // 4
    rows_in, rows_out, rows_down = width // count, channels // count, hid // count
    rows = pltpu.VMEM((tokens, channels), f32)

    def low(*dims):
        return pltpu.VMEM(dims, bf16)

    def full(*dims):
        return pltpu.VMEM(dims, f32)

    outs = dict(
        stream_grad=(shape_of(tokens, width), VMEM),
        out_rows=(shape_of(tokens, width, dtype=bf16), VMEM),
        small_out=(shape_of(rows_out, tokens), VMEM),
        flat_out=(shape_of(8, width), VMEM),
        down_out=(shape_of(rows_down, width), ANY),
        gate_out=(shape_of(rows_in, hid), ANY),
        up_out=(shape_of(rows_in, hid), ANY),
        out_out=(shape_of(rows_out, width), ANY),
        gin_out=(shape_of(rows_in, channels), ANY),
        cin_out=(shape_of(rows_in, channels), ANY),
    )
    quads = count // 4

    def unit(part, columns):
        lands = [low(half >> (k + 1), part, columns) for k in range(n_bits)]
        return [low(half // 2, part, columns), *lands, full(half // 2, part, columns)]

    def sems(size):
        return pltpu.SemaphoreType.DMA((size,))

    halves = [count >> (k + 1) for k in range(len(bits))]
    scratch = dict(
        left_hidden=low(quads, 2, rows_down, 2 * tokens),
        left_two=low(quads, 2, rows_in, 2 * tokens),
        left_one=low(quads, 2, rows_in, 2 * tokens),
        left_gated=low(quads, 2, rows_out, 2 * tokens),
        right_down=low(2 * tokens, width),
        right_two=low(2 * tokens, 2 * hid),
        right_out=low(2 * tokens, width),
        right_in=low(2 * tokens, 2 * channels),
        mixer=low(2, 2, quarter, width),
        weights=low(channels, width),
        scan=rows,
        step=rows,
        drive=rows,
        push=rows,
        decay_rows=full(tokens, 128),
        into=full(tokens, states, 128),
        out_of=full(tokens, states, 128),
        into_wide=full(tokens, states, 128),
        out_wide=full(tokens, states, 128),
        hist=full(2, tokens, states, 128),
        step_sum=full(8, channels),
        starts=full(states, channels),
        rate_sum=full(states, channels),
        step_low_grad=low(tokens, channels),
        chain_move=full(len(bits), states + 8, channels),
        chain_land=full(len(bits), states + 8, channels),
        part=low(2, 2, quarter, width),
        total=low(2, 2, quarter, width),
        first_land=low(2, quarter, width),
        second_land=low(quarter, width),
        second_move=low(quarter, width),
        raw_move=full(2, tokens, narrow),
        raw_land=full(2, tokens, narrow),
        raw_low=low(tokens, narrow),
        step_low=low(tokens, rank),
        grad_pre=full(tokens + 8, channels),
        extended=full(tokens + 16, channels),
        flat_move=full(len(bits), 8, width),
        flat_land=full(len(bits), 8, width),
        small_work=[full(size, 2, rows_out, tokens) for size in halves],
        small_away=[low(size, rows_out, tokens) for size in halves],
        small_land=[low(size, rows_out, tokens) for size in halves],
        down=unit(rows_down, width),
        gate=unit(rows_in, hid),
        up=unit(rows_in, hid),
        out=unit(rows_out, width),
        gin=unit(rows_in, channels),
        cin=unit(rows_in, channels),
        load_sems=sems(32),
        write_sems=sems(6),
        pair_sends=sems(8),
        pair_receives=sems(8),
        shared_sends=sems(4),
        shared_receives=sems(4),
        unit_sends=sems(6 * n_bits),
        unit_receives=sems(6 * n_bits),
        sum_sends=sems(12),
        sum_receives=sems(12),
        chain_sends=sems(len(bits)),
        chain_receives=sems(len(bits)),
        raw_sends=sems(3),
        raw_receives=sems(3),
        last_sends=sems(2 * len(bits)),
        last_receives=sems(2 * len(bits)),
    )
    names, shapes = [(name, 0) for name in [*ins, *hbm_ins, *outs]], []
    for name, held in scratch.items():
        listed = isinstance(held, list)
        names.append((name, len(held) if listed else 0))
        shapes += held if listed else [held]
    places = [VMEM for _ in ins]
    places[0] = pl.BlockSpec(memory_space=pltpu.SMEM)
    made = pl.pallas_call(
        functools.partial(backward_kernel, bits, names),
        out_shape=[shape for shape, _ in outs.values()],
        in_specs=places + [ANY] * len(hbm_ins),
        out_specs=[spec for _, spec in outs.values()],
        scratch_shapes=shapes,
        compiler_params=pltpu.CompilerParams(
            collective_id=ident, has_side_effects=True, vmem_limit_bytes=63 * 2**20
        ),
        name="block_backward",
    )(*ins.values(), *hbm_ins.values())
    return types.SimpleNamespace(**dict(zip(outs, made)))


def rms_gain(values, gain_row):
    return values * lax.rsqrt(jnp.mean(values * values, axis=-1, keepdims=True) + 1e-06) * gain_row


def swiglu(gate_up):
    return jax.nn.silu(gate_up[:, 0]) * gate_up[:, 1]


def local(
    seq_count,
    stream,
    doc_bounds,
    norm_gains,
    w_in,
    chan_vectors,
    decay_logs,
    w_x,
    small_gains,
    w_dt,
    w_out,
    w_gate_up,
    w_down,
    cotangent,
):
    tokens, width = stream.shape
    rank, (states, channels) = w_dt.shape[0], decay_logs.shape

    def turned(values):
        return values.T.reshape(seq_count // 4, 2, 2, values.shape[1] // seq_count, tokens)

    stream_in = stream.astype(f32)
    normed_low = rms_gain(stream_in, norm_gains[0]).astype(bf16)
    w_in_flat = w_in.reshape(width, 2 * channels)
    in_proj = jnp.dot(normed_low, w_in_flat, preferred_element_type=f32).astype(bf16)
    one_in = turned(normed_low)
    (
        halo, pre_conv, conv_low, raw_proj, step_pre, into, out_of, scan_out, gated_low,
        last_state, mixer_low, before, one_came, cot_came,
    ) = mixer_forward(
        doc_bounds, in_proj, chan_vectors, decay_logs, w_x, small_gains[None], w_dt, w_out,
        one_in, cotangent, seq_count, 1,
    )
    middle = stream_in + mixer_low.reshape(tokens, width).astype(f32)
    normed_two_low = rms_gain(middle, norm_gains[1]).astype(bf16)
    gate_up = jnp.einsum("td,dkf->tkf", normed_two_low, w_gate_up, preferred_element_type=f32)
    hidden_act, act_back = jax.vjp(swiglu, gate_up)
    hidden_low = hidden_act.astype(bf16)
    hidden_grad = jnp.einsum("td,fd->tf", cotangent, w_down, preferred_element_type=f32)
    (gate_up_grad,) = act_back(hidden_grad)
    gate_up_low = gate_up_grad.astype(bf16)
    normed_two_part = jnp.einsum("tkf,dkf->td", gate_up_low, w_gate_up, preferred_element_type=f32)
    feed_part = jnp.dot(hidden_low, w_down, preferred_element_type=f32)

    def quartered(values):
        return values.astype(bf16).reshape(2, 2, tokens // 4, width)

    made = backward(
        dict(
            bounds=doc_bounds, stream=stream, gains=norm_gains, proj=in_proj, halo=halo,
            pre=pre_conv, low=conv_low, raw=raw_proj, step_pre=step_pre, last_state=last_state,
            chan=chan_vectors, logs=decay_logs, w_x=w_x, w_dt=w_dt, small_gains=small_gains[None],
        ),
        dict(
            two_part=quartered(normed_two_part), feed_part=quartered(feed_part),
            mixer_in=mixer_low, cot=cotangent, cot_came=cot_came,
            gate_up_in=gate_up_low.reshape(tokens, -1), two_in=turned(normed_two_low),
            hidden_in=turned(hidden_low), gated_in=turned(gated_low), one_in=one_in,
            one_came=one_came, w_out=w_out, w_in=w_in_flat, scan_in=scan_out, into_in=into,
            out_of_in=out_of, hist_in=before,
        ),
        seq_count,
        2,
    )
    small, flat = made.small_out, made.flat_out
    at = w_x.shape[1]
    x_part, small = small[:, :at], small[:, at:].T
    dt_part, decay_out = small[:rank], small[rank : rank + states]
    chan_part = small[rank + states : rank + states + 7]
    me = lax.axis_index("seq")
    gain_width = width // seq_count
    gains_part = lax.dynamic_slice_in_dim(flat[:2], me * gain_width, gain_width, 1)
    small_width = small_gains.shape[0] // seq_count
    small_part = lax.dynamic_slice_in_dim(flat[2], me * small_width, small_width, 0)
    rms_values = jnp.sqrt(jnp.sum(flat[3:6], axis=1) / (tokens * seq_count * width))
    return (
        made.out_rows,
        made.stream_grad,
        gains_part,
        jnp.stack([made.cin_out, made.gin_out], 1),
        chan_part,
        decay_out,
        x_part,
        small_part,
        dt_part,
        made.out_out,
        jnp.stack([made.gate_out, made.up_out], 1),
        made.down_out,
        rms_values,
    )


def solution(mesh):
    in_specs = (
        P("seq", None),
        P(),
        P(),
        P(None, None, "ch"),
        P(None, "ch"),
        P(None, "ch"),
        P("ch", None),
        P(),
        P(None, "ch"),
        P("ch", None),
        P(None, None, "ch"),
        P("ch", None),
        P("seq", None),
    )
    out_specs = (
        P("seq", None),
        P("seq", None),
        P(None, "seq"),
        P("seq", None, "ch"),
        P(None, ("ch", "seq")),
        P(None, ("ch", "seq")),
        P(("ch", "seq"), None),
        P("seq"),
        P(None, ("ch", "seq")),
        P(("ch", "seq"), None),
        P("seq", None, "ch"),
        P(("ch", "seq"), None),
        P(),
    )
    return jax.shard_map(
        functools.partial(local, mesh.shape["seq"]),
        mesh=mesh,
        in_specs=in_specs,
        out_specs=out_specs,
        check_vma=False,
    )
```

```python
import functools
import math
import types

import jax
import jax.numpy as jnp
from jax import lax
from jax.experimental import pallas as pl
from jax.experimental.pallas import tpu as pltpu
from jax.sharding import PartitionSpec as P

f32 = jnp.float32
bf16 = jnp.bfloat16
LOG2E = math.log2(math.e)
LN2 = math.log(2.0)
RESET = 1e30
UNROLL = 8
LANES = 256
VMEM = pl.BlockSpec(memory_space=pltpu.VMEM)


def shape_of(*dims, dtype=f32):
    return jax.ShapeDtypeStruct(dims, dtype)


def cost(us):
    return pl.CostEstimate(flops=int(us * 1e9), bytes_accessed=int(us * 1e6), transcendentals=0)


def widened(column, width):
    return jnp.concatenate([column] * (width // 128), 1)


ANY = pl.BlockSpec(memory_space=pl.ANY)


def sent(source, target, sends, receives, slot, axis, partner):
    copy = pltpu.make_async_remote_copy(
        src_ref=source,
        dst_ref=target,
        send_sem=sends.at[slot],
        recv_sem=receives.at[slot],
        device_id={axis: partner},
        device_id_type=pl.DeviceIdType.MESH,
    )
    copy.start()
    return copy


def bits_of(count):
    return [1 << k for k in range(count.bit_length() - 1)]


def flipped(me, bit):
    mine = lax.rem(me // bit, 2)
    return mine, me + bit - 2 * bit * mine


CHUNK = 32


def sigmoid(values):
    return 1.0 / (1.0 + jnp.exp(-values))


def softplus(values):
    return jnp.maximum(values, 0.0) + jnp.log1p(jnp.exp(-jnp.abs(values)))


def row_doc(places, bounds):
    return (places >= bounds[0]).astype(jnp.int32) + (places >= bounds[1]).astype(jnp.int32)


def tap_mask(places, bounds, offset):
    source = places - offset
    same = row_doc(source, bounds) == row_doc(places, bounds)
    return jnp.where((source >= 0) & same, 1.0, 0.0)


def mean_square(values):
    return jnp.mean(values * values, axis=-1, keepdims=True)


def three_norms(raw, gains, rank, states):
    low, mid, high = raw[:, :rank], raw[:, rank : rank + states], raw[:, rank + states :]
    low_scale = lax.rsqrt(mean_square(low) + 1e-06)
    mid_scale = lax.rsqrt(jnp.maximum(mean_square(mid), 0.1))
    high_scale = lax.rsqrt(jnp.maximum(mean_square(high), 0.1))
    return (
        low * low_scale * gains[:, :rank],
        mid * mid_scale * gains[:, rank : rank + states],
        high * high_scale * gains[:, rank + states :],
    )


def widen(values, wide, first, count):
    states = values.shape[1]
    eye = (
        lax.broadcasted_iota(jnp.int32, (states, states), 0)
        == lax.broadcasted_iota(jnp.int32, (states, states), 1)
    ).astype(f32)
    spread = jnp.sum(values[:, None, :] * eye[None], axis=-1, keepdims=True)
    wide[pl.ds(first, count)] = jnp.broadcast_to(spread, (count, states, 128))


def greeted(axis_partners):
    barrier = pltpu.get_barrier_semaphore()
    for axis, partner in axis_partners:
        pl.semaphore_signal(
            barrier, inc=1, device_id={axis: partner}, device_id_type=pl.DeviceIdType.MESH
        )
    pl.semaphore_wait(barrier, len(axis_partners))


def chained(forward, bits, state, steps, rates, moving, landed, sends, receives, base):
    me = lax.axis_index("seq")
    states = state.shape[0]
    all_state, all_steps = state, steps
    mine_state, mine_steps = jnp.zeros_like(all_state), jnp.zeros_like(all_steps)
    for k, bit in enumerate(bits):
        mine, partner = flipped(me, bit)
        moving[k, :states] = all_state
        moving[k, states:] = all_steps
        sent(moving.at[k], landed.at[k], sends, receives, base + k, "seq", partner).wait()
        other_state, other_steps = landed[k, :states], landed[k, states:]
        earlier = (mine == 1) if forward else (mine == 0)
        through = jnp.exp2(rates * mine_steps[:1])
        mine_state = jnp.where(earlier, mine_state + through * other_state, mine_state)
        mine_steps = jnp.where(earlier, mine_steps + other_steps, mine_steps)
        after = jnp.exp2(rates * all_steps[:1]) * other_state + all_state
        ahead_of = jnp.exp2(rates * other_steps[:1]) * all_state + other_state
        all_state = jnp.where(earlier, after, ahead_of)
        all_steps = all_steps + other_steps
    return mine_state


def forward_kernel(
    bits, bounds, proj, chan, logs, w_x, gains, w_dt, w_out, one_in, cot,
    halo, pre_out, low_out, raw_out, step_pre_out, into, out_of, scan_out, gated_out, last_state,
    mixer, hist_out, one_came, cot_came,
    extended, raw_move, raw_land, step, drive, starts, moving, landed, part, first_land,
    second_move, second_land, hist, sends, receives, hist_sem, shared_sends, shared_receives,
    sum_sends, sum_receives,
):
    tokens, channels = low_out.shape
    rank, states = w_dt.shape[0], logs.shape[0]
    chunks = tokens // CHUNK
    ch_me, me = lax.axis_index("ch"), lax.axis_index("seq")
    seq_count = 1 << len(bits)
    low, across = flipped(ch_me, 1)
    high, along = flipped(ch_me, 2)
    following, previous = lax.rem(me + 1, seq_count), lax.rem(me + seq_count - 1, seq_count)
    greeted(
        [("ch", across), ("ch", along), ("seq", following), ("seq", previous)]
        + [("seq", flipped(me, bit)[1]) for bit in bits]
    )
    halo_copy = sent(
        proj.at[pl.ds(tokens - 16, 16), pl.ds(0, channels)], halo, sends, receives, 0, "seq",
        following,
    )
    mine, pair = flipped(me, bits[1])
    half = one_in.shape[0] // 2
    some = pl.ds(low * half, half)
    at = pl.ds(pl.multiple_of(low * (tokens // 2), tokens // 2), tokens // 2)
    shared = [
        (one_in.at[some, 1 - mine], one_came.at[some]),
        (cot.at[at], cot_came.at[at]),
    ]
    shared_copies = [
        sent(source, target, shared_sends, shared_receives, k, "seq", pair)
        for k, (source, target) in enumerate(shared)
    ]
    rates = -jnp.exp(logs[...]) * LOG2E

    def spread(index, _):
        first = pl.multiple_of(index * CHUNK, CHUNK)
        extended[pl.ds(first + 16, CHUNK)] = proj[pl.ds(first, CHUNK), :channels].astype(f32)
        return 0

    lax.fori_loop(0, chunks, spread, 0)

    def convolved(index, _):
        first = pl.multiple_of(index * CHUNK, CHUNK)
        places = me * tokens + first + lax.broadcasted_iota(jnp.int32, (CHUNK, 128), 0)
        window = extended[pl.ds(first, CHUNK + 16)]
        summed = chan[4:5]
        for k in range(4):
            mask = widened(tap_mask(places, bounds, 3 - k), channels)
            summed = summed + chan[k : k + 1] * window[13 + k : 13 + k + CHUNK] * mask
        pre_out[pl.ds(first, CHUNK)] = summed
        low_out[pl.ds(first, CHUNK)] = (summed * sigmoid(summed)).astype(bf16)
        return 0

    lax.fori_loop(1, chunks, convolved, 0)
    halo_copy.wait()
    extended[0:16] = halo[...].astype(f32)
    convolved(0, 0)
    raw_move[0] = jnp.dot(low_out[...], w_x[...], preferred_element_type=f32)
    sent(raw_move.at[0], raw_land.at[0], sends, receives, 1, "ch", across).wait()
    raw_move[1] = raw_move[0] + raw_land[0]
    sent(raw_move.at[1], raw_land.at[1], sends, receives, 2, "ch", along).wait()

    def stepped(index, total):
        first = pl.multiple_of(index * CHUNK, CHUNK)
        rows = pl.ds(first, CHUNK)
        raw = raw_move[1, rows] + raw_land[1, rows]
        raw_out[rows] = raw
        step_norm, input_norm, output_norm = three_norms(raw, gains[...], rank, states)
        widen(input_norm, into, first, CHUNK)
        widen(output_norm, out_of, first, CHUNK)
        pre = (
            jnp.dot(step_norm.astype(bf16), w_dt[...], preferred_element_type=f32) + chan[5:6]
        )
        step_pre_out[rows] = pre
        size = softplus(pre)
        drive[rows] = size * low_out[rows].astype(f32)
        places = me * tokens + first + lax.broadcasted_iota(jnp.int32, (CHUNK, 128), 0)
        resets = jnp.where((places == bounds[0]) | (places == bounds[1]), RESET, 0.0)
        size = size + widened(resets, channels)
        step[rows] = size
        return total + jnp.sum(size, axis=0, keepdims=True)

    total = lax.fori_loop(0, chunks, stepped, jnp.zeros((1, channels), f32))
    blocks = [slice(j, j + LANES) for j in range(0, channels, LANES)]
    for lanes in blocks:
        block_rates = rates[:, lanes]

        def ended(index, state, lanes=lanes, block_rates=block_rates):
            first = pl.multiple_of(index * UNROLL, UNROLL)
            steps, drives = step[pl.ds(first, UNROLL), lanes], drive[pl.ds(first, UNROLL), lanes]
            for k in range(UNROLL):
                decay = jnp.exp2(steps[k : k + 1] * block_rates)
                state = decay * state + widened(into[first + k], LANES) * drives[k : k + 1]
            return state

        starts[:, lanes] = lax.fori_loop(
            0, tokens // UNROLL, ended, jnp.zeros((states, LANES), f32)
        )
    starts[...] = chained(
        True, bits, starts[...], jnp.broadcast_to(total, (8, channels)), rates, moving, landed,
        sends, receives, 7,
    )
    hist_copies = []
    for number, lanes in enumerate(blocks):
        block_rates = rates[:, lanes]
        skip = chan[6:7, lanes]

        def walked(index, state, lanes=lanes, block_rates=block_rates, skip=skip):
            first = pl.multiple_of(index * UNROLL, UNROLL)
            steps, drives = step[pl.ds(first, UNROLL), lanes], drive[pl.ds(first, UNROLL), lanes]
            rows = []
            for k in range(UNROLL):
                hist[first + k, :, lanes] = state
                decay = jnp.exp2(steps[k : k + 1] * block_rates)
                state = decay * state + widened(into[first + k], LANES) * drives[k : k + 1]
                rows.append(
                    jnp.sum(widened(out_of[first + k], LANES) * state, axis=0, keepdims=True)
                )
            scan_out[pl.ds(first, UNROLL), lanes] = jnp.concatenate(rows, 0)
            return state

        last_state[:, lanes] = lax.fori_loop(0, tokens // UNROLL, walked, starts[:, lanes])
        copy = pltpu.make_async_copy(
            hist.at[:, :, lanes], hist_out.at[:, :, lanes], hist_sem.at[number]
        )
        copy.start()
        hist_copies.append(copy)

    def gate(index, _):
        first = pl.multiple_of(index * CHUNK, CHUNK)
        rows = pl.ds(first, CHUNK)
        scanned = scan_out[rows] + chan[6:7] * low_out[rows].astype(f32)
        scan_out[rows] = scanned
        gate_pre = proj[rows, channels:].astype(f32)
        gated_out[rows] = (scanned * gate_pre * sigmoid(gate_pre)).astype(bf16)
        return 0

    lax.fori_loop(0, chunks, gate, 0)
    quarter = tokens // 4
    width = w_out.shape[1]
    for k, (_, target) in enumerate(shared):
        shared_copies[k].wait()
        shared_copies[k] = sent(
            target, target, shared_sends, shared_receives, 2 + k, "ch", across
        )

    def mixed(index, _):
        first = pl.multiple_of(index * 256, 256)
        product = jnp.dot(
            gated_out[...], w_out[:, pl.ds(first, 256)], preferred_element_type=f32
        ).astype(bf16)
        for k in range(4):
            part[k // 2, k % 2, :, pl.ds(first, 256)] = product[k * quarter : (k + 1) * quarter]
        return 0

    held = types.SimpleNamespace(
        first_land=first_land, second_land=second_land, second_move=second_move, total=mixer,
        sum_sends=sum_sends, sum_receives=sum_receives,
    )
    sums = [four_summed(held, (low, across, high, along), part, 0, k) for k in range(2)]
    for k, item in enumerate(sums):
        lax.fori_loop(k * width // 512, (k + 1) * width // 512, mixed, 0)
        next(item)
    for _ in in_turn(*sums):
        pass
    for copy in hist_copies + shared_copies:
        copy.wait()


def mixer_forward(bounds, proj, chan, logs, w_x, gains, w_dt, w_out, one_in, cot, count, ident):
    bits = bits_of(count)
    tokens, channels = proj.shape[0], proj.shape[1] // 2
    states, rank, width = logs.shape[0], w_dt.shape[0], w_out.shape[1]
    quarter, narrow = tokens // 4, w_x.shape[1]
    rows = shape_of(tokens, channels)
    low_rows = shape_of(tokens, channels, dtype=bf16)
    wide = shape_of(tokens, states, 128)
    slots = pltpu.VMEM((len(bits), states + 8, channels), f32)
    raws = pltpu.VMEM((2, tokens, narrow), f32)
    out = pl.pallas_call(
        functools.partial(forward_kernel, bits),
        out_shape=[
            shape_of(16, channels, dtype=bf16), rows, low_rows, shape_of(tokens, narrow), rows,
            wide, wide, rows, low_rows, shape_of(states, channels),
            shape_of(2, 2, quarter, width, dtype=bf16), shape_of(tokens, states, channels),
            shape_of(one_in.shape[0], *one_in.shape[2:], dtype=bf16),
            shape_of(tokens, width, dtype=bf16),
        ],
        in_specs=[pl.BlockSpec(memory_space=pltpu.SMEM)] + [VMEM] * 7 + [ANY] * 2,
        out_specs=[VMEM] * 11 + [ANY] * 3,
        scratch_shapes=[
            pltpu.VMEM((tokens + 16, channels), f32), raws, raws,
            pltpu.VMEM((tokens, channels), f32), pltpu.VMEM((tokens, channels), f32),
            pltpu.VMEM((states, channels), f32), slots, slots,
            pltpu.VMEM((2, 2, quarter, width), bf16), pltpu.VMEM((2, quarter, width), bf16),
            pltpu.VMEM((quarter, width), bf16), pltpu.VMEM((quarter, width), bf16),
            pltpu.VMEM((tokens, states, channels), f32),
            pltpu.SemaphoreType.DMA((7 + len(bits),)), pltpu.SemaphoreType.DMA((7 + len(bits),)),
            pltpu.SemaphoreType.DMA((channels // LANES,)),
            pltpu.SemaphoreType.DMA((4,)), pltpu.SemaphoreType.DMA((4,)),
            pltpu.SemaphoreType.DMA((8,)), pltpu.SemaphoreType.DMA((8,)),
        ],
        compiler_params=pltpu.CompilerParams(
            collective_id=ident, has_side_effects=True, vmem_limit_bytes=56 * 2**20
        ),
        cost_estimate=cost(6),
        name="mixer_forward",
    )(bounds, proj, chan, logs, w_x, gains, w_dt, w_out, one_in, cot)
    return out


class Unit:
    def __init__(self, left, right, columns, refs, sends, receives, slot, bits, result):
        self.left, self.right, self.columns = left, right, columns
        away, *self.land, self.kept = refs
        self.away = [away.at[pl.ds(0, land.shape[0])] for land in self.land]
        self.sends, self.receives, self.slot, self.bits = sends, receives, slot, bits
        self.result = result
        self.stage = 0
        self.copy = None

    def made(self, *needed):
        for item in needed:
            item.wait()
        mine, partner = flipped(lax.axis_index("seq"), self.bits[0])
        self.make(1 - mine, self.away[0])
        self.stage = 1
        self.go = lambda: self.begin(partner, mine)
        return self

    def begin(self, partner, mine):
        self.copy = self.start(0, partner)
        self.make(mine, self.kept)

    def begun(self):
        _, partner = flipped(lax.axis_index("seq"), self.bits[0])
        self.stage = 1
        self.copy = self.start(0, partner)

    def resume(self):
        self.stage = 2
        if len(self.bits) > 1:
            _, partner = flipped(lax.axis_index("seq"), self.bits[1])
            self.copy = self.start(1, partner)

    def next(self, send_on=True):
        stage, me = self.stage, lax.axis_index("seq")
        if stage > len(self.bits):
            return
        self.stage += 1
        left_over = stage == len(self.bits)
        self.copy.wait()
        count = self.land[stage - 1].shape[0]
        rows = self.kept.shape[1]
        part = 32 if rows % 32 == 0 else rows
        parts = rows // part

        def total(index, at):
            return self.kept[index, at] + self.land[stage - 1][index, at].astype(f32)

        if left_over:

            def finish(step, _):
                at = pl.ds(pl.multiple_of(step * part, part), part)
                self.kept[0, at] = total(0, at)
                return 0

            lax.fori_loop(0, parts, finish, 0)
            self.written = self.result(self.kept.at[0])
            return
        mine, partner = flipped(me, self.bits[stage])

        def send(step, _):
            index = lax.div(step, parts)
            at = pl.ds(pl.multiple_of(lax.rem(step, parts) * part, part), part)
            self.away[stage][index, at] = total(2 * index + 1 - mine, at).astype(bf16)
            return 0

        lax.fori_loop(0, (count // 2) * parts, send, 0)
        if send_on:
            self.copy = self.start(stage, partner)

        def keep(step, _):
            index = lax.div(step, parts)
            at = pl.ds(pl.multiple_of(lax.rem(step, parts) * part, part), part)
            self.kept[index, at] = total(2 * index + mine, at)
            return 0

        lax.fori_loop(0, (count // 2) * parts, keep, 0)

    def start(self, stage, partner):
        return sent(
            self.away[stage], self.land[stage], self.sends, self.receives, self.slot + stage,
            "seq", partner,
        )

    def make(self, side, target):
        first, width = self.columns
        tile = width if width <= 512 else 512 if width % 512 == 0 else 384
        tiles = width // tile
        count, rows = target.shape[:2]
        together = count if rows % 16 == 0 else 1

        def block(step, _):
            index = lax.div(step, tiles)
            column = pl.multiple_of(lax.rem(step, tiles) * tile, tile)
            left = self.left[:, side] if together > 1 else self.left[pl.ds(index, 1), side]
            product = jnp.dot(
                left.reshape(together * rows, left.shape[2]),
                self.right[:, pl.ds(first + column, tile)],
                preferred_element_type=f32,
            ).astype(target.dtype)
            at = pl.ds(0, count) if together > 1 else pl.ds(index, 1)
            target[at, :, pl.ds(column, tile)] = product.reshape(together, rows, tile)
            return 0

        lax.fori_loop(0, count // together * tiles, block, 0)


def norm_back(values, scale, gains, grad, free=True):
    weighted = gains * grad
    result = scale * weighted
    inner = jnp.mean(values * weighted, axis=-1, keepdims=True)
    return result - jnp.where(free, 1.0, 0.0) * values * (scale * scale * scale) * inner, (
        grad * values * scale
    )


def silu_slope(values):
    part = sigmoid(values)
    return part * (1.0 + values * (1.0 - part))


def narrowed(wide, first, count):
    states = wide.shape[1]
    eye = (
        lax.broadcasted_iota(jnp.int32, (states, states), 0)
        == lax.broadcasted_iota(jnp.int32, (states, states), 1)
    ).astype(f32)
    sums = jnp.sum(wide[pl.ds(first, count)], axis=-1, keepdims=True)
    return jnp.sum(sums * eye[None], axis=1)


def dot_rows(left, right):
    return lax.dot_general(left, right, (((1,), (1,)), ((), ())), preferred_element_type=f32)


class Once:
    def __init__(self, *copies, then=None):
        self.copies, self.then = copies, then

    def wait(self):
        for copy in self.copies:
            copy.wait()
        self.copies = ()
        if self.then is not None:
            after, self.then = self.then, None
            after().wait()


def named(names, refs):
    refs, found = list(refs), {}
    for name, count in names:
        taken, refs = refs[: count or 1], refs[count or 1 :]
        found[name] = taken if count else taken[0]
    return types.SimpleNamespace(**found)


def four_summed(r, place, value, base, part):
    low, across, high, along = place
    half = value.shape[3] // 2
    cols = pl.ds(part * half, half)
    first, second, moving = (
        r.first_land.at[:, :, cols], r.second_land.at[:, cols], r.second_move.at[:, cols]
    )
    total, value = r.total.at[:, :, :, cols], value.at[:, :, :, cols]
    sends, receives, base = r.sum_sends, r.sum_receives, base + 4 * part
    copy = sent(value.at[:, 1 - low], first, sends, receives, base, "ch", across)
    yield
    copy.wait()
    moving[...] = (
        value[1 - high, low].astype(f32) + first[1 - high].astype(f32)
    ).astype(bf16)
    copy = sent(moving, second, sends, receives, base + 1, "ch", along)
    yield
    copy.wait()
    total[high, low] = (
        value[high, low].astype(f32) + first[high].astype(f32) + second[...].astype(f32)
    ).astype(bf16)
    own = total.at[high, low]
    copy = sent(own, own, sends, receives, base + 2, "ch", along)
    yield
    copy.wait()
    both = total.at[:, low]
    copy = sent(both, both, sends, receives, base + 3, "ch", across)
    yield
    copy.wait()
    yield


def in_turn(*steps):
    for _ in range(4):
        yield
        for item in steps:
            next(item)
    yield


def feed_forward_kernel(bits, names, *refs):
    r = named(names, refs)
    tokens, width = r.stream.shape
    quarter, chunks, seq_count = tokens // 4, tokens // CHUNK, 1 << len(bits)
    ch_me, me = lax.axis_index("ch"), lax.axis_index("seq")
    low, across = flipped(ch_me, 1)
    high, along = flipped(ch_me, 2)
    pair_bit, rest_bits = bits[1], [bits[0], *bits[2:]]
    mine, pair = flipped(me, pair_bit)
    hid = r.w_down_in.shape[0]
    tile = 256
    tiles = range(0, hid, tile)
    own, other = pl.ds(0, tokens), pl.ds(tokens, tokens)
    slots = []

    def load(source, target):
        copy = pltpu.make_async_copy(source, target, r.load_sems.at[len(slots)])
        copy.start()
        slots.append(0)
        return Once(copy)

    cot_own = load(r.cot, r.right_down.at[own])
    loads = []
    for at in tiles:
        loads.append(
            [
                load(r.w_gate_up_in.at[:, pl.ds(at, tile)], r.w_gate_up.at[:, pl.ds(at, tile)]),
                load(
                    r.w_gate_up_in.at[:, pl.ds(hid + at, tile)],
                    r.w_gate_up.at[:, pl.ds(hid + at, tile)],
                ),
                load(r.w_down_in.at[pl.ds(at, tile)], r.w_down.at[pl.ds(at, tile)]),
            ]
        )
    cot_other = load(r.cot_came, r.right_down.at[other])
    greeted(
        [("ch", across), ("ch", along), ("seq", pair), ("seq", flipped(me, rest_bits[0])[1])]
    )

    def norm_two(index, _):
        rows = pl.ds(pl.multiple_of(index * CHUNK, CHUNK), CHUNK)
        per = quarter // CHUNK
        part = lax.div(index, per)
        at = pl.ds(pl.multiple_of(lax.rem(index, per) * CHUNK, CHUNK), CHUNK)
        mixed = r.mixer[lax.div(part, 2), lax.rem(part, 2), at].astype(f32)
        middle = r.stream[rows].astype(f32) + mixed
        scale = lax.rsqrt(mean_square(middle) + 1e-06)
        r.normed[rows] = (middle * scale * r.gains[1:2]).astype(bf16)
        return 0

    lax.fori_loop(0, chunks, norm_two, 0)

    def turn(values, first, turned):
        rows = turned.shape[3]
        across_rows = values.T
        for k in range(values.shape[1] // rows):
            owner = first // rows + k
            turned[owner // 4, (owner // 2) % 2, owner % 2] = across_rows[
                k * rows : (k + 1) * rows
            ]

    group = 384
    for at in range(0, width, group):
        turn(r.normed[:, at : at + group], at, r.two_turned)
    half = r.two_turned.shape[0] // 2
    some = pl.ds(low * half, half)
    target = r.left_two.at[some, :, :, other]
    two_copy = sent(
        r.two_turned.at[some, 1 - mine], target, r.pair_sends, r.pair_receives, 0, "seq", pair
    )
    r.left_two[:, :, :, own] = r.two_turned[:, mine]
    cot_own.wait()
    hidden_copies, quads_sent = [], 0
    for number, at in enumerate(tiles):
        for item in loads[number]:
            item.wait()
        gate = jnp.dot(
            r.normed[...], r.w_gate_up[:, pl.ds(at, tile)], preferred_element_type=f32
        )
        up = jnp.dot(
            r.normed[...], r.w_gate_up[:, pl.ds(hid + at, tile)], preferred_element_type=f32
        )
        part = sigmoid(gate)
        act = gate * part
        hidden = (act * up).astype(bf16)
        r.hidden[:, pl.ds(at, tile)] = hidden
        turn(hidden, at, r.hidden_turned)
        grad = dot_rows(r.right_down[own], r.w_down[pl.ds(at, tile)])
        r.right_two[own, pl.ds(at, tile)] = (
            grad * up * (part * (1.0 + gate * (1.0 - part)))
        ).astype(bf16)
        r.right_two[own, pl.ds(hid + at, tile)] = (grad * act).astype(bf16)
        quads = (at + tile) // r.hidden_turned.shape[3] // 4
        if quads > quads_sent:
            some = pl.ds(quads_sent, quads - quads_sent)
            hidden_copies.append(
                sent(
                    r.hidden_turned.at[some, 1 - mine], r.left_hidden.at[some, :, :, other],
                    r.pair_sends, r.pair_receives, 3 + len(hidden_copies), "seq", pair,
                )
            )
            quads_sent = quads
    gate_copy = sent(
        r.right_two.at[own, pl.ds(0, hid)], r.right_two.at[other, pl.ds(0, hid)], r.pair_sends,
        r.pair_receives, 1, "seq", pair,
    )
    r.left_hidden[:, :, :, own] = r.hidden_turned[:, mine]

    def store(values, target, at):
        for k in range(4):
            target[k // 2, k % 2, :, pl.ds(at, tile)] = values[k * quarter : (k + 1) * quarter]

    def two_part(index, _):
        at = pl.multiple_of(index * tile, tile)
        store(dot_rows(r.right_two[own], r.w_gate_up[pl.ds(at, tile)]).astype(bf16), r.part, at)
        return 0

    sums = [four_summed(r, (low, across, high, along), r.part, 0, k) for k in range(2)]
    for k, item in enumerate(sums):
        lax.fori_loop(k * width // (2 * tile), (k + 1) * width // (2 * tile), two_part, 0)
        next(item)
    total = in_turn(*sums)
    next(total)

    def feed_part(index, _):
        at = pl.multiple_of(index * tile, tile)
        product = jnp.dot(
            r.hidden[...], r.w_down[:, pl.ds(at, tile)], preferred_element_type=f32
        )
        store(product.astype(bf16), r.feed_part, at)
        return 0

    n_bits = len(rest_bits)
    part = width // 2
    down, down_late = (
        Unit(r.left_hidden, r.right_down, (k * part, part), r.down, r.unit_sends,
             r.unit_receives, 0, rest_bits, None)
        for k in range(2)
    )
    next(total)
    cot_other.wait()
    down.made(*hidden_copies).go()
    next(total)
    lax.fori_loop(0, width // tile, feed_part, 0)
    next(total)
    side, _ = flipped(me, rest_bits[0])
    down_late.make(1 - side, r.late_away)
    down_late.make(side, r.late_kept)
    two_copy.wait()
    two_copy = sent(target, target, r.pair_sends, r.pair_receives, 2, "ch", across)
    next(total)
    two_copy.wait()
    gate_copy.wait()
    if n_bits > 1:
        down.next(send_on=False)
    r.down_away[...] = down.away[1][...]
    kept = r.down_kept.shape[0]
    r.down_kept[...] = down.kept[0:kept]


def feed_forward(ins, hbm_ins, count, ident):
    bits = bits_of(count)
    n_bits = len(bits) - 1
    tokens, width = ins["stream"].shape
    hid = hbm_ins["w_down_in"].shape[0]
    half, quarter = count // 2, tokens // 4
    rows_in, rows_down = width // count, hid // count

    def low(*dims):
        return pltpu.VMEM(dims, bf16)

    def sems(size):
        return pltpu.SemaphoreType.DMA((size,))

    lands = [low(half >> (k + 1), rows_down, width // 2) for k in range(n_bits)]
    outs = dict(
        total=shape_of(2, 2, quarter, width, dtype=bf16),
        feed_part=shape_of(2, 2, quarter, width, dtype=bf16),
        left_two=shape_of(count // 4, 2, rows_in, 2 * tokens, dtype=bf16),
        right_two=shape_of(2 * tokens, 2 * hid, dtype=bf16),
        down_away=shape_of(half >> 2, rows_down, width // 2, dtype=bf16),
        down_kept=shape_of(half >> 2, rows_down, width // 2),
        late_away=shape_of(half >> 1, rows_down, width // 2, dtype=bf16),
        late_kept=shape_of(half >> 1, rows_down, width // 2),
    )
    scratch = dict(
        w_gate_up=low(width, 2 * hid),
        w_down=low(hid, width),
        normed=low(tokens, width),
        hidden=low(tokens, hid),
        two_turned=low(count // 4, 2, 2, rows_in, tokens),
        hidden_turned=low(count // 4, 2, 2, rows_down, tokens),
        left_hidden=low(count // 4, 2, rows_down, 2 * tokens),
        right_down=low(2 * tokens, width),
        part=low(2, 2, quarter, width),
        first_land=low(2, quarter, width),
        second_land=low(quarter, width),
        second_move=low(quarter, width),
        down=[low(half // 2, rows_down, width // 2), *lands, pltpu.VMEM((half // 2, rows_down, width // 2), f32)],
        load_sems=sems(2 + 3 * (hid // 256)),
        pair_sends=sems(7),
        pair_receives=sems(7),
        sum_sends=sems(8),
        sum_receives=sems(8),
        unit_sends=sems(n_bits),
        unit_receives=sems(n_bits),
    )
    names, shapes = [(name, 0) for name in [*ins, *hbm_ins, *outs]], []
    for name, held in scratch.items():
        listed = isinstance(held, list)
        names.append((name, len(held) if listed else 0))
        shapes += held if listed else [held]
    made = pl.pallas_call(
        functools.partial(feed_forward_kernel, bits, names),
        out_shape=list(outs.values()),
        in_specs=[VMEM] * len(ins) + [ANY] * len(hbm_ins),
        out_specs=[VMEM] * len(outs),
        scratch_shapes=shapes,
        compiler_params=pltpu.CompilerParams(
            collective_id=ident, has_side_effects=True, vmem_limit_bytes=56 * 2**20
        ),
        name="feed_forward",
    )(*ins.values(), *hbm_ins.values())
    return types.SimpleNamespace(**dict(zip(outs, made)))


def backward_kernel(bits, names, *refs):
    r = named(names, refs)
    tokens, width = r.stream.shape
    channels, rank, states = r.low.shape[1], r.w_dt.shape[0], r.logs.shape[0]
    quarter, chunks = tokens // 4, tokens // CHUNK
    ch_me, me = lax.axis_index("ch"), lax.axis_index("seq")
    seq_count = 1 << len(bits)
    low, across = flipped(ch_me, 1)
    high, along = flipped(ch_me, 2)
    pair_bit, rest_bits = bits[1], [bits[0], *bits[2:]]
    mine, pair = flipped(me, pair_bit)
    following, previous = lax.rem(me + 1, seq_count), lax.rem(me + seq_count - 1, seq_count)
    load_slots, pair_slots, shared_slots, write_slots = ([] for _ in range(4))

    def slot_of(slots):
        slots.append(0)
        return len(slots) - 1

    def load(source, target):
        copy = pltpu.make_async_copy(source, target, r.load_sems.at[slot_of(load_slots)])
        copy.start()
        return Once(copy)

    own, other = pl.ds(0, tokens), pl.ds(tokens, tokens)
    mixer_own = load(r.mixer_in, r.mixer)
    cot_own = load(r.cot, r.cot_rows)
    weights = load(r.w_out, r.weights)
    scan_own = load(r.scan_in, r.scan)
    out_of_own = load(r.out_of_in, r.out_of)
    into_own = load(r.into_in, r.into)
    hid = r.right_two_in.shape[1] // 2
    down_away = load(r.down_away_in, r.down[0].at[pl.ds(0, r.down_away_in.shape[0])])
    late_away = load(r.late_away_in, r.late[0])
    two_own = load(r.left_two_in, r.left_two)
    gate_up_own = load(r.right_two_in.at[own], r.right_two.at[own])
    gate_other = load(
        r.right_two_in.at[other, pl.ds(0, hid)], r.right_two.at[other, pl.ds(0, hid)]
    )
    down_kept = load(r.down_kept_in, r.down[-1].at[pl.ds(0, r.down_kept_in.shape[0])])
    late_kept = load(r.late_kept_in, r.late[-1])
    part_in = load(r.feed_part, r.part)
    one_own = load(r.one_in.at[:, mine], r.left_one.at[:, :, :, own])
    one_other = load(r.one_came, r.left_one.at[:, :, :, other])
    gated_own = load(r.gated_in.at[:, mine], r.left_gated.at[:, :, :, own])
    blocks = [slice(j, j + 128) for j in range(0, channels, 128)]
    hists = [load(r.hist_in.at[:, :, blocks[k]], r.hist.at[k]) for k in range(2)]

    greeted(
        [("ch", across), ("ch", along), ("seq", following), ("seq", previous)]
        + [("seq", flipped(me, bit)[1]) for bit in bits]
    )

    def swap(source, target):
        slot = slot_of(pair_slots)
        return Once(sent(source, target, r.pair_sends, r.pair_receives, slot, "seq", pair))

    def swap_shared(source, target):
        slot = 2 * slot_of(shared_slots)
        copy = sent(source, target, r.shared_sends, r.shared_receives, slot, "seq", pair)
        return Once(
            copy,
            then=lambda: sent(
                target, target, r.shared_sends, r.shared_receives, slot + 1, "ch", across
            ),
        )

    n_bits = len(rest_bits)

    def writer(target):
        def write(source):
            copy = pltpu.make_async_copy(source, target, r.write_sems.at[slot_of(write_slots)])
            copy.start()
            return copy

        return write

    def unit(left, right, columns, refs, slot, target):
        return Unit(
            left, right, columns, refs, r.unit_sends, r.unit_receives, slot * n_bits, rest_bits,
            writer(target),
        )

    part = width // 2
    down, late = (
        unit(None, None, None, refs, k, r.down_out.at[:, pl.ds(k * part, part)])
        for k, refs in enumerate((r.down, r.late))
    )
    part = hid // 2
    quarters = [
        unit(
            r.left_two, r.right_two, (k * part, part), refs, 2 + k,
            (r.gate_out, r.up_out)[k // 2].at[:, pl.ds(k % 2 * part, part)],
        )
        for k, refs in enumerate((r.gate0, r.gate1, r.up0, r.up1))
    ]
    gate0, gate1, up0, up1 = quarters
    out = unit(r.left_gated, r.right_out, (0, width), r.out, 6, r.out_out)
    gin = unit(r.left_one, r.right_in, (channels, channels), r.gin, 7, r.gin_out)
    part = channels // 2
    cins = [
        unit(
            r.left_one, r.right_in, (k * part, part), refs, 8 + k,
            r.cin_out.at[:, pl.ds(k * part, part)],
        )
        for k, refs in enumerate((r.cin0, r.cin1))
    ]

    up_other = swap(
        r.right_two_in.at[own, pl.ds(hid, hid)], r.right_two.at[other, pl.ds(hid, hid)]
    )
    down_away.wait()
    down.resume()
    late_away.wait()
    late.begun()

    summed = functools.partial(four_summed, r, (low, across, high, along))


    rates = -jnp.exp(r.logs[...]) * LOG2E

    def places_of(first, count):
        return me * tokens + first + lax.broadcasted_iota(jnp.int32, (count, 128), 0)

    def resteps():
        def body(index, total):
            first = pl.multiple_of(index * CHUNK, CHUNK)
            rows = pl.ds(first, CHUNK)
            size = softplus(r.step_pre[rows])
            r.drive[rows] = size * r.low[rows].astype(f32)
            places = places_of(first, CHUNK)
            resets = jnp.where((places == r.bounds[0]) | (places == r.bounds[1]), RESET, 0.0)
            size = size + widened(resets, channels)
            r.step[rows] = size
            return total + jnp.sum(size, axis=0, keepdims=True)

        r.step_sum[...] = jnp.broadcast_to(
            lax.fori_loop(0, chunks, body, jnp.zeros((1, channels), f32)), (8, channels)
        )

    resteps()
    mixer_own.wait()
    cot_own.wait()

    def quarter_rows(index):
        per = quarter // CHUNK
        part = lax.div(index, per)
        at = pl.ds(pl.multiple_of(lax.rem(index, per) * CHUNK, CHUNK), CHUNK)
        return lax.div(part, 2), lax.rem(part, 2), at

    def norm_two(index, total):
        first = pl.multiple_of(index * CHUNK, CHUNK)
        rows = pl.ds(first, CHUNK)
        a, b, at = quarter_rows(index)
        middle = r.stream[rows].astype(f32) + r.mixer[a, b, at].astype(f32)
        scale = lax.rsqrt(mean_square(middle) + 1e-06)
        back, gain = norm_back(middle, scale, r.gains[1:2], r.two_total[a, b, at].astype(f32))
        grad = r.cot_rows[rows].astype(f32) + back
        r.stream_grad[rows] = grad
        r.right_out[rows] = grad.astype(bf16)
        return total + jnp.sum(gain, axis=0, keepdims=True)

    gain_two = lax.fori_loop(0, chunks, norm_two, jnp.zeros((1, width), f32))
    r.flat_move[0] = jnp.zeros_like(r.flat_move[0])
    r.flat_move[0, 1:2] = gain_two
    weights.wait()
    scan_own.wait()
    skips = []
    for j in range(0, channels, 256):
        lanes = slice(j, j + 256)
        gated_grad = dot_rows(r.right_out[own], r.weights[pl.ds(j, 256)])
        gate_pre = r.proj[:, channels + j : channels + j + 256].astype(f32)
        part = sigmoid(gate_pre)
        slope = part * (1.0 + gate_pre * (1.0 - part))
        r.right_in[own, channels + j : channels + j + 256] = (
            gated_grad * r.scan[:, lanes] * slope
        ).astype(bf16)
        grad = gated_grad * gate_pre * part
        r.scan[:, lanes] = grad
        skips.append(jnp.sum(grad * r.low[:, lanes].astype(f32), axis=0, keepdims=True))
    skip_grad = jnp.concatenate(skips, 1)
    weights = load(r.w_in.at[pl.ds(0, channels)], r.weights)
    out_of_own.wait()
    for j in range(0, channels, LANES):
        lanes = slice(j, j + LANES)

        def ended(index, carried, lanes=lanes, block_rates=rates[:, j : j + LANES]):
            first = pl.multiple_of(tokens - UNROLL - index * UNROLL, UNROLL)
            steps, grads = r.step[pl.ds(first, UNROLL), lanes], r.scan[pl.ds(first, UNROLL), lanes]
            for k in reversed(range(UNROLL)):
                decay = jnp.exp2(steps[k : k + 1] * block_rates)
                carried = decay * (widened(r.out_of[first + k], LANES) * grads[k : k + 1] + carried)
            return carried

        r.starts[:, lanes] = lax.fori_loop(
            0, tokens // UNROLL, ended, jnp.zeros((states, LANES), f32)
        )

    def handed():
        all_state, all_steps = r.starts[...], r.step_sum[...]
        mine_state, mine_steps = jnp.zeros_like(all_state), jnp.zeros_like(all_steps)
        for k, bit in enumerate(bits):
            side, partner = flipped(me, bit)
            r.chain_move[k, :states] = all_state
            r.chain_move[k, states:] = all_steps
            copy = sent(r.chain_move.at[k], r.chain_land.at[k], r.chain_sends, r.chain_receives,
                        k, "seq", partner)
            yield
            copy.wait()
            other_state, other_steps = r.chain_land[k, :states], r.chain_land[k, states:]
            earlier = side == 0
            through = jnp.exp2(rates * mine_steps[:1])
            mine_state = jnp.where(earlier, mine_state + through * other_state, mine_state)
            mine_steps = jnp.where(earlier, mine_steps + other_steps, mine_steps)
            after = jnp.exp2(rates * all_steps[:1]) * other_state + all_state
            ahead_of = jnp.exp2(rates * other_steps[:1]) * all_state + other_state
            all_state = jnp.where(earlier, after, ahead_of)
            all_steps = all_steps + other_steps
        r.starts[...] = mine_state
        yield

    chain = handed()
    next(chain)
    gate0.made(two_own, gate_up_own, gate_other)
    next(chain)
    gate0.go()
    gate1.made()
    next(chain)
    late_kept.wait()
    late.next()
    gate1.go()
    up0.made(up_other)
    for _ in chain:
        pass
    first = pl.multiple_of(low * (tokens // 2), tokens // 2)
    mixer_other = swap_shared(
        r.right_out.at[pl.ds(first, tokens // 2)],
        r.right_out.at[pl.ds(tokens + first, tokens // 2)],
    )
    gated_other = swap(r.gated_in.at[:, 1 - mine], r.left_gated.at[:, :, :, other])
    gin_other = swap(
        r.right_in.at[own, pl.ds(channels, channels)],
        r.right_in.at[other, pl.ds(channels, channels)],
    )
    up0.go()
    up1.made().go()

    part_in.wait()
    feed_sums = [summed(r.part, 0, k) for k in range(2)]
    into_own.wait()

    def results():
        totals = lax.fori_loop(
            0, chunks, results_of, tuple(jnp.zeros((1, width), f32) for _ in range(3))
        )
        for number, total in enumerate(totals):
            r.flat_move[0, 3 + number : 4 + number] = total

    def feed_start():
        for item in feed_sums:
            next(item)
        return in_turn(*feed_sums)

    feed = []
    between = [
        lambda: (feed.append(feed_start()), next(feed[0]), gate0.next()),
        lambda: next(feed[0]),
        lambda: (next(feed[0]), gate1.next()),
        lambda: next(feed[0]),
        lambda: (next(feed[0]), up0.next()),
        lambda: (results(), out.made(gated_own, mixer_other, gated_other).go()),
    ]

    def results_of(index, totals):
        rows = pl.ds(pl.multiple_of(index * CHUNK, CHUNK), CHUNK)
        a, b, at = quarter_rows(index)
        mixed, feed = r.mixer[a, b, at].astype(f32), r.total[a, b, at].astype(f32)
        result = r.stream[rows].astype(f32) + mixed + feed
        r.out_rows[rows] = result.astype(bf16)
        return tuple(
            total + jnp.sum(v * v, axis=0, keepdims=True)
            for total, v in zip(totals, (result, mixed, feed))
        )

    r.into_wide[...] = jnp.zeros_like(r.into_wide)
    r.out_wide[...] = jnp.zeros_like(r.out_wide)
    for number, lanes in enumerate(blocks):
        hists[number].wait()
        hist = r.hist.at[number % 2]
        block_rates = rates[:, lanes]

        def walked(index, carry, lanes=lanes, block_rates=block_rates, hist=hist):
            carried, state, total = carry
            first = pl.multiple_of(tokens - UNROLL - index * UNROLL, UNROLL)
            some = pl.ds(first, UNROLL)
            steps, drives, grads = r.step[some, lanes], r.drive[some, lanes], r.scan[some, lanes]
            decay_list, push_list = [None] * UNROLL, [None] * UNROLL
            for k in reversed(range(UNROLL)):
                place = first + k
                grad_row = grads[k : k + 1]
                decay = jnp.exp2(steps[k : k + 1] * block_rates)
                adjoint = r.out_of[place] * grad_row + carried
                carried = decay * adjoint
                r.out_wide[place] = r.out_wide[place] + state * grad_row
                r.into_wide[place] = r.into_wide[place] + adjoint * drives[k : k + 1]
                state = hist[place]
                share = carried * state
                total = total + share * steps[k : k + 1]
                decay_list[k] = jnp.sum(share * block_rates, axis=0, keepdims=True)
                push_list[k] = jnp.sum(r.into[place] * adjoint, axis=0, keepdims=True)
            r.decay_rows[some, :] = jnp.concatenate(decay_list, 0)
            r.push[some, lanes] = jnp.concatenate(push_list, 0)
            return (carried, state, total)

        _, _, total = lax.fori_loop(
            0,
            tokens // UNROLL,
            walked,
            (r.starts[:, lanes], r.last_state[:, lanes], jnp.zeros((states, 128), f32)),
        )
        r.rate_sum[:, lanes] = total * (rates[:, lanes] * LN2)

        def gathered(index, _, lanes=lanes):
            rows = pl.ds(pl.multiple_of(index * CHUNK, CHUNK), CHUNK)
            used, pushed = r.low[rows, lanes].astype(f32), r.push[rows, lanes]
            pre = r.step_pre[rows, lanes]
            grad = (LN2 * r.decay_rows[rows] + pushed * used) * sigmoid(pre)
            r.step_low_grad[rows, lanes] = grad.astype(bf16)
            r.push[rows, lanes] = pushed * softplus(pre) + r.chan[6:7, lanes] * r.scan[rows, lanes]
            return 0

        lax.fori_loop(0, chunks, gathered, 0)
        if number + 2 < len(blocks):
            hists.append(load(r.hist_in.at[:, :, blocks[number + 2]], r.hist.at[number % 2]))
        if number < len(between):
            between[number]()
    for later in between[len(blocks) :]:
        later()

    def norm_grads(index, _):
        first = pl.multiple_of(index * CHUNK, CHUNK)
        rows = pl.ds(first, CHUNK)
        low_part = dot_rows(r.step_low_grad[rows], r.w_dt[...])
        r.raw_move[0, rows] = jnp.concatenate(
            [low_part, narrowed(r.into_wide, first, CHUNK), narrowed(r.out_wide, first, CHUNK)], 1
        )
        return 0

    lax.fori_loop(0, chunks, norm_grads, 0)
    copy = sent(r.raw_move.at[0], r.raw_land.at[0], r.raw_sends, r.raw_receives, 0, "ch", across)
    gin.made(one_own, one_other, gin_other)
    copy.wait()
    r.raw_move[1] = r.raw_move[0] + r.raw_land[0]
    copy = sent(r.raw_move.at[1], r.raw_land.at[1], r.raw_sends, r.raw_receives, 1, "ch", along)
    up1.next()
    copy.wait()

    def raw_back(index, total):
        rows = pl.ds(pl.multiple_of(index * CHUNK, CHUNK), CHUNK)
        grads, raw = r.raw_move[1, rows] + r.raw_land[1, rows], r.raw[rows]
        gains = r.small_gains[...]
        values, sums_to = [], []
        for start, stop, floor in ((0, rank, None), (rank, rank + states, 0.1),
                                   (rank + states, rank + 2 * states, 0.1)):
            value = raw[:, start:stop]
            square = mean_square(value)
            if floor is None:
                scale, free = lax.rsqrt(square + 1e-06), True
            else:
                scale, free = lax.rsqrt(jnp.maximum(square, floor)), square > floor
            back, gain = norm_back(value, scale, gains[:, start:stop], grads[:, start:stop], free)
            values.append(back)
            sums_to.append(jnp.sum(gain, axis=0, keepdims=True))
        norm = raw[:, :rank] * lax.rsqrt(mean_square(raw[:, :rank]) + 1e-06) * gains[:, :rank]
        r.raw_low[rows] = jnp.concatenate(values, 1).astype(bf16)
        r.step_low[rows] = norm.astype(bf16)
        return total + jnp.concatenate(sums_to, 1)

    small = lax.fori_loop(0, chunks, raw_back, jnp.zeros((1, rank + 2 * states), f32))
    r.flat_move[0, 2:3, : rank + 2 * states] = small

    def conv_back(index, total):
        first = pl.multiple_of(index * CHUNK, CHUNK)
        rows = pl.ds(first, CHUNK)
        grad = r.push[rows] + dot_rows(r.raw_low[rows], r.w_x[...])
        grad = grad * silu_slope(r.pre[rows])
        r.grad_pre[rows] = grad
        return total + jnp.sum(grad, axis=0, keepdims=True)

    tap_bias = lax.fori_loop(0, chunks, conv_back, jnp.zeros((1, channels), f32))
    copy = sent(r.grad_pre.at[pl.ds(0, 8)], r.grad_pre.at[pl.ds(tokens, 8)], r.raw_sends,
                r.raw_receives, 2, "seq", previous)
    gin.go()
    r.extended[0:16] = r.halo[...].astype(f32)

    def extend(index, _):
        first = pl.multiple_of(index * CHUNK, CHUNK)
        r.extended[pl.ds(first + 16, CHUNK)] = r.proj[pl.ds(first, CHUNK), :channels].astype(f32)
        return 0

    lax.fori_loop(0, chunks, extend, 0)

    def taps(index, totals):
        first = pl.multiple_of(index * CHUNK, CHUNK)
        places = places_of(first, CHUNK)
        window = r.extended[pl.ds(first, CHUNK + 16)]
        grad = r.grad_pre[pl.ds(first, CHUNK)]
        return tuple(
            totals[k]
            + jnp.sum(
                grad
                * widened(tap_mask(places, r.bounds, 3 - k), channels)
                * window[13 + k : 13 + k + CHUNK],
                axis=0,
                keepdims=True,
            )
            for k in range(4)
        )

    tap_grads = lax.fori_loop(
        0, chunks, taps, tuple(jnp.zeros((1, channels), f32) for _ in range(4))
    )
    copy.wait()

    def conv_in_back(index, _):
        first = pl.multiple_of(index * CHUNK, CHUNK)
        window = r.grad_pre[pl.ds(first, CHUNK + 8)]
        grad = jnp.zeros((CHUNK, channels), f32)
        for k in range(4):
            places = places_of(first + 3 - k, CHUNK)
            mask = jnp.where(
                places < seq_count * tokens, tap_mask(places, r.bounds, 3 - k), 0.0
            )
            grad = grad + r.chan[k : k + 1] * widened(mask, channels) * window[3 - k : 3 - k + CHUNK]
        r.right_in[pl.ds(first, CHUNK), :channels] = grad.astype(bf16)
        return 0

    lax.fori_loop(0, chunks, conv_in_back, 0)
    cin_others = [
        swap(
            r.right_in.at[own, pl.ds(*item.columns)], r.right_in.at[other, pl.ds(*item.columns)]
        )
        for item in cins
    ]

    def small_columns():
        narrow = r.w_x.shape[1]
        pack = r.step
        pack[0:narrow] = lax.dot_general(
            r.raw_low[...], r.low[...], (((0,), (0,)), ((), ())), preferred_element_type=f32
        )
        pack[narrow : narrow + rank] = lax.dot_general(
            r.step_low[...], r.step_low_grad[...], (((0,), (0,)), ((), ())),
            preferred_element_type=f32,
        )
        at = narrow + rank
        pack[at : at + states] = r.rate_sum[...]
        at += states
        bias = jnp.sum(r.step_low_grad[...].astype(f32), axis=0, keepdims=True)
        pack[at : at + 8] = jnp.concatenate(
            [*tap_grads, tap_bias, bias, skip_grad, jnp.zeros((1, channels), f32)], 0
        )
        at += 8
        pack[at:] = jnp.zeros((pack.shape[0] - at, channels), f32)
        turned = pack[...].T
        r.small_work[0][...] = turned.reshape(r.small_work[0].shape)

    def small_summed():
        for k, bit in enumerate(bits):
            side, partner = flipped(me, bit)
            work, away, land = r.small_work[k], r.small_away[k], r.small_land[k]
            away[...] = work[:, 1 - side].astype(bf16)
            copy = sent(away, land, r.last_sends, r.last_receives, k, "seq", partner)
            yield
            copy.wait()
            total = work[:, side] + land[...].astype(f32)
            target = r.small_work[k + 1] if k + 1 < len(bits) else r.small_out
            target[...] = total.reshape(target.shape)
        yield

    small_columns()
    small_sum = small_summed()
    next(small_sum)

    one_sums = [summed(r.part, 8, k) for k in range(2)]
    for number in range(width // channels):
        weights.wait()

        def one_part(index, _, first=number * channels):
            at = pl.multiple_of(index * 256, 256)
            product = dot_rows(r.right_in[own], r.weights[pl.ds(at, 256)]).astype(bf16)
            for k in range(4):
                r.part[k // 2, k % 2, :, pl.ds(first + at, 256)] = product[
                    k * quarter : (k + 1) * quarter
                ]
            return 0

        lax.fori_loop(0, channels // 256, one_part, 0)
        next(one_sums[number])
        if (number + 1) * channels < width:
            weights = load(r.w_in.at[pl.ds((number + 1) * channels, channels)], r.weights)
    one_sum = in_turn(*one_sums)
    next(one_sum)

    def gain_part(index, total):
        rows = pl.ds(pl.multiple_of(index * CHUNK, CHUNK), CHUNK)
        a, b, at = quarter_rows(index)
        value = r.stream[rows].astype(f32)
        scale = lax.rsqrt(mean_square(value) + 1e-06)
        return total + jnp.sum(r.part[a, b, at].astype(f32) * value * scale, axis=0, keepdims=True)

    r.flat_move[0] = r.flat_move[0] * 0.25
    r.flat_move[0, 0:1] = lax.fori_loop(0, chunks, gain_part, jnp.zeros((1, width), f32))
    ways = [("ch", across), ("ch", along)] + [("seq", flipped(me, bit)[1]) for bit in bits]

    def flat_summed():
        for k, (axis, partner) in enumerate(ways):
            copy = sent(r.flat_move.at[k], r.flat_land.at[k], r.flat_sends, r.flat_receives, k,
                        axis, partner)
            yield
            copy.wait()
            target = r.flat_move.at[k + 1] if k + 1 < len(ways) else r.flat_out
            target[...] = r.flat_move[k] + r.flat_land[k]
        yield

    flat_sum = flat_summed()
    next(flat_sum)

    out.next()
    next(one_sum)
    next(flat_sum)
    cins[0].made(cin_others[0]).go()
    next(one_sum)
    next(flat_sum)
    cins[1].made(cin_others[1]).go()
    next(one_sum)
    next(flat_sum)
    next(small_sum)
    gin.next()
    next(one_sum)

    def norm_one(index, _):
        rows = pl.ds(pl.multiple_of(index * CHUNK, CHUNK), CHUNK)
        a, b, at = quarter_rows(index)
        value = r.stream[rows].astype(f32)
        scale = lax.rsqrt(mean_square(value) + 1e-06)
        back, _ = norm_back(value, scale, r.gains[0:1], r.total[a, b, at].astype(f32))
        r.stream_grad[rows] = r.stream_grad[rows] + back
        return 0

    lax.fori_loop(0, chunks, norm_one, 0)
    down_kept.wait()
    for item in (down, late, *quarters):
        item.next()
    cins[0].next()
    next(flat_sum)
    next(small_sum)
    cins[1].next()
    for waiting in (flat_sum, small_sum):
        for _ in waiting:
            pass
    pending = [out, gin, *cins, down, late, *quarters]
    for _ in range(len(bits)):
        for item in pending:
            item.next()
    for item in pending:
        item.written.wait()


def backward(ins, hbm_ins, count, ident):
    bits = bits_of(count)
    n_bits = len(bits) - 1
    tokens, width = ins["stream"].shape
    channels, rank, states = ins["low"].shape[1], ins["w_dt"].shape[0], ins["logs"].shape[0]
    hid = hbm_ins["right_two_in"].shape[1] // 2
    narrow = ins["w_x"].shape[1]
    half, quarter = count // 2, tokens // 4
    rows_in, rows_out, rows_down = width // count, channels // count, hid // count
    rows = pltpu.VMEM((tokens, channels), f32)

    def low(*dims):
        return pltpu.VMEM(dims, bf16)

    def full(*dims):
        return pltpu.VMEM(dims, f32)

    outs = dict(
        stream_grad=(shape_of(tokens, width), VMEM),
        out_rows=(shape_of(tokens, width, dtype=bf16), VMEM),
        small_out=(shape_of(rows_out, tokens), VMEM),
        flat_out=(shape_of(8, width), VMEM),
        down_out=(shape_of(rows_down, width), ANY),
        gate_out=(shape_of(rows_in, hid), ANY),
        up_out=(shape_of(rows_in, hid), ANY),
        out_out=(shape_of(rows_out, width), ANY),
        gin_out=(shape_of(rows_in, channels), ANY),
        cin_out=(shape_of(rows_in, channels), ANY),
    )
    quads = count // 4

    def unit(part, columns):
        lands = [low(half >> (k + 1), part, columns) for k in range(n_bits)]
        return [low(half // 2, part, columns), *lands, full(half // 2, part, columns)]

    def sems(size):
        return pltpu.SemaphoreType.DMA((size,))

    halves = [count >> (k + 1) for k in range(len(bits))]
    scratch = dict(
        left_two=low(quads, 2, rows_in, 2 * tokens),
        left_one=low(quads, 2, rows_in, 2 * tokens),
        left_gated=low(quads, 2, rows_out, 2 * tokens),
        cot_rows=low(tokens, width),
        right_two=low(2 * tokens, 2 * hid),
        right_out=low(2 * tokens, width),
        right_in=low(2 * tokens, 2 * channels),
        mixer=low(2, 2, quarter, width),
        weights=low(channels, width),
        scan=rows,
        step=rows,
        drive=rows,
        push=rows,
        decay_rows=full(tokens, 128),
        into=full(tokens, states, 128),
        out_of=full(tokens, states, 128),
        into_wide=full(tokens, states, 128),
        out_wide=full(tokens, states, 128),
        hist=full(2, tokens, states, 128),
        step_sum=full(8, channels),
        starts=full(states, channels),
        rate_sum=full(states, channels),
        step_low_grad=low(tokens, channels),
        chain_move=full(len(bits), states + 8, channels),
        chain_land=full(len(bits), states + 8, channels),
        part=low(2, 2, quarter, width),
        total=low(2, 2, quarter, width),
        first_land=low(2, quarter, width),
        second_land=low(quarter, width),
        second_move=low(quarter, width),
        raw_move=full(2, tokens, narrow),
        raw_land=full(2, tokens, narrow),
        raw_low=low(tokens, narrow),
        step_low=low(tokens, rank),
        grad_pre=full(tokens + 8, channels),
        extended=full(tokens + 16, channels),
        flat_move=full(2 + len(bits), 8, width),
        flat_land=full(2 + len(bits), 8, width),
        small_work=[full(size, 2, rows_out, tokens) for size in halves],
        small_away=[low(size, rows_out, tokens) for size in halves],
        small_land=[low(size, rows_out, tokens) for size in halves],
        down=unit(rows_down, width // 2),
        late=unit(rows_down, width // 2),
        gate0=unit(rows_in, hid // 2),
        gate1=unit(rows_in, hid // 2),
        up0=unit(rows_in, hid // 2),
        up1=unit(rows_in, hid // 2),
        out=unit(rows_out, width),
        gin=unit(rows_in, channels),
        cin0=unit(rows_in, channels // 2),
        cin1=unit(rows_in, channels // 2),
        load_sems=sems(32),
        write_sems=sems(10),
        pair_sends=sems(8),
        pair_receives=sems(8),
        shared_sends=sems(4),
        shared_receives=sems(4),
        unit_sends=sems(10 * n_bits),
        unit_receives=sems(10 * n_bits),
        sum_sends=sems(16),
        sum_receives=sems(16),
        chain_sends=sems(len(bits)),
        chain_receives=sems(len(bits)),
        raw_sends=sems(3),
        raw_receives=sems(3),
        last_sends=sems(len(bits)),
        last_receives=sems(len(bits)),
        flat_sends=sems(2 + len(bits)),
        flat_receives=sems(2 + len(bits)),
    )
    names, shapes = [(name, 0) for name in [*ins, *hbm_ins, *outs]], []
    for name, held in scratch.items():
        listed = isinstance(held, list)
        names.append((name, len(held) if listed else 0))
        shapes += held if listed else [held]
    places = [VMEM for _ in ins]
    places[0] = pl.BlockSpec(memory_space=pltpu.SMEM)
    made = pl.pallas_call(
        functools.partial(backward_kernel, bits, names),
        out_shape=[shape for shape, _ in outs.values()],
        in_specs=places + [ANY] * len(hbm_ins),
        out_specs=[spec for _, spec in outs.values()],
        scratch_shapes=shapes,
        compiler_params=pltpu.CompilerParams(
            collective_id=ident, has_side_effects=True, vmem_limit_bytes=63 * 2**20
        ),
        name="block_backward",
    )(*ins.values(), *hbm_ins.values())
    return types.SimpleNamespace(**dict(zip(outs, made)))


def rms_gain(values, gain_row):
    return values * lax.rsqrt(jnp.mean(values * values, axis=-1, keepdims=True) + 1e-06) * gain_row


def local(
    seq_count,
    stream,
    doc_bounds,
    norm_gains,
    w_in,
    chan_vectors,
    decay_logs,
    w_x,
    small_gains,
    w_dt,
    w_out,
    w_gate_up,
    w_down,
    cotangent,
):
    tokens, width = stream.shape
    rank, (states, channels) = w_dt.shape[0], decay_logs.shape

    def turned(values):
        return values.T.reshape(seq_count // 4, 2, 2, values.shape[1] // seq_count, tokens)

    stream_in = stream.astype(f32)
    normed_low = rms_gain(stream_in, norm_gains[0]).astype(bf16)
    w_in_flat = w_in.reshape(width, 2 * channels)
    in_proj = jnp.dot(normed_low, w_in_flat, preferred_element_type=f32).astype(bf16)
    one_in = turned(normed_low)
    (
        halo, pre_conv, conv_low, raw_proj, step_pre, into, out_of, scan_out, gated_low,
        last_state, mixer_low, before, one_came, cot_came,
    ) = mixer_forward(
        doc_bounds, in_proj, chan_vectors, decay_logs, w_x, small_gains[None], w_dt, w_out,
        one_in, cotangent, seq_count, 1,
    )
    mid = feed_forward(
        dict(stream=stream, mixer=mixer_low, gains=norm_gains),
        dict(
            cot=cotangent, cot_came=cot_came, w_gate_up_in=w_gate_up.reshape(width, -1),
            w_down_in=w_down,
        ),
        seq_count,
        3,
    )
    made = backward(
        dict(
            bounds=doc_bounds, stream=stream, gains=norm_gains, two_total=mid.total,
            proj=in_proj, halo=halo,
            pre=pre_conv, low=conv_low, raw=raw_proj, step_pre=step_pre, last_state=last_state,
            chan=chan_vectors, logs=decay_logs, w_x=w_x, w_dt=w_dt, small_gains=small_gains[None],
        ),
        dict(
            feed_part=mid.feed_part, left_two_in=mid.left_two, right_two_in=mid.right_two,
            down_away_in=mid.down_away, down_kept_in=mid.down_kept,
            late_away_in=mid.late_away, late_kept_in=mid.late_kept, mixer_in=mixer_low,
            cot=cotangent, gated_in=turned(gated_low), one_in=one_in,
            one_came=one_came, w_out=w_out, w_in=w_in_flat, scan_in=scan_out, into_in=into,
            out_of_in=out_of, hist_in=before,
        ),
        seq_count,
        2,
    )
    small, flat = made.small_out, made.flat_out
    at = w_x.shape[1]
    x_part, small = small[:, :at], small[:, at:].T
    dt_part, decay_out = small[:rank], small[rank : rank + states]
    chan_part = small[rank + states : rank + states + 7]
    me = lax.axis_index("seq")
    gain_width = width // seq_count
    gains_part = lax.dynamic_slice_in_dim(flat[:2], me * gain_width, gain_width, 1)
    small_width = small_gains.shape[0] // seq_count
    small_part = lax.dynamic_slice_in_dim(flat[2], me * small_width, small_width, 0)
    rms_values = jnp.sqrt(jnp.sum(flat[3:6], axis=1) / (tokens * seq_count * width))
    return (
        made.out_rows,
        made.stream_grad,
        gains_part,
        jnp.stack([made.cin_out, made.gin_out], 1),
        chan_part,
        decay_out,
        x_part,
        small_part,
        dt_part,
        made.out_out,
        jnp.stack([made.gate_out, made.up_out], 1),
        made.down_out,
        rms_values,
    )


def solution(mesh):
    in_specs = (
        P("seq", None),
        P(),
        P(),
        P(None, None, "ch"),
        P(None, "ch"),
        P(None, "ch"),
        P("ch", None),
        P(),
        P(None, "ch"),
        P("ch", None),
        P(None, None, "ch"),
        P("ch", None),
        P("seq", None),
    )
    out_specs = (
        P("seq", None),
        P("seq", None),
        P(None, "seq"),
        P("seq", None, "ch"),
        P(None, ("ch", "seq")),
        P(None, ("ch", "seq")),
        P(("ch", "seq"), None),
        P("seq"),
        P(None, ("ch", "seq")),
        P(("ch", "seq"), None),
        P("seq", None, "ch"),
        P(("ch", "seq"), None),
        P(),
    )
    return jax.shard_map(
        functools.partial(local, mesh.shape["seq"]),
        mesh=mesh,
        in_specs=in_specs,
        out_specs=out_specs,
        check_vma=False,
    )
```

```python
import functools
import math
import types

import jax
import jax.numpy as jnp
from jax import lax
from jax.experimental import pallas as pl
from jax.experimental.pallas import tpu as pltpu
from jax.sharding import PartitionSpec as P

f32 = jnp.float32
bf16 = jnp.bfloat16
LOG2E = math.log2(math.e)
LN2 = math.log(2.0)
RESET = 1e30
UNROLL = 8
LANES = 256
VMEM = pl.BlockSpec(memory_space=pltpu.VMEM)


def shape_of(*dims, dtype=f32):
    return jax.ShapeDtypeStruct(dims, dtype)


def cost(us):
    return pl.CostEstimate(flops=int(us * 1e9), bytes_accessed=int(us * 1e6), transcendentals=0)


def widened(column, width):
    return jnp.concatenate([column] * (width // 128), 1)


ANY = pl.BlockSpec(memory_space=pl.ANY)


def sent(source, target, sends, receives, slot, axis, partner):
    copy = pltpu.make_async_remote_copy(
        src_ref=source,
        dst_ref=target,
        send_sem=sends.at[slot],
        recv_sem=receives.at[slot],
        device_id={axis: partner},
        device_id_type=pl.DeviceIdType.MESH,
    )
    copy.start()
    return copy


def bits_of(count):
    return [1 << k for k in range(count.bit_length() - 1)]


def flipped(me, bit):
    mine = lax.rem(me // bit, 2)
    return mine, me + bit - 2 * bit * mine


CHUNK = 32


def sigmoid(values):
    return 1.0 / (1.0 + jnp.exp(-values))


def softplus(values):
    return jnp.maximum(values, 0.0) + jnp.log1p(jnp.exp(-jnp.abs(values)))


def row_doc(places, bounds):
    return (places >= bounds[0]).astype(jnp.int32) + (places >= bounds[1]).astype(jnp.int32)


def tap_mask(places, bounds, offset):
    source = places - offset
    same = row_doc(source, bounds) == row_doc(places, bounds)
    return jnp.where((source >= 0) & same, 1.0, 0.0)


def mean_square(values):
    return jnp.mean(values * values, axis=-1, keepdims=True)


def three_norms(raw, gains, rank, states):
    low, mid, high = raw[:, :rank], raw[:, rank : rank + states], raw[:, rank + states :]
    low_scale = lax.rsqrt(mean_square(low) + 1e-06)
    mid_scale = lax.rsqrt(jnp.maximum(mean_square(mid), 0.1))
    high_scale = lax.rsqrt(jnp.maximum(mean_square(high), 0.1))
    return (
        low * low_scale * gains[:, :rank],
        mid * mid_scale * gains[:, rank : rank + states],
        high * high_scale * gains[:, rank + states :],
    )


def widen(values, wide, first, count):
    states = values.shape[1]
    eye = (
        lax.broadcasted_iota(jnp.int32, (states, states), 0)
        == lax.broadcasted_iota(jnp.int32, (states, states), 1)
    ).astype(f32)
    spread = jnp.sum(values[:, None, :] * eye[None], axis=-1, keepdims=True)
    wide[pl.ds(first, count)] = jnp.broadcast_to(spread, (count, states, 128))


def greeted(axis_partners):
    barrier = pltpu.get_barrier_semaphore()
    for axis, partner in axis_partners:
        pl.semaphore_signal(
            barrier, inc=1, device_id={axis: partner}, device_id_type=pl.DeviceIdType.MESH
        )
    pl.semaphore_wait(barrier, len(axis_partners))


def handed_on(forward, state, steps, rates, r):
    me, count = lax.axis_index("seq"), r.state_land.shape[0] + 1
    r.state_move[...] = state.astype(bf16)
    r.steps_move[...] = steps
    copies = []
    for k in range(1, count):
        to = lax.rem(me + k, count)
        for source, land, sends, receives in (
            (r.state_move, r.state_land, r.state_sends, r.state_receives),
            (r.steps_move, r.steps_land, r.steps_sends, r.steps_receives),
        ):
            copies.append(sent(source, land.at[k - 1], sends, receives, k - 1, "seq", to))
    yield
    for copy in copies:
        copy.wait()
    total = jnp.zeros_like(state)
    passed = jnp.zeros_like(steps)
    for k in range(1, count):
        slot = k - 1 if forward else count - k - 1
        valid = (me >= k) if forward else (me + k < count)
        term = jnp.exp2(rates * passed) * r.state_land[slot].astype(f32)
        total = total + jnp.where(valid, term, 0.0)
        passed = passed + jnp.where(valid, r.steps_land[slot], 0.0)
    yield total


def handing(count, states, channels):
    sems = pltpu.SemaphoreType.DMA((count - 1,))
    return dict(
        state_move=pltpu.VMEM((states, channels), bf16),
        steps_move=pltpu.VMEM((1, channels), f32),
        state_land=pltpu.VMEM((count - 1, states, channels), bf16),
        steps_land=pltpu.VMEM((count - 1, 1, channels), f32),
        state_sends=sems,
        state_receives=sems,
        steps_sends=sems,
        steps_receives=sems,
    )


def forward_kernel(
    bits, bounds, proj, chan, logs, w_x, gains, w_dt, w_out, one_in, cot,
    halo, pre_out, low_out, raw_out, step_pre_out, into, out_of, scan_out, gated_out, last_state,
    mixer, hist_out, one_came, cot_came,
    extended, raw_move, raw_land, step, drive, starts, part, first_land,
    second_move, second_land, hist, sends, receives, hist_sem, shared_sends, shared_receives,
    sum_sends, sum_receives, *handed,
):
    tokens, channels = low_out.shape
    rank, states = w_dt.shape[0], logs.shape[0]
    chunks = tokens // CHUNK
    ch_me, me = lax.axis_index("ch"), lax.axis_index("seq")
    seq_count = 1 << len(bits)
    low, across = flipped(ch_me, 1)
    high, along = flipped(ch_me, 2)
    following = lax.rem(me + 1, seq_count)
    greeted(
        [("ch", across), ("ch", along)]
        + [("seq", lax.rem(me + k, seq_count)) for k in range(1, seq_count)]
    )
    halo_copy = sent(
        proj.at[pl.ds(tokens - 16, 16), pl.ds(0, channels)], halo, sends, receives, 0, "seq",
        following,
    )
    mine, pair = flipped(me, bits[1])
    half = one_in.shape[0] // 2
    some = pl.ds(low * half, half)
    at = pl.ds(pl.multiple_of(low * (tokens // 2), tokens // 2), tokens // 2)
    shared = [
        (one_in.at[some, 1 - mine], one_came.at[some]),
        (cot.at[at], cot_came.at[at]),
    ]
    shared_copies = [
        sent(source, target, shared_sends, shared_receives, k, "seq", pair)
        for k, (source, target) in enumerate(shared)
    ]
    rates = -jnp.exp(logs[...]) * LOG2E

    def spread(index, _):
        first = pl.multiple_of(index * CHUNK, CHUNK)
        extended[pl.ds(first + 16, CHUNK)] = proj[pl.ds(first, CHUNK), :channels].astype(f32)
        return 0

    lax.fori_loop(0, chunks, spread, 0)

    def convolved(index, _):
        first = pl.multiple_of(index * CHUNK, CHUNK)
        places = me * tokens + first + lax.broadcasted_iota(jnp.int32, (CHUNK, 128), 0)
        window = extended[pl.ds(first, CHUNK + 16)]
        summed = chan[4:5]
        for k in range(4):
            mask = widened(tap_mask(places, bounds, 3 - k), channels)
            summed = summed + chan[k : k + 1] * window[13 + k : 13 + k + CHUNK] * mask
        pre_out[pl.ds(first, CHUNK)] = summed
        low_out[pl.ds(first, CHUNK)] = (summed * sigmoid(summed)).astype(bf16)
        return 0

    lax.fori_loop(1, chunks, convolved, 0)
    halo_copy.wait()
    extended[0:16] = halo[...].astype(f32)
    convolved(0, 0)
    raw_move[0] = jnp.dot(low_out[...], w_x[...], preferred_element_type=f32)
    sent(raw_move.at[0], raw_land.at[0], sends, receives, 1, "ch", across).wait()
    raw_move[1] = raw_move[0] + raw_land[0]
    sent(raw_move.at[1], raw_land.at[1], sends, receives, 2, "ch", along).wait()

    def stepped(index, total):
        first = pl.multiple_of(index * CHUNK, CHUNK)
        rows = pl.ds(first, CHUNK)
        raw = raw_move[1, rows] + raw_land[1, rows]
        raw_out[rows] = raw
        step_norm, input_norm, output_norm = three_norms(raw, gains[...], rank, states)
        widen(input_norm, into, first, CHUNK)
        widen(output_norm, out_of, first, CHUNK)
        pre = (
            jnp.dot(step_norm.astype(bf16), w_dt[...], preferred_element_type=f32) + chan[5:6]
        )
        step_pre_out[rows] = pre
        size = softplus(pre)
        drive[rows] = size * low_out[rows].astype(f32)
        places = me * tokens + first + lax.broadcasted_iota(jnp.int32, (CHUNK, 128), 0)
        resets = jnp.where((places == bounds[0]) | (places == bounds[1]), RESET, 0.0)
        size = size + widened(resets, channels)
        step[rows] = size
        return total + jnp.sum(size, axis=0, keepdims=True)

    total = lax.fori_loop(0, chunks, stepped, jnp.zeros((1, channels), f32))
    blocks = [slice(j, j + LANES) for j in range(0, channels, LANES)]
    for lanes in blocks:
        block_rates = rates[:, lanes]

        def ended(index, state, lanes=lanes, block_rates=block_rates):
            first = pl.multiple_of(index * UNROLL, UNROLL)
            steps, drives = step[pl.ds(first, UNROLL), lanes], drive[pl.ds(first, UNROLL), lanes]
            for k in range(UNROLL):
                decay = jnp.exp2(steps[k : k + 1] * block_rates)
                state = decay * state + widened(into[first + k], LANES) * drives[k : k + 1]
            return state

        starts[:, lanes] = lax.fori_loop(
            0, tokens // UNROLL, ended, jnp.zeros((states, LANES), f32)
        )
    hand = types.SimpleNamespace(**dict(zip(handing(2, 8, 128), handed)))
    handed_in = handed_on(True, starts[...], total, rates, hand)
    next(handed_in)
    starts[...] = next(handed_in)
    hist_copies = []
    for number, lanes in enumerate(blocks):
        block_rates = rates[:, lanes]
        skip = chan[6:7, lanes]

        def walked(index, state, lanes=lanes, block_rates=block_rates, skip=skip):
            first = pl.multiple_of(index * UNROLL, UNROLL)
            steps, drives = step[pl.ds(first, UNROLL), lanes], drive[pl.ds(first, UNROLL), lanes]
            rows = []
            for k in range(UNROLL):
                hist[first + k, :, lanes] = state
                decay = jnp.exp2(steps[k : k + 1] * block_rates)
                state = decay * state + widened(into[first + k], LANES) * drives[k : k + 1]
                rows.append(
                    jnp.sum(widened(out_of[first + k], LANES) * state, axis=0, keepdims=True)
                )
            scan_out[pl.ds(first, UNROLL), lanes] = jnp.concatenate(rows, 0)
            return state

        last_state[:, lanes] = lax.fori_loop(0, tokens // UNROLL, walked, starts[:, lanes])
        copy = pltpu.make_async_copy(
            hist.at[:, :, lanes], hist_out.at[:, :, lanes], hist_sem.at[number]
        )
        copy.start()
        hist_copies.append(copy)

    def gate(index, _):
        first = pl.multiple_of(index * CHUNK, CHUNK)
        rows = pl.ds(first, CHUNK)
        scanned = scan_out[rows] + chan[6:7] * low_out[rows].astype(f32)
        scan_out[rows] = scanned
        gate_pre = proj[rows, channels:].astype(f32)
        gated_out[rows] = (scanned * gate_pre * sigmoid(gate_pre)).astype(bf16)
        return 0

    lax.fori_loop(0, chunks, gate, 0)
    quarter = tokens // 4
    width = w_out.shape[1]
    for k, (_, target) in enumerate(shared):
        shared_copies[k].wait()
        shared_copies[k] = sent(
            target, target, shared_sends, shared_receives, 2 + k, "ch", across
        )

    def mixed(index, _):
        first = pl.multiple_of(index * 256, 256)
        product = jnp.dot(
            gated_out[...], w_out[:, pl.ds(first, 256)], preferred_element_type=f32
        ).astype(bf16)
        for k in range(4):
            part[k // 2, k % 2, :, pl.ds(first, 256)] = product[k * quarter : (k + 1) * quarter]
        return 0

    held = types.SimpleNamespace(
        first_land=first_land, second_land=second_land, second_move=second_move, total=mixer,
        sum_sends=sum_sends, sum_receives=sum_receives,
    )
    sums = [four_summed(held, (low, across, high, along), part, 0, k) for k in range(2)]
    for k, item in enumerate(sums):
        lax.fori_loop(k * width // 512, (k + 1) * width // 512, mixed, 0)
        next(item)
    for _ in in_turn(*sums):
        pass
    for copy in hist_copies + shared_copies:
        copy.wait()


def mixer_forward(bounds, proj, chan, logs, w_x, gains, w_dt, w_out, one_in, cot, count, ident):
    bits = bits_of(count)
    tokens, channels = proj.shape[0], proj.shape[1] // 2
    states, rank, width = logs.shape[0], w_dt.shape[0], w_out.shape[1]
    quarter, narrow = tokens // 4, w_x.shape[1]
    rows = shape_of(tokens, channels)
    low_rows = shape_of(tokens, channels, dtype=bf16)
    wide = shape_of(tokens, states, 128)
    raws = pltpu.VMEM((2, tokens, narrow), f32)
    out = pl.pallas_call(
        functools.partial(forward_kernel, bits),
        out_shape=[
            shape_of(16, channels, dtype=bf16), rows, low_rows, shape_of(tokens, narrow), rows,
            wide, wide, rows, low_rows, shape_of(states, channels),
            shape_of(2, 2, quarter, width, dtype=bf16), shape_of(tokens, states, channels),
            shape_of(one_in.shape[0], *one_in.shape[2:], dtype=bf16),
            shape_of(tokens, width, dtype=bf16),
        ],
        in_specs=[pl.BlockSpec(memory_space=pltpu.SMEM)] + [VMEM] * 7 + [ANY] * 2,
        out_specs=[VMEM] * 11 + [ANY] * 3,
        scratch_shapes=[
            pltpu.VMEM((tokens + 16, channels), f32), raws, raws,
            pltpu.VMEM((tokens, channels), f32), pltpu.VMEM((tokens, channels), f32),
            pltpu.VMEM((states, channels), f32),
            pltpu.VMEM((2, 2, quarter, width), bf16), pltpu.VMEM((2, quarter, width), bf16),
            pltpu.VMEM((quarter, width), bf16), pltpu.VMEM((quarter, width), bf16),
            pltpu.VMEM((tokens, states, channels), f32),
            pltpu.SemaphoreType.DMA((3,)), pltpu.SemaphoreType.DMA((3,)),
            pltpu.SemaphoreType.DMA((channels // LANES,)),
            pltpu.SemaphoreType.DMA((4,)), pltpu.SemaphoreType.DMA((4,)),
            pltpu.SemaphoreType.DMA((8,)), pltpu.SemaphoreType.DMA((8,)),
            *handing(count, states, channels).values(),
        ],
        compiler_params=pltpu.CompilerParams(
            collective_id=ident, has_side_effects=True, vmem_limit_bytes=56 * 2**20
        ),
        cost_estimate=cost(6),
        name="mixer_forward",
    )(bounds, proj, chan, logs, w_x, gains, w_dt, w_out, one_in, cot)
    return out


class Unit:
    def __init__(self, left, right, columns, refs, sends, receives, slot, bits, result):
        self.left, self.right, self.columns = left, right, columns
        away, *self.land, self.kept = refs
        self.away = [away.at[pl.ds(0, land.shape[0])] for land in self.land]
        self.sends, self.receives, self.slot, self.bits = sends, receives, slot, bits
        self.result = result
        self.stage = 0
        self.copy = None

    def made(self, *needed):
        for item in needed:
            item.wait()
        mine, partner = flipped(lax.axis_index("seq"), self.bits[0])
        self.make(1 - mine, self.away[0])
        self.stage = 1
        self.go = lambda: self.begin(partner, mine)
        return self

    def begin(self, partner, mine):
        self.copy = self.start(0, partner)
        self.make(mine, self.kept)

    def begun(self):
        _, partner = flipped(lax.axis_index("seq"), self.bits[0])
        self.stage = 1
        self.copy = self.start(0, partner)

    def resume(self):
        self.stage = 2
        if len(self.bits) > 1:
            _, partner = flipped(lax.axis_index("seq"), self.bits[1])
            self.copy = self.start(1, partner)

    def next(self, send_on=True):
        stage, me = self.stage, lax.axis_index("seq")
        if stage > len(self.bits):
            return
        self.stage += 1
        left_over = stage == len(self.bits)
        self.copy.wait()
        count = self.land[stage - 1].shape[0]
        rows = self.kept.shape[1]
        part = 32 if rows % 32 == 0 else rows
        parts = rows // part

        def total(index, at):
            return self.kept[index, at] + self.land[stage - 1][index, at].astype(f32)

        if left_over:

            def finish(step, _):
                at = pl.ds(pl.multiple_of(step * part, part), part)
                self.kept[0, at] = total(0, at)
                return 0

            lax.fori_loop(0, parts, finish, 0)
            self.written = self.result(self.kept.at[0])
            return
        mine, partner = flipped(me, self.bits[stage])

        def send(step, _):
            index = lax.div(step, parts)
            at = pl.ds(pl.multiple_of(lax.rem(step, parts) * part, part), part)
            self.away[stage][index, at] = total(2 * index + 1 - mine, at).astype(bf16)
            return 0

        lax.fori_loop(0, (count // 2) * parts, send, 0)
        if send_on:
            self.copy = self.start(stage, partner)

        def keep(step, _):
            index = lax.div(step, parts)
            at = pl.ds(pl.multiple_of(lax.rem(step, parts) * part, part), part)
            self.kept[index, at] = total(2 * index + mine, at)
            return 0

        lax.fori_loop(0, (count // 2) * parts, keep, 0)

    def start(self, stage, partner):
        return sent(
            self.away[stage], self.land[stage], self.sends, self.receives, self.slot + stage,
            "seq", partner,
        )

    def make(self, side, target):
        first, width = self.columns
        tile = width if width <= 512 else 512 if width % 512 == 0 else 384
        tiles = width // tile
        count, rows = target.shape[:2]
        together = count if rows % 16 == 0 else 1

        def block(step, _):
            index = lax.div(step, tiles)
            column = pl.multiple_of(lax.rem(step, tiles) * tile, tile)
            left = self.left[:, side] if together > 1 else self.left[pl.ds(index, 1), side]
            product = jnp.dot(
                left.reshape(together * rows, left.shape[2]),
                self.right[:, pl.ds(first + column, tile)],
                preferred_element_type=f32,
            ).astype(target.dtype)
            at = pl.ds(0, count) if together > 1 else pl.ds(index, 1)
            target[at, :, pl.ds(column, tile)] = product.reshape(together, rows, tile)
            return 0

        lax.fori_loop(0, count // together * tiles, block, 0)


def norm_back(values, scale, gains, grad, free=True):
    weighted = gains * grad
    result = scale * weighted
    inner = jnp.mean(values * weighted, axis=-1, keepdims=True)
    return result - jnp.where(free, 1.0, 0.0) * values * (scale * scale * scale) * inner, (
        grad * values * scale
    )


def silu_slope(values):
    part = sigmoid(values)
    return part * (1.0 + values * (1.0 - part))


def narrowed(wide, first, count):
    states = wide.shape[1]
    eye = (
        lax.broadcasted_iota(jnp.int32, (states, states), 0)
        == lax.broadcasted_iota(jnp.int32, (states, states), 1)
    ).astype(f32)
    sums = jnp.sum(wide[pl.ds(first, count)], axis=-1, keepdims=True)
    return jnp.sum(sums * eye[None], axis=1)


def dot_rows(left, right):
    return lax.dot_general(left, right, (((1,), (1,)), ((), ())), preferred_element_type=f32)


class Once:
    def __init__(self, *copies, then=None):
        self.copies, self.then = copies, then

    def wait(self):
        for copy in self.copies:
            copy.wait()
        self.copies = ()
        if self.then is not None:
            after, self.then = self.then, None
            after().wait()


def named(names, refs):
    refs, found = list(refs), {}
    for name, count in names:
        taken, refs = refs[: count or 1], refs[count or 1 :]
        found[name] = taken if count else taken[0]
    return types.SimpleNamespace(**found)


def four_summed(r, place, value, base, part):
    low, across, high, along = place
    half = value.shape[3] // 2
    cols = pl.ds(part * half, half)
    first, second, moving = (
        r.first_land.at[:, :, cols], r.second_land.at[:, cols], r.second_move.at[:, cols]
    )
    total, value = r.total.at[:, :, :, cols], value.at[:, :, :, cols]
    sends, receives, base = r.sum_sends, r.sum_receives, base + 4 * part
    copy = sent(value.at[:, 1 - low], first, sends, receives, base, "ch", across)
    yield
    copy.wait()
    moving[...] = (
        value[1 - high, low].astype(f32) + first[1 - high].astype(f32)
    ).astype(bf16)
    copy = sent(moving, second, sends, receives, base + 1, "ch", along)
    yield
    copy.wait()
    total[high, low] = (
        value[high, low].astype(f32) + first[high].astype(f32) + second[...].astype(f32)
    ).astype(bf16)
    own = total.at[high, low]
    copy = sent(own, own, sends, receives, base + 2, "ch", along)
    yield
    copy.wait()
    both = total.at[:, low]
    copy = sent(both, both, sends, receives, base + 3, "ch", across)
    yield
    copy.wait()
    yield


def in_turn(*steps):
    for _ in range(4):
        yield
        for item in steps:
            next(item)
    yield


def feed_forward_kernel(bits, names, *refs):
    r = named(names, refs)
    tokens, width = r.stream.shape
    quarter, chunks, seq_count = tokens // 4, tokens // CHUNK, 1 << len(bits)
    ch_me, me = lax.axis_index("ch"), lax.axis_index("seq")
    low, across = flipped(ch_me, 1)
    high, along = flipped(ch_me, 2)
    pair_bit, rest_bits = bits[1], [bits[0], *bits[2:]]
    mine, pair = flipped(me, pair_bit)
    hid = r.w_down_in.shape[0]
    tile = 256
    tiles = range(0, hid, tile)
    own, other = pl.ds(0, tokens), pl.ds(tokens, tokens)
    slots = []

    def load(source, target):
        copy = pltpu.make_async_copy(source, target, r.load_sems.at[len(slots)])
        copy.start()
        slots.append(0)
        return Once(copy)

    cot_own = load(r.cot, r.right_down.at[own])
    loads = []
    for at in tiles:
        loads.append(
            [
                load(r.w_gate_up_in.at[:, pl.ds(at, tile)], r.w_gate_up.at[:, pl.ds(at, tile)]),
                load(
                    r.w_gate_up_in.at[:, pl.ds(hid + at, tile)],
                    r.w_gate_up.at[:, pl.ds(hid + at, tile)],
                ),
                load(r.w_down_in.at[pl.ds(at, tile)], r.w_down.at[pl.ds(at, tile)]),
            ]
        )
    cot_other = load(r.cot_came, r.right_down.at[other])
    greeted(
        [("ch", across), ("ch", along), ("seq", pair), ("seq", flipped(me, rest_bits[0])[1])]
    )

    def norm_two(index, _):
        rows = pl.ds(pl.multiple_of(index * CHUNK, CHUNK), CHUNK)
        per = quarter // CHUNK
        part = lax.div(index, per)
        at = pl.ds(pl.multiple_of(lax.rem(index, per) * CHUNK, CHUNK), CHUNK)
        mixed = r.mixer[lax.div(part, 2), lax.rem(part, 2), at].astype(f32)
        middle = r.stream[rows].astype(f32) + mixed
        scale = lax.rsqrt(mean_square(middle) + 1e-06)
        r.normed[rows] = (middle * scale * r.gains[1:2]).astype(bf16)
        return 0

    lax.fori_loop(0, chunks, norm_two, 0)

    def turn(values, first, turned):
        rows = turned.shape[3]
        across_rows = values.T
        for k in range(values.shape[1] // rows):
            owner = first // rows + k
            turned[owner // 4, (owner // 2) % 2, owner % 2] = across_rows[
                k * rows : (k + 1) * rows
            ]

    group = 384
    for at in range(0, width, group):
        turn(r.normed[:, at : at + group], at, r.two_turned)
    half = r.two_turned.shape[0] // 2
    some = pl.ds(low * half, half)
    target = r.left_two.at[some, :, :, other]
    two_copy = sent(
        r.two_turned.at[some, 1 - mine], target, r.pair_sends, r.pair_receives, 0, "seq", pair
    )
    r.left_two[:, :, :, own] = r.two_turned[:, mine]
    cot_own.wait()
    hidden_copies, quads_sent = [], 0
    for number, at in enumerate(tiles):
        for item in loads[number]:
            item.wait()
        gate = jnp.dot(
            r.normed[...], r.w_gate_up[:, pl.ds(at, tile)], preferred_element_type=f32
        )
        up = jnp.dot(
            r.normed[...], r.w_gate_up[:, pl.ds(hid + at, tile)], preferred_element_type=f32
        )
        part = sigmoid(gate)
        act = gate * part
        hidden = (act * up).astype(bf16)
        r.hidden[:, pl.ds(at, tile)] = hidden
        turn(hidden, at, r.hidden_turned)
        grad = dot_rows(r.right_down[own], r.w_down[pl.ds(at, tile)])
        r.right_two[own, pl.ds(at, tile)] = (
            grad * up * (part * (1.0 + gate * (1.0 - part)))
        ).astype(bf16)
        r.right_two[own, pl.ds(hid + at, tile)] = (grad * act).astype(bf16)
        quads = (at + tile) // r.hidden_turned.shape[3] // 4
        if quads > quads_sent:
            some = pl.ds(quads_sent, quads - quads_sent)
            hidden_copies.append(
                sent(
                    r.hidden_turned.at[some, 1 - mine], r.left_hidden.at[some, :, :, other],
                    r.pair_sends, r.pair_receives, 3 + len(hidden_copies), "seq", pair,
                )
            )
            quads_sent = quads
    gate_copy = sent(
        r.right_two.at[own, pl.ds(0, hid)], r.right_two.at[other, pl.ds(0, hid)], r.pair_sends,
        r.pair_receives, 1, "seq", pair,
    )
    r.left_hidden[:, :, :, own] = r.hidden_turned[:, mine]

    def store(values, target, at):
        for k in range(4):
            target[k // 2, k % 2, :, pl.ds(at, tile)] = values[k * quarter : (k + 1) * quarter]

    def two_part(index, _):
        at = pl.multiple_of(index * tile, tile)
        store(dot_rows(r.right_two[own], r.w_gate_up[pl.ds(at, tile)]).astype(bf16), r.part, at)
        return 0

    sums = [four_summed(r, (low, across, high, along), r.part, 0, k) for k in range(2)]
    for k, item in enumerate(sums):
        lax.fori_loop(k * width // (2 * tile), (k + 1) * width // (2 * tile), two_part, 0)
        next(item)
    total = in_turn(*sums)
    next(total)

    def feed_part(index, _):
        at = pl.multiple_of(index * tile, tile)
        product = jnp.dot(
            r.hidden[...], r.w_down[:, pl.ds(at, tile)], preferred_element_type=f32
        )
        store(product.astype(bf16), r.feed_part, at)
        return 0

    n_bits = len(rest_bits)
    part = width // 2
    down, down_late = (
        Unit(r.left_hidden, r.right_down, (k * part, part), r.down, r.unit_sends,
             r.unit_receives, 0, rest_bits, None)
        for k in range(2)
    )
    next(total)
    cot_other.wait()
    down.made(*hidden_copies).go()
    next(total)
    lax.fori_loop(0, width // tile, feed_part, 0)
    next(total)
    side, _ = flipped(me, rest_bits[0])
    down_late.make(1 - side, r.late_away)
    down_late.make(side, r.late_kept)
    two_copy.wait()
    two_copy = sent(target, target, r.pair_sends, r.pair_receives, 2, "ch", across)
    next(total)
    two_copy.wait()
    gate_copy.wait()
    if n_bits > 1:
        down.next(send_on=False)
    r.down_away[...] = down.away[1][...]
    kept = r.down_kept.shape[0]
    r.down_kept[...] = down.kept[0:kept]


def feed_forward(ins, hbm_ins, count, ident):
    bits = bits_of(count)
    n_bits = len(bits) - 1
    tokens, width = ins["stream"].shape
    hid = hbm_ins["w_down_in"].shape[0]
    half, quarter = count // 2, tokens // 4
    rows_in, rows_down = width // count, hid // count

    def low(*dims):
        return pltpu.VMEM(dims, bf16)

    def sems(size):
        return pltpu.SemaphoreType.DMA((size,))

    lands = [low(half >> (k + 1), rows_down, width // 2) for k in range(n_bits)]
    outs = dict(
        total=shape_of(2, 2, quarter, width, dtype=bf16),
        feed_part=shape_of(2, 2, quarter, width, dtype=bf16),
        left_two=shape_of(count // 4, 2, rows_in, 2 * tokens, dtype=bf16),
        right_two=shape_of(2 * tokens, 2 * hid, dtype=bf16),
        down_away=shape_of(half >> 2, rows_down, width // 2, dtype=bf16),
        down_kept=shape_of(half >> 2, rows_down, width // 2),
        late_away=shape_of(half >> 1, rows_down, width // 2, dtype=bf16),
        late_kept=shape_of(half >> 1, rows_down, width // 2),
    )
    scratch = dict(
        w_gate_up=low(width, 2 * hid),
        w_down=low(hid, width),
        normed=low(tokens, width),
        hidden=low(tokens, hid),
        two_turned=low(count // 4, 2, 2, rows_in, tokens),
        hidden_turned=low(count // 4, 2, 2, rows_down, tokens),
        left_hidden=low(count // 4, 2, rows_down, 2 * tokens),
        right_down=low(2 * tokens, width),
        part=low(2, 2, quarter, width),
        first_land=low(2, quarter, width),
        second_land=low(quarter, width),
        second_move=low(quarter, width),
        down=[low(half // 2, rows_down, width // 2), *lands, pltpu.VMEM((half // 2, rows_down, width // 2), f32)],
        load_sems=sems(2 + 3 * (hid // 256)),
        pair_sends=sems(7),
        pair_receives=sems(7),
        sum_sends=sems(8),
        sum_receives=sems(8),
        unit_sends=sems(n_bits),
        unit_receives=sems(n_bits),
    )
    names, shapes = [(name, 0) for name in [*ins, *hbm_ins, *outs]], []
    for name, held in scratch.items():
        listed = isinstance(held, list)
        names.append((name, len(held) if listed else 0))
        shapes += held if listed else [held]
    made = pl.pallas_call(
        functools.partial(feed_forward_kernel, bits, names),
        out_shape=list(outs.values()),
        in_specs=[VMEM] * len(ins) + [ANY] * len(hbm_ins),
        out_specs=[VMEM] * len(outs),
        scratch_shapes=shapes,
        compiler_params=pltpu.CompilerParams(
            collective_id=ident, has_side_effects=True, vmem_limit_bytes=56 * 2**20
        ),
        name="feed_forward",
    )(*ins.values(), *hbm_ins.values())
    return types.SimpleNamespace(**dict(zip(outs, made)))


def backward_kernel(bits, names, *refs):
    r = named(names, refs)
    tokens, width = r.stream.shape
    channels, rank, states = r.low.shape[1], r.w_dt.shape[0], r.logs.shape[0]
    quarter, chunks = tokens // 4, tokens // CHUNK
    ch_me, me = lax.axis_index("ch"), lax.axis_index("seq")
    seq_count = 1 << len(bits)
    low, across = flipped(ch_me, 1)
    high, along = flipped(ch_me, 2)
    pair_bit, rest_bits = bits[1], [bits[0], *bits[2:]]
    mine, pair = flipped(me, pair_bit)
    previous = lax.rem(me + seq_count - 1, seq_count)
    load_slots, pair_slots, shared_slots, write_slots = ([] for _ in range(4))

    def slot_of(slots):
        slots.append(0)
        return len(slots) - 1

    def load(source, target):
        copy = pltpu.make_async_copy(source, target, r.load_sems.at[slot_of(load_slots)])
        copy.start()
        return Once(copy)

    own, other = pl.ds(0, tokens), pl.ds(tokens, tokens)
    mixer_own = load(r.mixer_in, r.mixer)
    cot_own = load(r.cot, r.cot_rows)
    weights = load(r.w_out, r.weights)
    scan_own = load(r.scan_in, r.scan)
    out_of_own = load(r.out_of_in, r.out_of)
    into_own = load(r.into_in, r.into)
    hid = r.right_two_in.shape[1] // 2
    down_away = load(r.down_away_in, r.down[0].at[pl.ds(0, r.down_away_in.shape[0])])
    late_away = load(r.late_away_in, r.late[0])
    two_own = load(r.left_two_in, r.left_two)
    gate_up_own = load(r.right_two_in.at[own], r.right_two.at[own])
    gate_other = load(
        r.right_two_in.at[other, pl.ds(0, hid)], r.right_two.at[other, pl.ds(0, hid)]
    )
    down_kept = load(r.down_kept_in, r.down[-1].at[pl.ds(0, r.down_kept_in.shape[0])])
    late_kept = load(r.late_kept_in, r.late[-1])
    part_in = load(r.feed_part, r.part)
    one_own = load(r.one_in.at[:, mine], r.left_one.at[:, :, :, own])
    one_other = load(r.one_came, r.left_one.at[:, :, :, other])
    gated_own = load(r.gated_in.at[:, mine], r.left_gated.at[:, :, :, own])
    blocks = [slice(j, j + 128) for j in range(0, channels, 128)]
    hists = [load(r.hist_in.at[:, :, blocks[k]], r.hist.at[k]) for k in range(2)]

    greeted(
        [("ch", across), ("ch", along)]
        + [("seq", lax.rem(me + k, seq_count)) for k in range(1, seq_count)]
    )

    def swap(source, target):
        slot = slot_of(pair_slots)
        return Once(sent(source, target, r.pair_sends, r.pair_receives, slot, "seq", pair))

    def swap_shared(source, target):
        slot = 2 * slot_of(shared_slots)
        copy = sent(source, target, r.shared_sends, r.shared_receives, slot, "seq", pair)
        return Once(
            copy,
            then=lambda: sent(
                target, target, r.shared_sends, r.shared_receives, slot + 1, "ch", across
            ),
        )

    n_bits = len(rest_bits)

    def writer(target):
        def write(source):
            copy = pltpu.make_async_copy(source, target, r.write_sems.at[slot_of(write_slots)])
            copy.start()
            return copy

        return write

    def unit(left, right, columns, refs, slot, target):
        return Unit(
            left, right, columns, refs, r.unit_sends, r.unit_receives, slot * n_bits, rest_bits,
            writer(target),
        )

    part = width // 2
    down, late = (
        unit(None, None, None, refs, k, r.down_out.at[:, pl.ds(k * part, part)])
        for k, refs in enumerate((r.down, r.late))
    )
    part = hid // 2
    quarters = [
        unit(
            r.left_two, r.right_two, (k * part, part), refs, 2 + k,
            (r.gate_out, r.up_out)[k // 2].at[:, pl.ds(k % 2 * part, part)],
        )
        for k, refs in enumerate((r.gate0, r.gate1, r.up0, r.up1))
    ]
    gate0, gate1, up0, up1 = quarters
    out = unit(r.left_gated, r.right_out, (0, width), r.out, 6, r.out_out)
    gin = unit(r.left_one, r.right_in, (channels, channels), r.gin, 7, r.gin_out)
    part = channels // 2
    cins = [
        unit(
            r.left_one, r.right_in, (k * part, part), refs, 8 + k,
            r.cin_out.at[:, pl.ds(k * part, part)],
        )
        for k, refs in enumerate((r.cin0, r.cin1))
    ]

    up_other = swap(
        r.right_two_in.at[own, pl.ds(hid, hid)], r.right_two.at[other, pl.ds(hid, hid)]
    )
    down_away.wait()
    down.resume()
    late_away.wait()
    late.begun()

    summed = functools.partial(four_summed, r, (low, across, high, along))


    rates = -jnp.exp(r.logs[...]) * LOG2E

    def places_of(first, count):
        return me * tokens + first + lax.broadcasted_iota(jnp.int32, (count, 128), 0)

    def resteps():
        def body(index, total):
            first = pl.multiple_of(index * CHUNK, CHUNK)
            rows = pl.ds(first, CHUNK)
            size = softplus(r.step_pre[rows])
            r.drive[rows] = size * r.low[rows].astype(f32)
            places = places_of(first, CHUNK)
            resets = jnp.where((places == r.bounds[0]) | (places == r.bounds[1]), RESET, 0.0)
            size = size + widened(resets, channels)
            r.step[rows] = size
            return total + jnp.sum(size, axis=0, keepdims=True)

        r.step_sum[...] = jnp.broadcast_to(
            lax.fori_loop(0, chunks, body, jnp.zeros((1, channels), f32)), (8, channels)
        )

    resteps()
    mixer_own.wait()
    cot_own.wait()

    def quarter_rows(index):
        per = quarter // CHUNK
        part = lax.div(index, per)
        at = pl.ds(pl.multiple_of(lax.rem(index, per) * CHUNK, CHUNK), CHUNK)
        return lax.div(part, 2), lax.rem(part, 2), at

    def norm_two(index, total):
        first = pl.multiple_of(index * CHUNK, CHUNK)
        rows = pl.ds(first, CHUNK)
        a, b, at = quarter_rows(index)
        middle = r.stream[rows].astype(f32) + r.mixer[a, b, at].astype(f32)
        scale = lax.rsqrt(mean_square(middle) + 1e-06)
        back, gain = norm_back(middle, scale, r.gains[1:2], r.two_total[a, b, at].astype(f32))
        grad = r.cot_rows[rows].astype(f32) + back
        r.stream_grad[rows] = grad
        r.right_out[rows] = grad.astype(bf16)
        return total + jnp.sum(gain, axis=0, keepdims=True)

    gain_two = lax.fori_loop(0, chunks, norm_two, jnp.zeros((1, width), f32))
    r.flat_move[0] = jnp.zeros_like(r.flat_move[0])
    r.flat_move[0, 1:2] = gain_two
    weights.wait()
    scan_own.wait()
    skips = []
    for j in range(0, channels, 256):
        lanes = slice(j, j + 256)
        gated_grad = dot_rows(r.right_out[own], r.weights[pl.ds(j, 256)])
        gate_pre = r.proj[:, channels + j : channels + j + 256].astype(f32)
        part = sigmoid(gate_pre)
        slope = part * (1.0 + gate_pre * (1.0 - part))
        r.right_in[own, channels + j : channels + j + 256] = (
            gated_grad * r.scan[:, lanes] * slope
        ).astype(bf16)
        grad = gated_grad * gate_pre * part
        r.scan[:, lanes] = grad
        skips.append(jnp.sum(grad * r.low[:, lanes].astype(f32), axis=0, keepdims=True))
    skip_grad = jnp.concatenate(skips, 1)
    weights = load(r.w_in.at[pl.ds(0, channels)], r.weights)
    out_of_own.wait()
    for j in range(0, channels, LANES):
        lanes = slice(j, j + LANES)

        def ended(index, carried, lanes=lanes, block_rates=rates[:, j : j + LANES]):
            first = pl.multiple_of(tokens - UNROLL - index * UNROLL, UNROLL)
            steps, grads = r.step[pl.ds(first, UNROLL), lanes], r.scan[pl.ds(first, UNROLL), lanes]
            for k in reversed(range(UNROLL)):
                decay = jnp.exp2(steps[k : k + 1] * block_rates)
                carried = decay * (widened(r.out_of[first + k], LANES) * grads[k : k + 1] + carried)
            return carried

        r.starts[:, lanes] = lax.fori_loop(
            0, tokens // UNROLL, ended, jnp.zeros((states, LANES), f32)
        )

    chain = handed_on(False, r.starts[...], r.step_sum[0:1], rates, r)
    next(chain)
    gate0.made(two_own, gate_up_own, gate_other)
    gate1.made()
    r.starts[...] = next(chain)
    gate0.go()
    late_kept.wait()
    late.next()
    gate1.go()
    up0.made(up_other)
    first = pl.multiple_of(low * (tokens // 2), tokens // 2)
    mixer_other = swap_shared(
        r.right_out.at[pl.ds(first, tokens // 2)],
        r.right_out.at[pl.ds(tokens + first, tokens // 2)],
    )
    gated_other = swap(r.gated_in.at[:, 1 - mine], r.left_gated.at[:, :, :, other])
    gin_other = swap(
        r.right_in.at[own, pl.ds(channels, channels)],
        r.right_in.at[other, pl.ds(channels, channels)],
    )
    up0.go()
    up1.made().go()

    part_in.wait()
    feed_sums = [summed(r.part, 0, k) for k in range(2)]
    into_own.wait()

    def results():
        totals = lax.fori_loop(
            0, chunks, results_of, tuple(jnp.zeros((1, width), f32) for _ in range(3))
        )
        for number, total in enumerate(totals):
            r.flat_move[0, 3 + number : 4 + number] = total

    def feed_start():
        for item in feed_sums:
            next(item)
        return in_turn(*feed_sums)

    feed = []
    between = [
        lambda: (feed.append(feed_start()), next(feed[0]), gate0.next()),
        lambda: next(feed[0]),
        lambda: (next(feed[0]), gate1.next()),
        lambda: next(feed[0]),
        lambda: (next(feed[0]), up0.next()),
        lambda: (results(), out.made(gated_own, mixer_other, gated_other).go()),
    ]

    def results_of(index, totals):
        rows = pl.ds(pl.multiple_of(index * CHUNK, CHUNK), CHUNK)
        a, b, at = quarter_rows(index)
        mixed, feed = r.mixer[a, b, at].astype(f32), r.total[a, b, at].astype(f32)
        result = r.stream[rows].astype(f32) + mixed + feed
        r.out_rows[rows] = result.astype(bf16)
        return tuple(
            total + jnp.sum(v * v, axis=0, keepdims=True)
            for total, v in zip(totals, (result, mixed, feed))
        )

    r.into_wide[...] = jnp.zeros_like(r.into_wide)
    r.out_wide[...] = jnp.zeros_like(r.out_wide)
    for number, lanes in enumerate(blocks):
        hists[number].wait()
        hist = r.hist.at[number % 2]
        block_rates = rates[:, lanes]

        def walked(index, carry, lanes=lanes, block_rates=block_rates, hist=hist):
            carried, state, total = carry
            first = pl.multiple_of(tokens - UNROLL - index * UNROLL, UNROLL)
            some = pl.ds(first, UNROLL)
            steps, drives, grads = r.step[some, lanes], r.drive[some, lanes], r.scan[some, lanes]
            decay_list, push_list = [None] * UNROLL, [None] * UNROLL
            for k in reversed(range(UNROLL)):
                place = first + k
                grad_row = grads[k : k + 1]
                decay = jnp.exp2(steps[k : k + 1] * block_rates)
                adjoint = r.out_of[place] * grad_row + carried
                carried = decay * adjoint
                r.out_wide[place] = r.out_wide[place] + state * grad_row
                r.into_wide[place] = r.into_wide[place] + adjoint * drives[k : k + 1]
                state = hist[place]
                share = carried * state
                total = total + share * steps[k : k + 1]
                decay_list[k] = jnp.sum(share * block_rates, axis=0, keepdims=True)
                push_list[k] = jnp.sum(r.into[place] * adjoint, axis=0, keepdims=True)
            r.decay_rows[some, :] = jnp.concatenate(decay_list, 0)
            r.push[some, lanes] = jnp.concatenate(push_list, 0)
            return (carried, state, total)

        _, _, total = lax.fori_loop(
            0,
            tokens // UNROLL,
            walked,
            (r.starts[:, lanes], r.last_state[:, lanes], jnp.zeros((states, 128), f32)),
        )
        r.rate_sum[:, lanes] = total * (rates[:, lanes] * LN2)

        def gathered(index, _, lanes=lanes):
            rows = pl.ds(pl.multiple_of(index * CHUNK, CHUNK), CHUNK)
            used, pushed = r.low[rows, lanes].astype(f32), r.push[rows, lanes]
            pre = r.step_pre[rows, lanes]
            grad = (LN2 * r.decay_rows[rows] + pushed * used) * sigmoid(pre)
            r.step_low_grad[rows, lanes] = grad.astype(bf16)
            r.push[rows, lanes] = pushed * softplus(pre) + r.chan[6:7, lanes] * r.scan[rows, lanes]
            return 0

        lax.fori_loop(0, chunks, gathered, 0)
        if number + 2 < len(blocks):
            hists.append(load(r.hist_in.at[:, :, blocks[number + 2]], r.hist.at[number % 2]))
        if number < len(between):
            between[number]()
    for later in between[len(blocks) :]:
        later()

    def norm_grads(index, _):
        first = pl.multiple_of(index * CHUNK, CHUNK)
        rows = pl.ds(first, CHUNK)
        low_part = dot_rows(r.step_low_grad[rows], r.w_dt[...])
        r.raw_move[0, rows] = jnp.concatenate(
            [low_part, narrowed(r.into_wide, first, CHUNK), narrowed(r.out_wide, first, CHUNK)], 1
        )
        return 0

    lax.fori_loop(0, chunks, norm_grads, 0)
    copy = sent(r.raw_move.at[0], r.raw_land.at[0], r.raw_sends, r.raw_receives, 0, "ch", across)
    gin.made(one_own, one_other, gin_other)
    copy.wait()
    r.raw_move[1] = r.raw_move[0] + r.raw_land[0]
    copy = sent(r.raw_move.at[1], r.raw_land.at[1], r.raw_sends, r.raw_receives, 1, "ch", along)
    up1.next()
    copy.wait()

    def raw_back(index, total):
        rows = pl.ds(pl.multiple_of(index * CHUNK, CHUNK), CHUNK)
        grads, raw = r.raw_move[1, rows] + r.raw_land[1, rows], r.raw[rows]
        gains = r.small_gains[...]
        values, sums_to = [], []
        for start, stop, floor in ((0, rank, None), (rank, rank + states, 0.1),
                                   (rank + states, rank + 2 * states, 0.1)):
            value = raw[:, start:stop]
            square = mean_square(value)
            if floor is None:
                scale, free = lax.rsqrt(square + 1e-06), True
            else:
                scale, free = lax.rsqrt(jnp.maximum(square, floor)), square > floor
            back, gain = norm_back(value, scale, gains[:, start:stop], grads[:, start:stop], free)
            values.append(back)
            sums_to.append(jnp.sum(gain, axis=0, keepdims=True))
        norm = raw[:, :rank] * lax.rsqrt(mean_square(raw[:, :rank]) + 1e-06) * gains[:, :rank]
        r.raw_low[rows] = jnp.concatenate(values, 1).astype(bf16)
        r.step_low[rows] = norm.astype(bf16)
        return total + jnp.concatenate(sums_to, 1)

    small = lax.fori_loop(0, chunks, raw_back, jnp.zeros((1, rank + 2 * states), f32))
    r.flat_move[0, 2:3, : rank + 2 * states] = small

    def conv_back(index, total):
        first = pl.multiple_of(index * CHUNK, CHUNK)
        rows = pl.ds(first, CHUNK)
        grad = r.push[rows] + dot_rows(r.raw_low[rows], r.w_x[...])
        grad = grad * silu_slope(r.pre[rows])
        r.grad_pre[rows] = grad
        return total + jnp.sum(grad, axis=0, keepdims=True)

    tap_bias = lax.fori_loop(0, chunks, conv_back, jnp.zeros((1, channels), f32))
    copy = sent(r.grad_pre.at[pl.ds(0, 8)], r.grad_pre.at[pl.ds(tokens, 8)], r.raw_sends,
                r.raw_receives, 2, "seq", previous)
    gin.go()
    r.extended[0:16] = r.halo[...].astype(f32)

    def extend(index, _):
        first = pl.multiple_of(index * CHUNK, CHUNK)
        r.extended[pl.ds(first + 16, CHUNK)] = r.proj[pl.ds(first, CHUNK), :channels].astype(f32)
        return 0

    lax.fori_loop(0, chunks, extend, 0)

    def taps(index, totals):
        first = pl.multiple_of(index * CHUNK, CHUNK)
        places = places_of(first, CHUNK)
        window = r.extended[pl.ds(first, CHUNK + 16)]
        grad = r.grad_pre[pl.ds(first, CHUNK)]
        return tuple(
            totals[k]
            + jnp.sum(
                grad
                * widened(tap_mask(places, r.bounds, 3 - k), channels)
                * window[13 + k : 13 + k + CHUNK],
                axis=0,
                keepdims=True,
            )
            for k in range(4)
        )

    tap_grads = lax.fori_loop(
        0, chunks, taps, tuple(jnp.zeros((1, channels), f32) for _ in range(4))
    )
    copy.wait()

    def conv_in_back(index, _):
        first = pl.multiple_of(index * CHUNK, CHUNK)
        window = r.grad_pre[pl.ds(first, CHUNK + 8)]
        grad = jnp.zeros((CHUNK, channels), f32)
        for k in range(4):
            places = places_of(first + 3 - k, CHUNK)
            mask = jnp.where(
                places < seq_count * tokens, tap_mask(places, r.bounds, 3 - k), 0.0
            )
            grad = grad + r.chan[k : k + 1] * widened(mask, channels) * window[3 - k : 3 - k + CHUNK]
        r.right_in[pl.ds(first, CHUNK), :channels] = grad.astype(bf16)
        return 0

    lax.fori_loop(0, chunks, conv_in_back, 0)
    cin_others = [
        swap(
            r.right_in.at[own, pl.ds(*item.columns)], r.right_in.at[other, pl.ds(*item.columns)]
        )
        for item in cins
    ]

    def small_columns():
        narrow = r.w_x.shape[1]
        pack = r.step
        pack[0:narrow] = lax.dot_general(
            r.raw_low[...], r.low[...], (((0,), (0,)), ((), ())), preferred_element_type=f32
        )
        pack[narrow : narrow + rank] = lax.dot_general(
            r.step_low[...], r.step_low_grad[...], (((0,), (0,)), ((), ())),
            preferred_element_type=f32,
        )
        at = narrow + rank
        pack[at : at + states] = r.rate_sum[...]
        at += states
        bias = jnp.sum(r.step_low_grad[...].astype(f32), axis=0, keepdims=True)
        pack[at : at + 8] = jnp.concatenate(
            [*tap_grads, tap_bias, bias, skip_grad, jnp.zeros((1, channels), f32)], 0
        )
        at += 8
        pack[at:] = jnp.zeros((pack.shape[0] - at, channels), f32)
        turned = pack[...].T
        r.small_work[0][...] = turned.reshape(r.small_work[0].shape)

    def small_summed():
        for k, bit in enumerate(bits):
            side, partner = flipped(me, bit)
            work, away, land = r.small_work[k], r.small_away[k], r.small_land[k]
            away[...] = work[:, 1 - side].astype(bf16)
            copy = sent(away, land, r.last_sends, r.last_receives, k, "seq", partner)
            yield
            copy.wait()
            total = work[:, side] + land[...].astype(f32)
            target = r.small_work[k + 1] if k + 1 < len(bits) else r.small_out
            target[...] = total.reshape(target.shape)
        yield

    one_sums = [summed(r.part, 8, k) for k in range(2)]
    for number in range(width // channels):
        weights.wait()

        def one_part(index, _, first=number * channels):
            at = pl.multiple_of(index * 256, 256)
            product = dot_rows(r.right_in[own], r.weights[pl.ds(at, 256)]).astype(bf16)
            for k in range(4):
                r.part[k // 2, k % 2, :, pl.ds(first + at, 256)] = product[
                    k * quarter : (k + 1) * quarter
                ]
            return 0

        lax.fori_loop(0, channels // 256, one_part, 0)
        next(one_sums[number])
        if (number + 1) * channels < width:
            weights = load(r.w_in.at[pl.ds((number + 1) * channels, channels)], r.weights)
    one_sum = in_turn(*one_sums)
    next(one_sum)

    def gain_part(index, total):
        rows = pl.ds(pl.multiple_of(index * CHUNK, CHUNK), CHUNK)
        a, b, at = quarter_rows(index)
        value = r.stream[rows].astype(f32)
        scale = lax.rsqrt(mean_square(value) + 1e-06)
        return total + jnp.sum(r.part[a, b, at].astype(f32) * value * scale, axis=0, keepdims=True)

    r.flat_move[0] = r.flat_move[0] * 0.25
    r.flat_move[0, 0:1] = lax.fori_loop(0, chunks, gain_part, jnp.zeros((1, width), f32))
    ways = [("ch", across), ("ch", along)] + [("seq", flipped(me, bit)[1]) for bit in bits]

    def flat_summed():
        for k, (axis, partner) in enumerate(ways):
            copy = sent(r.flat_move.at[k], r.flat_land.at[k], r.flat_sends, r.flat_receives, k,
                        axis, partner)
            yield
            copy.wait()
            target = r.flat_move.at[k + 1] if k + 1 < len(ways) else r.flat_out
            target[...] = r.flat_move[k] + r.flat_land[k]
        yield

    flat_sum = flat_summed()
    next(flat_sum)

    cins[0].made(cin_others[0]).go()
    next(one_sum)
    next(flat_sum)
    out.next()
    cins[1].made(cin_others[1]).go()
    next(one_sum)
    next(flat_sum)
    small_columns()
    small_sum = small_summed()
    next(small_sum)
    next(one_sum)
    gin.next()
    next(flat_sum)
    next(one_sum)

    def norm_one(index, _):
        rows = pl.ds(pl.multiple_of(index * CHUNK, CHUNK), CHUNK)
        a, b, at = quarter_rows(index)
        value = r.stream[rows].astype(f32)
        scale = lax.rsqrt(mean_square(value) + 1e-06)
        back, _ = norm_back(value, scale, r.gains[0:1], r.total[a, b, at].astype(f32))
        r.stream_grad[rows] = r.stream_grad[rows] + back
        return 0

    lax.fori_loop(0, chunks, norm_one, 0)
    cins[0].next()
    next(small_sum)
    next(flat_sum)
    cins[1].next()
    down_kept.wait()
    for item in (down, late, *quarters):
        item.next()
    next(small_sum)
    for waiting in (flat_sum, small_sum):
        for _ in waiting:
            pass
    pending = [out, gin, *cins, down, late, *quarters]
    for _ in range(len(bits)):
        for item in pending:
            item.next()
    for item in pending:
        item.written.wait()


def backward(ins, hbm_ins, count, ident):
    bits = bits_of(count)
    n_bits = len(bits) - 1
    tokens, width = ins["stream"].shape
    channels, rank, states = ins["low"].shape[1], ins["w_dt"].shape[0], ins["logs"].shape[0]
    hid = hbm_ins["right_two_in"].shape[1] // 2
    narrow = ins["w_x"].shape[1]
    half, quarter = count // 2, tokens // 4
    rows_in, rows_out, rows_down = width // count, channels // count, hid // count
    rows = pltpu.VMEM((tokens, channels), f32)

    def low(*dims):
        return pltpu.VMEM(dims, bf16)

    def full(*dims):
        return pltpu.VMEM(dims, f32)

    outs = dict(
        stream_grad=(shape_of(tokens, width), VMEM),
        out_rows=(shape_of(tokens, width, dtype=bf16), VMEM),
        small_out=(shape_of(rows_out, tokens), VMEM),
        flat_out=(shape_of(8, width), VMEM),
        down_out=(shape_of(rows_down, width), ANY),
        gate_out=(shape_of(rows_in, hid), ANY),
        up_out=(shape_of(rows_in, hid), ANY),
        out_out=(shape_of(rows_out, width), ANY),
        gin_out=(shape_of(rows_in, channels), ANY),
        cin_out=(shape_of(rows_in, channels), ANY),
    )
    quads = count // 4

    def unit(part, columns):
        lands = [low(half >> (k + 1), part, columns) for k in range(n_bits)]
        return [low(half // 2, part, columns), *lands, full(half // 2, part, columns)]

    def sems(size):
        return pltpu.SemaphoreType.DMA((size,))

    halves = [count >> (k + 1) for k in range(len(bits))]
    scratch = dict(
        left_two=low(quads, 2, rows_in, 2 * tokens),
        left_one=low(quads, 2, rows_in, 2 * tokens),
        left_gated=low(quads, 2, rows_out, 2 * tokens),
        cot_rows=low(tokens, width),
        right_two=low(2 * tokens, 2 * hid),
        right_out=low(2 * tokens, width),
        right_in=low(2 * tokens, 2 * channels),
        mixer=low(2, 2, quarter, width),
        weights=low(channels, width),
        scan=rows,
        step=rows,
        drive=rows,
        push=rows,
        decay_rows=full(tokens, 128),
        into=full(tokens, states, 128),
        out_of=full(tokens, states, 128),
        into_wide=full(tokens, states, 128),
        out_wide=full(tokens, states, 128),
        hist=full(2, tokens, states, 128),
        step_sum=full(8, channels),
        starts=full(states, channels),
        rate_sum=full(states, channels),
        step_low_grad=low(tokens, channels),
        **handing(count, states, channels),
        part=low(2, 2, quarter, width),
        total=low(2, 2, quarter, width),
        first_land=low(2, quarter, width),
        second_land=low(quarter, width),
        second_move=low(quarter, width),
        raw_move=full(2, tokens, narrow),
        raw_land=full(2, tokens, narrow),
        raw_low=low(tokens, narrow),
        step_low=low(tokens, rank),
        grad_pre=full(tokens + 8, channels),
        extended=full(tokens + 16, channels),
        flat_move=full(2 + len(bits), 8, width),
        flat_land=full(2 + len(bits), 8, width),
        small_work=[full(size, 2, rows_out, tokens) for size in halves],
        small_away=[low(size, rows_out, tokens) for size in halves],
        small_land=[low(size, rows_out, tokens) for size in halves],
        down=unit(rows_down, width // 2),
        late=unit(rows_down, width // 2),
        gate0=unit(rows_in, hid // 2),
        gate1=unit(rows_in, hid // 2),
        up0=unit(rows_in, hid // 2),
        up1=unit(rows_in, hid // 2),
        out=unit(rows_out, width),
        gin=unit(rows_in, channels),
        cin0=unit(rows_in, channels // 2),
        cin1=unit(rows_in, channels // 2),
        load_sems=sems(32),
        write_sems=sems(10),
        pair_sends=sems(8),
        pair_receives=sems(8),
        shared_sends=sems(4),
        shared_receives=sems(4),
        unit_sends=sems(10 * n_bits),
        unit_receives=sems(10 * n_bits),
        sum_sends=sems(16),
        sum_receives=sems(16),
        raw_sends=sems(3),
        raw_receives=sems(3),
        last_sends=sems(len(bits)),
        last_receives=sems(len(bits)),
        flat_sends=sems(2 + len(bits)),
        flat_receives=sems(2 + len(bits)),
    )
    names, shapes = [(name, 0) for name in [*ins, *hbm_ins, *outs]], []
    for name, held in scratch.items():
        listed = isinstance(held, list)
        names.append((name, len(held) if listed else 0))
        shapes += held if listed else [held]
    places = [VMEM for _ in ins]
    places[0] = pl.BlockSpec(memory_space=pltpu.SMEM)
    made = pl.pallas_call(
        functools.partial(backward_kernel, bits, names),
        out_shape=[shape for shape, _ in outs.values()],
        in_specs=places + [ANY] * len(hbm_ins),
        out_specs=[spec for _, spec in outs.values()],
        scratch_shapes=shapes,
        compiler_params=pltpu.CompilerParams(
            collective_id=ident, has_side_effects=True, vmem_limit_bytes=63 * 2**20
        ),
        name="block_backward",
    )(*ins.values(), *hbm_ins.values())
    return types.SimpleNamespace(**dict(zip(outs, made)))


def rms_gain(values, gain_row):
    return values * lax.rsqrt(jnp.mean(values * values, axis=-1, keepdims=True) + 1e-06) * gain_row


def local(
    seq_count,
    stream,
    doc_bounds,
    norm_gains,
    w_in,
    chan_vectors,
    decay_logs,
    w_x,
    small_gains,
    w_dt,
    w_out,
    w_gate_up,
    w_down,
    cotangent,
):
    tokens, width = stream.shape
    rank, (states, channels) = w_dt.shape[0], decay_logs.shape

    def turned(values):
        return values.T.reshape(seq_count // 4, 2, 2, values.shape[1] // seq_count, tokens)

    stream_in = stream.astype(f32)
    normed_low = rms_gain(stream_in, norm_gains[0]).astype(bf16)
    w_in_flat = w_in.reshape(width, 2 * channels)
    in_proj = jnp.dot(normed_low, w_in_flat, preferred_element_type=f32).astype(bf16)
    one_in = turned(normed_low)
    (
        halo, pre_conv, conv_low, raw_proj, step_pre, into, out_of, scan_out, gated_low,
        last_state, mixer_low, before, one_came, cot_came,
    ) = mixer_forward(
        doc_bounds, in_proj, chan_vectors, decay_logs, w_x, small_gains[None], w_dt, w_out,
        one_in, cotangent, seq_count, 1,
    )
    mid = feed_forward(
        dict(stream=stream, mixer=mixer_low, gains=norm_gains),
        dict(
            cot=cotangent, cot_came=cot_came, w_gate_up_in=w_gate_up.reshape(width, -1),
            w_down_in=w_down,
        ),
        seq_count,
        3,
    )
    made = backward(
        dict(
            bounds=doc_bounds, stream=stream, gains=norm_gains, two_total=mid.total,
            proj=in_proj, halo=halo,
            pre=pre_conv, low=conv_low, raw=raw_proj, step_pre=step_pre, last_state=last_state,
            chan=chan_vectors, logs=decay_logs, w_x=w_x, w_dt=w_dt, small_gains=small_gains[None],
        ),
        dict(
            feed_part=mid.feed_part, left_two_in=mid.left_two, right_two_in=mid.right_two,
            down_away_in=mid.down_away, down_kept_in=mid.down_kept,
            late_away_in=mid.late_away, late_kept_in=mid.late_kept, mixer_in=mixer_low,
            cot=cotangent, gated_in=turned(gated_low), one_in=one_in,
            one_came=one_came, w_out=w_out, w_in=w_in_flat, scan_in=scan_out, into_in=into,
            out_of_in=out_of, hist_in=before,
        ),
        seq_count,
        2,
    )
    small, flat = made.small_out, made.flat_out
    at = w_x.shape[1]
    x_part, small = small[:, :at], small[:, at:].T
    dt_part, decay_out = small[:rank], small[rank : rank + states]
    chan_part = small[rank + states : rank + states + 7]
    me = lax.axis_index("seq")
    gain_width = width // seq_count
    gains_part = lax.dynamic_slice_in_dim(flat[:2], me * gain_width, gain_width, 1)
    small_width = small_gains.shape[0] // seq_count
    small_part = lax.dynamic_slice_in_dim(flat[2], me * small_width, small_width, 0)
    rms_values = jnp.sqrt(jnp.sum(flat[3:6], axis=1) / (tokens * seq_count * width))
    return (
        made.out_rows,
        made.stream_grad,
        gains_part,
        jnp.stack([made.cin_out, made.gin_out], 1),
        chan_part,
        decay_out,
        x_part,
        small_part,
        dt_part,
        made.out_out,
        jnp.stack([made.gate_out, made.up_out], 1),
        made.down_out,
        rms_values,
    )


def solution(mesh):
    in_specs = (
        P("seq", None),
        P(),
        P(),
        P(None, None, "ch"),
        P(None, "ch"),
        P(None, "ch"),
        P("ch", None),
        P(),
        P(None, "ch"),
        P("ch", None),
        P(None, None, "ch"),
        P("ch", None),
        P("seq", None),
    )
    out_specs = (
        P("seq", None),
        P("seq", None),
        P(None, "seq"),
        P("seq", None, "ch"),
        P(None, ("ch", "seq")),
        P(None, ("ch", "seq")),
        P(("ch", "seq"), None),
        P("seq"),
        P(None, ("ch", "seq")),
        P(("ch", "seq"), None),
        P("seq", None, "ch"),
        P(("ch", "seq"), None),
        P(),
    )
    return jax.shard_map(
        functools.partial(local, mesh.shape["seq"]),
        mesh=mesh,
        in_specs=in_specs,
        out_specs=out_specs,
        check_vma=False,
    )
```

```python
import functools
import math
import types

import jax
import jax.numpy as jnp
from jax import lax
from jax.experimental import pallas as pl
from jax.experimental.pallas import tpu as pltpu
from jax.sharding import PartitionSpec as P

f32 = jnp.float32
bf16 = jnp.bfloat16
LOG2E = math.log2(math.e)
LN2 = math.log(2.0)
RESET = 1e30
UNROLL = 8
LANES = 256
VMEM = pl.BlockSpec(memory_space=pltpu.VMEM)


def shape_of(*dims, dtype=f32):
    return jax.ShapeDtypeStruct(dims, dtype)


def cost(us):
    return pl.CostEstimate(flops=int(us * 1e9), bytes_accessed=int(us * 1e6), transcendentals=0)


def widened(column, width):
    return jnp.concatenate([column] * (width // 128), 1)


ANY = pl.BlockSpec(memory_space=pl.ANY)


def sent(source, target, sends, receives, slot, axis, partner):
    copy = pltpu.make_async_remote_copy(
        src_ref=source,
        dst_ref=target,
        send_sem=sends.at[slot],
        recv_sem=receives.at[slot],
        device_id={axis: partner},
        device_id_type=pl.DeviceIdType.MESH,
    )
    copy.start()
    return copy


def bits_of(count):
    return [1 << k for k in range(count.bit_length() - 1)]


def flipped(me, bit):
    mine = lax.rem(me // bit, 2)
    return mine, me + bit - 2 * bit * mine


CHUNK = 32


def sigmoid(values):
    return 1.0 / (1.0 + jnp.exp(-values))


def softplus(values):
    return jnp.maximum(values, 0.0) + jnp.log1p(jnp.exp(-jnp.abs(values)))


def row_doc(places, bounds):
    return (places >= bounds[0]).astype(jnp.int32) + (places >= bounds[1]).astype(jnp.int32)


def tap_mask(places, bounds, offset):
    source = places - offset
    same = row_doc(source, bounds) == row_doc(places, bounds)
    return jnp.where((source >= 0) & same, 1.0, 0.0)


def mean_square(values):
    return jnp.mean(values * values, axis=-1, keepdims=True)


def three_norms(raw, gains, rank, states):
    low, mid, high = raw[:, :rank], raw[:, rank : rank + states], raw[:, rank + states :]
    low_scale = lax.rsqrt(mean_square(low) + 1e-06)
    mid_scale = lax.rsqrt(jnp.maximum(mean_square(mid), 0.1))
    high_scale = lax.rsqrt(jnp.maximum(mean_square(high), 0.1))
    return (
        low * low_scale * gains[:, :rank],
        mid * mid_scale * gains[:, rank : rank + states],
        high * high_scale * gains[:, rank + states :],
    )


def widen(values, wide, first, count):
    states = values.shape[1]
    eye = (
        lax.broadcasted_iota(jnp.int32, (states, states), 0)
        == lax.broadcasted_iota(jnp.int32, (states, states), 1)
    ).astype(f32)
    spread = jnp.sum(values[:, None, :] * eye[None], axis=-1, keepdims=True)
    wide[pl.ds(first, count)] = jnp.broadcast_to(spread, (count, states, 128))


def greeted(axis_partners):
    barrier = pltpu.get_barrier_semaphore()
    for axis, partner in axis_partners:
        pl.semaphore_signal(
            barrier, inc=1, device_id={axis: partner}, device_id_type=pl.DeviceIdType.MESH
        )
    pl.semaphore_wait(barrier, len(axis_partners))


def handed_on(forward, state, steps, rates, r):
    me, count = lax.axis_index("seq"), r.state_land.shape[0] + 1
    r.state_move[...] = state.astype(bf16)
    r.steps_move[...] = steps
    copies = []
    for k in range(1, count):
        to = lax.rem(me + k, count)
        for source, land, sends, receives in (
            (r.state_move, r.state_land, r.state_sends, r.state_receives),
            (r.steps_move, r.steps_land, r.steps_sends, r.steps_receives),
        ):
            copies.append(sent(source, land.at[k - 1], sends, receives, k - 1, "seq", to))
    yield
    for copy in copies:
        copy.wait()
    total = jnp.zeros_like(state)
    passed = jnp.zeros_like(steps)
    for k in range(1, count):
        slot = k - 1 if forward else count - k - 1
        valid = (me >= k) if forward else (me + k < count)
        term = jnp.exp2(rates * passed) * r.state_land[slot].astype(f32)
        total = total + jnp.where(valid, term, 0.0)
        passed = passed + jnp.where(valid, r.steps_land[slot], 0.0)
    yield total


def handing(count, states, channels):
    sems = pltpu.SemaphoreType.DMA((count - 1,))
    return dict(
        state_move=pltpu.VMEM((states, channels), bf16),
        steps_move=pltpu.VMEM((1, channels), f32),
        state_land=pltpu.VMEM((count - 1, states, channels), bf16),
        steps_land=pltpu.VMEM((count - 1, 1, channels), f32),
        state_sends=sems,
        state_receives=sems,
        steps_sends=sems,
        steps_receives=sems,
    )


def turn(values, first, turned):
    rows = turned.shape[3]
    across_rows = values.T
    for k in range(values.shape[1] // rows):
        owner = first // rows + k
        turned[owner // 4, (owner // 2) % 2, owner % 2] = across_rows[k * rows : (k + 1) * rows]


def forward_kernel(
    bits, bounds, stream, norm_gains, chan, logs, w_x, gains, w_dt, w_out, w_in, cot,
    proj, one_in, halo, pre_out, low_out, raw_out, step_pre_out, into, out_of, scan_out, gated_out, last_state,
    mixer, hist_out, one_came, cot_came,
    extended, raw_move, raw_land, step, drive, starts, part, first_land,
    second_move, second_land, hist, sends, receives, hist_sem, shared_sends, shared_receives,
    sum_sends, sum_receives, weights, normed, weight_sem, *handed,
):
    tokens, channels = low_out.shape
    rank, states = w_dt.shape[0], logs.shape[0]
    chunks = tokens // CHUNK
    width = stream.shape[1]
    loads = []
    for k in range(width // 512):
        cols = pl.ds(k * 512, 512)
        copy = pltpu.make_async_copy(w_in.at[:, cols], weights.at[:, cols], weight_sem.at[k])
        copy.start()
        loads.append(copy)
    ch_me, me = lax.axis_index("ch"), lax.axis_index("seq")
    seq_count = 1 << len(bits)
    low, across = flipped(ch_me, 1)
    high, along = flipped(ch_me, 2)
    following = lax.rem(me + 1, seq_count)
    greeted(
        [("ch", across), ("ch", along)]
        + [("seq", lax.rem(me + k, seq_count)) for k in range(1, seq_count)]
    )
    def norm_one(index, _):
        rows = pl.ds(pl.multiple_of(index * CHUNK, CHUNK), CHUNK)
        value = stream[rows].astype(f32)
        scale = lax.rsqrt(mean_square(value) + 1e-06)
        normed[rows] = (value * scale * norm_gains[0:1]).astype(bf16)
        return 0

    lax.fori_loop(0, chunks, norm_one, 0)

    def project(index, _):
        cols = pl.ds(pl.multiple_of(index * 256, 256), 256)
        proj[:, cols] = jnp.dot(
            normed[...], weights[:, cols], preferred_element_type=f32
        ).astype(bf16)
        return 0

    for copy in loads:
        copy.wait()
    lax.fori_loop(0, channels // 256, project, 0)
    halo_copy = sent(
        proj.at[pl.ds(tokens - 16, 16), pl.ds(0, channels)], halo, sends, receives, 0, "seq",
        following,
    )
    for at in range(0, width, 384):
        turn(normed[:, at : at + 384], at, one_in)
    mine, pair = flipped(me, bits[1])
    half = one_in.shape[0] // 2
    some = pl.ds(low * half, half)
    at = pl.ds(pl.multiple_of(low * (tokens // 2), tokens // 2), tokens // 2)
    shared = [
        (one_in.at[some, 1 - mine], one_came.at[some]),
        (cot.at[at], cot_came.at[at]),
    ]
    shared_copies = [
        sent(source, target, shared_sends, shared_receives, k, "seq", pair)
        for k, (source, target) in enumerate(shared)
    ]
    lax.fori_loop(channels // 256, 2 * channels // 256, project, 0)
    rates = -jnp.exp(logs[...]) * LOG2E

    def spread(index, _):
        first = pl.multiple_of(index * CHUNK, CHUNK)
        extended[pl.ds(first + 16, CHUNK)] = proj[pl.ds(first, CHUNK), :channels].astype(f32)
        return 0

    lax.fori_loop(0, chunks, spread, 0)

    def convolved(index, _):
        first = pl.multiple_of(index * CHUNK, CHUNK)
        places = me * tokens + first + lax.broadcasted_iota(jnp.int32, (CHUNK, 128), 0)
        window = extended[pl.ds(first, CHUNK + 16)]
        summed = chan[4:5]
        for k in range(4):
            mask = widened(tap_mask(places, bounds, 3 - k), channels)
            summed = summed + chan[k : k + 1] * window[13 + k : 13 + k + CHUNK] * mask
        pre_out[pl.ds(first, CHUNK)] = summed
        low_out[pl.ds(first, CHUNK)] = (summed * sigmoid(summed)).astype(bf16)
        return 0

    lax.fori_loop(1, chunks, convolved, 0)
    halo_copy.wait()
    extended[0:16] = halo[...].astype(f32)
    convolved(0, 0)
    raw_move[0] = jnp.dot(low_out[...], w_x[...], preferred_element_type=f32)
    sent(raw_move.at[0], raw_land.at[0], sends, receives, 1, "ch", across).wait()
    raw_move[1] = raw_move[0] + raw_land[0]
    sent(raw_move.at[1], raw_land.at[1], sends, receives, 2, "ch", along).wait()

    def stepped(index, total):
        first = pl.multiple_of(index * CHUNK, CHUNK)
        rows = pl.ds(first, CHUNK)
        raw = raw_move[1, rows] + raw_land[1, rows]
        raw_out[rows] = raw
        step_norm, input_norm, output_norm = three_norms(raw, gains[...], rank, states)
        widen(input_norm, into, first, CHUNK)
        widen(output_norm, out_of, first, CHUNK)
        pre = (
            jnp.dot(step_norm.astype(bf16), w_dt[...], preferred_element_type=f32) + chan[5:6]
        )
        step_pre_out[rows] = pre
        size = softplus(pre)
        drive[rows] = size * low_out[rows].astype(f32)
        places = me * tokens + first + lax.broadcasted_iota(jnp.int32, (CHUNK, 128), 0)
        resets = jnp.where((places == bounds[0]) | (places == bounds[1]), RESET, 0.0)
        size = size + widened(resets, channels)
        step[rows] = size
        return total + jnp.sum(size, axis=0, keepdims=True)

    total = lax.fori_loop(0, chunks, stepped, jnp.zeros((1, channels), f32))
    blocks = [slice(j, j + LANES) for j in range(0, channels, LANES)]
    for lanes in blocks:
        block_rates = rates[:, lanes]

        def ended(index, state, lanes=lanes, block_rates=block_rates):
            first = pl.multiple_of(index * UNROLL, UNROLL)
            steps, drives = step[pl.ds(first, UNROLL), lanes], drive[pl.ds(first, UNROLL), lanes]
            for k in range(UNROLL):
                decay = jnp.exp2(steps[k : k + 1] * block_rates)
                state = decay * state + widened(into[first + k], LANES) * drives[k : k + 1]
            return state

        starts[:, lanes] = lax.fori_loop(
            0, tokens // UNROLL, ended, jnp.zeros((states, LANES), f32)
        )
    hand = types.SimpleNamespace(**dict(zip(handing(2, 8, 128), handed)))
    handed_in = handed_on(True, starts[...], total, rates, hand)
    next(handed_in)
    starts[...] = next(handed_in)
    hist_copies = []
    for number, lanes in enumerate(blocks):
        block_rates = rates[:, lanes]
        skip = chan[6:7, lanes]

        def walked(index, state, lanes=lanes, block_rates=block_rates, skip=skip):
            first = pl.multiple_of(index * UNROLL, UNROLL)
            steps, drives = step[pl.ds(first, UNROLL), lanes], drive[pl.ds(first, UNROLL), lanes]
            rows = []
            for k in range(UNROLL):
                hist[first + k, :, lanes] = state
                decay = jnp.exp2(steps[k : k + 1] * block_rates)
                state = decay * state + widened(into[first + k], LANES) * drives[k : k + 1]
                rows.append(
                    jnp.sum(widened(out_of[first + k], LANES) * state, axis=0, keepdims=True)
                )
            scan_out[pl.ds(first, UNROLL), lanes] = jnp.concatenate(rows, 0)
            return state

        last_state[:, lanes] = lax.fori_loop(0, tokens // UNROLL, walked, starts[:, lanes])
        copy = pltpu.make_async_copy(
            hist.at[:, :, lanes], hist_out.at[:, :, lanes], hist_sem.at[number]
        )
        copy.start()
        hist_copies.append(copy)

    def gate(index, _):
        first = pl.multiple_of(index * CHUNK, CHUNK)
        rows = pl.ds(first, CHUNK)
        scanned = scan_out[rows] + chan[6:7] * low_out[rows].astype(f32)
        scan_out[rows] = scanned
        gate_pre = proj[rows, channels:].astype(f32)
        gated_out[rows] = (scanned * gate_pre * sigmoid(gate_pre)).astype(bf16)
        return 0

    lax.fori_loop(0, chunks, gate, 0)
    quarter = tokens // 4
    for k, (_, target) in enumerate(shared):
        shared_copies[k].wait()
        shared_copies[k] = sent(
            target, target, shared_sends, shared_receives, 2 + k, "ch", across
        )

    def mixed(index, _):
        first = pl.multiple_of(index * 256, 256)
        product = jnp.dot(
            gated_out[...], w_out[:, pl.ds(first, 256)], preferred_element_type=f32
        ).astype(bf16)
        for k in range(4):
            part[k // 2, k % 2, :, pl.ds(first, 256)] = product[k * quarter : (k + 1) * quarter]
        return 0

    held = types.SimpleNamespace(
        first_land=first_land, second_land=second_land, second_move=second_move, total=mixer,
        sum_sends=sum_sends, sum_receives=sum_receives,
    )
    sums = [four_summed(held, (low, across, high, along), part, 0, k) for k in range(2)]
    for k, item in enumerate(sums):
        lax.fori_loop(k * width // 512, (k + 1) * width // 512, mixed, 0)
        next(item)
    for _ in in_turn(*sums):
        pass
    for copy in hist_copies + shared_copies:
        copy.wait()


def mixer_forward(
    bounds, stream, norm_gains, chan, logs, w_x, gains, w_dt, w_out, w_in, cot, count, ident
):
    bits = bits_of(count)
    tokens, channels = stream.shape[0], w_out.shape[0]
    states, rank, width = logs.shape[0], w_dt.shape[0], w_out.shape[1]
    quarter, narrow = tokens // 4, w_x.shape[1]
    rows = shape_of(tokens, channels)
    low_rows = shape_of(tokens, channels, dtype=bf16)
    wide = shape_of(tokens, states, 128)
    raws = pltpu.VMEM((2, tokens, narrow), f32)
    out = pl.pallas_call(
        functools.partial(forward_kernel, bits),
        out_shape=[
            shape_of(tokens, 2 * channels, dtype=bf16),
            shape_of(count // 4, 2, 2, width // count, tokens, dtype=bf16),
            shape_of(16, channels, dtype=bf16), rows, low_rows, shape_of(tokens, narrow), rows,
            wide, wide, rows, low_rows, shape_of(states, channels),
            shape_of(2, 2, quarter, width, dtype=bf16), shape_of(tokens, states, channels),
            shape_of(count // 4, 2, width // count, tokens, dtype=bf16),
            shape_of(tokens, width, dtype=bf16),
        ],
        in_specs=[pl.BlockSpec(memory_space=pltpu.SMEM)] + [VMEM] * 8 + [ANY] * 2,
        out_specs=[VMEM] * 13 + [ANY] * 3,
        scratch_shapes=[
            pltpu.VMEM((tokens + 16, channels), f32), raws, raws,
            pltpu.VMEM((tokens, channels), f32), pltpu.VMEM((tokens, channels), f32),
            pltpu.VMEM((states, channels), f32),
            pltpu.VMEM((2, 2, quarter, width), bf16), pltpu.VMEM((2, quarter, width), bf16),
            pltpu.VMEM((quarter, width), bf16), pltpu.VMEM((quarter, width), bf16),
            pltpu.VMEM((tokens, states, channels), f32),
            pltpu.SemaphoreType.DMA((3,)), pltpu.SemaphoreType.DMA((3,)),
            pltpu.SemaphoreType.DMA((channels // LANES,)),
            pltpu.SemaphoreType.DMA((4,)), pltpu.SemaphoreType.DMA((4,)),
            pltpu.SemaphoreType.DMA((8,)), pltpu.SemaphoreType.DMA((8,)),
            pltpu.VMEM(w_in.shape, bf16), pltpu.VMEM((tokens, width), bf16),
            pltpu.SemaphoreType.DMA((width // 512,)),
            *handing(count, states, channels).values(),
        ],
        compiler_params=pltpu.CompilerParams(
            collective_id=ident, has_side_effects=True, vmem_limit_bytes=56 * 2**20
        ),
        cost_estimate=cost(6),
        name="mixer_forward",
    )(bounds, stream, norm_gains, chan, logs, w_x, gains, w_dt, w_out, w_in, cot)
    return out


class Unit:
    def __init__(self, left, right, columns, refs, sends, receives, slot, bits, result):
        self.left, self.right, self.columns = left, right, columns
        away, *self.land, self.kept = refs
        self.away = [away.at[pl.ds(0, land.shape[0])] for land in self.land]
        self.sends, self.receives, self.slot, self.bits = sends, receives, slot, bits
        self.result = result
        self.stage = 0
        self.copy = None

    def made(self, *needed):
        for item in needed:
            item.wait()
        mine, partner = flipped(lax.axis_index("seq"), self.bits[0])
        self.make(1 - mine, self.away[0])
        self.stage = 1
        self.go = lambda: self.begin(partner, mine)
        return self

    def begin(self, partner, mine):
        self.copy = self.start(0, partner)
        self.make(mine, self.kept)

    def begun(self):
        _, partner = flipped(lax.axis_index("seq"), self.bits[0])
        self.stage = 1
        self.copy = self.start(0, partner)

    def resume(self):
        self.stage = 2
        if len(self.bits) > 1:
            _, partner = flipped(lax.axis_index("seq"), self.bits[1])
            self.copy = self.start(1, partner)

    def next(self, send_on=True):
        stage, me = self.stage, lax.axis_index("seq")
        if stage > len(self.bits):
            return
        self.stage += 1
        left_over = stage == len(self.bits)
        self.copy.wait()
        count = self.land[stage - 1].shape[0]
        rows = self.kept.shape[1]
        part = 32 if rows % 32 == 0 else rows
        parts = rows // part

        def total(index, at):
            return self.kept[index, at] + self.land[stage - 1][index, at].astype(f32)

        if left_over:

            def finish(step, _):
                at = pl.ds(pl.multiple_of(step * part, part), part)
                self.kept[0, at] = total(0, at)
                return 0

            lax.fori_loop(0, parts, finish, 0)
            self.written = self.result(self.kept.at[0])
            return
        mine, partner = flipped(me, self.bits[stage])

        def send(step, _):
            index = lax.div(step, parts)
            at = pl.ds(pl.multiple_of(lax.rem(step, parts) * part, part), part)
            self.away[stage][index, at] = total(2 * index + 1 - mine, at).astype(bf16)
            return 0

        lax.fori_loop(0, (count // 2) * parts, send, 0)
        if send_on:
            self.copy = self.start(stage, partner)

        def keep(step, _):
            index = lax.div(step, parts)
            at = pl.ds(pl.multiple_of(lax.rem(step, parts) * part, part), part)
            self.kept[index, at] = total(2 * index + mine, at)
            return 0

        lax.fori_loop(0, (count // 2) * parts, keep, 0)

    def start(self, stage, partner):
        return sent(
            self.away[stage], self.land[stage], self.sends, self.receives, self.slot + stage,
            "seq", partner,
        )

    def make(self, side, target):
        first, width = self.columns
        tile = width if width <= 512 else 512 if width % 512 == 0 else 384
        tiles = width // tile
        count, rows = target.shape[:2]
        together = count if rows % 16 == 0 else 1

        def block(step, _):
            index = lax.div(step, tiles)
            column = pl.multiple_of(lax.rem(step, tiles) * tile, tile)
            left = self.left[:, side] if together > 1 else self.left[pl.ds(index, 1), side]
            product = jnp.dot(
                left.reshape(together * rows, left.shape[2]),
                self.right[:, pl.ds(first + column, tile)],
                preferred_element_type=f32,
            ).astype(target.dtype)
            at = pl.ds(0, count) if together > 1 else pl.ds(index, 1)
            target[at, :, pl.ds(column, tile)] = product.reshape(together, rows, tile)
            return 0

        lax.fori_loop(0, count // together * tiles, block, 0)


def norm_back(values, scale, gains, grad, free=True):
    weighted = gains * grad
    result = scale * weighted
    inner = jnp.mean(values * weighted, axis=-1, keepdims=True)
    return result - jnp.where(free, 1.0, 0.0) * values * (scale * scale * scale) * inner, (
        grad * values * scale
    )


def silu_slope(values):
    part = sigmoid(values)
    return part * (1.0 + values * (1.0 - part))


def narrowed(wide, first, count):
    states = wide.shape[1]
    eye = (
        lax.broadcasted_iota(jnp.int32, (states, states), 0)
        == lax.broadcasted_iota(jnp.int32, (states, states), 1)
    ).astype(f32)
    sums = jnp.sum(wide[pl.ds(first, count)], axis=-1, keepdims=True)
    return jnp.sum(sums * eye[None], axis=1)


def dot_rows(left, right):
    return lax.dot_general(left, right, (((1,), (1,)), ((), ())), preferred_element_type=f32)


class Once:
    def __init__(self, *copies, then=None):
        self.copies, self.then = copies, then

    def wait(self):
        for copy in self.copies:
            copy.wait()
        self.copies = ()
        if self.then is not None:
            after, self.then = self.then, None
            after().wait()


def named(names, refs):
    refs, found = list(refs), {}
    for name, count in names:
        taken, refs = refs[: count or 1], refs[count or 1 :]
        found[name] = taken if count else taken[0]
    return types.SimpleNamespace(**found)


def four_summed(r, place, value, base, part):
    low, across, high, along = place
    half = value.shape[3] // 2
    cols = pl.ds(part * half, half)
    first, second, moving = (
        r.first_land.at[:, :, cols], r.second_land.at[:, cols], r.second_move.at[:, cols]
    )
    total, value = r.total.at[:, :, :, cols], value.at[:, :, :, cols]
    sends, receives, base = r.sum_sends, r.sum_receives, base + 4 * part
    copy = sent(value.at[:, 1 - low], first, sends, receives, base, "ch", across)
    yield
    copy.wait()
    moving[...] = (
        value[1 - high, low].astype(f32) + first[1 - high].astype(f32)
    ).astype(bf16)
    copy = sent(moving, second, sends, receives, base + 1, "ch", along)
    yield
    copy.wait()
    total[high, low] = (
        value[high, low].astype(f32) + first[high].astype(f32) + second[...].astype(f32)
    ).astype(bf16)
    own = total.at[high, low]
    copy = sent(own, own, sends, receives, base + 2, "ch", along)
    yield
    copy.wait()
    both = total.at[:, low]
    copy = sent(both, both, sends, receives, base + 3, "ch", across)
    yield
    copy.wait()
    yield


def in_turn(*steps):
    for _ in range(4):
        yield
        for item in steps:
            next(item)
    yield


def feed_forward_kernel(bits, names, *refs):
    r = named(names, refs)
    tokens, width = r.stream.shape
    quarter, chunks, seq_count = tokens // 4, tokens // CHUNK, 1 << len(bits)
    ch_me, me = lax.axis_index("ch"), lax.axis_index("seq")
    low, across = flipped(ch_me, 1)
    high, along = flipped(ch_me, 2)
    pair_bit, rest_bits = bits[1], [bits[0], *bits[2:]]
    mine, pair = flipped(me, pair_bit)
    hid = r.w_down_in.shape[0]
    tile = 256
    tiles = range(0, hid, tile)
    own, other = pl.ds(0, tokens), pl.ds(tokens, tokens)
    slots = []

    def load(source, target):
        copy = pltpu.make_async_copy(source, target, r.load_sems.at[len(slots)])
        copy.start()
        slots.append(0)
        return Once(copy)

    cot_own = load(r.cot, r.right_down.at[own])
    loads = []
    for at in tiles:
        loads.append(
            [
                load(r.w_gate_up_in.at[:, pl.ds(at, tile)], r.w_gate_up.at[:, pl.ds(at, tile)]),
                load(
                    r.w_gate_up_in.at[:, pl.ds(hid + at, tile)],
                    r.w_gate_up.at[:, pl.ds(hid + at, tile)],
                ),
                load(r.w_down_in.at[pl.ds(at, tile)], r.w_down.at[pl.ds(at, tile)]),
            ]
        )
    cot_other = load(r.cot_came, r.right_down.at[other])
    greeted(
        [("ch", across), ("ch", along), ("seq", pair), ("seq", flipped(me, rest_bits[0])[1])]
    )

    def norm_two(index, _):
        rows = pl.ds(pl.multiple_of(index * CHUNK, CHUNK), CHUNK)
        per = quarter // CHUNK
        part = lax.div(index, per)
        at = pl.ds(pl.multiple_of(lax.rem(index, per) * CHUNK, CHUNK), CHUNK)
        mixed = r.mixer[lax.div(part, 2), lax.rem(part, 2), at].astype(f32)
        middle = r.stream[rows].astype(f32) + mixed
        scale = lax.rsqrt(mean_square(middle) + 1e-06)
        r.normed[rows] = (middle * scale * r.gains[1:2]).astype(bf16)
        return 0

    lax.fori_loop(0, chunks, norm_two, 0)

    group = 384
    for at in range(0, width, group):
        turn(r.normed[:, at : at + group], at, r.two_turned)
    half = r.two_turned.shape[0] // 2
    some = pl.ds(low * half, half)
    target = r.left_two.at[some, :, :, other]
    two_copy = sent(
        r.two_turned.at[some, 1 - mine], target, r.pair_sends, r.pair_receives, 0, "seq", pair
    )
    r.left_two[:, :, :, own] = r.two_turned[:, mine]
    cot_own.wait()
    hidden_copies, quads_sent = [], 0
    for number, at in enumerate(tiles):
        for item in loads[number]:
            item.wait()
        gate = jnp.dot(
            r.normed[...], r.w_gate_up[:, pl.ds(at, tile)], preferred_element_type=f32
        )
        up = jnp.dot(
            r.normed[...], r.w_gate_up[:, pl.ds(hid + at, tile)], preferred_element_type=f32
        )
        part = sigmoid(gate)
        act = gate * part
        hidden = (act * up).astype(bf16)
        r.hidden[:, pl.ds(at, tile)] = hidden
        turn(hidden, at, r.hidden_turned)
        grad = dot_rows(r.right_down[own], r.w_down[pl.ds(at, tile)])
        r.right_two[own, pl.ds(at, tile)] = (
            grad * up * (part * (1.0 + gate * (1.0 - part)))
        ).astype(bf16)
        r.right_two[own, pl.ds(hid + at, tile)] = (grad * act).astype(bf16)
        quads = (at + tile) // r.hidden_turned.shape[3] // 4
        if quads > quads_sent:
            some = pl.ds(quads_sent, quads - quads_sent)
            hidden_copies.append(
                sent(
                    r.hidden_turned.at[some, 1 - mine], r.left_hidden.at[some, :, :, other],
                    r.pair_sends, r.pair_receives, 3 + len(hidden_copies), "seq", pair,
                )
            )
            quads_sent = quads
    gate_copy = sent(
        r.right_two.at[own, pl.ds(0, hid)], r.right_two.at[other, pl.ds(0, hid)], r.pair_sends,
        r.pair_receives, 1, "seq", pair,
    )
    r.left_hidden[:, :, :, own] = r.hidden_turned[:, mine]

    def store(values, target, at):
        for k in range(4):
            target[k // 2, k % 2, :, pl.ds(at, tile)] = values[k * quarter : (k + 1) * quarter]

    def two_part(index, _):
        at = pl.multiple_of(index * tile, tile)
        store(dot_rows(r.right_two[own], r.w_gate_up[pl.ds(at, tile)]).astype(bf16), r.part, at)
        return 0

    sums = [four_summed(r, (low, across, high, along), r.part, 0, k) for k in range(2)]
    for k, item in enumerate(sums):
        lax.fori_loop(k * width // (2 * tile), (k + 1) * width // (2 * tile), two_part, 0)
        next(item)
    total = in_turn(*sums)
    next(total)

    def feed_part(index, _):
        at = pl.multiple_of(index * tile, tile)
        product = jnp.dot(
            r.hidden[...], r.w_down[:, pl.ds(at, tile)], preferred_element_type=f32
        )
        store(product.astype(bf16), r.feed_part, at)
        return 0

    n_bits = len(rest_bits)
    part = width // 2
    down, down_late = (
        Unit(r.left_hidden, r.right_down, (k * part, part), r.down, r.unit_sends,
             r.unit_receives, 0, rest_bits, None)
        for k in range(2)
    )
    next(total)
    cot_other.wait()
    down.made(*hidden_copies).go()
    next(total)
    lax.fori_loop(0, width // tile, feed_part, 0)
    next(total)
    side, _ = flipped(me, rest_bits[0])
    down_late.make(1 - side, r.late_away)
    down_late.make(side, r.late_kept)
    two_copy.wait()
    two_copy = sent(target, target, r.pair_sends, r.pair_receives, 2, "ch", across)
    next(total)
    two_copy.wait()
    gate_copy.wait()
    if n_bits > 1:
        down.next(send_on=False)
    r.down_away[...] = down.away[1][...]
    kept = r.down_kept.shape[0]
    r.down_kept[...] = down.kept[0:kept]


def feed_forward(ins, hbm_ins, count, ident):
    bits = bits_of(count)
    n_bits = len(bits) - 1
    tokens, width = ins["stream"].shape
    hid = hbm_ins["w_down_in"].shape[0]
    half, quarter = count // 2, tokens // 4
    rows_in, rows_down = width // count, hid // count

    def low(*dims):
        return pltpu.VMEM(dims, bf16)

    def sems(size):
        return pltpu.SemaphoreType.DMA((size,))

    lands = [low(half >> (k + 1), rows_down, width // 2) for k in range(n_bits)]
    outs = dict(
        total=shape_of(2, 2, quarter, width, dtype=bf16),
        feed_part=shape_of(2, 2, quarter, width, dtype=bf16),
        left_two=shape_of(count // 4, 2, rows_in, 2 * tokens, dtype=bf16),
        right_two=shape_of(2 * tokens, 2 * hid, dtype=bf16),
        down_away=shape_of(half >> 2, rows_down, width // 2, dtype=bf16),
        down_kept=shape_of(half >> 2, rows_down, width // 2),
        late_away=shape_of(half >> 1, rows_down, width // 2, dtype=bf16),
        late_kept=shape_of(half >> 1, rows_down, width // 2),
    )
    scratch = dict(
        w_gate_up=low(width, 2 * hid),
        w_down=low(hid, width),
        normed=low(tokens, width),
        hidden=low(tokens, hid),
        two_turned=low(count // 4, 2, 2, rows_in, tokens),
        hidden_turned=low(count // 4, 2, 2, rows_down, tokens),
        left_hidden=low(count // 4, 2, rows_down, 2 * tokens),
        right_down=low(2 * tokens, width),
        part=low(2, 2, quarter, width),
        first_land=low(2, quarter, width),
        second_land=low(quarter, width),
        second_move=low(quarter, width),
        down=[low(half // 2, rows_down, width // 2), *lands, pltpu.VMEM((half // 2, rows_down, width // 2), f32)],
        load_sems=sems(2 + 3 * (hid // 256)),
        pair_sends=sems(7),
        pair_receives=sems(7),
        sum_sends=sems(8),
        sum_receives=sems(8),
        unit_sends=sems(n_bits),
        unit_receives=sems(n_bits),
    )
    names, shapes = [(name, 0) for name in [*ins, *hbm_ins, *outs]], []
    for name, held in scratch.items():
        listed = isinstance(held, list)
        names.append((name, len(held) if listed else 0))
        shapes += held if listed else [held]
    made = pl.pallas_call(
        functools.partial(feed_forward_kernel, bits, names),
        out_shape=list(outs.values()),
        in_specs=[VMEM] * len(ins) + [ANY] * len(hbm_ins),
        out_specs=[VMEM] * len(outs),
        scratch_shapes=shapes,
        compiler_params=pltpu.CompilerParams(
            collective_id=ident, has_side_effects=True, vmem_limit_bytes=56 * 2**20
        ),
        name="feed_forward",
    )(*ins.values(), *hbm_ins.values())
    return types.SimpleNamespace(**dict(zip(outs, made)))


def backward_kernel(bits, names, *refs):
    r = named(names, refs)
    tokens, width = r.stream.shape
    channels, rank, states = r.low.shape[1], r.w_dt.shape[0], r.logs.shape[0]
    quarter, chunks = tokens // 4, tokens // CHUNK
    ch_me, me = lax.axis_index("ch"), lax.axis_index("seq")
    seq_count = 1 << len(bits)
    low, across = flipped(ch_me, 1)
    high, along = flipped(ch_me, 2)
    pair_bit, rest_bits = bits[1], [bits[0], *bits[2:]]
    mine, pair = flipped(me, pair_bit)
    previous = lax.rem(me + seq_count - 1, seq_count)
    load_slots, pair_slots, shared_slots, write_slots = ([] for _ in range(4))

    def slot_of(slots):
        slots.append(0)
        return len(slots) - 1

    def load(source, target):
        copy = pltpu.make_async_copy(source, target, r.load_sems.at[slot_of(load_slots)])
        copy.start()
        return Once(copy)

    own, other = pl.ds(0, tokens), pl.ds(tokens, tokens)
    mixer_own = load(r.mixer_in, r.mixer)
    cot_own = load(r.cot, r.cot_rows)
    weights = load(r.w_out, r.weights)
    scan_own = load(r.scan_in, r.scan)
    out_of_own = load(r.out_of_in, r.out_of)
    into_own = load(r.into_in, r.into)
    hid = r.right_two_in.shape[1] // 2
    down_away = load(r.down_away_in, r.down[0].at[pl.ds(0, r.down_away_in.shape[0])])
    late_away = load(r.late_away_in, r.late[0])
    two_own = load(r.left_two_in, r.left_two)
    gate_up_own = load(r.right_two_in.at[own], r.right_two.at[own])
    gate_other = load(
        r.right_two_in.at[other, pl.ds(0, hid)], r.right_two.at[other, pl.ds(0, hid)]
    )
    down_kept = load(r.down_kept_in, r.down[-1].at[pl.ds(0, r.down_kept_in.shape[0])])
    late_kept = load(r.late_kept_in, r.late[-1])
    part_in = load(r.feed_part, r.part)
    one_own = load(r.one_in.at[:, mine], r.left_one.at[:, :, :, own])
    one_other = load(r.one_came, r.left_one.at[:, :, :, other])
    gated_own = load(r.gated_in.at[:, mine], r.left_gated.at[:, :, :, own])
    blocks = [slice(j, j + 128) for j in range(0, channels, 128)]
    hists = [load(r.hist_in.at[:, :, blocks[k]], r.hist.at[k]) for k in range(2)]

    greeted(
        [("ch", across), ("ch", along)]
        + [("seq", lax.rem(me + k, seq_count)) for k in range(1, seq_count)]
    )

    def swap(source, target):
        slot = slot_of(pair_slots)
        return Once(sent(source, target, r.pair_sends, r.pair_receives, slot, "seq", pair))

    def swap_shared(source, target):
        slot = 2 * slot_of(shared_slots)
        copy = sent(source, target, r.shared_sends, r.shared_receives, slot, "seq", pair)
        return Once(
            copy,
            then=lambda: sent(
                target, target, r.shared_sends, r.shared_receives, slot + 1, "ch", across
            ),
        )

    n_bits = len(rest_bits)

    def writer(target):
        def write(source):
            copy = pltpu.make_async_copy(source, target, r.write_sems.at[slot_of(write_slots)])
            copy.start()
            return copy

        return write

    def unit(left, right, columns, refs, slot, target):
        return Unit(
            left, right, columns, refs, r.unit_sends, r.unit_receives, slot * n_bits, rest_bits,
            writer(target),
        )

    part = width // 2
    down, late = (
        unit(None, None, None, refs, k, r.down_out.at[:, pl.ds(k * part, part)])
        for k, refs in enumerate((r.down, r.late))
    )
    part = hid // 2
    quarters = [
        unit(
            r.left_two, r.right_two, (k * part, part), refs, 2 + k,
            (r.gate_out, r.up_out)[k // 2].at[:, pl.ds(k % 2 * part, part)],
        )
        for k, refs in enumerate((r.gate0, r.gate1, r.up0, r.up1))
    ]
    gate0, gate1, up0, up1 = quarters
    out = unit(r.left_gated, r.right_out, (0, width), r.out, 6, r.out_out)
    gin = unit(r.left_one, r.right_in, (channels, channels), r.gin, 7, r.gin_out)
    part = channels // 2
    cins = [
        unit(
            r.left_one, r.right_in, (k * part, part), refs, 8 + k,
            r.cin_out.at[:, pl.ds(k * part, part)],
        )
        for k, refs in enumerate((r.cin0, r.cin1))
    ]

    up_other = swap(
        r.right_two_in.at[own, pl.ds(hid, hid)], r.right_two.at[other, pl.ds(hid, hid)]
    )
    down_away.wait()
    down.resume()
    late_away.wait()
    late.begun()

    summed = functools.partial(four_summed, r, (low, across, high, along))


    rates = -jnp.exp(r.logs[...]) * LOG2E

    def places_of(first, count):
        return me * tokens + first + lax.broadcasted_iota(jnp.int32, (count, 128), 0)

    def resteps():
        def body(index, total):
            first = pl.multiple_of(index * CHUNK, CHUNK)
            rows = pl.ds(first, CHUNK)
            size = softplus(r.step_pre[rows])
            r.drive[rows] = size * r.low[rows].astype(f32)
            places = places_of(first, CHUNK)
            resets = jnp.where((places == r.bounds[0]) | (places == r.bounds[1]), RESET, 0.0)
            size = size + widened(resets, channels)
            r.step[rows] = size
            return total + jnp.sum(size, axis=0, keepdims=True)

        r.step_sum[...] = jnp.broadcast_to(
            lax.fori_loop(0, chunks, body, jnp.zeros((1, channels), f32)), (8, channels)
        )

    resteps()
    mixer_own.wait()
    cot_own.wait()

    def quarter_rows(index):
        per = quarter // CHUNK
        part = lax.div(index, per)
        at = pl.ds(pl.multiple_of(lax.rem(index, per) * CHUNK, CHUNK), CHUNK)
        return lax.div(part, 2), lax.rem(part, 2), at

    def norm_two(index, total):
        first = pl.multiple_of(index * CHUNK, CHUNK)
        rows = pl.ds(first, CHUNK)
        a, b, at = quarter_rows(index)
        middle = r.stream[rows].astype(f32) + r.mixer[a, b, at].astype(f32)
        scale = lax.rsqrt(mean_square(middle) + 1e-06)
        back, gain = norm_back(middle, scale, r.gains[1:2], r.two_total[a, b, at].astype(f32))
        grad = r.cot_rows[rows].astype(f32) + back
        r.stream_grad[rows] = grad
        r.right_out[rows] = grad.astype(bf16)
        return total + jnp.sum(gain, axis=0, keepdims=True)

    gain_two = lax.fori_loop(0, chunks, norm_two, jnp.zeros((1, width), f32))
    r.flat_move[0] = jnp.zeros_like(r.flat_move[0])
    r.flat_move[0, 1:2] = gain_two
    weights.wait()
    scan_own.wait()
    skips = []
    for j in range(0, channels, 256):
        lanes = slice(j, j + 256)
        gated_grad = dot_rows(r.right_out[own], r.weights[pl.ds(j, 256)])
        gate_pre = r.proj[:, channels + j : channels + j + 256].astype(f32)
        part = sigmoid(gate_pre)
        slope = part * (1.0 + gate_pre * (1.0 - part))
        r.right_in[own, channels + j : channels + j + 256] = (
            gated_grad * r.scan[:, lanes] * slope
        ).astype(bf16)
        grad = gated_grad * gate_pre * part
        r.scan[:, lanes] = grad
        skips.append(jnp.sum(grad * r.low[:, lanes].astype(f32), axis=0, keepdims=True))
    skip_grad = jnp.concatenate(skips, 1)
    weights = load(r.w_in.at[pl.ds(0, channels)], r.weights)
    out_of_own.wait()
    for j in range(0, channels, LANES):
        lanes = slice(j, j + LANES)

        def ended(index, carried, lanes=lanes, block_rates=rates[:, j : j + LANES]):
            first = pl.multiple_of(tokens - UNROLL - index * UNROLL, UNROLL)
            steps, grads = r.step[pl.ds(first, UNROLL), lanes], r.scan[pl.ds(first, UNROLL), lanes]
            for k in reversed(range(UNROLL)):
                decay = jnp.exp2(steps[k : k + 1] * block_rates)
                carried = decay * (widened(r.out_of[first + k], LANES) * grads[k : k + 1] + carried)
            return carried

        r.starts[:, lanes] = lax.fori_loop(
            0, tokens // UNROLL, ended, jnp.zeros((states, LANES), f32)
        )

    chain = handed_on(False, r.starts[...], r.step_sum[0:1], rates, r)
    next(chain)
    gate0.made(two_own, gate_up_own, gate_other)
    gate1.made()
    r.starts[...] = next(chain)
    gate0.go()
    late_kept.wait()
    late.next()
    gate1.go()
    up0.made(up_other)
    first = pl.multiple_of(low * (tokens // 2), tokens // 2)
    mixer_other = swap_shared(
        r.right_out.at[pl.ds(first, tokens // 2)],
        r.right_out.at[pl.ds(tokens + first, tokens // 2)],
    )
    gated_other = swap(r.gated_in.at[:, 1 - mine], r.left_gated.at[:, :, :, other])
    gin_other = swap(
        r.right_in.at[own, pl.ds(channels, channels)],
        r.right_in.at[other, pl.ds(channels, channels)],
    )
    up0.go()
    up1.made().go()

    part_in.wait()
    feed_sums = [summed(r.part, 0, k) for k in range(2)]
    into_own.wait()

    def results():
        totals = lax.fori_loop(
            0, chunks, results_of, tuple(jnp.zeros((1, width), f32) for _ in range(3))
        )
        for number, total in enumerate(totals):
            r.flat_move[0, 3 + number : 4 + number] = total

    def feed_start():
        for item in feed_sums:
            next(item)
        return in_turn(*feed_sums)

    feed = []
    between = [
        lambda: (feed.append(feed_start()), next(feed[0]), gate0.next()),
        lambda: next(feed[0]),
        lambda: (next(feed[0]), gate1.next()),
        lambda: next(feed[0]),
        lambda: (next(feed[0]), up0.next()),
        lambda: (results(), out.made(gated_own, mixer_other, gated_other).go()),
    ]

    def results_of(index, totals):
        rows = pl.ds(pl.multiple_of(index * CHUNK, CHUNK), CHUNK)
        a, b, at = quarter_rows(index)
        mixed, feed = r.mixer[a, b, at].astype(f32), r.total[a, b, at].astype(f32)
        result = r.stream[rows].astype(f32) + mixed + feed
        r.out_rows[rows] = result.astype(bf16)
        return tuple(
            total + jnp.sum(v * v, axis=0, keepdims=True)
            for total, v in zip(totals, (result, mixed, feed))
        )

    r.into_wide[...] = jnp.zeros_like(r.into_wide)
    r.out_wide[...] = jnp.zeros_like(r.out_wide)
    for number, lanes in enumerate(blocks):
        hists[number].wait()
        hist = r.hist.at[number % 2]
        block_rates = rates[:, lanes]

        def walked(index, carry, lanes=lanes, block_rates=block_rates, hist=hist):
            carried, state, total = carry
            first = pl.multiple_of(tokens - UNROLL - index * UNROLL, UNROLL)
            some = pl.ds(first, UNROLL)
            steps, drives, grads = r.step[some, lanes], r.drive[some, lanes], r.scan[some, lanes]
            decay_list, push_list = [None] * UNROLL, [None] * UNROLL
            for k in reversed(range(UNROLL)):
                place = first + k
                grad_row = grads[k : k + 1]
                decay = jnp.exp2(steps[k : k + 1] * block_rates)
                adjoint = r.out_of[place] * grad_row + carried
                carried = decay * adjoint
                r.out_wide[place] = r.out_wide[place] + state * grad_row
                r.into_wide[place] = r.into_wide[place] + adjoint * drives[k : k + 1]
                state = hist[place]
                share = carried * state
                total = total + share * steps[k : k + 1]
                decay_list[k] = jnp.sum(share * block_rates, axis=0, keepdims=True)
                push_list[k] = jnp.sum(r.into[place] * adjoint, axis=0, keepdims=True)
            r.decay_rows[some, :] = jnp.concatenate(decay_list, 0)
            r.push[some, lanes] = jnp.concatenate(push_list, 0)
            return (carried, state, total)

        _, _, total = lax.fori_loop(
            0,
            tokens // UNROLL,
            walked,
            (r.starts[:, lanes], r.last_state[:, lanes], jnp.zeros((states, 128), f32)),
        )
        r.rate_sum[:, lanes] = total * (rates[:, lanes] * LN2)

        def gathered(index, _, lanes=lanes):
            rows = pl.ds(pl.multiple_of(index * CHUNK, CHUNK), CHUNK)
            used, pushed = r.low[rows, lanes].astype(f32), r.push[rows, lanes]
            pre = r.step_pre[rows, lanes]
            grad = (LN2 * r.decay_rows[rows] + pushed * used) * sigmoid(pre)
            r.step_low_grad[rows, lanes] = grad.astype(bf16)
            r.push[rows, lanes] = pushed * softplus(pre) + r.chan[6:7, lanes] * r.scan[rows, lanes]
            return 0

        lax.fori_loop(0, chunks, gathered, 0)
        if number + 2 < len(blocks):
            hists.append(load(r.hist_in.at[:, :, blocks[number + 2]], r.hist.at[number % 2]))
        if number < len(between):
            between[number]()
    for later in between[len(blocks) :]:
        later()

    def norm_grads(index, _):
        first = pl.multiple_of(index * CHUNK, CHUNK)
        rows = pl.ds(first, CHUNK)
        low_part = dot_rows(r.step_low_grad[rows], r.w_dt[...])
        r.raw_move[0, rows] = jnp.concatenate(
            [low_part, narrowed(r.into_wide, first, CHUNK), narrowed(r.out_wide, first, CHUNK)], 1
        )
        return 0

    lax.fori_loop(0, chunks, norm_grads, 0)
    copy = sent(r.raw_move.at[0], r.raw_land.at[0], r.raw_sends, r.raw_receives, 0, "ch", across)
    gin.made(one_own, one_other, gin_other)
    copy.wait()
    r.raw_move[1] = r.raw_move[0] + r.raw_land[0]
    copy = sent(r.raw_move.at[1], r.raw_land.at[1], r.raw_sends, r.raw_receives, 1, "ch", along)
    up1.next()
    copy.wait()

    def raw_back(index, total):
        rows = pl.ds(pl.multiple_of(index * CHUNK, CHUNK), CHUNK)
        grads, raw = r.raw_move[1, rows] + r.raw_land[1, rows], r.raw[rows]
        gains = r.small_gains[...]
        values, sums_to = [], []
        for start, stop, floor in ((0, rank, None), (rank, rank + states, 0.1),
                                   (rank + states, rank + 2 * states, 0.1)):
            value = raw[:, start:stop]
            square = mean_square(value)
            if floor is None:
                scale, free = lax.rsqrt(square + 1e-06), True
            else:
                scale, free = lax.rsqrt(jnp.maximum(square, floor)), square > floor
            back, gain = norm_back(value, scale, gains[:, start:stop], grads[:, start:stop], free)
            values.append(back)
            sums_to.append(jnp.sum(gain, axis=0, keepdims=True))
        norm = raw[:, :rank] * lax.rsqrt(mean_square(raw[:, :rank]) + 1e-06) * gains[:, :rank]
        r.raw_low[rows] = jnp.concatenate(values, 1).astype(bf16)
        r.step_low[rows] = norm.astype(bf16)
        return total + jnp.concatenate(sums_to, 1)

    small = lax.fori_loop(0, chunks, raw_back, jnp.zeros((1, rank + 2 * states), f32))
    r.flat_move[0, 2:3, : rank + 2 * states] = small

    def conv_back(index, total):
        first = pl.multiple_of(index * CHUNK, CHUNK)
        rows = pl.ds(first, CHUNK)
        grad = r.push[rows] + dot_rows(r.raw_low[rows], r.w_x[...])
        grad = grad * silu_slope(r.pre[rows])
        r.grad_pre[rows] = grad
        return total + jnp.sum(grad, axis=0, keepdims=True)

    tap_bias = lax.fori_loop(0, chunks, conv_back, jnp.zeros((1, channels), f32))
    copy = sent(r.grad_pre.at[pl.ds(0, 8)], r.grad_pre.at[pl.ds(tokens, 8)], r.raw_sends,
                r.raw_receives, 2, "seq", previous)
    gin.go()
    r.extended[0:16] = r.halo[...].astype(f32)

    def extend(index, _):
        first = pl.multiple_of(index * CHUNK, CHUNK)
        r.extended[pl.ds(first + 16, CHUNK)] = r.proj[pl.ds(first, CHUNK), :channels].astype(f32)
        return 0

    lax.fori_loop(0, chunks, extend, 0)

    def taps(index, totals):
        first = pl.multiple_of(index * CHUNK, CHUNK)
        places = places_of(first, CHUNK)
        window = r.extended[pl.ds(first, CHUNK + 16)]
        grad = r.grad_pre[pl.ds(first, CHUNK)]
        return tuple(
            totals[k]
            + jnp.sum(
                grad
                * widened(tap_mask(places, r.bounds, 3 - k), channels)
                * window[13 + k : 13 + k + CHUNK],
                axis=0,
                keepdims=True,
            )
            for k in range(4)
        )

    tap_grads = lax.fori_loop(
        0, chunks, taps, tuple(jnp.zeros((1, channels), f32) for _ in range(4))
    )
    copy.wait()

    def conv_in_back(index, _):
        first = pl.multiple_of(index * CHUNK, CHUNK)
        window = r.grad_pre[pl.ds(first, CHUNK + 8)]
        grad = jnp.zeros((CHUNK, channels), f32)
        for k in range(4):
            places = places_of(first + 3 - k, CHUNK)
            mask = jnp.where(
                places < seq_count * tokens, tap_mask(places, r.bounds, 3 - k), 0.0
            )
            grad = grad + r.chan[k : k + 1] * widened(mask, channels) * window[3 - k : 3 - k + CHUNK]
        r.right_in[pl.ds(first, CHUNK), :channels] = grad.astype(bf16)
        return 0

    lax.fori_loop(0, chunks, conv_in_back, 0)
    cin_others = [
        swap(
            r.right_in.at[own, pl.ds(*item.columns)], r.right_in.at[other, pl.ds(*item.columns)]
        )
        for item in cins
    ]

    def small_columns():
        narrow = r.w_x.shape[1]
        pack = r.step
        pack[0:narrow] = lax.dot_general(
            r.raw_low[...], r.low[...], (((0,), (0,)), ((), ())), preferred_element_type=f32
        )
        pack[narrow : narrow + rank] = lax.dot_general(
            r.step_low[...], r.step_low_grad[...], (((0,), (0,)), ((), ())),
            preferred_element_type=f32,
        )
        at = narrow + rank
        pack[at : at + states] = r.rate_sum[...]
        at += states
        bias = jnp.sum(r.step_low_grad[...].astype(f32), axis=0, keepdims=True)
        pack[at : at + 8] = jnp.concatenate(
            [*tap_grads, tap_bias, bias, skip_grad, jnp.zeros((1, channels), f32)], 0
        )
        at += 8
        pack[at:] = jnp.zeros((pack.shape[0] - at, channels), f32)
        turned = pack[...].T
        r.small_work[0][...] = turned.reshape(r.small_work[0].shape)

    def small_summed():
        for k, bit in enumerate(bits):
            side, partner = flipped(me, bit)
            work, away, land = r.small_work[k], r.small_away[k], r.small_land[k]
            away[...] = work[:, 1 - side].astype(bf16)
            copy = sent(away, land, r.last_sends, r.last_receives, k, "seq", partner)
            yield
            copy.wait()
            total = work[:, side] + land[...].astype(f32)
            target = r.small_work[k + 1] if k + 1 < len(bits) else r.small_out
            target[...] = total.reshape(target.shape)
        yield

    one_sums = [summed(r.part, 8, k) for k in range(2)]
    for number in range(width // channels):
        weights.wait()

        def one_part(index, _, first=number * channels):
            at = pl.multiple_of(index * 256, 256)
            product = dot_rows(r.right_in[own], r.weights[pl.ds(at, 256)]).astype(bf16)
            for k in range(4):
                r.part[k // 2, k % 2, :, pl.ds(first + at, 256)] = product[
                    k * quarter : (k + 1) * quarter
                ]
            return 0

        lax.fori_loop(0, channels // 256, one_part, 0)
        next(one_sums[number])
        if (number + 1) * channels < width:
            weights = load(r.w_in.at[pl.ds((number + 1) * channels, channels)], r.weights)
    one_sum = in_turn(*one_sums)
    next(one_sum)

    def gain_part(index, total):
        rows = pl.ds(pl.multiple_of(index * CHUNK, CHUNK), CHUNK)
        a, b, at = quarter_rows(index)
        value = r.stream[rows].astype(f32)
        scale = lax.rsqrt(mean_square(value) + 1e-06)
        return total + jnp.sum(r.part[a, b, at].astype(f32) * value * scale, axis=0, keepdims=True)

    r.flat_move[0] = r.flat_move[0] * 0.25
    r.flat_move[0, 0:1] = lax.fori_loop(0, chunks, gain_part, jnp.zeros((1, width), f32))
    ways = [("ch", across), ("ch", along)] + [("seq", flipped(me, bit)[1]) for bit in bits]

    def flat_summed():
        for k, (axis, partner) in enumerate(ways):
            copy = sent(r.flat_move.at[k], r.flat_land.at[k], r.flat_sends, r.flat_receives, k,
                        axis, partner)
            yield
            copy.wait()
            target = r.flat_move.at[k + 1] if k + 1 < len(ways) else r.flat_out
            target[...] = r.flat_move[k] + r.flat_land[k]
        yield

    flat_sum = flat_summed()
    next(flat_sum)

    cins[0].made(cin_others[0]).go()
    next(one_sum)
    next(flat_sum)
    out.next()
    cins[1].made(cin_others[1]).go()
    next(one_sum)
    next(flat_sum)
    small_columns()
    small_sum = small_summed()
    next(small_sum)
    next(one_sum)
    gin.next()
    next(flat_sum)
    next(one_sum)

    def norm_one(index, _):
        rows = pl.ds(pl.multiple_of(index * CHUNK, CHUNK), CHUNK)
        a, b, at = quarter_rows(index)
        value = r.stream[rows].astype(f32)
        scale = lax.rsqrt(mean_square(value) + 1e-06)
        back, _ = norm_back(value, scale, r.gains[0:1], r.total[a, b, at].astype(f32))
        r.stream_grad[rows] = r.stream_grad[rows] + back
        return 0

    lax.fori_loop(0, chunks, norm_one, 0)
    cins[0].next()
    next(small_sum)
    next(flat_sum)
    cins[1].next()
    down_kept.wait()
    for item in (down, late, *quarters):
        item.next()
    next(small_sum)
    for waiting in (flat_sum, small_sum):
        for _ in waiting:
            pass
    pending = [out, gin, *cins, down, late, *quarters]
    for _ in range(len(bits)):
        for item in pending:
            item.next()
    for item in pending:
        item.written.wait()


def backward(ins, hbm_ins, count, ident):
    bits = bits_of(count)
    n_bits = len(bits) - 1
    tokens, width = ins["stream"].shape
    channels, rank, states = ins["low"].shape[1], ins["w_dt"].shape[0], ins["logs"].shape[0]
    hid = hbm_ins["right_two_in"].shape[1] // 2
    narrow = ins["w_x"].shape[1]
    half, quarter = count // 2, tokens // 4
    rows_in, rows_out, rows_down = width // count, channels // count, hid // count
    rows = pltpu.VMEM((tokens, channels), f32)

    def low(*dims):
        return pltpu.VMEM(dims, bf16)

    def full(*dims):
        return pltpu.VMEM(dims, f32)

    outs = dict(
        stream_grad=(shape_of(tokens, width), VMEM),
        out_rows=(shape_of(tokens, width, dtype=bf16), VMEM),
        small_out=(shape_of(rows_out, tokens), VMEM),
        flat_out=(shape_of(8, width), VMEM),
        down_out=(shape_of(rows_down, width), ANY),
        gate_out=(shape_of(rows_in, hid), ANY),
        up_out=(shape_of(rows_in, hid), ANY),
        out_out=(shape_of(rows_out, width), ANY),
        gin_out=(shape_of(rows_in, channels), ANY),
        cin_out=(shape_of(rows_in, channels), ANY),
    )
    quads = count // 4

    def unit(part, columns):
        lands = [low(half >> (k + 1), part, columns) for k in range(n_bits)]
        return [low(half // 2, part, columns), *lands, full(half // 2, part, columns)]

    def sems(size):
        return pltpu.SemaphoreType.DMA((size,))

    halves = [count >> (k + 1) for k in range(len(bits))]
    scratch = dict(
        left_two=low(quads, 2, rows_in, 2 * tokens),
        left_one=low(quads, 2, rows_in, 2 * tokens),
        left_gated=low(quads, 2, rows_out, 2 * tokens),
        cot_rows=low(tokens, width),
        right_two=low(2 * tokens, 2 * hid),
        right_out=low(2 * tokens, width),
        right_in=low(2 * tokens, 2 * channels),
        mixer=low(2, 2, quarter, width),
        weights=low(channels, width),
        scan=rows,
        step=rows,
        drive=rows,
        push=rows,
        decay_rows=full(tokens, 128),
        into=full(tokens, states, 128),
        out_of=full(tokens, states, 128),
        into_wide=full(tokens, states, 128),
        out_wide=full(tokens, states, 128),
        hist=full(2, tokens, states, 128),
        step_sum=full(8, channels),
        starts=full(states, channels),
        rate_sum=full(states, channels),
        step_low_grad=low(tokens, channels),
        **handing(count, states, channels),
        part=low(2, 2, quarter, width),
        total=low(2, 2, quarter, width),
        first_land=low(2, quarter, width),
        second_land=low(quarter, width),
        second_move=low(quarter, width),
        raw_move=full(2, tokens, narrow),
        raw_land=full(2, tokens, narrow),
        raw_low=low(tokens, narrow),
        step_low=low(tokens, rank),
        grad_pre=full(tokens + 8, channels),
        extended=full(tokens + 16, channels),
        flat_move=full(2 + len(bits), 8, width),
        flat_land=full(2 + len(bits), 8, width),
        small_work=[full(size, 2, rows_out, tokens) for size in halves],
        small_away=[low(size, rows_out, tokens) for size in halves],
        small_land=[low(size, rows_out, tokens) for size in halves],
        down=unit(rows_down, width // 2),
        late=unit(rows_down, width // 2),
        gate0=unit(rows_in, hid // 2),
        gate1=unit(rows_in, hid // 2),
        up0=unit(rows_in, hid // 2),
        up1=unit(rows_in, hid // 2),
        out=unit(rows_out, width),
        gin=unit(rows_in, channels),
        cin0=unit(rows_in, channels // 2),
        cin1=unit(rows_in, channels // 2),
        load_sems=sems(32),
        write_sems=sems(10),
        pair_sends=sems(8),
        pair_receives=sems(8),
        shared_sends=sems(4),
        shared_receives=sems(4),
        unit_sends=sems(10 * n_bits),
        unit_receives=sems(10 * n_bits),
        sum_sends=sems(16),
        sum_receives=sems(16),
        raw_sends=sems(3),
        raw_receives=sems(3),
        last_sends=sems(len(bits)),
        last_receives=sems(len(bits)),
        flat_sends=sems(2 + len(bits)),
        flat_receives=sems(2 + len(bits)),
    )
    names, shapes = [(name, 0) for name in [*ins, *hbm_ins, *outs]], []
    for name, held in scratch.items():
        listed = isinstance(held, list)
        names.append((name, len(held) if listed else 0))
        shapes += held if listed else [held]
    places = [VMEM for _ in ins]
    places[0] = pl.BlockSpec(memory_space=pltpu.SMEM)
    made = pl.pallas_call(
        functools.partial(backward_kernel, bits, names),
        out_shape=[shape for shape, _ in outs.values()],
        in_specs=places + [ANY] * len(hbm_ins),
        out_specs=[spec for _, spec in outs.values()],
        scratch_shapes=shapes,
        compiler_params=pltpu.CompilerParams(
            collective_id=ident, has_side_effects=True, vmem_limit_bytes=63 * 2**20
        ),
        name="block_backward",
    )(*ins.values(), *hbm_ins.values())
    return types.SimpleNamespace(**dict(zip(outs, made)))


def finish_kernel(cells, names, *refs):
    r = named(names, refs)
    me = lax.axis_index("seq")
    moves = [
        (r.out_rows, r.out), (r.stream_grad, r.stream), (r.out_out, r.w_out),
        (r.down_out, r.w_down), (r.gate_out, r.w_gate_up.at[:, 0]),
        (r.up_out, r.w_gate_up.at[:, 1]), (r.cin_out, r.w_in.at[:, 0]),
        (r.gin_out, r.w_in.at[:, 1]),
    ]
    little = [(r.small_out, r.small_here), (r.flat_out, r.flat_here)]
    loads = [
        pltpu.make_async_copy(source, here, r.sems.at[k])
        for k, (source, here) in enumerate(
            [*little, *((source, here) for (source, _), here in zip(moves, r.here))]
        )
    ]
    for copy in loads:
        copy.start()
    copies = []
    for k, (_, target) in enumerate(moves):
        loads[k + 2].wait()
        copy = pltpu.make_async_copy(r.here[k], target, r.out_sems.at[k])
        copy.start()
        copies.append(copy)
    for copy in loads[:2]:
        copy.wait()
    narrow, rank, states = r.x.shape[1], r.dt.shape[0], r.decay.shape[0]
    small = r.small_here[...]
    r.x[...] = small[:, :narrow]
    turned = small[:, narrow:].T
    r.dt[...] = turned[:rank]
    r.decay[...] = turned[rank : rank + states]
    r.chan[...] = turned[rank + states : rank + states + 7]
    flat = r.flat_here[...]
    width = flat.shape[1]
    count = width // r.gains.shape[1]
    gains, tail = jnp.zeros(r.gains.shape, f32), jnp.zeros(r.small.shape, f32)
    for k in range(count):
        gain_at, tail_at = k * r.gains.shape[1], k * r.small.shape[1]
        mine = me == k
        gains = gains + jnp.where(mine, flat[0:2, gain_at : gain_at + r.gains.shape[1]], 0.0)
        tail = tail + jnp.where(mine, flat[2:3, tail_at : tail_at + r.small.shape[1]], 0.0)
    r.gains[...] = gains
    r.small[...] = tail
    r.rms[...] = jnp.sqrt(jnp.sum(flat[3:6], axis=1, keepdims=True) / cells)
    for copy in copies:
        copy.wait()


def finish(made, cells, narrow, rank, states, count):
    rows_out = made.small_out.shape[0]
    width = made.flat_out.shape[1]
    rows_in, hid = made.gate_out.shape
    channels = made.cin_out.shape[1]
    outs = dict(
        out=shape_of(*made.out_rows.shape, dtype=bf16),
        stream=shape_of(*made.stream_grad.shape),
        gains=shape_of(2, width // count),
        w_in=shape_of(rows_in, 2, channels),
        chan=shape_of(7, rows_out),
        decay=shape_of(states, rows_out),
        x=shape_of(rows_out, narrow),
        small=shape_of(1, narrow // count),
        dt=shape_of(rank, rows_out),
        w_out=shape_of(*made.out_out.shape),
        w_gate_up=shape_of(rows_in, 2, hid),
        w_down=shape_of(*made.down_out.shape),
        rms=shape_of(3, 1),
    )
    ins = vars(made)
    held = [
        made.out_rows, made.stream_grad, made.out_out, made.down_out, made.gate_out, made.up_out,
        made.cin_out, made.gin_out, made.small_out, made.flat_out,
    ]
    places = [pltpu.VMEM(item.shape, item.dtype) for item in held]
    names = [(name, 0) for name in [*ins, *outs]]
    rest = dict(here=8, small_here=0, flat_here=0, sems=0, out_sems=0)
    names += list(rest.items())
    big = {id(outs[name]) for name in ("out", "stream", "w_in", "w_out", "w_gate_up", "w_down")}
    done = pl.pallas_call(
        functools.partial(finish_kernel, cells, names),
        out_shape=list(outs.values()),
        in_specs=[ANY for _ in ins],
        out_specs=[ANY if id(item) in big else VMEM for item in outs.values()],
        scratch_shapes=[*places, pltpu.SemaphoreType.DMA((10,)), pltpu.SemaphoreType.DMA((8,))],
        compiler_params=pltpu.CompilerParams(vmem_limit_bytes=62 * 2**20),
        name="finish",
    )(*ins.values())
    out, stream, gains, w_in, chan, decay, x, small, dt, w_out, w_gate_up, w_down, rms = done
    return (
        out, stream, gains, w_in, chan, decay, x, small.reshape(-1), dt, w_out, w_gate_up, w_down,
        rms.reshape(-1),
    )


def local(
    seq_count,
    stream,
    doc_bounds,
    norm_gains,
    w_in,
    chan_vectors,
    decay_logs,
    w_x,
    small_gains,
    w_dt,
    w_out,
    w_gate_up,
    w_down,
    cotangent,
):
    tokens, width = stream.shape
    rank, (states, channels) = w_dt.shape[0], decay_logs.shape

    def turned(values):
        return values.T.reshape(seq_count // 4, 2, 2, values.shape[1] // seq_count, tokens)

    w_in_flat = w_in.reshape(width, 2 * channels)
    (
        in_proj, one_in, halo, pre_conv, conv_low, raw_proj, step_pre, into, out_of, scan_out, gated_low,
        last_state, mixer_low, before, one_came, cot_came,
    ) = mixer_forward(
        doc_bounds, stream, norm_gains, chan_vectors, decay_logs, w_x, small_gains[None], w_dt,
        w_out, w_in_flat, cotangent, seq_count, 1,
    )
    mid = feed_forward(
        dict(stream=stream, mixer=mixer_low, gains=norm_gains),
        dict(
            cot=cotangent, cot_came=cot_came, w_gate_up_in=w_gate_up.reshape(width, -1),
            w_down_in=w_down,
        ),
        seq_count,
        3,
    )
    made = backward(
        dict(
            bounds=doc_bounds, stream=stream, gains=norm_gains, two_total=mid.total,
            proj=in_proj, halo=halo,
            pre=pre_conv, low=conv_low, raw=raw_proj, step_pre=step_pre, last_state=last_state,
            chan=chan_vectors, logs=decay_logs, w_x=w_x, w_dt=w_dt, small_gains=small_gains[None],
        ),
        dict(
            feed_part=mid.feed_part, left_two_in=mid.left_two, right_two_in=mid.right_two,
            down_away_in=mid.down_away, down_kept_in=mid.down_kept,
            late_away_in=mid.late_away, late_kept_in=mid.late_kept, mixer_in=mixer_low,
            cot=cotangent, gated_in=turned(gated_low), one_in=one_in,
            one_came=one_came, w_out=w_out, w_in=w_in_flat, scan_in=scan_out, into_in=into,
            out_of_in=out_of, hist_in=before,
        ),
        seq_count,
        2,
    )
    return finish(
        made, tokens * seq_count * width, w_x.shape[1], rank, states, seq_count
    )


def solution(mesh):
    in_specs = (
        P("seq", None),
        P(),
        P(),
        P(None, None, "ch"),
        P(None, "ch"),
        P(None, "ch"),
        P("ch", None),
        P(),
        P(None, "ch"),
        P("ch", None),
        P(None, None, "ch"),
        P("ch", None),
        P("seq", None),
    )
    out_specs = (
        P("seq", None),
        P("seq", None),
        P(None, "seq"),
        P("seq", None, "ch"),
        P(None, ("ch", "seq")),
        P(None, ("ch", "seq")),
        P(("ch", "seq"), None),
        P("seq"),
        P(None, ("ch", "seq")),
        P(("ch", "seq"), None),
        P("seq", None, "ch"),
        P(("ch", "seq"), None),
        P(),
    )
    return jax.shard_map(
        functools.partial(local, mesh.shape["seq"]),
        mesh=mesh,
        in_specs=in_specs,
        out_specs=out_specs,
        check_vma=False,
    )
```

```python
import functools
import math
import types

import jax
import jax.numpy as jnp
from jax import lax
from jax.experimental import pallas as pl
from jax.experimental.pallas import tpu as pltpu
from jax.sharding import PartitionSpec as P

f32 = jnp.float32
bf16 = jnp.bfloat16
LOG2E = math.log2(math.e)
LN2 = math.log(2.0)
RESET = 1e30
UNROLL = 8
LANES = 256
VMEM = pl.BlockSpec(memory_space=pltpu.VMEM)


def shape_of(*dims, dtype=f32):
    return jax.ShapeDtypeStruct(dims, dtype)


def cost(us):
    return pl.CostEstimate(flops=int(us * 1e9), bytes_accessed=int(us * 1e6), transcendentals=0)


def widened(column, width):
    return jnp.concatenate([column] * (width // 128), 1)


ANY = pl.BlockSpec(memory_space=pl.ANY)


def sent(source, target, sends, receives, slot, axis, partner):
    copy = pltpu.make_async_remote_copy(
        src_ref=source,
        dst_ref=target,
        send_sem=sends.at[slot],
        recv_sem=receives.at[slot],
        device_id={axis: partner},
        device_id_type=pl.DeviceIdType.MESH,
    )
    copy.start()
    return copy


def bits_of(count):
    return [1 << k for k in range(count.bit_length() - 1)]


def flipped(me, bit):
    mine = lax.rem(me // bit, 2)
    return mine, me + bit - 2 * bit * mine


CHUNK = 32


def sigmoid(values):
    return 1.0 / (1.0 + jnp.exp(-values))


def softplus(values):
    return jnp.maximum(values, 0.0) + jnp.log1p(jnp.exp(-jnp.abs(values)))


def row_doc(places, bounds):
    return (places >= bounds[0]).astype(jnp.int32) + (places >= bounds[1]).astype(jnp.int32)


def tap_mask(places, bounds, offset):
    source = places - offset
    same = row_doc(source, bounds) == row_doc(places, bounds)
    return jnp.where((source >= 0) & same, 1.0, 0.0)


def mean_square(values):
    return jnp.mean(values * values, axis=-1, keepdims=True)


def three_norms(raw, gains, rank, states):
    low, mid, high = raw[:, :rank], raw[:, rank : rank + states], raw[:, rank + states :]
    low_scale = lax.rsqrt(mean_square(low) + 1e-06)
    mid_scale = lax.rsqrt(jnp.maximum(mean_square(mid), 0.1))
    high_scale = lax.rsqrt(jnp.maximum(mean_square(high), 0.1))
    return (
        low * low_scale * gains[:, :rank],
        mid * mid_scale * gains[:, rank : rank + states],
        high * high_scale * gains[:, rank + states :],
    )


def widen(values, wide, first, count):
    states = values.shape[1]
    eye = (
        lax.broadcasted_iota(jnp.int32, (states, states), 0)
        == lax.broadcasted_iota(jnp.int32, (states, states), 1)
    ).astype(f32)
    spread = jnp.sum(values[:, None, :] * eye[None], axis=-1, keepdims=True)
    wide[pl.ds(first, count)] = jnp.broadcast_to(spread, (count, states, 128))


def greeted(axis_partners):
    barrier = pltpu.get_barrier_semaphore()
    for axis, partner in axis_partners:
        pl.semaphore_signal(
            barrier, inc=1, device_id={axis: partner}, device_id_type=pl.DeviceIdType.MESH
        )
    pl.semaphore_wait(barrier, len(axis_partners))


def handed_on(forward, state, steps, rates, r):
    me, count = lax.axis_index("seq"), r.state_land.shape[0] + 1
    r.state_move[...] = state.astype(bf16)
    r.steps_move[...] = steps
    copies = []
    for k in range(1, count):
        to = lax.rem(me + k, count)
        for source, land, sends, receives in (
            (r.state_move, r.state_land, r.state_sends, r.state_receives),
            (r.steps_move, r.steps_land, r.steps_sends, r.steps_receives),
        ):
            copies.append(sent(source, land.at[k - 1], sends, receives, k - 1, "seq", to))
    yield
    for copy in copies:
        copy.wait()
    total = jnp.zeros_like(state)
    passed = jnp.zeros_like(steps)
    for k in range(1, count):
        slot = k - 1 if forward else count - k - 1
        valid = (me >= k) if forward else (me + k < count)
        term = jnp.exp2(rates * passed) * r.state_land[slot].astype(f32)
        total = total + jnp.where(valid, term, 0.0)
        passed = passed + jnp.where(valid, r.steps_land[slot], 0.0)
    yield total


def handing(count, states, channels):
    sems = pltpu.SemaphoreType.DMA((count - 1,))
    return dict(
        state_move=pltpu.VMEM((states, channels), bf16),
        steps_move=pltpu.VMEM((1, channels), f32),
        state_land=pltpu.VMEM((count - 1, states, channels), bf16),
        steps_land=pltpu.VMEM((count - 1, 1, channels), f32),
        state_sends=sems,
        state_receives=sems,
        steps_sends=sems,
        steps_receives=sems,
    )


def turn(values, first, turned):
    rows = turned.shape[3]
    across_rows = values.T
    for k in range(values.shape[1] // rows):
        owner = first // rows + k
        turned[owner // 4, (owner // 2) % 2, owner % 2] = across_rows[k * rows : (k + 1) * rows]


def forward_kernel(
    bits, bounds, stream, norm_gains, chan, logs, w_x, gains, w_dt, w_out, w_in, cot, w_pairs,
    proj, one_in, halo, pre_out, low_out, raw_out, step_pre_out, into, out_of, scan_out, gated_out, last_state,
    mixer, hist_out, one_came, cot_came, w_flat,
    extended, raw_move, raw_land, step, drive, starts, part, first_land,
    second_move, second_land, hist, sends, receives, hist_sem, shared_sends, shared_receives,
    sum_sends, sum_receives, weights, normed, weight_sem, pairs, flat, pair_sems, *handed,
):
    tokens, channels = low_out.shape
    rank, states = w_dt.shape[0], logs.shape[0]
    chunks = tokens // CHUNK
    width = stream.shape[1]
    loads = []
    for k in range(width // 512):
        cols = pl.ds(k * 512, 512)
        copy = pltpu.make_async_copy(w_in.at[:, cols], weights.at[:, cols], weight_sem.at[k])
        copy.start()
        loads.append(copy)
    pair_copies = [pltpu.make_async_copy(w_pairs, pairs, pair_sems.at[0])]
    pair_copies[0].start()
    ahead = [0]

    def relay(count):
        first = ahead[0]
        ahead[0] = last = min(first + count, width // CHUNK)
        if first == 0:
            pair_copies.pop().wait()
        hid = pairs.shape[2]

        def laid(index, _):
            rows = pl.ds(pl.multiple_of(index * CHUNK, CHUNK), CHUNK)
            flat[rows, 0:hid] = pairs[rows, 0, :]
            flat[rows, hid:] = pairs[rows, 1, :]
            return 0

        lax.fori_loop(first, last, laid, 0)
        rows = pl.ds(first * CHUNK, (last - first) * CHUNK)
        copy = pltpu.make_async_copy(
            flat.at[rows], w_flat.at[rows], pair_sems.at[1 + len(pair_copies)]
        )
        copy.start()
        pair_copies.append(copy)

    ch_me, me = lax.axis_index("ch"), lax.axis_index("seq")
    seq_count = 1 << len(bits)
    low, across = flipped(ch_me, 1)
    high, along = flipped(ch_me, 2)
    following = lax.rem(me + 1, seq_count)
    greeted(
        [("ch", across), ("ch", along)]
        + [("seq", lax.rem(me + k, seq_count)) for k in range(1, seq_count)]
    )
    def norm_one(index, _):
        rows = pl.ds(pl.multiple_of(index * CHUNK, CHUNK), CHUNK)
        value = stream[rows].astype(f32)
        scale = lax.rsqrt(mean_square(value) + 1e-06)
        normed[rows] = (value * scale * norm_gains[0:1]).astype(bf16)
        return 0

    lax.fori_loop(0, chunks, norm_one, 0)

    def project(index, _):
        cols = pl.ds(pl.multiple_of(index * 256, 256), 256)
        proj[:, cols] = jnp.dot(
            normed[...], weights[:, cols], preferred_element_type=f32
        ).astype(bf16)
        return 0

    for copy in loads:
        copy.wait()
    lax.fori_loop(0, channels // 256, project, 0)
    halo_copy = sent(
        proj.at[pl.ds(tokens - 16, 16), pl.ds(0, channels)], halo, sends, receives, 0, "seq",
        following,
    )
    for at in range(0, width, 384):
        turn(normed[:, at : at + 384], at, one_in)
    mine, pair = flipped(me, bits[1])
    half = one_in.shape[0] // 2
    some = pl.ds(low * half, half)
    at = pl.ds(pl.multiple_of(low * (tokens // 2), tokens // 2), tokens // 2)
    shared = [
        (one_in.at[some, 1 - mine], one_came.at[some]),
        (cot.at[at], cot_came.at[at]),
    ]
    shared_copies = [
        sent(source, target, shared_sends, shared_receives, k, "seq", pair)
        for k, (source, target) in enumerate(shared)
    ]
    lax.fori_loop(channels // 256, 2 * channels // 256, project, 0)
    rates = -jnp.exp(logs[...]) * LOG2E

    def spread(index, _):
        first = pl.multiple_of(index * CHUNK, CHUNK)
        extended[pl.ds(first + 16, CHUNK)] = proj[pl.ds(first, CHUNK), :channels].astype(f32)
        return 0

    lax.fori_loop(0, chunks, spread, 0)

    def convolved(index, _):
        first = pl.multiple_of(index * CHUNK, CHUNK)
        places = me * tokens + first + lax.broadcasted_iota(jnp.int32, (CHUNK, 128), 0)
        window = extended[pl.ds(first, CHUNK + 16)]
        summed = chan[4:5]
        for k in range(4):
            mask = widened(tap_mask(places, bounds, 3 - k), channels)
            summed = summed + chan[k : k + 1] * window[13 + k : 13 + k + CHUNK] * mask
        pre_out[pl.ds(first, CHUNK)] = summed
        low_out[pl.ds(first, CHUNK)] = (summed * sigmoid(summed)).astype(bf16)
        return 0

    lax.fori_loop(1, chunks, convolved, 0)
    halo_copy.wait()
    extended[0:16] = halo[...].astype(f32)
    convolved(0, 0)
    raw_move[0] = jnp.dot(low_out[...], w_x[...], preferred_element_type=f32)
    copy = sent(raw_move.at[0], raw_land.at[0], sends, receives, 1, "ch", across)
    relay(4)
    copy.wait()
    raw_move[1] = raw_move[0] + raw_land[0]
    copy = sent(raw_move.at[1], raw_land.at[1], sends, receives, 2, "ch", along)
    relay(9)
    copy.wait()

    def stepped(index, total):
        first = pl.multiple_of(index * CHUNK, CHUNK)
        rows = pl.ds(first, CHUNK)
        raw = raw_move[1, rows] + raw_land[1, rows]
        raw_out[rows] = raw
        step_norm, input_norm, output_norm = three_norms(raw, gains[...], rank, states)
        widen(input_norm, into, first, CHUNK)
        widen(output_norm, out_of, first, CHUNK)
        pre = (
            jnp.dot(step_norm.astype(bf16), w_dt[...], preferred_element_type=f32) + chan[5:6]
        )
        step_pre_out[rows] = pre
        size = softplus(pre)
        drive[rows] = size * low_out[rows].astype(f32)
        places = me * tokens + first + lax.broadcasted_iota(jnp.int32, (CHUNK, 128), 0)
        resets = jnp.where((places == bounds[0]) | (places == bounds[1]), RESET, 0.0)
        size = size + widened(resets, channels)
        step[rows] = size
        return total + jnp.sum(size, axis=0, keepdims=True)

    total = lax.fori_loop(0, chunks, stepped, jnp.zeros((1, channels), f32))
    blocks = [slice(j, j + LANES) for j in range(0, channels, LANES)]
    for lanes in blocks:
        block_rates = rates[:, lanes]

        def ended(index, state, lanes=lanes, block_rates=block_rates):
            first = pl.multiple_of(index * UNROLL, UNROLL)
            steps, drives = step[pl.ds(first, UNROLL), lanes], drive[pl.ds(first, UNROLL), lanes]
            for k in range(UNROLL):
                decay = jnp.exp2(steps[k : k + 1] * block_rates)
                state = decay * state + widened(into[first + k], LANES) * drives[k : k + 1]
            return state

        starts[:, lanes] = lax.fori_loop(
            0, tokens // UNROLL, ended, jnp.zeros((states, LANES), f32)
        )
    hand = types.SimpleNamespace(**dict(zip(handing(2, 8, 128), handed)))
    handed_in = handed_on(True, starts[...], total, rates, hand)
    next(handed_in)
    relay(14)
    starts[...] = next(handed_in)
    hist_copies = []
    for number, lanes in enumerate(blocks):
        block_rates = rates[:, lanes]
        skip = chan[6:7, lanes]

        def walked(index, state, lanes=lanes, block_rates=block_rates, skip=skip):
            first = pl.multiple_of(index * UNROLL, UNROLL)
            steps, drives = step[pl.ds(first, UNROLL), lanes], drive[pl.ds(first, UNROLL), lanes]
            rows = []
            for k in range(UNROLL):
                hist[first + k, :, lanes] = state
                decay = jnp.exp2(steps[k : k + 1] * block_rates)
                state = decay * state + widened(into[first + k], LANES) * drives[k : k + 1]
                rows.append(
                    jnp.sum(widened(out_of[first + k], LANES) * state, axis=0, keepdims=True)
                )
            scan_out[pl.ds(first, UNROLL), lanes] = jnp.concatenate(rows, 0)
            return state

        last_state[:, lanes] = lax.fori_loop(0, tokens // UNROLL, walked, starts[:, lanes])
        copy = pltpu.make_async_copy(
            hist.at[:, :, lanes], hist_out.at[:, :, lanes], hist_sem.at[number]
        )
        copy.start()
        hist_copies.append(copy)

    def gate(index, _):
        first = pl.multiple_of(index * CHUNK, CHUNK)
        rows = pl.ds(first, CHUNK)
        scanned = scan_out[rows] + chan[6:7] * low_out[rows].astype(f32)
        scan_out[rows] = scanned
        gate_pre = proj[rows, channels:].astype(f32)
        gated_out[rows] = (scanned * gate_pre * sigmoid(gate_pre)).astype(bf16)
        return 0

    lax.fori_loop(0, chunks, gate, 0)
    quarter = tokens // 4
    for k, (_, target) in enumerate(shared):
        shared_copies[k].wait()
        shared_copies[k] = sent(
            target, target, shared_sends, shared_receives, 2 + k, "ch", across
        )

    def mixed(index, _):
        first = pl.multiple_of(index * 256, 256)
        product = jnp.dot(
            gated_out[...], w_out[:, pl.ds(first, 256)], preferred_element_type=f32
        ).astype(bf16)
        for k in range(4):
            part[k // 2, k % 2, :, pl.ds(first, 256)] = product[k * quarter : (k + 1) * quarter]
        return 0

    held = types.SimpleNamespace(
        first_land=first_land, second_land=second_land, second_move=second_move, total=mixer,
        sum_sends=sum_sends, sum_receives=sum_receives,
    )
    sums = [four_summed(held, (low, across, high, along), part, 0, k) for k in range(2)]
    for k, item in enumerate(sums):
        lax.fori_loop(k * width // 512, (k + 1) * width // 512, mixed, 0)
        next(item)
    turns = in_turn(*sums)
    for count in (3, 8, 8, width):
        next(turns)
        if ahead[0] < width // CHUNK:
            relay(count)
    next(turns)
    for copy in hist_copies + shared_copies + pair_copies:
        copy.wait()


def mixer_forward(
    bounds, stream, norm_gains, chan, logs, w_x, gains, w_dt, w_out, w_in, cot, w_pairs, count,
    ident,
):
    bits = bits_of(count)
    tokens, channels = stream.shape[0], w_out.shape[0]
    states, rank, width = logs.shape[0], w_dt.shape[0], w_out.shape[1]
    quarter, narrow = tokens // 4, w_x.shape[1]
    rows = shape_of(tokens, channels)
    low_rows = shape_of(tokens, channels, dtype=bf16)
    wide = shape_of(tokens, states, 128)
    raws = pltpu.VMEM((2, tokens, narrow), f32)
    out = pl.pallas_call(
        functools.partial(forward_kernel, bits),
        out_shape=[
            shape_of(tokens, 2 * channels, dtype=bf16),
            shape_of(count // 4, 2, 2, width // count, tokens, dtype=bf16),
            shape_of(16, channels, dtype=bf16), rows, low_rows, shape_of(tokens, narrow), rows,
            wide, wide, rows, low_rows, shape_of(states, channels),
            shape_of(2, 2, quarter, width, dtype=bf16), shape_of(tokens, states, channels),
            shape_of(count // 4, 2, width // count, tokens, dtype=bf16),
            shape_of(tokens, width, dtype=bf16),
            shape_of(width, 2 * w_pairs.shape[2], dtype=bf16),
        ],
        in_specs=[pl.BlockSpec(memory_space=pltpu.SMEM)] + [VMEM] * 8 + [ANY] * 3,
        out_specs=[VMEM] * 13 + [ANY] * 4,
        scratch_shapes=[
            pltpu.VMEM((tokens + 16, channels), f32), raws, raws,
            pltpu.VMEM((tokens, channels), f32), pltpu.VMEM((tokens, channels), f32),
            pltpu.VMEM((states, channels), f32),
            pltpu.VMEM((2, 2, quarter, width), bf16), pltpu.VMEM((2, quarter, width), bf16),
            pltpu.VMEM((quarter, width), bf16), pltpu.VMEM((quarter, width), bf16),
            pltpu.VMEM((tokens, states, channels), f32),
            pltpu.SemaphoreType.DMA((3,)), pltpu.SemaphoreType.DMA((3,)),
            pltpu.SemaphoreType.DMA((channels // LANES,)),
            pltpu.SemaphoreType.DMA((4,)), pltpu.SemaphoreType.DMA((4,)),
            pltpu.SemaphoreType.DMA((8,)), pltpu.SemaphoreType.DMA((8,)),
            pltpu.VMEM(w_in.shape, bf16), pltpu.VMEM((tokens, width), bf16),
            pltpu.SemaphoreType.DMA((width // 512,)),
            pltpu.VMEM(w_pairs.shape, bf16), pltpu.VMEM((width, 2 * w_pairs.shape[2]), bf16),
            pltpu.SemaphoreType.DMA((9,)),
            *handing(count, states, channels).values(),
        ],
        compiler_params=pltpu.CompilerParams(
            collective_id=ident, has_side_effects=True, vmem_limit_bytes=56 * 2**20
        ),
        cost_estimate=cost(6),
        name="mixer_forward",
    )(bounds, stream, norm_gains, chan, logs, w_x, gains, w_dt, w_out, w_in, cot, w_pairs)
    return out


class Unit:
    def __init__(self, left, right, columns, refs, sends, receives, slot, bits, result):
        self.left, self.right, self.columns = left, right, columns
        away, *self.land, self.kept = refs
        self.away = [away.at[pl.ds(0, land.shape[0])] for land in self.land]
        self.sends, self.receives, self.slot, self.bits = sends, receives, slot, bits
        self.result = result
        self.stage = 0
        self.copy = None

    def made(self, *needed):
        for item in needed:
            item.wait()
        mine, partner = flipped(lax.axis_index("seq"), self.bits[0])
        self.make(1 - mine, self.away[0])
        self.stage = 1
        self.go = lambda: self.begin(partner, mine)
        return self

    def begin(self, partner, mine):
        self.copy = self.start(0, partner)
        self.make(mine, self.kept)

    def begun(self):
        _, partner = flipped(lax.axis_index("seq"), self.bits[0])
        self.stage = 1
        self.copy = self.start(0, partner)

    def resume(self):
        self.stage = 2
        if len(self.bits) > 1:
            _, partner = flipped(lax.axis_index("seq"), self.bits[1])
            self.copy = self.start(1, partner)

    def next(self, send_on=True):
        stage, me = self.stage, lax.axis_index("seq")
        if stage > len(self.bits):
            return
        self.stage += 1
        left_over = stage == len(self.bits)
        self.copy.wait()
        count = self.land[stage - 1].shape[0]
        rows = self.kept.shape[1]
        part = 32 if rows % 32 == 0 else rows
        parts = rows // part

        def total(index, at):
            return self.kept[index, at] + self.land[stage - 1][index, at].astype(f32)

        if left_over:

            def finish(step, _):
                at = pl.ds(pl.multiple_of(step * part, part), part)
                self.kept[0, at] = total(0, at)
                return 0

            lax.fori_loop(0, parts, finish, 0)
            self.written = self.result(self.kept.at[0])
            return
        mine, partner = flipped(me, self.bits[stage])

        def send(step, _):
            index = lax.div(step, parts)
            at = pl.ds(pl.multiple_of(lax.rem(step, parts) * part, part), part)
            self.away[stage][index, at] = total(2 * index + 1 - mine, at).astype(bf16)
            return 0

        lax.fori_loop(0, (count // 2) * parts, send, 0)
        if send_on:
            self.copy = self.start(stage, partner)

        def keep(step, _):
            index = lax.div(step, parts)
            at = pl.ds(pl.multiple_of(lax.rem(step, parts) * part, part), part)
            self.kept[index, at] = total(2 * index + mine, at)
            return 0

        lax.fori_loop(0, (count // 2) * parts, keep, 0)

    def start(self, stage, partner):
        return sent(
            self.away[stage], self.land[stage], self.sends, self.receives, self.slot + stage,
            "seq", partner,
        )

    def make(self, side, target):
        first, width = self.columns
        tile = width if width <= 512 else 512 if width % 512 == 0 else 384
        tiles = width // tile
        count, rows = target.shape[:2]
        together = count if rows % 16 == 0 else 1

        def block(step, _):
            index = lax.div(step, tiles)
            column = pl.multiple_of(lax.rem(step, tiles) * tile, tile)
            left = self.left[:, side] if together > 1 else self.left[pl.ds(index, 1), side]
            product = jnp.dot(
                left.reshape(together * rows, left.shape[2]),
                self.right[:, pl.ds(first + column, tile)],
                preferred_element_type=f32,
            ).astype(target.dtype)
            at = pl.ds(0, count) if together > 1 else pl.ds(index, 1)
            target[at, :, pl.ds(column, tile)] = product.reshape(together, rows, tile)
            return 0

        lax.fori_loop(0, count // together * tiles, block, 0)


def norm_back(values, scale, gains, grad, free=True):
    weighted = gains * grad
    result = scale * weighted
    inner = jnp.mean(values * weighted, axis=-1, keepdims=True)
    return result - jnp.where(free, 1.0, 0.0) * values * (scale * scale * scale) * inner, (
        grad * values * scale
    )


def silu_slope(values):
    part = sigmoid(values)
    return part * (1.0 + values * (1.0 - part))


def narrowed(wide, first, count):
    states = wide.shape[1]
    eye = (
        lax.broadcasted_iota(jnp.int32, (states, states), 0)
        == lax.broadcasted_iota(jnp.int32, (states, states), 1)
    ).astype(f32)
    sums = jnp.sum(wide[pl.ds(first, count)], axis=-1, keepdims=True)
    return jnp.sum(sums * eye[None], axis=1)


def dot_rows(left, right):
    return lax.dot_general(left, right, (((1,), (1,)), ((), ())), preferred_element_type=f32)


class Once:
    def __init__(self, *copies, then=None):
        self.copies, self.then = copies, then

    def wait(self):
        for copy in self.copies:
            copy.wait()
        self.copies = ()
        if self.then is not None:
            after, self.then = self.then, None
            after().wait()


def named(names, refs):
    refs, found = list(refs), {}
    for name, count in names:
        taken, refs = refs[: count or 1], refs[count or 1 :]
        found[name] = taken if count else taken[0]
    return types.SimpleNamespace(**found)


def four_summed(r, place, value, base, part):
    low, across, high, along = place
    half = value.shape[3] // 2
    cols = pl.ds(part * half, half)
    first, second, moving = (
        r.first_land.at[:, :, cols], r.second_land.at[:, cols], r.second_move.at[:, cols]
    )
    total, value = r.total.at[:, :, :, cols], value.at[:, :, :, cols]
    sends, receives, base = r.sum_sends, r.sum_receives, base + 4 * part
    copy = sent(value.at[:, 1 - low], first, sends, receives, base, "ch", across)
    yield
    copy.wait()
    moving[...] = (
        value[1 - high, low].astype(f32) + first[1 - high].astype(f32)
    ).astype(bf16)
    copy = sent(moving, second, sends, receives, base + 1, "ch", along)
    yield
    copy.wait()
    total[high, low] = (
        value[high, low].astype(f32) + first[high].astype(f32) + second[...].astype(f32)
    ).astype(bf16)
    own = total.at[high, low]
    copy = sent(own, own, sends, receives, base + 2, "ch", along)
    yield
    copy.wait()
    both = total.at[:, low]
    copy = sent(both, both, sends, receives, base + 3, "ch", across)
    yield
    copy.wait()
    yield


def in_turn(*steps):
    for _ in range(4):
        yield
        for item in steps:
            next(item)
    yield


def feed_forward_kernel(bits, names, *refs):
    r = named(names, refs)
    tokens, width = r.stream.shape
    quarter, chunks, seq_count = tokens // 4, tokens // CHUNK, 1 << len(bits)
    ch_me, me = lax.axis_index("ch"), lax.axis_index("seq")
    low, across = flipped(ch_me, 1)
    high, along = flipped(ch_me, 2)
    pair_bit, rest_bits = bits[1], [bits[0], *bits[2:]]
    mine, pair = flipped(me, pair_bit)
    hid = r.w_down_in.shape[0]
    tile = 256
    tiles = range(0, hid, tile)
    own, other = pl.ds(0, tokens), pl.ds(tokens, tokens)
    slots = []

    def load(source, target):
        copy = pltpu.make_async_copy(source, target, r.load_sems.at[len(slots)])
        copy.start()
        slots.append(0)
        return Once(copy)

    cot_own = load(r.cot, r.right_down.at[own])
    loads = []
    for at in tiles:
        loads.append(
            [
                load(r.w_gate_up_in.at[:, pl.ds(at, tile)], r.w_gate_up.at[:, pl.ds(at, tile)]),
                load(
                    r.w_gate_up_in.at[:, pl.ds(hid + at, tile)],
                    r.w_gate_up.at[:, pl.ds(hid + at, tile)],
                ),
                load(r.w_down_in.at[pl.ds(at, tile)], r.w_down.at[pl.ds(at, tile)]),
            ]
        )
    cot_other = load(r.cot_came, r.right_down.at[other])
    greeted(
        [("ch", across), ("ch", along), ("seq", pair), ("seq", flipped(me, rest_bits[0])[1])]
    )

    def norm_two(index, _):
        rows = pl.ds(pl.multiple_of(index * CHUNK, CHUNK), CHUNK)
        per = quarter // CHUNK
        part = lax.div(index, per)
        at = pl.ds(pl.multiple_of(lax.rem(index, per) * CHUNK, CHUNK), CHUNK)
        mixed = r.mixer[lax.div(part, 2), lax.rem(part, 2), at].astype(f32)
        middle = r.stream[rows].astype(f32) + mixed
        scale = lax.rsqrt(mean_square(middle) + 1e-06)
        r.normed[rows] = (middle * scale * r.gains[1:2]).astype(bf16)
        return 0

    lax.fori_loop(0, chunks, norm_two, 0)

    group = 384
    for at in range(0, width, group):
        turn(r.normed[:, at : at + group], at, r.two_turned)
    half = r.two_turned.shape[0] // 2
    some = pl.ds(low * half, half)
    target = r.left_two.at[some, :, :, other]
    two_copy = sent(
        r.two_turned.at[some, 1 - mine], target, r.pair_sends, r.pair_receives, 0, "seq", pair
    )
    r.left_two[:, :, :, own] = r.two_turned[:, mine]
    cot_own.wait()
    hidden_copies, quads_sent = [], 0
    for number, at in enumerate(tiles):
        for item in loads[number]:
            item.wait()
        gate = jnp.dot(
            r.normed[...], r.w_gate_up[:, pl.ds(at, tile)], preferred_element_type=f32
        )
        up = jnp.dot(
            r.normed[...], r.w_gate_up[:, pl.ds(hid + at, tile)], preferred_element_type=f32
        )
        part = sigmoid(gate)
        act = gate * part
        hidden = (act * up).astype(bf16)
        r.hidden[:, pl.ds(at, tile)] = hidden
        turn(hidden, at, r.hidden_turned)
        grad = dot_rows(r.right_down[own], r.w_down[pl.ds(at, tile)])
        r.right_two[own, pl.ds(at, tile)] = (
            grad * up * (part * (1.0 + gate * (1.0 - part)))
        ).astype(bf16)
        r.right_two[own, pl.ds(hid + at, tile)] = (grad * act).astype(bf16)
        quads = (at + tile) // r.hidden_turned.shape[3] // 4
        if quads > quads_sent:
            some = pl.ds(quads_sent, quads - quads_sent)
            hidden_copies.append(
                sent(
                    r.hidden_turned.at[some, 1 - mine], r.left_hidden.at[some, :, :, other],
                    r.pair_sends, r.pair_receives, 3 + len(hidden_copies), "seq", pair,
                )
            )
            quads_sent = quads
    gate_copy = sent(
        r.right_two.at[own, pl.ds(0, hid)], r.right_two.at[other, pl.ds(0, hid)], r.pair_sends,
        r.pair_receives, 1, "seq", pair,
    )
    r.left_hidden[:, :, :, own] = r.hidden_turned[:, mine]

    def store(values, target, at):
        for k in range(4):
            target[k // 2, k % 2, :, pl.ds(at, tile)] = values[k * quarter : (k + 1) * quarter]

    def two_part(index, _):
        at = pl.multiple_of(index * tile, tile)
        store(dot_rows(r.right_two[own], r.w_gate_up[pl.ds(at, tile)]).astype(bf16), r.part, at)
        return 0

    sums = [four_summed(r, (low, across, high, along), r.part, 0, k) for k in range(2)]
    for k, item in enumerate(sums):
        lax.fori_loop(k * width // (2 * tile), (k + 1) * width // (2 * tile), two_part, 0)
        next(item)
    total = in_turn(*sums)
    next(total)

    def feed_part(index, _):
        at = pl.multiple_of(index * tile, tile)
        product = jnp.dot(
            r.hidden[...], r.w_down[:, pl.ds(at, tile)], preferred_element_type=f32
        )
        store(product.astype(bf16), r.feed_part, at)
        return 0

    n_bits = len(rest_bits)
    part = width // 2
    down, down_late = (
        Unit(r.left_hidden, r.right_down, (k * part, part), r.down, r.unit_sends,
             r.unit_receives, 0, rest_bits, None)
        for k in range(2)
    )
    next(total)
    cot_other.wait()
    down.made(*hidden_copies).go()
    next(total)
    lax.fori_loop(0, width // tile, feed_part, 0)
    next(total)
    side, _ = flipped(me, rest_bits[0])
    down_late.make(1 - side, r.late_away)
    down_late.make(side, r.late_kept)
    two_copy.wait()
    two_copy = sent(target, target, r.pair_sends, r.pair_receives, 2, "ch", across)
    next(total)
    two_copy.wait()
    gate_copy.wait()
    if n_bits > 1:
        down.next(send_on=False)
    r.down_away[...] = down.away[1][...]
    kept = r.down_kept.shape[0]
    r.down_kept[...] = down.kept[0:kept]


def feed_forward(ins, hbm_ins, count, ident):
    bits = bits_of(count)
    n_bits = len(bits) - 1
    tokens, width = ins["stream"].shape
    hid = hbm_ins["w_down_in"].shape[0]
    half, quarter = count // 2, tokens // 4
    rows_in, rows_down = width // count, hid // count

    def low(*dims):
        return pltpu.VMEM(dims, bf16)

    def sems(size):
        return pltpu.SemaphoreType.DMA((size,))

    lands = [low(half >> (k + 1), rows_down, width // 2) for k in range(n_bits)]
    outs = dict(
        total=shape_of(2, 2, quarter, width, dtype=bf16),
        feed_part=shape_of(2, 2, quarter, width, dtype=bf16),
        left_two=shape_of(count // 4, 2, rows_in, 2 * tokens, dtype=bf16),
        right_two=shape_of(2 * tokens, 2 * hid, dtype=bf16),
        down_away=shape_of(half >> 2, rows_down, width // 2, dtype=bf16),
        down_kept=shape_of(half >> 2, rows_down, width // 2),
        late_away=shape_of(half >> 1, rows_down, width // 2, dtype=bf16),
        late_kept=shape_of(half >> 1, rows_down, width // 2),
    )
    scratch = dict(
        w_gate_up=low(width, 2 * hid),
        w_down=low(hid, width),
        normed=low(tokens, width),
        hidden=low(tokens, hid),
        two_turned=low(count // 4, 2, 2, rows_in, tokens),
        hidden_turned=low(count // 4, 2, 2, rows_down, tokens),
        left_hidden=low(count // 4, 2, rows_down, 2 * tokens),
        right_down=low(2 * tokens, width),
        part=low(2, 2, quarter, width),
        first_land=low(2, quarter, width),
        second_land=low(quarter, width),
        second_move=low(quarter, width),
        down=[low(half // 2, rows_down, width // 2), *lands, pltpu.VMEM((half // 2, rows_down, width // 2), f32)],
        load_sems=sems(2 + 3 * (hid // 256)),
        pair_sends=sems(7),
        pair_receives=sems(7),
        sum_sends=sems(8),
        sum_receives=sems(8),
        unit_sends=sems(n_bits),
        unit_receives=sems(n_bits),
    )
    names, shapes = [(name, 0) for name in [*ins, *hbm_ins, *outs]], []
    for name, held in scratch.items():
        listed = isinstance(held, list)
        names.append((name, len(held) if listed else 0))
        shapes += held if listed else [held]
    made = pl.pallas_call(
        functools.partial(feed_forward_kernel, bits, names),
        out_shape=list(outs.values()),
        in_specs=[VMEM] * len(ins) + [ANY] * len(hbm_ins),
        out_specs=[VMEM] * len(outs),
        scratch_shapes=shapes,
        compiler_params=pltpu.CompilerParams(
            collective_id=ident, has_side_effects=True, vmem_limit_bytes=56 * 2**20
        ),
        name="feed_forward",
    )(*ins.values(), *hbm_ins.values())
    return types.SimpleNamespace(**dict(zip(outs, made)))


def backward_kernel(bits, names, *refs):
    r = named(names, refs)
    tokens, width = r.stream.shape
    channels, rank, states = r.low.shape[1], r.w_dt.shape[0], r.logs.shape[0]
    quarter, chunks = tokens // 4, tokens // CHUNK
    ch_me, me = lax.axis_index("ch"), lax.axis_index("seq")
    seq_count = 1 << len(bits)
    low, across = flipped(ch_me, 1)
    high, along = flipped(ch_me, 2)
    pair_bit, rest_bits = bits[1], [bits[0], *bits[2:]]
    mine, pair = flipped(me, pair_bit)
    previous = lax.rem(me + seq_count - 1, seq_count)
    load_slots, pair_slots, shared_slots, write_slots = ([] for _ in range(4))

    def slot_of(slots):
        slots.append(0)
        return len(slots) - 1

    def load(source, target):
        copy = pltpu.make_async_copy(source, target, r.load_sems.at[slot_of(load_slots)])
        copy.start()
        return Once(copy)

    own, other = pl.ds(0, tokens), pl.ds(tokens, tokens)
    mixer_own = load(r.mixer_in, r.mixer)
    cot_own = load(r.cot, r.cot_rows)
    weights = load(r.w_out, r.weights)
    scan_own = load(r.scan_in, r.scan)
    out_of_own = load(r.out_of_in, r.out_of)
    into_own = load(r.into_in, r.into)
    hid = r.right_two_in.shape[1] // 2
    down_away = load(r.down_away_in, r.down[0].at[pl.ds(0, r.down_away_in.shape[0])])
    late_away = load(r.late_away_in, r.late[0])
    two_own = load(r.left_two_in, r.left_two)
    gate_up_own = load(r.right_two_in.at[own], r.right_two.at[own])
    gate_other = load(
        r.right_two_in.at[other, pl.ds(0, hid)], r.right_two.at[other, pl.ds(0, hid)]
    )
    down_kept = load(r.down_kept_in, r.down[-1].at[pl.ds(0, r.down_kept_in.shape[0])])
    late_kept = load(r.late_kept_in, r.late[-1])
    part_in = load(r.feed_part, r.part)
    one_own = load(r.one_in.at[:, mine], r.left_one.at[:, :, :, own])
    one_other = load(r.one_came, r.left_one.at[:, :, :, other])
    gated_own = load(r.gated_in.at[:, mine], r.left_gated.at[:, :, :, own])
    blocks = [slice(j, j + 128) for j in range(0, channels, 128)]
    hists = [load(r.hist_in.at[:, :, blocks[k]], r.hist.at[k]) for k in range(2)]

    greeted(
        [("ch", across), ("ch", along)]
        + [("seq", lax.rem(me + k, seq_count)) for k in range(1, seq_count)]
    )

    def swap(source, target):
        slot = slot_of(pair_slots)
        return Once(sent(source, target, r.pair_sends, r.pair_receives, slot, "seq", pair))

    def swap_shared(source, target):
        slot = 2 * slot_of(shared_slots)
        copy = sent(source, target, r.shared_sends, r.shared_receives, slot, "seq", pair)
        return Once(
            copy,
            then=lambda: sent(
                target, target, r.shared_sends, r.shared_receives, slot + 1, "ch", across
            ),
        )

    n_bits = len(rest_bits)

    def writer(target):
        def write(source):
            copy = pltpu.make_async_copy(source, target, r.write_sems.at[slot_of(write_slots)])
            copy.start()
            return copy

        return write

    def unit(left, right, columns, refs, slot, target):
        return Unit(
            left, right, columns, refs, r.unit_sends, r.unit_receives, slot * n_bits, rest_bits,
            writer(target),
        )

    part = width // 2
    down, late = (
        unit(None, None, None, refs, k, r.down_out.at[:, pl.ds(k * part, part)])
        for k, refs in enumerate((r.down, r.late))
    )
    part = hid // 2
    quarters = [
        unit(
            r.left_two, r.right_two, (k * part, part), refs, 2 + k,
            (r.gate_out, r.up_out)[k // 2].at[:, pl.ds(k % 2 * part, part)],
        )
        for k, refs in enumerate((r.gate0, r.gate1, r.up0, r.up1))
    ]
    gate0, gate1, up0, up1 = quarters
    out = unit(r.left_gated, r.right_out, (0, width), r.out, 6, r.out_out)
    gin = unit(r.left_one, r.right_in, (channels, channels), r.gin, 7, r.gin_out)
    part = channels // 2
    cins = [
        unit(
            r.left_one, r.right_in, (k * part, part), refs, 8 + k,
            r.cin_out.at[:, pl.ds(k * part, part)],
        )
        for k, refs in enumerate((r.cin0, r.cin1))
    ]

    up_other = swap(
        r.right_two_in.at[own, pl.ds(hid, hid)], r.right_two.at[other, pl.ds(hid, hid)]
    )
    down_away.wait()
    down.resume()
    late_away.wait()
    late.begun()

    summed = functools.partial(four_summed, r, (low, across, high, along))


    rates = -jnp.exp(r.logs[...]) * LOG2E

    def places_of(first, count):
        return me * tokens + first + lax.broadcasted_iota(jnp.int32, (count, 128), 0)

    def resteps():
        def body(index, total):
            first = pl.multiple_of(index * CHUNK, CHUNK)
            rows = pl.ds(first, CHUNK)
            size = softplus(r.step_pre[rows])
            r.drive[rows] = size * r.low[rows].astype(f32)
            places = places_of(first, CHUNK)
            resets = jnp.where((places == r.bounds[0]) | (places == r.bounds[1]), RESET, 0.0)
            size = size + widened(resets, channels)
            r.step[rows] = size
            return total + jnp.sum(size, axis=0, keepdims=True)

        r.step_sum[...] = jnp.broadcast_to(
            lax.fori_loop(0, chunks, body, jnp.zeros((1, channels), f32)), (8, channels)
        )

    resteps()
    mixer_own.wait()
    cot_own.wait()

    def quarter_rows(index):
        per = quarter // CHUNK
        part = lax.div(index, per)
        at = pl.ds(pl.multiple_of(lax.rem(index, per) * CHUNK, CHUNK), CHUNK)
        return lax.div(part, 2), lax.rem(part, 2), at

    def norm_two(index, total):
        first = pl.multiple_of(index * CHUNK, CHUNK)
        rows = pl.ds(first, CHUNK)
        a, b, at = quarter_rows(index)
        middle = r.stream[rows].astype(f32) + r.mixer[a, b, at].astype(f32)
        scale = lax.rsqrt(mean_square(middle) + 1e-06)
        back, gain = norm_back(middle, scale, r.gains[1:2], r.two_total[a, b, at].astype(f32))
        grad = r.cot_rows[rows].astype(f32) + back
        r.stream_grad[rows] = grad
        r.right_out[rows] = grad.astype(bf16)
        return total + jnp.sum(gain, axis=0, keepdims=True)

    gain_two = lax.fori_loop(0, chunks, norm_two, jnp.zeros((1, width), f32))
    r.flat_move[0] = jnp.zeros_like(r.flat_move[0])
    r.flat_move[0, 1:2] = gain_two
    weights.wait()
    scan_own.wait()
    skips = []
    for j in range(0, channels, 256):
        lanes = slice(j, j + 256)
        gated_grad = dot_rows(r.right_out[own], r.weights[pl.ds(j, 256)])
        gate_pre = r.proj[:, channels + j : channels + j + 256].astype(f32)
        part = sigmoid(gate_pre)
        slope = part * (1.0 + gate_pre * (1.0 - part))
        r.right_in[own, channels + j : channels + j + 256] = (
            gated_grad * r.scan[:, lanes] * slope
        ).astype(bf16)
        grad = gated_grad * gate_pre * part
        r.scan[:, lanes] = grad
        skips.append(jnp.sum(grad * r.low[:, lanes].astype(f32), axis=0, keepdims=True))
    skip_grad = jnp.concatenate(skips, 1)
    weights = load(r.w_in.at[pl.ds(0, channels)], r.weights)
    out_of_own.wait()
    for j in range(0, channels, LANES):
        lanes = slice(j, j + LANES)

        def ended(index, carried, lanes=lanes, block_rates=rates[:, j : j + LANES]):
            first = pl.multiple_of(tokens - UNROLL - index * UNROLL, UNROLL)
            steps, grads = r.step[pl.ds(first, UNROLL), lanes], r.scan[pl.ds(first, UNROLL), lanes]
            for k in reversed(range(UNROLL)):
                decay = jnp.exp2(steps[k : k + 1] * block_rates)
                carried = decay * (widened(r.out_of[first + k], LANES) * grads[k : k + 1] + carried)
            return carried

        r.starts[:, lanes] = lax.fori_loop(
            0, tokens // UNROLL, ended, jnp.zeros((states, LANES), f32)
        )

    chain = handed_on(False, r.starts[...], r.step_sum[0:1], rates, r)
    next(chain)
    gate0.made(two_own, gate_up_own, gate_other)
    gate1.made()
    r.starts[...] = next(chain)
    gate0.go()
    late_kept.wait()
    late.next()
    gate1.go()
    up0.made(up_other)
    first = pl.multiple_of(low * (tokens // 2), tokens // 2)
    mixer_other = swap_shared(
        r.right_out.at[pl.ds(first, tokens // 2)],
        r.right_out.at[pl.ds(tokens + first, tokens // 2)],
    )
    gated_other = swap(r.gated_in.at[:, 1 - mine], r.left_gated.at[:, :, :, other])
    gin_other = swap(
        r.right_in.at[own, pl.ds(channels, channels)],
        r.right_in.at[other, pl.ds(channels, channels)],
    )
    up0.go()
    up1.made().go()

    part_in.wait()
    feed_sums = [summed(r.part, 0, k) for k in range(2)]
    into_own.wait()

    def results():
        totals = lax.fori_loop(
            0, chunks, results_of, tuple(jnp.zeros((1, width), f32) for _ in range(3))
        )
        for number, total in enumerate(totals):
            r.flat_move[0, 3 + number : 4 + number] = total

    def feed_start():
        for item in feed_sums:
            next(item)
        return in_turn(*feed_sums)

    feed = []
    between = [
        lambda: (feed.append(feed_start()), next(feed[0]), gate0.next()),
        lambda: next(feed[0]),
        lambda: (next(feed[0]), gate1.next()),
        lambda: next(feed[0]),
        lambda: (next(feed[0]), up0.next()),
        lambda: (results(), out.made(gated_own, mixer_other, gated_other).go()),
    ]

    def results_of(index, totals):
        rows = pl.ds(pl.multiple_of(index * CHUNK, CHUNK), CHUNK)
        a, b, at = quarter_rows(index)
        mixed, feed = r.mixer[a, b, at].astype(f32), r.total[a, b, at].astype(f32)
        result = r.stream[rows].astype(f32) + mixed + feed
        r.out_rows[rows] = result.astype(bf16)
        return tuple(
            total + jnp.sum(v * v, axis=0, keepdims=True)
            for total, v in zip(totals, (result, mixed, feed))
        )

    r.into_wide[...] = jnp.zeros_like(r.into_wide)
    r.out_wide[...] = jnp.zeros_like(r.out_wide)
    for number, lanes in enumerate(blocks):
        hists[number].wait()
        hist = r.hist.at[number % 2]
        block_rates = rates[:, lanes]

        def walked(index, carry, lanes=lanes, block_rates=block_rates, hist=hist):
            carried, state, total = carry
            first = pl.multiple_of(tokens - UNROLL - index * UNROLL, UNROLL)
            some = pl.ds(first, UNROLL)
            steps, drives, grads = r.step[some, lanes], r.drive[some, lanes], r.scan[some, lanes]
            decay_list, push_list = [None] * UNROLL, [None] * UNROLL
            for k in reversed(range(UNROLL)):
                place = first + k
                grad_row = grads[k : k + 1]
                decay = jnp.exp2(steps[k : k + 1] * block_rates)
                adjoint = r.out_of[place] * grad_row + carried
                carried = decay * adjoint
                r.out_wide[place] = r.out_wide[place] + state * grad_row
                r.into_wide[place] = r.into_wide[place] + adjoint * drives[k : k + 1]
                state = hist[place]
                share = carried * state
                total = total + share * steps[k : k + 1]
                decay_list[k] = jnp.sum(share * block_rates, axis=0, keepdims=True)
                push_list[k] = jnp.sum(r.into[place] * adjoint, axis=0, keepdims=True)
            r.decay_rows[some, :] = jnp.concatenate(decay_list, 0)
            r.push[some, lanes] = jnp.concatenate(push_list, 0)
            return (carried, state, total)

        _, _, total = lax.fori_loop(
            0,
            tokens // UNROLL,
            walked,
            (r.starts[:, lanes], r.last_state[:, lanes], jnp.zeros((states, 128), f32)),
        )
        r.rate_sum[:, lanes] = total * (rates[:, lanes] * LN2)

        def gathered(index, _, lanes=lanes):
            rows = pl.ds(pl.multiple_of(index * CHUNK, CHUNK), CHUNK)
            used, pushed = r.low[rows, lanes].astype(f32), r.push[rows, lanes]
            pre = r.step_pre[rows, lanes]
            grad = (LN2 * r.decay_rows[rows] + pushed * used) * sigmoid(pre)
            r.step_low_grad[rows, lanes] = grad.astype(bf16)
            r.push[rows, lanes] = pushed * softplus(pre) + r.chan[6:7, lanes] * r.scan[rows, lanes]
            return 0

        lax.fori_loop(0, chunks, gathered, 0)
        if number + 2 < len(blocks):
            hists.append(load(r.hist_in.at[:, :, blocks[number + 2]], r.hist.at[number % 2]))
        if number < len(between):
            between[number]()
    for later in between[len(blocks) :]:
        later()

    def norm_grads(index, _):
        first = pl.multiple_of(index * CHUNK, CHUNK)
        rows = pl.ds(first, CHUNK)
        low_part = dot_rows(r.step_low_grad[rows], r.w_dt[...])
        r.raw_move[0, rows] = jnp.concatenate(
            [low_part, narrowed(r.into_wide, first, CHUNK), narrowed(r.out_wide, first, CHUNK)], 1
        )
        return 0

    lax.fori_loop(0, chunks, norm_grads, 0)
    copy = sent(r.raw_move.at[0], r.raw_land.at[0], r.raw_sends, r.raw_receives, 0, "ch", across)
    gin.made(one_own, one_other, gin_other)
    copy.wait()
    r.raw_move[1] = r.raw_move[0] + r.raw_land[0]
    copy = sent(r.raw_move.at[1], r.raw_land.at[1], r.raw_sends, r.raw_receives, 1, "ch", along)
    up1.next()
    copy.wait()

    def raw_back(index, total):
        rows = pl.ds(pl.multiple_of(index * CHUNK, CHUNK), CHUNK)
        grads, raw = r.raw_move[1, rows] + r.raw_land[1, rows], r.raw[rows]
        gains = r.small_gains[...]
        values, sums_to = [], []
        for start, stop, floor in ((0, rank, None), (rank, rank + states, 0.1),
                                   (rank + states, rank + 2 * states, 0.1)):
            value = raw[:, start:stop]
            square = mean_square(value)
            if floor is None:
                scale, free = lax.rsqrt(square + 1e-06), True
            else:
                scale, free = lax.rsqrt(jnp.maximum(square, floor)), square > floor
            back, gain = norm_back(value, scale, gains[:, start:stop], grads[:, start:stop], free)
            values.append(back)
            sums_to.append(jnp.sum(gain, axis=0, keepdims=True))
        norm = raw[:, :rank] * lax.rsqrt(mean_square(raw[:, :rank]) + 1e-06) * gains[:, :rank]
        r.raw_low[rows] = jnp.concatenate(values, 1).astype(bf16)
        r.step_low[rows] = norm.astype(bf16)
        return total + jnp.concatenate(sums_to, 1)

    small = lax.fori_loop(0, chunks, raw_back, jnp.zeros((1, rank + 2 * states), f32))
    r.flat_move[0, 2:3, : rank + 2 * states] = small

    def conv_back(index, total):
        first = pl.multiple_of(index * CHUNK, CHUNK)
        rows = pl.ds(first, CHUNK)
        grad = r.push[rows] + dot_rows(r.raw_low[rows], r.w_x[...])
        grad = grad * silu_slope(r.pre[rows])
        r.grad_pre[rows] = grad
        return total + jnp.sum(grad, axis=0, keepdims=True)

    tap_bias = lax.fori_loop(0, chunks, conv_back, jnp.zeros((1, channels), f32))
    copy = sent(r.grad_pre.at[pl.ds(0, 8)], r.grad_pre.at[pl.ds(tokens, 8)], r.raw_sends,
                r.raw_receives, 2, "seq", previous)
    gin.go()
    r.extended[0:16] = r.halo[...].astype(f32)

    def extend(index, _):
        first = pl.multiple_of(index * CHUNK, CHUNK)
        r.extended[pl.ds(first + 16, CHUNK)] = r.proj[pl.ds(first, CHUNK), :channels].astype(f32)
        return 0

    lax.fori_loop(0, chunks, extend, 0)

    def taps(index, totals):
        first = pl.multiple_of(index * CHUNK, CHUNK)
        places = places_of(first, CHUNK)
        window = r.extended[pl.ds(first, CHUNK + 16)]
        grad = r.grad_pre[pl.ds(first, CHUNK)]
        return tuple(
            totals[k]
            + jnp.sum(
                grad
                * widened(tap_mask(places, r.bounds, 3 - k), channels)
                * window[13 + k : 13 + k + CHUNK],
                axis=0,
                keepdims=True,
            )
            for k in range(4)
        )

    tap_grads = lax.fori_loop(
        0, chunks, taps, tuple(jnp.zeros((1, channels), f32) for _ in range(4))
    )
    copy.wait()

    def conv_in_back(index, _):
        first = pl.multiple_of(index * CHUNK, CHUNK)
        window = r.grad_pre[pl.ds(first, CHUNK + 8)]
        grad = jnp.zeros((CHUNK, channels), f32)
        for k in range(4):
            places = places_of(first + 3 - k, CHUNK)
            mask = jnp.where(
                places < seq_count * tokens, tap_mask(places, r.bounds, 3 - k), 0.0
            )
            grad = grad + r.chan[k : k + 1] * widened(mask, channels) * window[3 - k : 3 - k + CHUNK]
        r.right_in[pl.ds(first, CHUNK), :channels] = grad.astype(bf16)
        return 0

    lax.fori_loop(0, chunks, conv_in_back, 0)
    cin_others = [
        swap(
            r.right_in.at[own, pl.ds(*item.columns)], r.right_in.at[other, pl.ds(*item.columns)]
        )
        for item in cins
    ]

    def small_columns():
        narrow = r.w_x.shape[1]
        pack = r.step
        pack[0:narrow] = lax.dot_general(
            r.raw_low[...], r.low[...], (((0,), (0,)), ((), ())), preferred_element_type=f32
        )
        pack[narrow : narrow + rank] = lax.dot_general(
            r.step_low[...], r.step_low_grad[...], (((0,), (0,)), ((), ())),
            preferred_element_type=f32,
        )
        at = narrow + rank
        pack[at : at + states] = r.rate_sum[...]
        at += states
        bias = jnp.sum(r.step_low_grad[...].astype(f32), axis=0, keepdims=True)
        pack[at : at + 8] = jnp.concatenate(
            [*tap_grads, tap_bias, bias, skip_grad, jnp.zeros((1, channels), f32)], 0
        )
        at += 8
        pack[at:] = jnp.zeros((pack.shape[0] - at, channels), f32)
        turned = pack[...].T
        r.small_work[0][...] = turned.reshape(r.small_work[0].shape)

    def small_summed():
        for k, bit in enumerate(bits):
            side, partner = flipped(me, bit)
            work, away, land = r.small_work[k], r.small_away[k], r.small_land[k]
            away[...] = work[:, 1 - side].astype(bf16)
            copy = sent(away, land, r.last_sends, r.last_receives, k, "seq", partner)
            yield
            copy.wait()
            total = work[:, side] + land[...].astype(f32)
            target = r.small_work[k + 1] if k + 1 < len(bits) else r.small_out
            target[...] = total.reshape(target.shape)
        yield

    one_sums = [summed(r.part, 8, k) for k in range(2)]
    for number in range(width // channels):
        weights.wait()

        def one_part(index, _, first=number * channels):
            at = pl.multiple_of(index * 256, 256)
            product = dot_rows(r.right_in[own], r.weights[pl.ds(at, 256)]).astype(bf16)
            for k in range(4):
                r.part[k // 2, k % 2, :, pl.ds(first + at, 256)] = product[
                    k * quarter : (k + 1) * quarter
                ]
            return 0

        lax.fori_loop(0, channels // 256, one_part, 0)
        next(one_sums[number])
        if (number + 1) * channels < width:
            weights = load(r.w_in.at[pl.ds((number + 1) * channels, channels)], r.weights)
    one_sum = in_turn(*one_sums)
    next(one_sum)

    def gain_part(index, total):
        rows = pl.ds(pl.multiple_of(index * CHUNK, CHUNK), CHUNK)
        a, b, at = quarter_rows(index)
        value = r.stream[rows].astype(f32)
        scale = lax.rsqrt(mean_square(value) + 1e-06)
        return total + jnp.sum(r.part[a, b, at].astype(f32) * value * scale, axis=0, keepdims=True)

    r.flat_move[0] = r.flat_move[0] * 0.25
    r.flat_move[0, 0:1] = lax.fori_loop(0, chunks, gain_part, jnp.zeros((1, width), f32))
    ways = [("ch", across), ("ch", along)] + [("seq", flipped(me, bit)[1]) for bit in bits]

    def flat_summed():
        for k, (axis, partner) in enumerate(ways):
            copy = sent(r.flat_move.at[k], r.flat_land.at[k], r.flat_sends, r.flat_receives, k,
                        axis, partner)
            yield
            copy.wait()
            target = r.flat_move.at[k + 1] if k + 1 < len(ways) else r.flat_out
            target[...] = r.flat_move[k] + r.flat_land[k]
        yield

    flat_sum = flat_summed()
    next(flat_sum)

    cins[0].made(cin_others[0]).go()
    next(one_sum)
    next(flat_sum)
    out.next()
    cins[1].made(cin_others[1]).go()
    next(one_sum)
    next(flat_sum)
    small_columns()
    small_sum = small_summed()
    next(small_sum)
    next(one_sum)
    gin.next()
    next(flat_sum)
    next(one_sum)

    def norm_one(index, _):
        rows = pl.ds(pl.multiple_of(index * CHUNK, CHUNK), CHUNK)
        a, b, at = quarter_rows(index)
        value = r.stream[rows].astype(f32)
        scale = lax.rsqrt(mean_square(value) + 1e-06)
        back, _ = norm_back(value, scale, r.gains[0:1], r.total[a, b, at].astype(f32))
        r.stream_grad[rows] = r.stream_grad[rows] + back
        return 0

    lax.fori_loop(0, chunks, norm_one, 0)
    cins[0].next()
    next(small_sum)
    next(flat_sum)
    cins[1].next()
    down_kept.wait()
    for item in (down, late, *quarters):
        item.next()
    next(small_sum)
    for waiting in (flat_sum, small_sum):
        for _ in waiting:
            pass
    pending = [out, gin, *cins, down, late, *quarters]
    for _ in range(len(bits)):
        for item in pending:
            item.next()
    for item in pending:
        item.written.wait()


def backward(ins, hbm_ins, count, ident):
    bits = bits_of(count)
    n_bits = len(bits) - 1
    tokens, width = ins["stream"].shape
    channels, rank, states = ins["low"].shape[1], ins["w_dt"].shape[0], ins["logs"].shape[0]
    hid = hbm_ins["right_two_in"].shape[1] // 2
    narrow = ins["w_x"].shape[1]
    half, quarter = count // 2, tokens // 4
    rows_in, rows_out, rows_down = width // count, channels // count, hid // count
    rows = pltpu.VMEM((tokens, channels), f32)

    def low(*dims):
        return pltpu.VMEM(dims, bf16)

    def full(*dims):
        return pltpu.VMEM(dims, f32)

    outs = dict(
        stream_grad=(shape_of(tokens, width), VMEM),
        out_rows=(shape_of(tokens, width, dtype=bf16), VMEM),
        small_out=(shape_of(rows_out, tokens), VMEM),
        flat_out=(shape_of(8, width), VMEM),
        down_out=(shape_of(rows_down, width), ANY),
        gate_out=(shape_of(rows_in, hid), ANY),
        up_out=(shape_of(rows_in, hid), ANY),
        out_out=(shape_of(rows_out, width), ANY),
        gin_out=(shape_of(rows_in, channels), ANY),
        cin_out=(shape_of(rows_in, channels), ANY),
    )
    quads = count // 4

    def unit(part, columns):
        lands = [low(half >> (k + 1), part, columns) for k in range(n_bits)]
        return [low(half // 2, part, columns), *lands, full(half // 2, part, columns)]

    def sems(size):
        return pltpu.SemaphoreType.DMA((size,))

    halves = [count >> (k + 1) for k in range(len(bits))]
    scratch = dict(
        left_two=low(quads, 2, rows_in, 2 * tokens),
        left_one=low(quads, 2, rows_in, 2 * tokens),
        left_gated=low(quads, 2, rows_out, 2 * tokens),
        cot_rows=low(tokens, width),
        right_two=low(2 * tokens, 2 * hid),
        right_out=low(2 * tokens, width),
        right_in=low(2 * tokens, 2 * channels),
        mixer=low(2, 2, quarter, width),
        weights=low(channels, width),
        scan=rows,
        step=rows,
        drive=rows,
        push=rows,
        decay_rows=full(tokens, 128),
        into=full(tokens, states, 128),
        out_of=full(tokens, states, 128),
        into_wide=full(tokens, states, 128),
        out_wide=full(tokens, states, 128),
        hist=full(2, tokens, states, 128),
        step_sum=full(8, channels),
        starts=full(states, channels),
        rate_sum=full(states, channels),
        step_low_grad=low(tokens, channels),
        **handing(count, states, channels),
        part=low(2, 2, quarter, width),
        total=low(2, 2, quarter, width),
        first_land=low(2, quarter, width),
        second_land=low(quarter, width),
        second_move=low(quarter, width),
        raw_move=full(2, tokens, narrow),
        raw_land=full(2, tokens, narrow),
        raw_low=low(tokens, narrow),
        step_low=low(tokens, rank),
        grad_pre=full(tokens + 8, channels),
        extended=full(tokens + 16, channels),
        flat_move=full(2 + len(bits), 8, width),
        flat_land=full(2 + len(bits), 8, width),
        small_work=[full(size, 2, rows_out, tokens) for size in halves],
        small_away=[low(size, rows_out, tokens) for size in halves],
        small_land=[low(size, rows_out, tokens) for size in halves],
        down=unit(rows_down, width // 2),
        late=unit(rows_down, width // 2),
        gate0=unit(rows_in, hid // 2),
        gate1=unit(rows_in, hid // 2),
        up0=unit(rows_in, hid // 2),
        up1=unit(rows_in, hid // 2),
        out=unit(rows_out, width),
        gin=unit(rows_in, channels),
        cin0=unit(rows_in, channels // 2),
        cin1=unit(rows_in, channels // 2),
        load_sems=sems(32),
        write_sems=sems(10),
        pair_sends=sems(8),
        pair_receives=sems(8),
        shared_sends=sems(4),
        shared_receives=sems(4),
        unit_sends=sems(10 * n_bits),
        unit_receives=sems(10 * n_bits),
        sum_sends=sems(16),
        sum_receives=sems(16),
        raw_sends=sems(3),
        raw_receives=sems(3),
        last_sends=sems(len(bits)),
        last_receives=sems(len(bits)),
        flat_sends=sems(2 + len(bits)),
        flat_receives=sems(2 + len(bits)),
    )
    names, shapes = [(name, 0) for name in [*ins, *hbm_ins, *outs]], []
    for name, held in scratch.items():
        listed = isinstance(held, list)
        names.append((name, len(held) if listed else 0))
        shapes += held if listed else [held]
    places = [VMEM for _ in ins]
    places[0] = pl.BlockSpec(memory_space=pltpu.SMEM)
    made = pl.pallas_call(
        functools.partial(backward_kernel, bits, names),
        out_shape=[shape for shape, _ in outs.values()],
        in_specs=places + [ANY] * len(hbm_ins),
        out_specs=[spec for _, spec in outs.values()],
        scratch_shapes=shapes,
        compiler_params=pltpu.CompilerParams(
            collective_id=ident, has_side_effects=True, vmem_limit_bytes=63 * 2**20
        ),
        name="block_backward",
    )(*ins.values(), *hbm_ins.values())
    return types.SimpleNamespace(**dict(zip(outs, made)))


def finish_kernel(cells, names, *refs):
    r = named(names, refs)
    me = lax.axis_index("seq")
    moves = [
        (r.out_rows, r.out), (r.stream_grad, r.stream), (r.out_out, r.w_out),
        (r.down_out, r.w_down), (r.gate_out, r.w_gate_up.at[:, 0]),
        (r.up_out, r.w_gate_up.at[:, 1]), (r.cin_out, r.w_in.at[:, 0]),
        (r.gin_out, r.w_in.at[:, 1]),
    ]
    little = [(r.small_out, r.small_here), (r.flat_out, r.flat_here)]
    loads = [
        pltpu.make_async_copy(source, here, r.sems.at[k])
        for k, (source, here) in enumerate(
            [*little, *((source, here) for (source, _), here in zip(moves, r.here))]
        )
    ]
    for copy in loads:
        copy.start()
    copies = []
    for k, (_, target) in enumerate(moves):
        loads[k + 2].wait()
        copy = pltpu.make_async_copy(r.here[k], target, r.out_sems.at[k])
        copy.start()
        copies.append(copy)
    for copy in loads[:2]:
        copy.wait()
    narrow, rank, states = r.x.shape[1], r.dt.shape[0], r.decay.shape[0]
    small = r.small_here[...]
    r.x[...] = small[:, :narrow]
    turned = small[:, narrow:].T
    r.dt[...] = turned[:rank]
    r.decay[...] = turned[rank : rank + states]
    r.chan[...] = turned[rank + states : rank + states + 7]
    flat = r.flat_here[...]
    width = flat.shape[1]
    count = width // r.gains.shape[1]
    gains, tail = jnp.zeros(r.gains.shape, f32), jnp.zeros(r.small.shape, f32)
    for k in range(count):
        gain_at, tail_at = k * r.gains.shape[1], k * r.small.shape[1]
        mine = me == k
        gains = gains + jnp.where(mine, flat[0:2, gain_at : gain_at + r.gains.shape[1]], 0.0)
        tail = tail + jnp.where(mine, flat[2:3, tail_at : tail_at + r.small.shape[1]], 0.0)
    r.gains[...] = gains
    r.small[...] = tail
    totals = [jnp.sum(flat[3 + k : 4 + k], axis=1, keepdims=True) for k in range(3)]
    r.rms[...] = jnp.sqrt(jnp.concatenate(totals, 1) / cells)
    for copy in copies:
        copy.wait()


def finish(made, cells, narrow, rank, states, count):
    rows_out = made.small_out.shape[0]
    width = made.flat_out.shape[1]
    rows_in, hid = made.gate_out.shape
    channels = made.cin_out.shape[1]
    outs = dict(
        out=shape_of(*made.out_rows.shape, dtype=bf16),
        stream=shape_of(*made.stream_grad.shape),
        gains=shape_of(2, width // count),
        w_in=shape_of(rows_in, 2, channels),
        chan=shape_of(7, rows_out),
        decay=shape_of(states, rows_out),
        x=shape_of(rows_out, narrow),
        small=shape_of(1, narrow // count),
        dt=shape_of(rank, rows_out),
        w_out=shape_of(*made.out_out.shape),
        w_gate_up=shape_of(rows_in, 2, hid),
        w_down=shape_of(*made.down_out.shape),
        rms=shape_of(1, 3),
    )
    ins = vars(made)
    held = [
        made.out_rows, made.stream_grad, made.out_out, made.down_out, made.gate_out, made.up_out,
        made.cin_out, made.gin_out, made.small_out, made.flat_out,
    ]
    places = [pltpu.VMEM(item.shape, item.dtype) for item in held]
    names = [(name, 0) for name in [*ins, *outs]]
    rest = dict(here=8, small_here=0, flat_here=0, sems=0, out_sems=0)
    names += list(rest.items())
    big = {id(outs[name]) for name in ("out", "stream", "w_in", "w_out", "w_gate_up", "w_down")}
    done = pl.pallas_call(
        functools.partial(finish_kernel, cells, names),
        out_shape=list(outs.values()),
        in_specs=[ANY for _ in ins],
        out_specs=[ANY if id(item) in big else VMEM for item in outs.values()],
        scratch_shapes=[*places, pltpu.SemaphoreType.DMA((10,)), pltpu.SemaphoreType.DMA((8,))],
        compiler_params=pltpu.CompilerParams(vmem_limit_bytes=62 * 2**20),
        name="finish",
    )(*ins.values())
    out, stream, gains, w_in, chan, decay, x, small, dt, w_out, w_gate_up, w_down, rms = done
    return (
        out, stream, gains, w_in, chan, decay, x, small.reshape(-1), dt, w_out, w_gate_up, w_down,
        rms.reshape(-1),
    )


def local(
    seq_count,
    stream,
    doc_bounds,
    norm_gains,
    w_in,
    chan_vectors,
    decay_logs,
    w_x,
    small_gains,
    w_dt,
    w_out,
    w_gate_up,
    w_down,
    cotangent,
):
    tokens, width = stream.shape
    rank, (states, channels) = w_dt.shape[0], decay_logs.shape

    def turned(values):
        return values.T.reshape(seq_count // 4, 2, 2, values.shape[1] // seq_count, tokens)

    w_in_flat = w_in.reshape(width, 2 * channels)
    (
        in_proj, one_in, halo, pre_conv, conv_low, raw_proj, step_pre, into, out_of, scan_out, gated_low,
        last_state, mixer_low, before, one_came, cot_came, w_gate_up_flat,
    ) = mixer_forward(
        doc_bounds, stream, norm_gains, chan_vectors, decay_logs, w_x, small_gains[None], w_dt,
        w_out, w_in_flat, cotangent, w_gate_up, seq_count, 1,
    )
    mid = feed_forward(
        dict(stream=stream, mixer=mixer_low, gains=norm_gains),
        dict(
            cot=cotangent, cot_came=cot_came, w_gate_up_in=w_gate_up_flat,
            w_down_in=w_down,
        ),
        seq_count,
        3,
    )
    made = backward(
        dict(
            bounds=doc_bounds, stream=stream, gains=norm_gains, two_total=mid.total,
            proj=in_proj, halo=halo,
            pre=pre_conv, low=conv_low, raw=raw_proj, step_pre=step_pre, last_state=last_state,
            chan=chan_vectors, logs=decay_logs, w_x=w_x, w_dt=w_dt, small_gains=small_gains[None],
        ),
        dict(
            feed_part=mid.feed_part, left_two_in=mid.left_two, right_two_in=mid.right_two,
            down_away_in=mid.down_away, down_kept_in=mid.down_kept,
            late_away_in=mid.late_away, late_kept_in=mid.late_kept, mixer_in=mixer_low,
            cot=cotangent, gated_in=turned(gated_low), one_in=one_in,
            one_came=one_came, w_out=w_out, w_in=w_in_flat, scan_in=scan_out, into_in=into,
            out_of_in=out_of, hist_in=before,
        ),
        seq_count,
        2,
    )
    return finish(
        made, tokens * seq_count * width, w_x.shape[1], rank, states, seq_count
    )


def solution(mesh):
    in_specs = (
        P("seq", None),
        P(),
        P(),
        P(None, None, "ch"),
        P(None, "ch"),
        P(None, "ch"),
        P("ch", None),
        P(),
        P(None, "ch"),
        P("ch", None),
        P(None, None, "ch"),
        P("ch", None),
        P("seq", None),
    )
    out_specs = (
        P("seq", None),
        P("seq", None),
        P(None, "seq"),
        P("seq", None, "ch"),
        P(None, ("ch", "seq")),
        P(None, ("ch", "seq")),
        P(("ch", "seq"), None),
        P("seq"),
        P(None, ("ch", "seq")),
        P(("ch", "seq"), None),
        P("seq", None, "ch"),
        P(("ch", "seq"), None),
        P(),
    )
    return jax.shard_map(
        functools.partial(local, mesh.shape["seq"]),
        mesh=mesh,
        in_specs=in_specs,
        out_specs=out_specs,
        check_vma=False,
    )
```

```python
import functools
import math
import types

import jax
import jax.numpy as jnp
from jax import lax
from jax.experimental import pallas as pl
from jax.experimental.pallas import tpu as pltpu
from jax.sharding import PartitionSpec as P

f32 = jnp.float32
bf16 = jnp.bfloat16
LOG2E = math.log2(math.e)
LN2 = math.log(2.0)
RESET = 1e30
UNROLL = 8
LANES = 256
VMEM = pl.BlockSpec(memory_space=pltpu.VMEM)


def shape_of(*dims, dtype=f32):
    return jax.ShapeDtypeStruct(dims, dtype)


def cost(us):
    return pl.CostEstimate(flops=int(us * 1e9), bytes_accessed=int(us * 1e6), transcendentals=0)


def widened(column, width):
    return jnp.concatenate([column] * (width // 128), 1)


ANY = pl.BlockSpec(memory_space=pl.ANY)


def sent(source, target, sends, receives, slot, axis, partner):
    copy = pltpu.make_async_remote_copy(
        src_ref=source,
        dst_ref=target,
        send_sem=sends.at[slot],
        recv_sem=receives.at[slot],
        device_id={axis: partner},
        device_id_type=pl.DeviceIdType.MESH,
    )
    copy.start()
    return copy


def bits_of(count):
    return [1 << k for k in range(count.bit_length() - 1)]


def flipped(me, bit):
    mine = lax.rem(me // bit, 2)
    return mine, me + bit - 2 * bit * mine


CHUNK = 32


def sigmoid(values):
    return 1.0 / (1.0 + jnp.exp(-values))


def softplus(values):
    return jnp.maximum(values, 0.0) + jnp.log1p(jnp.exp(-jnp.abs(values)))


def row_doc(places, bounds):
    return (places >= bounds[0]).astype(jnp.int32) + (places >= bounds[1]).astype(jnp.int32)


def tap_mask(places, bounds, offset):
    source = places - offset
    same = row_doc(source, bounds) == row_doc(places, bounds)
    return jnp.where((source >= 0) & same, 1.0, 0.0)


def mean_square(values):
    return jnp.mean(values * values, axis=-1, keepdims=True)


def three_norms(raw, gains, rank, states):
    low, mid, high = raw[:, :rank], raw[:, rank : rank + states], raw[:, rank + states :]
    low_scale = lax.rsqrt(mean_square(low) + 1e-06)
    mid_scale = lax.rsqrt(jnp.maximum(mean_square(mid), 0.1))
    high_scale = lax.rsqrt(jnp.maximum(mean_square(high), 0.1))
    return (
        low * low_scale * gains[:, :rank],
        mid * mid_scale * gains[:, rank : rank + states],
        high * high_scale * gains[:, rank + states :],
    )


def widen(values, wide, first, count):
    states = values.shape[1]
    eye = (
        lax.broadcasted_iota(jnp.int32, (states, states), 0)
        == lax.broadcasted_iota(jnp.int32, (states, states), 1)
    ).astype(f32)
    spread = jnp.sum(values[:, None, :] * eye[None], axis=-1, keepdims=True)
    wide[pl.ds(first, count)] = jnp.broadcast_to(spread, (count, states, 128))


def greeted(axis_partners):
    barrier = pltpu.get_barrier_semaphore()
    for axis, partner in axis_partners:
        pl.semaphore_signal(
            barrier, inc=1, device_id={axis: partner}, device_id_type=pl.DeviceIdType.MESH
        )
    pl.semaphore_wait(barrier, len(axis_partners))


def handed_on(forward, state, steps, rates, r):
    me, count = lax.axis_index("seq"), r.state_land.shape[0] + 1
    r.state_move[...] = state.astype(bf16)
    r.steps_move[...] = steps
    copies = []
    for k in range(1, count):
        to = lax.rem(me + k, count)
        for source, land, sends, receives in (
            (r.state_move, r.state_land, r.state_sends, r.state_receives),
            (r.steps_move, r.steps_land, r.steps_sends, r.steps_receives),
        ):
            copies.append(sent(source, land.at[k - 1], sends, receives, k - 1, "seq", to))
    yield
    for copy in copies:
        copy.wait()
    total = jnp.zeros_like(state)
    passed = jnp.zeros_like(steps)
    for k in range(1, count):
        slot = k - 1 if forward else count - k - 1
        valid = (me >= k) if forward else (me + k < count)
        term = jnp.exp2(rates * passed) * r.state_land[slot].astype(f32)
        total = total + jnp.where(valid, term, 0.0)
        passed = passed + jnp.where(valid, r.steps_land[slot], 0.0)
    yield total


def handing(count, states, channels):
    sems = pltpu.SemaphoreType.DMA((count - 1,))
    return dict(
        state_move=pltpu.VMEM((states, channels), bf16),
        steps_move=pltpu.VMEM((1, channels), f32),
        state_land=pltpu.VMEM((count - 1, states, channels), bf16),
        steps_land=pltpu.VMEM((count - 1, 1, channels), f32),
        state_sends=sems,
        state_receives=sems,
        steps_sends=sems,
        steps_receives=sems,
    )


def turn(values, first, turned):
    rows = turned.shape[3]
    across_rows = values.T
    for k in range(values.shape[1] // rows):
        owner = first // rows + k
        turned[owner // 4, (owner // 2) % 2, owner % 2] = across_rows[k * rows : (k + 1) * rows]


def forward_kernel(
    bits, bounds, stream, norm_gains, chan, logs, w_x, gains, w_dt, w_out, w_in, cot, w_pairs,
    proj, one_in, halo, pre_out, low_out, raw_out, step_pre_out, into, out_of, scan_out, gated_out, last_state,
    mixer, turned_gate, hist_out, one_came, cot_came, w_flat,
    extended, raw_move, raw_land, step, drive, starts, part, first_land,
    second_move, second_land, hist, sends, receives, hist_sem, shared_sends, shared_receives,
    sum_sends, sum_receives, weights, normed, weight_sem, pairs, flat, pair_sems, *handed,
):
    tokens, channels = low_out.shape
    rank, states = w_dt.shape[0], logs.shape[0]
    chunks = tokens // CHUNK
    width = stream.shape[1]
    loads = []
    for k in range(width // 512):
        cols = pl.ds(k * 512, 512)
        copy = pltpu.make_async_copy(w_in.at[:, cols], weights.at[:, cols], weight_sem.at[k])
        copy.start()
        loads.append(copy)
    pair_copies = [pltpu.make_async_copy(w_pairs, pairs, pair_sems.at[0])]
    pair_copies[0].start()
    ahead = [0]

    def relay(count):
        first = ahead[0]
        ahead[0] = last = min(first + count, width // CHUNK)
        if first == 0:
            pair_copies.pop().wait()
        hid = pairs.shape[2]

        def laid(index, _):
            rows = pl.ds(pl.multiple_of(index * CHUNK, CHUNK), CHUNK)
            flat[rows, 0:hid] = pairs[rows, 0, :]
            flat[rows, hid:] = pairs[rows, 1, :]
            return 0

        lax.fori_loop(first, last, laid, 0)
        rows = pl.ds(first * CHUNK, (last - first) * CHUNK)
        copy = pltpu.make_async_copy(
            flat.at[rows], w_flat.at[rows], pair_sems.at[1 + len(pair_copies)]
        )
        copy.start()
        pair_copies.append(copy)

    ch_me, me = lax.axis_index("ch"), lax.axis_index("seq")
    seq_count = 1 << len(bits)
    low, across = flipped(ch_me, 1)
    high, along = flipped(ch_me, 2)
    following = lax.rem(me + 1, seq_count)
    greeted(
        [("ch", across), ("ch", along)]
        + [("seq", lax.rem(me + k, seq_count)) for k in range(1, seq_count)]
    )
    def norm_one(index, _):
        rows = pl.ds(pl.multiple_of(index * CHUNK, CHUNK), CHUNK)
        value = stream[rows].astype(f32)
        scale = lax.rsqrt(mean_square(value) + 1e-06)
        normed[rows] = (value * scale * norm_gains[0:1]).astype(bf16)
        return 0

    lax.fori_loop(0, chunks, norm_one, 0)

    def project(index, _):
        cols = pl.ds(pl.multiple_of(index * 256, 256), 256)
        proj[:, cols] = jnp.dot(
            normed[...], weights[:, cols], preferred_element_type=f32
        ).astype(bf16)
        return 0

    for copy in loads:
        copy.wait()
    lax.fori_loop(0, channels // 256, project, 0)
    halo_copy = sent(
        proj.at[pl.ds(tokens - 16, 16), pl.ds(0, channels)], halo, sends, receives, 0, "seq",
        following,
    )
    for at in range(0, width, 384):
        turn(normed[:, at : at + 384], at, one_in)
    mine, pair = flipped(me, bits[1])
    half = one_in.shape[0] // 2
    some = pl.ds(low * half, half)
    at = pl.ds(pl.multiple_of(low * (tokens // 2), tokens // 2), tokens // 2)
    shared = [
        (one_in.at[some, 1 - mine], one_came.at[some]),
        (cot.at[at], cot_came.at[at]),
    ]
    shared_copies = [
        sent(source, target, shared_sends, shared_receives, k, "seq", pair)
        for k, (source, target) in enumerate(shared)
    ]
    lax.fori_loop(channels // 256, 2 * channels // 256, project, 0)
    rates = -jnp.exp(logs[...]) * LOG2E

    def spread(index, _):
        first = pl.multiple_of(index * CHUNK, CHUNK)
        extended[pl.ds(first + 16, CHUNK)] = proj[pl.ds(first, CHUNK), :channels].astype(f32)
        return 0

    lax.fori_loop(0, chunks, spread, 0)

    def convolved(index, _):
        first = pl.multiple_of(index * CHUNK, CHUNK)
        places = me * tokens + first + lax.broadcasted_iota(jnp.int32, (CHUNK, 128), 0)
        window = extended[pl.ds(first, CHUNK + 16)]
        summed = chan[4:5]
        for k in range(4):
            mask = widened(tap_mask(places, bounds, 3 - k), channels)
            summed = summed + chan[k : k + 1] * window[13 + k : 13 + k + CHUNK] * mask
        pre_out[pl.ds(first, CHUNK)] = summed
        low_out[pl.ds(first, CHUNK)] = (summed * sigmoid(summed)).astype(bf16)
        return 0

    lax.fori_loop(1, chunks, convolved, 0)
    halo_copy.wait()
    extended[0:16] = halo[...].astype(f32)
    convolved(0, 0)
    raw_move[0] = jnp.dot(low_out[...], w_x[...], preferred_element_type=f32)
    copy = sent(raw_move.at[0], raw_land.at[0], sends, receives, 1, "ch", across)
    relay(4)
    copy.wait()
    raw_move[1] = raw_move[0] + raw_land[0]
    copy = sent(raw_move.at[1], raw_land.at[1], sends, receives, 2, "ch", along)
    relay(9)
    copy.wait()

    def stepped(index, total):
        first = pl.multiple_of(index * CHUNK, CHUNK)
        rows = pl.ds(first, CHUNK)
        raw = raw_move[1, rows] + raw_land[1, rows]
        raw_out[rows] = raw
        step_norm, input_norm, output_norm = three_norms(raw, gains[...], rank, states)
        widen(input_norm, into, first, CHUNK)
        widen(output_norm, out_of, first, CHUNK)
        pre = (
            jnp.dot(step_norm.astype(bf16), w_dt[...], preferred_element_type=f32) + chan[5:6]
        )
        step_pre_out[rows] = pre
        size = softplus(pre)
        drive[rows] = size * low_out[rows].astype(f32)
        places = me * tokens + first + lax.broadcasted_iota(jnp.int32, (CHUNK, 128), 0)
        resets = jnp.where((places == bounds[0]) | (places == bounds[1]), RESET, 0.0)
        size = size + widened(resets, channels)
        step[rows] = size
        return total + jnp.sum(size, axis=0, keepdims=True)

    total = lax.fori_loop(0, chunks, stepped, jnp.zeros((1, channels), f32))
    blocks = [slice(j, j + LANES) for j in range(0, channels, LANES)]
    for lanes in blocks:
        block_rates = rates[:, lanes]

        def ended(index, state, lanes=lanes, block_rates=block_rates):
            first = pl.multiple_of(index * UNROLL, UNROLL)
            steps, drives = step[pl.ds(first, UNROLL), lanes], drive[pl.ds(first, UNROLL), lanes]
            for k in range(UNROLL):
                decay = jnp.exp2(steps[k : k + 1] * block_rates)
                state = decay * state + widened(into[first + k], LANES) * drives[k : k + 1]
            return state

        starts[:, lanes] = lax.fori_loop(
            0, tokens // UNROLL, ended, jnp.zeros((states, LANES), f32)
        )
    hand = types.SimpleNamespace(**dict(zip(handing(2, 8, 128), handed)))
    handed_in = handed_on(True, starts[...], total, rates, hand)
    next(handed_in)
    relay(14)
    starts[...] = next(handed_in)
    hist_copies = []
    for number, lanes in enumerate(blocks):
        block_rates = rates[:, lanes]
        skip = chan[6:7, lanes]

        def walked(index, state, lanes=lanes, block_rates=block_rates, skip=skip):
            first = pl.multiple_of(index * UNROLL, UNROLL)
            steps, drives = step[pl.ds(first, UNROLL), lanes], drive[pl.ds(first, UNROLL), lanes]
            rows = []
            for k in range(UNROLL):
                hist[first + k, :, lanes] = state
                decay = jnp.exp2(steps[k : k + 1] * block_rates)
                state = decay * state + widened(into[first + k], LANES) * drives[k : k + 1]
                rows.append(
                    jnp.sum(widened(out_of[first + k], LANES) * state, axis=0, keepdims=True)
                )
            scan_out[pl.ds(first, UNROLL), lanes] = jnp.concatenate(rows, 0)
            return state

        last_state[:, lanes] = lax.fori_loop(0, tokens // UNROLL, walked, starts[:, lanes])
        copy = pltpu.make_async_copy(
            hist.at[:, :, lanes], hist_out.at[:, :, lanes], hist_sem.at[number]
        )
        copy.start()
        hist_copies.append(copy)

    def gate(index, _):
        first = pl.multiple_of(index * CHUNK, CHUNK)
        rows = pl.ds(first, CHUNK)
        scanned = scan_out[rows] + chan[6:7] * low_out[rows].astype(f32)
        scan_out[rows] = scanned
        gate_pre = proj[rows, channels:].astype(f32)
        gated_out[rows] = (scanned * gate_pre * sigmoid(gate_pre)).astype(bf16)
        return 0

    lax.fori_loop(0, chunks, gate, 0)
    quarter = tokens // 4
    for k, (_, target) in enumerate(shared):
        shared_copies[k].wait()
        shared_copies[k] = sent(
            target, target, shared_sends, shared_receives, 2 + k, "ch", across
        )

    def mixed(index, _):
        first = pl.multiple_of(index * 256, 256)
        product = jnp.dot(
            gated_out[...], w_out[:, pl.ds(first, 256)], preferred_element_type=f32
        ).astype(bf16)
        for k in range(4):
            part[k // 2, k % 2, :, pl.ds(first, 256)] = product[k * quarter : (k + 1) * quarter]
        return 0

    held = types.SimpleNamespace(
        first_land=first_land, second_land=second_land, second_move=second_move, total=mixer,
        sum_sends=sum_sends, sum_receives=sum_receives,
    )
    sums = [four_summed(held, (low, across, high, along), part, 0, k) for k in range(2)]
    for k, item in enumerate(sums):
        lax.fori_loop(k * width // 512, (k + 1) * width // 512, mixed, 0)
        next(item)
    turns = in_turn(*sums)
    for at in range(0, channels, 384):
        turn(gated_out[:, at : at + 384], at, turned_gate)
    for count in (3, 8, 8, width):
        next(turns)
        if ahead[0] < width // CHUNK:
            relay(count)
    next(turns)
    for copy in hist_copies + shared_copies + pair_copies:
        copy.wait()


def mixer_forward(
    bounds, stream, norm_gains, chan, logs, w_x, gains, w_dt, w_out, w_in, cot, w_pairs, count,
    ident,
):
    bits = bits_of(count)
    tokens, channels = stream.shape[0], w_out.shape[0]
    states, rank, width = logs.shape[0], w_dt.shape[0], w_out.shape[1]
    quarter, narrow = tokens // 4, w_x.shape[1]
    rows = shape_of(tokens, channels)
    low_rows = shape_of(tokens, channels, dtype=bf16)
    wide = shape_of(tokens, states, 128)
    raws = pltpu.VMEM((2, tokens, narrow), f32)
    out = pl.pallas_call(
        functools.partial(forward_kernel, bits),
        out_shape=[
            shape_of(tokens, 2 * channels, dtype=bf16),
            shape_of(count // 4, 2, 2, width // count, tokens, dtype=bf16),
            shape_of(16, channels, dtype=bf16), rows, low_rows, shape_of(tokens, narrow), rows,
            wide, wide, rows, low_rows, shape_of(states, channels),
            shape_of(2, 2, quarter, width, dtype=bf16),
            shape_of(count // 4, 2, 2, channels // count, tokens, dtype=bf16),
            shape_of(tokens, states, channels),
            shape_of(count // 4, 2, width // count, tokens, dtype=bf16),
            shape_of(tokens, width, dtype=bf16),
            shape_of(width, 2 * w_pairs.shape[2], dtype=bf16),
        ],
        in_specs=[pl.BlockSpec(memory_space=pltpu.SMEM)] + [VMEM] * 8 + [ANY] * 3,
        out_specs=[VMEM] * 14 + [ANY] * 4,
        scratch_shapes=[
            pltpu.VMEM((tokens + 16, channels), f32), raws, raws,
            pltpu.VMEM((tokens, channels), f32), pltpu.VMEM((tokens, channels), f32),
            pltpu.VMEM((states, channels), f32),
            pltpu.VMEM((2, 2, quarter, width), bf16), pltpu.VMEM((2, quarter, width), bf16),
            pltpu.VMEM((quarter, width), bf16), pltpu.VMEM((quarter, width), bf16),
            pltpu.VMEM((tokens, states, channels), f32),
            pltpu.SemaphoreType.DMA((3,)), pltpu.SemaphoreType.DMA((3,)),
            pltpu.SemaphoreType.DMA((channels // LANES,)),
            pltpu.SemaphoreType.DMA((4,)), pltpu.SemaphoreType.DMA((4,)),
            pltpu.SemaphoreType.DMA((8,)), pltpu.SemaphoreType.DMA((8,)),
            pltpu.VMEM(w_in.shape, bf16), pltpu.VMEM((tokens, width), bf16),
            pltpu.SemaphoreType.DMA((width // 512,)),
            pltpu.VMEM(w_pairs.shape, bf16), pltpu.VMEM((width, 2 * w_pairs.shape[2]), bf16),
            pltpu.SemaphoreType.DMA((9,)),
            *handing(count, states, channels).values(),
        ],
        compiler_params=pltpu.CompilerParams(
            collective_id=ident, has_side_effects=True, vmem_limit_bytes=56 * 2**20
        ),
        cost_estimate=cost(6),
        name="mixer_forward",
    )(bounds, stream, norm_gains, chan, logs, w_x, gains, w_dt, w_out, w_in, cot, w_pairs)
    return out


class Unit:
    def __init__(self, left, right, columns, refs, sends, receives, slot, bits, result):
        self.left, self.right, self.columns = left, right, columns
        away, *self.land, self.kept = refs
        self.away = [away.at[pl.ds(0, land.shape[0])] for land in self.land]
        self.sends, self.receives, self.slot, self.bits = sends, receives, slot, bits
        self.result = result
        self.stage = 0
        self.copy = None

    def made(self, *needed):
        for item in needed:
            item.wait()
        mine, partner = flipped(lax.axis_index("seq"), self.bits[0])
        self.make(1 - mine, self.away[0])
        self.stage = 1
        self.go = lambda: self.begin(partner, mine)
        return self

    def begin(self, partner, mine):
        self.copy = self.start(0, partner)
        self.make(mine, self.kept)

    def begun(self):
        _, partner = flipped(lax.axis_index("seq"), self.bits[0])
        self.stage = 1
        self.copy = self.start(0, partner)

    def resume(self):
        self.stage = 2
        if len(self.bits) > 1:
            _, partner = flipped(lax.axis_index("seq"), self.bits[1])
            self.copy = self.start(1, partner)

    def next(self, send_on=True):
        stage, me = self.stage, lax.axis_index("seq")
        if stage > len(self.bits):
            return
        self.stage += 1
        left_over = stage == len(self.bits)
        self.copy.wait()
        count = self.land[stage - 1].shape[0]
        rows = self.kept.shape[1]
        part = 32 if rows % 32 == 0 else rows
        parts = rows // part

        def total(index, at):
            return self.kept[index, at] + self.land[stage - 1][index, at].astype(f32)

        if left_over:

            def finish(step, _):
                at = pl.ds(pl.multiple_of(step * part, part), part)
                self.kept[0, at] = total(0, at)
                return 0

            lax.fori_loop(0, parts, finish, 0)
            self.written = self.result(self.kept.at[0])
            return
        mine, partner = flipped(me, self.bits[stage])

        def send(step, _):
            index = lax.div(step, parts)
            at = pl.ds(pl.multiple_of(lax.rem(step, parts) * part, part), part)
            self.away[stage][index, at] = total(2 * index + 1 - mine, at).astype(bf16)
            return 0

        lax.fori_loop(0, (count // 2) * parts, send, 0)
        if send_on:
            self.copy = self.start(stage, partner)

        def keep(step, _):
            index = lax.div(step, parts)
            at = pl.ds(pl.multiple_of(lax.rem(step, parts) * part, part), part)
            self.kept[index, at] = total(2 * index + mine, at)
            return 0

        lax.fori_loop(0, (count // 2) * parts, keep, 0)

    def start(self, stage, partner):
        return sent(
            self.away[stage], self.land[stage], self.sends, self.receives, self.slot + stage,
            "seq", partner,
        )

    def make(self, side, target):
        first, width = self.columns
        tile = width if width <= 512 else 512 if width % 512 == 0 else 384
        tiles = width // tile
        count, rows = target.shape[:2]
        together = count if rows % 16 == 0 else 1

        def block(step, _):
            index = lax.div(step, tiles)
            column = pl.multiple_of(lax.rem(step, tiles) * tile, tile)
            left = self.left[:, side] if together > 1 else self.left[pl.ds(index, 1), side]
            product = jnp.dot(
                left.reshape(together * rows, left.shape[2]),
                self.right[:, pl.ds(first + column, tile)],
                preferred_element_type=f32,
            ).astype(target.dtype)
            at = pl.ds(0, count) if together > 1 else pl.ds(index, 1)
            target[at, :, pl.ds(column, tile)] = product.reshape(together, rows, tile)
            return 0

        lax.fori_loop(0, count // together * tiles, block, 0)


def norm_back(values, scale, gains, grad, free=True):
    weighted = gains * grad
    result = scale * weighted
    inner = jnp.mean(values * weighted, axis=-1, keepdims=True)
    return result - jnp.where(free, 1.0, 0.0) * values * (scale * scale * scale) * inner, (
        grad * values * scale
    )


def silu_slope(values):
    part = sigmoid(values)
    return part * (1.0 + values * (1.0 - part))


def narrowed(wide, first, count):
    states = wide.shape[1]
    eye = (
        lax.broadcasted_iota(jnp.int32, (states, states), 0)
        == lax.broadcasted_iota(jnp.int32, (states, states), 1)
    ).astype(f32)
    sums = jnp.sum(wide[pl.ds(first, count)], axis=-1, keepdims=True)
    return jnp.sum(sums * eye[None], axis=1)


def dot_rows(left, right):
    return lax.dot_general(left, right, (((1,), (1,)), ((), ())), preferred_element_type=f32)


class Once:
    def __init__(self, *copies, then=None):
        self.copies, self.then = copies, then

    def wait(self):
        for copy in self.copies:
            copy.wait()
        self.copies = ()
        if self.then is not None:
            after, self.then = self.then, None
            after().wait()


def named(names, refs):
    refs, found = list(refs), {}
    for name, count in names:
        taken, refs = refs[: count or 1], refs[count or 1 :]
        found[name] = taken if count else taken[0]
    return types.SimpleNamespace(**found)


def four_summed(r, place, value, base, part):
    low, across, high, along = place
    half = value.shape[3] // 2
    cols = pl.ds(part * half, half)
    first, second, moving = (
        r.first_land.at[:, :, cols], r.second_land.at[:, cols], r.second_move.at[:, cols]
    )
    total, value = r.total.at[:, :, :, cols], value.at[:, :, :, cols]
    sends, receives, base = r.sum_sends, r.sum_receives, base + 4 * part
    copy = sent(value.at[:, 1 - low], first, sends, receives, base, "ch", across)
    yield
    copy.wait()
    moving[...] = (
        value[1 - high, low].astype(f32) + first[1 - high].astype(f32)
    ).astype(bf16)
    copy = sent(moving, second, sends, receives, base + 1, "ch", along)
    yield
    copy.wait()
    total[high, low] = (
        value[high, low].astype(f32) + first[high].astype(f32) + second[...].astype(f32)
    ).astype(bf16)
    own = total.at[high, low]
    copy = sent(own, own, sends, receives, base + 2, "ch", along)
    yield
    copy.wait()
    both = total.at[:, low]
    copy = sent(both, both, sends, receives, base + 3, "ch", across)
    yield
    copy.wait()
    yield


def in_turn(*steps):
    for _ in range(4):
        yield
        for item in steps:
            next(item)
    yield


def feed_forward_kernel(bits, names, *refs):
    r = named(names, refs)
    tokens, width = r.stream.shape
    quarter, chunks, seq_count = tokens // 4, tokens // CHUNK, 1 << len(bits)
    ch_me, me = lax.axis_index("ch"), lax.axis_index("seq")
    low, across = flipped(ch_me, 1)
    high, along = flipped(ch_me, 2)
    pair_bit, rest_bits = bits[1], [bits[0], *bits[2:]]
    mine, pair = flipped(me, pair_bit)
    hid = r.w_down_in.shape[0]
    tile = 256
    tiles = range(0, hid, tile)
    own, other = pl.ds(0, tokens), pl.ds(tokens, tokens)
    slots = []

    def load(source, target):
        copy = pltpu.make_async_copy(source, target, r.load_sems.at[len(slots)])
        copy.start()
        slots.append(0)
        return Once(copy)

    cot_own = load(r.cot, r.right_down.at[own])
    loads = []
    for at in tiles:
        loads.append(
            [
                load(r.w_gate_up_in.at[:, pl.ds(at, tile)], r.w_gate_up.at[:, pl.ds(at, tile)]),
                load(
                    r.w_gate_up_in.at[:, pl.ds(hid + at, tile)],
                    r.w_gate_up.at[:, pl.ds(hid + at, tile)],
                ),
                load(r.w_down_in.at[pl.ds(at, tile)], r.w_down.at[pl.ds(at, tile)]),
            ]
        )
    cot_other = load(r.cot_came, r.right_down.at[other])
    greeted(
        [("ch", across), ("ch", along), ("seq", pair), ("seq", flipped(me, rest_bits[0])[1])]
    )

    def norm_two(index, _):
        rows = pl.ds(pl.multiple_of(index * CHUNK, CHUNK), CHUNK)
        per = quarter // CHUNK
        part = lax.div(index, per)
        at = pl.ds(pl.multiple_of(lax.rem(index, per) * CHUNK, CHUNK), CHUNK)
        mixed = r.mixer[lax.div(part, 2), lax.rem(part, 2), at].astype(f32)
        middle = r.stream[rows].astype(f32) + mixed
        scale = lax.rsqrt(mean_square(middle) + 1e-06)
        r.normed[rows] = (middle * scale * r.gains[1:2]).astype(bf16)
        return 0

    lax.fori_loop(0, chunks, norm_two, 0)

    group = 384
    for at in range(0, width, group):
        turn(r.normed[:, at : at + group], at, r.two_turned)
    half = r.two_turned.shape[0] // 2
    some = pl.ds(low * half, half)
    target = r.left_two.at[some, :, :, other]
    two_copy = sent(
        r.two_turned.at[some, 1 - mine], target, r.pair_sends, r.pair_receives, 0, "seq", pair
    )
    r.left_two[:, :, :, own] = r.two_turned[:, mine]
    cot_own.wait()
    hidden_copies, quads_sent = [], 0
    for number, at in enumerate(tiles):
        for item in loads[number]:
            item.wait()
        gate = jnp.dot(
            r.normed[...], r.w_gate_up[:, pl.ds(at, tile)], preferred_element_type=f32
        )
        up = jnp.dot(
            r.normed[...], r.w_gate_up[:, pl.ds(hid + at, tile)], preferred_element_type=f32
        )
        part = sigmoid(gate)
        act = gate * part
        hidden = (act * up).astype(bf16)
        r.hidden[:, pl.ds(at, tile)] = hidden
        turn(hidden, at, r.hidden_turned)
        grad = dot_rows(r.right_down[own], r.w_down[pl.ds(at, tile)])
        r.right_two[own, pl.ds(at, tile)] = (
            grad * up * (part * (1.0 + gate * (1.0 - part)))
        ).astype(bf16)
        r.right_two[own, pl.ds(hid + at, tile)] = (grad * act).astype(bf16)
        quads = (at + tile) // r.hidden_turned.shape[3] // 4
        if quads > quads_sent:
            some = pl.ds(quads_sent, quads - quads_sent)
            hidden_copies.append(
                sent(
                    r.hidden_turned.at[some, 1 - mine], r.left_hidden.at[some, :, :, other],
                    r.pair_sends, r.pair_receives, 3 + len(hidden_copies), "seq", pair,
                )
            )
            quads_sent = quads
    gate_copy = sent(
        r.right_two.at[own, pl.ds(0, hid)], r.right_two.at[other, pl.ds(0, hid)], r.pair_sends,
        r.pair_receives, 1, "seq", pair,
    )
    r.left_hidden[:, :, :, own] = r.hidden_turned[:, mine]

    def store(values, target, at):
        for k in range(4):
            target[k // 2, k % 2, :, pl.ds(at, tile)] = values[k * quarter : (k + 1) * quarter]

    def two_part(index, _):
        at = pl.multiple_of(index * tile, tile)
        store(dot_rows(r.right_two[own], r.w_gate_up[pl.ds(at, tile)]).astype(bf16), r.part, at)
        return 0

    sums = [four_summed(r, (low, across, high, along), r.part, 0, k) for k in range(2)]
    for k, item in enumerate(sums):
        lax.fori_loop(k * width // (2 * tile), (k + 1) * width // (2 * tile), two_part, 0)
        next(item)
    total = in_turn(*sums)
    next(total)

    def feed_part(index, _):
        at = pl.multiple_of(index * tile, tile)
        product = jnp.dot(
            r.hidden[...], r.w_down[:, pl.ds(at, tile)], preferred_element_type=f32
        )
        store(product.astype(bf16), r.feed_part, at)
        return 0

    n_bits = len(rest_bits)
    part = width // 2
    down, down_late = (
        Unit(r.left_hidden, r.right_down, (k * part, part), r.down, r.unit_sends,
             r.unit_receives, 0, rest_bits, None)
        for k in range(2)
    )
    next(total)
    cot_other.wait()
    down.made(*hidden_copies).go()
    next(total)
    lax.fori_loop(0, width // tile, feed_part, 0)
    next(total)
    side, _ = flipped(me, rest_bits[0])
    down_late.make(1 - side, r.late_away)
    down_late.make(side, r.late_kept)
    two_copy.wait()
    two_copy = sent(target, target, r.pair_sends, r.pair_receives, 2, "ch", across)
    next(total)
    two_copy.wait()
    gate_copy.wait()
    if n_bits > 1:
        down.next(send_on=False)
    r.down_away[...] = down.away[1][...]
    kept = r.down_kept.shape[0]
    r.down_kept[...] = down.kept[0:kept]


def feed_forward(ins, hbm_ins, count, ident):
    bits = bits_of(count)
    n_bits = len(bits) - 1
    tokens, width = ins["stream"].shape
    hid = hbm_ins["w_down_in"].shape[0]
    half, quarter = count // 2, tokens // 4
    rows_in, rows_down = width // count, hid // count

    def low(*dims):
        return pltpu.VMEM(dims, bf16)

    def sems(size):
        return pltpu.SemaphoreType.DMA((size,))

    lands = [low(half >> (k + 1), rows_down, width // 2) for k in range(n_bits)]
    outs = dict(
        total=shape_of(2, 2, quarter, width, dtype=bf16),
        feed_part=shape_of(2, 2, quarter, width, dtype=bf16),
        left_two=shape_of(count // 4, 2, rows_in, 2 * tokens, dtype=bf16),
        right_two=shape_of(2 * tokens, 2 * hid, dtype=bf16),
        down_away=shape_of(half >> 2, rows_down, width // 2, dtype=bf16),
        down_kept=shape_of(half >> 2, rows_down, width // 2),
        late_away=shape_of(half >> 1, rows_down, width // 2, dtype=bf16),
        late_kept=shape_of(half >> 1, rows_down, width // 2),
    )
    scratch = dict(
        w_gate_up=low(width, 2 * hid),
        w_down=low(hid, width),
        normed=low(tokens, width),
        hidden=low(tokens, hid),
        two_turned=low(count // 4, 2, 2, rows_in, tokens),
        hidden_turned=low(count // 4, 2, 2, rows_down, tokens),
        left_hidden=low(count // 4, 2, rows_down, 2 * tokens),
        right_down=low(2 * tokens, width),
        part=low(2, 2, quarter, width),
        first_land=low(2, quarter, width),
        second_land=low(quarter, width),
        second_move=low(quarter, width),
        down=[low(half // 2, rows_down, width // 2), *lands, pltpu.VMEM((half // 2, rows_down, width // 2), f32)],
        load_sems=sems(2 + 3 * (hid // 256)),
        pair_sends=sems(7),
        pair_receives=sems(7),
        sum_sends=sems(8),
        sum_receives=sems(8),
        unit_sends=sems(n_bits),
        unit_receives=sems(n_bits),
    )
    names, shapes = [(name, 0) for name in [*ins, *hbm_ins, *outs]], []
    for name, held in scratch.items():
        listed = isinstance(held, list)
        names.append((name, len(held) if listed else 0))
        shapes += held if listed else [held]
    made = pl.pallas_call(
        functools.partial(feed_forward_kernel, bits, names),
        out_shape=list(outs.values()),
        in_specs=[VMEM] * len(ins) + [ANY] * len(hbm_ins),
        out_specs=[VMEM] * len(outs),
        scratch_shapes=shapes,
        compiler_params=pltpu.CompilerParams(
            collective_id=ident, has_side_effects=True, vmem_limit_bytes=56 * 2**20
        ),
        name="feed_forward",
    )(*ins.values(), *hbm_ins.values())
    return types.SimpleNamespace(**dict(zip(outs, made)))


def backward_kernel(bits, names, *refs):
    r = named(names, refs)
    tokens, width = r.stream.shape
    channels, rank, states = r.low.shape[1], r.w_dt.shape[0], r.logs.shape[0]
    quarter, chunks = tokens // 4, tokens // CHUNK
    ch_me, me = lax.axis_index("ch"), lax.axis_index("seq")
    seq_count = 1 << len(bits)
    low, across = flipped(ch_me, 1)
    high, along = flipped(ch_me, 2)
    pair_bit, rest_bits = bits[1], [bits[0], *bits[2:]]
    mine, pair = flipped(me, pair_bit)
    previous = lax.rem(me + seq_count - 1, seq_count)
    load_slots, pair_slots, shared_slots, write_slots = ([] for _ in range(4))

    def slot_of(slots):
        slots.append(0)
        return len(slots) - 1

    def load(source, target):
        copy = pltpu.make_async_copy(source, target, r.load_sems.at[slot_of(load_slots)])
        copy.start()
        return Once(copy)

    own, other = pl.ds(0, tokens), pl.ds(tokens, tokens)
    mixer_own = load(r.mixer_in, r.mixer)
    cot_own = load(r.cot, r.cot_rows)
    weights = load(r.w_out, r.weights)
    scan_own = load(r.scan_in, r.scan)
    out_of_own = load(r.out_of_in, r.out_of)
    into_own = load(r.into_in, r.into)
    hid = r.right_two_in.shape[1] // 2
    down_away = load(r.down_away_in, r.down[0].at[pl.ds(0, r.down_away_in.shape[0])])
    late_away = load(r.late_away_in, r.late[0])
    two_own = load(r.left_two_in, r.left_two)
    gate_up_own = load(r.right_two_in.at[own], r.right_two.at[own])
    gate_other = load(
        r.right_two_in.at[other, pl.ds(0, hid)], r.right_two.at[other, pl.ds(0, hid)]
    )
    down_kept = load(r.down_kept_in, r.down[-1].at[pl.ds(0, r.down_kept_in.shape[0])])
    late_kept = load(r.late_kept_in, r.late[-1])
    part_in = load(r.feed_part, r.part)
    one_own = load(r.one_in.at[:, mine], r.left_one.at[:, :, :, own])
    one_other = load(r.one_came, r.left_one.at[:, :, :, other])
    gated_own = load(r.gated_in.at[:, mine], r.left_gated.at[:, :, :, own])
    blocks = [slice(j, j + 128) for j in range(0, channels, 128)]
    hists = [load(r.hist_in.at[:, :, blocks[k]], r.hist.at[k]) for k in range(2)]

    greeted(
        [("ch", across), ("ch", along)]
        + [("seq", lax.rem(me + k, seq_count)) for k in range(1, seq_count)]
    )

    def swap(source, target):
        slot = slot_of(pair_slots)
        return Once(sent(source, target, r.pair_sends, r.pair_receives, slot, "seq", pair))

    def swap_shared(source, target):
        slot = 2 * slot_of(shared_slots)
        copy = sent(source, target, r.shared_sends, r.shared_receives, slot, "seq", pair)
        return Once(
            copy,
            then=lambda: sent(
                target, target, r.shared_sends, r.shared_receives, slot + 1, "ch", across
            ),
        )

    n_bits = len(rest_bits)

    def writer(target):
        def write(source):
            copy = pltpu.make_async_copy(source, target, r.write_sems.at[slot_of(write_slots)])
            copy.start()
            return copy

        return write

    def unit(left, right, columns, refs, slot, target):
        return Unit(
            left, right, columns, refs, r.unit_sends, r.unit_receives, slot * n_bits, rest_bits,
            writer(target),
        )

    part = width // 2
    down, late = (
        unit(None, None, None, refs, k, r.down_out.at[:, pl.ds(k * part, part)])
        for k, refs in enumerate((r.down, r.late))
    )
    part = hid // 2
    quarters = [
        unit(
            r.left_two, r.right_two, (k * part, part), refs, 2 + k,
            (r.gate_out, r.up_out)[k // 2].at[:, pl.ds(k % 2 * part, part)],
        )
        for k, refs in enumerate((r.gate0, r.gate1, r.up0, r.up1))
    ]
    gate0, gate1, up0, up1 = quarters
    part = width // 2
    outs = [
        unit(
            r.left_gated, r.right_out, (k * part, part), refs, 6 + 4 * k,
            r.out_out.at[:, pl.ds(k * part, part)],
        )
        for k, refs in enumerate((r.out0, r.out1))
    ]
    gin = unit(r.left_one, r.right_in, (channels, channels), r.gin, 7, r.gin_out)
    part = channels // 2
    cins = [
        unit(
            r.left_one, r.right_in, (k * part, part), refs, 8 + k,
            r.cin_out.at[:, pl.ds(k * part, part)],
        )
        for k, refs in enumerate((r.cin0, r.cin1))
    ]

    up_other = swap(
        r.right_two_in.at[own, pl.ds(hid, hid)], r.right_two.at[other, pl.ds(hid, hid)]
    )
    down_away.wait()
    down.resume()
    late_away.wait()
    late.begun()

    summed = functools.partial(four_summed, r, (low, across, high, along))


    rates = -jnp.exp(r.logs[...]) * LOG2E

    def places_of(first, count):
        return me * tokens + first + lax.broadcasted_iota(jnp.int32, (count, 128), 0)

    def resteps():
        def body(index, total):
            first = pl.multiple_of(index * CHUNK, CHUNK)
            rows = pl.ds(first, CHUNK)
            size = softplus(r.step_pre[rows])
            r.drive[rows] = size * r.low[rows].astype(f32)
            places = places_of(first, CHUNK)
            resets = jnp.where((places == r.bounds[0]) | (places == r.bounds[1]), RESET, 0.0)
            size = size + widened(resets, channels)
            r.step[rows] = size
            return total + jnp.sum(size, axis=0, keepdims=True)

        r.step_sum[...] = jnp.broadcast_to(
            lax.fori_loop(0, chunks, body, jnp.zeros((1, channels), f32)), (8, channels)
        )

    resteps()
    mixer_own.wait()
    cot_own.wait()

    def quarter_rows(index):
        per = quarter // CHUNK
        part = lax.div(index, per)
        at = pl.ds(pl.multiple_of(lax.rem(index, per) * CHUNK, CHUNK), CHUNK)
        return lax.div(part, 2), lax.rem(part, 2), at

    def norm_two(index, total):
        first = pl.multiple_of(index * CHUNK, CHUNK)
        rows = pl.ds(first, CHUNK)
        a, b, at = quarter_rows(index)
        middle = r.stream[rows].astype(f32) + r.mixer[a, b, at].astype(f32)
        scale = lax.rsqrt(mean_square(middle) + 1e-06)
        back, gain = norm_back(middle, scale, r.gains[1:2], r.two_total[a, b, at].astype(f32))
        grad = r.cot_rows[rows].astype(f32) + back
        r.stream_grad[rows] = grad
        r.right_out[rows] = grad.astype(bf16)
        return total + jnp.sum(gain, axis=0, keepdims=True)

    gain_two = lax.fori_loop(0, chunks, norm_two, jnp.zeros((1, width), f32))
    r.flat_move[0] = jnp.zeros_like(r.flat_move[0])
    r.flat_move[0, 1:2] = gain_two
    weights.wait()
    scan_own.wait()
    skips = []
    for j in range(0, channels, 256):
        lanes = slice(j, j + 256)
        gated_grad = dot_rows(r.right_out[own], r.weights[pl.ds(j, 256)])
        gate_pre = r.proj[:, channels + j : channels + j + 256].astype(f32)
        part = sigmoid(gate_pre)
        slope = part * (1.0 + gate_pre * (1.0 - part))
        r.right_in[own, channels + j : channels + j + 256] = (
            gated_grad * r.scan[:, lanes] * slope
        ).astype(bf16)
        grad = gated_grad * gate_pre * part
        r.scan[:, lanes] = grad
        skips.append(jnp.sum(grad * r.low[:, lanes].astype(f32), axis=0, keepdims=True))
    skip_grad = jnp.concatenate(skips, 1)
    weights = load(r.w_in.at[pl.ds(0, channels)], r.weights)
    out_of_own.wait()
    for j in range(0, channels, LANES):
        lanes = slice(j, j + LANES)

        def ended(index, carried, lanes=lanes, block_rates=rates[:, j : j + LANES]):
            first = pl.multiple_of(tokens - UNROLL - index * UNROLL, UNROLL)
            steps, grads = r.step[pl.ds(first, UNROLL), lanes], r.scan[pl.ds(first, UNROLL), lanes]
            for k in reversed(range(UNROLL)):
                decay = jnp.exp2(steps[k : k + 1] * block_rates)
                carried = decay * (widened(r.out_of[first + k], LANES) * grads[k : k + 1] + carried)
            return carried

        r.starts[:, lanes] = lax.fori_loop(
            0, tokens // UNROLL, ended, jnp.zeros((states, LANES), f32)
        )

    chain = handed_on(False, r.starts[...], r.step_sum[0:1], rates, r)
    next(chain)
    gate0.made(two_own, gate_up_own, gate_other)
    gate1.made()
    r.starts[...] = next(chain)
    gate0.go()
    late_kept.wait()
    late.next()
    gate1.go()
    up0.made(up_other)
    first = pl.multiple_of(low * (tokens // 2), tokens // 2)
    mixer_other = swap_shared(
        r.right_out.at[pl.ds(first, tokens // 2)],
        r.right_out.at[pl.ds(tokens + first, tokens // 2)],
    )
    gated_other = swap(r.gated_in.at[:, 1 - mine], r.left_gated.at[:, :, :, other])
    gin_other = swap(
        r.right_in.at[own, pl.ds(channels, channels)],
        r.right_in.at[other, pl.ds(channels, channels)],
    )
    up0.go()
    up1.made().go()

    part_in.wait()
    feed_sums = [summed(r.part, 0, k) for k in range(2)]
    into_own.wait()

    def results():
        totals = lax.fori_loop(
            0, chunks, results_of, tuple(jnp.zeros((1, width), f32) for _ in range(3))
        )
        for number, total in enumerate(totals):
            r.flat_move[0, 3 + number : 4 + number] = total

    def feed_start():
        for item in feed_sums:
            next(item)
        return in_turn(*feed_sums)

    feed = []
    between = [
        lambda: (feed.append(feed_start()), next(feed[0]), gate0.next()),
        lambda: next(feed[0]),
        lambda: (next(feed[0]), gate1.next()),
        lambda: next(feed[0]),
        lambda: (next(feed[0]), up0.next()),
        lambda: (
            results(), outs[0].made(gated_own, mixer_other, gated_other).go(), outs[1].made(),
        ),
    ]

    def results_of(index, totals):
        rows = pl.ds(pl.multiple_of(index * CHUNK, CHUNK), CHUNK)
        a, b, at = quarter_rows(index)
        mixed, feed = r.mixer[a, b, at].astype(f32), r.total[a, b, at].astype(f32)
        result = r.stream[rows].astype(f32) + mixed + feed
        r.out_rows[rows] = result.astype(bf16)
        return tuple(
            total + jnp.sum(v * v, axis=0, keepdims=True)
            for total, v in zip(totals, (result, mixed, feed))
        )

    r.into_wide[...] = jnp.zeros_like(r.into_wide)
    r.out_wide[...] = jnp.zeros_like(r.out_wide)
    for number, lanes in enumerate(blocks):
        hists[number].wait()
        hist = r.hist.at[number % 2]
        block_rates = rates[:, lanes]

        def walked(index, carry, lanes=lanes, block_rates=block_rates, hist=hist):
            carried, state, total = carry
            first = pl.multiple_of(tokens - UNROLL - index * UNROLL, UNROLL)
            some = pl.ds(first, UNROLL)
            steps, drives, grads = r.step[some, lanes], r.drive[some, lanes], r.scan[some, lanes]
            decay_list, push_list = [None] * UNROLL, [None] * UNROLL
            for k in reversed(range(UNROLL)):
                place = first + k
                grad_row = grads[k : k + 1]
                decay = jnp.exp2(steps[k : k + 1] * block_rates)
                adjoint = r.out_of[place] * grad_row + carried
                carried = decay * adjoint
                r.out_wide[place] = r.out_wide[place] + state * grad_row
                r.into_wide[place] = r.into_wide[place] + adjoint * drives[k : k + 1]
                state = hist[place]
                share = carried * state
                total = total + share * steps[k : k + 1]
                decay_list[k] = jnp.sum(share * block_rates, axis=0, keepdims=True)
                push_list[k] = jnp.sum(r.into[place] * adjoint, axis=0, keepdims=True)
            r.decay_rows[some, :] = jnp.concatenate(decay_list, 0)
            r.push[some, lanes] = jnp.concatenate(push_list, 0)
            return (carried, state, total)

        _, _, total = lax.fori_loop(
            0,
            tokens // UNROLL,
            walked,
            (r.starts[:, lanes], r.last_state[:, lanes], jnp.zeros((states, 128), f32)),
        )
        r.rate_sum[:, lanes] = total * (rates[:, lanes] * LN2)

        def gathered(index, _, lanes=lanes):
            rows = pl.ds(pl.multiple_of(index * CHUNK, CHUNK), CHUNK)
            used, pushed = r.low[rows, lanes].astype(f32), r.push[rows, lanes]
            pre = r.step_pre[rows, lanes]
            grad = (LN2 * r.decay_rows[rows] + pushed * used) * sigmoid(pre)
            r.step_low_grad[rows, lanes] = grad.astype(bf16)
            r.push[rows, lanes] = pushed * softplus(pre) + r.chan[6:7, lanes] * r.scan[rows, lanes]
            return 0

        lax.fori_loop(0, chunks, gathered, 0)
        if number + 2 < len(blocks):
            hists.append(load(r.hist_in.at[:, :, blocks[number + 2]], r.hist.at[number % 2]))
        if number < len(between):
            between[number]()
    for later in between[len(blocks) :]:
        later()

    def norm_grads(index, _):
        first = pl.multiple_of(index * CHUNK, CHUNK)
        rows = pl.ds(first, CHUNK)
        low_part = dot_rows(r.step_low_grad[rows], r.w_dt[...])
        r.raw_move[0, rows] = jnp.concatenate(
            [low_part, narrowed(r.into_wide, first, CHUNK), narrowed(r.out_wide, first, CHUNK)], 1
        )
        return 0

    lax.fori_loop(0, chunks, norm_grads, 0)
    copy = sent(r.raw_move.at[0], r.raw_land.at[0], r.raw_sends, r.raw_receives, 0, "ch", across)
    gin.made(one_own, one_other, gin_other)
    copy.wait()
    r.raw_move[1] = r.raw_move[0] + r.raw_land[0]
    copy = sent(r.raw_move.at[1], r.raw_land.at[1], r.raw_sends, r.raw_receives, 1, "ch", along)
    up1.next()
    copy.wait()

    def raw_back(index, total):
        rows = pl.ds(pl.multiple_of(index * CHUNK, CHUNK), CHUNK)
        grads, raw = r.raw_move[1, rows] + r.raw_land[1, rows], r.raw[rows]
        gains = r.small_gains[...]
        values, sums_to = [], []
        for start, stop, floor in ((0, rank, None), (rank, rank + states, 0.1),
                                   (rank + states, rank + 2 * states, 0.1)):
            value = raw[:, start:stop]
            square = mean_square(value)
            if floor is None:
                scale, free = lax.rsqrt(square + 1e-06), True
            else:
                scale, free = lax.rsqrt(jnp.maximum(square, floor)), square > floor
            back, gain = norm_back(value, scale, gains[:, start:stop], grads[:, start:stop], free)
            values.append(back)
            sums_to.append(jnp.sum(gain, axis=0, keepdims=True))
        norm = raw[:, :rank] * lax.rsqrt(mean_square(raw[:, :rank]) + 1e-06) * gains[:, :rank]
        r.raw_low[rows] = jnp.concatenate(values, 1).astype(bf16)
        r.step_low[rows] = norm.astype(bf16)
        return total + jnp.concatenate(sums_to, 1)

    small = lax.fori_loop(0, chunks, raw_back, jnp.zeros((1, rank + 2 * states), f32))
    r.flat_move[0, 2:3, : rank + 2 * states] = small

    def conv_back(index, total):
        first = pl.multiple_of(index * CHUNK, CHUNK)
        rows = pl.ds(first, CHUNK)
        grad = r.push[rows] + dot_rows(r.raw_low[rows], r.w_x[...])
        grad = grad * silu_slope(r.pre[rows])
        r.grad_pre[rows] = grad
        return total + jnp.sum(grad, axis=0, keepdims=True)

    tap_bias = lax.fori_loop(0, chunks, conv_back, jnp.zeros((1, channels), f32))
    copy = sent(r.grad_pre.at[pl.ds(0, 8)], r.grad_pre.at[pl.ds(tokens, 8)], r.raw_sends,
                r.raw_receives, 2, "seq", previous)
    outs[1].go()
    gin.go()
    r.extended[0:16] = r.halo[...].astype(f32)

    def extend(index, _):
        first = pl.multiple_of(index * CHUNK, CHUNK)
        r.extended[pl.ds(first + 16, CHUNK)] = r.proj[pl.ds(first, CHUNK), :channels].astype(f32)
        return 0

    lax.fori_loop(0, chunks, extend, 0)

    def taps(index, totals):
        first = pl.multiple_of(index * CHUNK, CHUNK)
        places = places_of(first, CHUNK)
        window = r.extended[pl.ds(first, CHUNK + 16)]
        grad = r.grad_pre[pl.ds(first, CHUNK)]
        return tuple(
            totals[k]
            + jnp.sum(
                grad
                * widened(tap_mask(places, r.bounds, 3 - k), channels)
                * window[13 + k : 13 + k + CHUNK],
                axis=0,
                keepdims=True,
            )
            for k in range(4)
        )

    tap_grads = lax.fori_loop(
        0, chunks, taps, tuple(jnp.zeros((1, channels), f32) for _ in range(4))
    )
    copy.wait()

    def conv_in_back(index, _):
        first = pl.multiple_of(index * CHUNK, CHUNK)
        window = r.grad_pre[pl.ds(first, CHUNK + 8)]
        grad = jnp.zeros((CHUNK, channels), f32)
        for k in range(4):
            places = places_of(first + 3 - k, CHUNK)
            mask = jnp.where(
                places < seq_count * tokens, tap_mask(places, r.bounds, 3 - k), 0.0
            )
            grad = grad + r.chan[k : k + 1] * widened(mask, channels) * window[3 - k : 3 - k + CHUNK]
        r.right_in[pl.ds(first, CHUNK), :channels] = grad.astype(bf16)
        return 0

    lax.fori_loop(0, chunks, conv_in_back, 0)
    cin_others = [
        swap(
            r.right_in.at[own, pl.ds(*item.columns)], r.right_in.at[other, pl.ds(*item.columns)]
        )
        for item in cins
    ]

    def small_columns():
        narrow = r.w_x.shape[1]
        pack = r.step
        pack[0:narrow] = lax.dot_general(
            r.raw_low[...], r.low[...], (((0,), (0,)), ((), ())), preferred_element_type=f32
        )
        pack[narrow : narrow + rank] = lax.dot_general(
            r.step_low[...], r.step_low_grad[...], (((0,), (0,)), ((), ())),
            preferred_element_type=f32,
        )
        at = narrow + rank
        pack[at : at + states] = r.rate_sum[...]
        at += states
        bias = jnp.sum(r.step_low_grad[...].astype(f32), axis=0, keepdims=True)
        pack[at : at + 8] = jnp.concatenate(
            [*tap_grads, tap_bias, bias, skip_grad, jnp.zeros((1, channels), f32)], 0
        )
        at += 8
        pack[at:] = jnp.zeros((pack.shape[0] - at, channels), f32)
        turned = pack[...].T
        r.small_work[0][...] = turned.reshape(r.small_work[0].shape)

    def small_summed():
        for k, bit in enumerate(bits):
            side, partner = flipped(me, bit)
            work, away, land = r.small_work[k], r.small_away[k], r.small_land[k]
            away[...] = work[:, 1 - side].astype(bf16)
            copy = sent(away, land, r.last_sends, r.last_receives, k, "seq", partner)
            yield
            copy.wait()
            total = work[:, side] + land[...].astype(f32)
            target = r.small_work[k + 1] if k + 1 < len(bits) else r.small_out
            target[...] = total.reshape(target.shape)
        yield

    one_sums = [summed(r.part, 8, k) for k in range(2)]
    for number in range(width // channels):
        weights.wait()

        def one_part(index, _, first=number * channels):
            at = pl.multiple_of(index * 256, 256)
            product = dot_rows(r.right_in[own], r.weights[pl.ds(at, 256)]).astype(bf16)
            for k in range(4):
                r.part[k // 2, k % 2, :, pl.ds(first + at, 256)] = product[
                    k * quarter : (k + 1) * quarter
                ]
            return 0

        lax.fori_loop(0, channels // 256, one_part, 0)
        next(one_sums[number])
        if (number + 1) * channels < width:
            weights = load(r.w_in.at[pl.ds((number + 1) * channels, channels)], r.weights)
    one_sum = in_turn(*one_sums)
    next(one_sum)

    def gain_part(index, total):
        rows = pl.ds(pl.multiple_of(index * CHUNK, CHUNK), CHUNK)
        a, b, at = quarter_rows(index)
        value = r.stream[rows].astype(f32)
        scale = lax.rsqrt(mean_square(value) + 1e-06)
        return total + jnp.sum(r.part[a, b, at].astype(f32) * value * scale, axis=0, keepdims=True)

    r.flat_move[0] = r.flat_move[0] * 0.25
    r.flat_move[0, 0:1] = lax.fori_loop(0, chunks, gain_part, jnp.zeros((1, width), f32))
    ways = [("ch", across), ("ch", along)] + [("seq", flipped(me, bit)[1]) for bit in bits]

    def flat_summed():
        for k, (axis, partner) in enumerate(ways):
            copy = sent(r.flat_move.at[k], r.flat_land.at[k], r.flat_sends, r.flat_receives, k,
                        axis, partner)
            yield
            copy.wait()
            target = r.flat_move.at[k + 1] if k + 1 < len(ways) else r.flat_out
            target[...] = r.flat_move[k] + r.flat_land[k]
        yield

    flat_sum = flat_summed()
    next(flat_sum)

    outs[0].next()
    cins[0].made(cin_others[0]).go()
    next(one_sum)
    next(flat_sum)
    outs[1].next()
    cins[1].made(cin_others[1]).go()
    next(one_sum)
    next(flat_sum)
    small_columns()
    small_sum = small_summed()
    next(small_sum)
    down_kept.wait()
    down.next()
    late.next()
    next(one_sum)
    gin.next()
    gate0.next()
    next(flat_sum)
    gate1.next()
    next(one_sum)

    def norm_one(index, _):
        rows = pl.ds(pl.multiple_of(index * CHUNK, CHUNK), CHUNK)
        a, b, at = quarter_rows(index)
        value = r.stream[rows].astype(f32)
        scale = lax.rsqrt(mean_square(value) + 1e-06)
        back, _ = norm_back(value, scale, r.gains[0:1], r.total[a, b, at].astype(f32))
        r.stream_grad[rows] = r.stream_grad[rows] + back
        return 0

    lax.fori_loop(0, chunks, norm_one, 0)
    cins[0].next()
    next(small_sum)
    next(flat_sum)
    cins[1].next()
    for item in (up0, up1):
        item.next()
    next(small_sum)
    for waiting in (flat_sum, small_sum):
        for _ in waiting:
            pass
    pending = [*outs, gin, *cins, down, late, *quarters]
    for _ in range(len(bits)):
        for item in pending:
            item.next()
    for item in pending:
        item.written.wait()


def backward(ins, hbm_ins, count, ident):
    bits = bits_of(count)
    n_bits = len(bits) - 1
    tokens, width = ins["stream"].shape
    channels, rank, states = ins["low"].shape[1], ins["w_dt"].shape[0], ins["logs"].shape[0]
    hid = hbm_ins["right_two_in"].shape[1] // 2
    narrow = ins["w_x"].shape[1]
    half, quarter = count // 2, tokens // 4
    rows_in, rows_out, rows_down = width // count, channels // count, hid // count
    rows = pltpu.VMEM((tokens, channels), f32)

    def low(*dims):
        return pltpu.VMEM(dims, bf16)

    def full(*dims):
        return pltpu.VMEM(dims, f32)

    outs = dict(
        stream_grad=(shape_of(tokens, width), VMEM),
        out_rows=(shape_of(tokens, width, dtype=bf16), VMEM),
        small_out=(shape_of(rows_out, tokens), VMEM),
        flat_out=(shape_of(8, width), VMEM),
        down_out=(shape_of(rows_down, width), ANY),
        gate_out=(shape_of(rows_in, hid), ANY),
        up_out=(shape_of(rows_in, hid), ANY),
        out_out=(shape_of(rows_out, width), ANY),
        gin_out=(shape_of(rows_in, channels), ANY),
        cin_out=(shape_of(rows_in, channels), ANY),
    )
    quads = count // 4

    def unit(part, columns):
        lands = [low(half >> (k + 1), part, columns) for k in range(n_bits)]
        return [low(half // 2, part, columns), *lands, full(half // 2, part, columns)]

    def sems(size):
        return pltpu.SemaphoreType.DMA((size,))

    halves = [count >> (k + 1) for k in range(len(bits))]
    scratch = dict(
        left_two=low(quads, 2, rows_in, 2 * tokens),
        left_one=low(quads, 2, rows_in, 2 * tokens),
        left_gated=low(quads, 2, rows_out, 2 * tokens),
        cot_rows=low(tokens, width),
        right_two=low(2 * tokens, 2 * hid),
        right_out=low(2 * tokens, width),
        right_in=low(2 * tokens, 2 * channels),
        mixer=low(2, 2, quarter, width),
        weights=low(channels, width),
        scan=rows,
        step=rows,
        drive=rows,
        push=rows,
        decay_rows=full(tokens, 128),
        into=full(tokens, states, 128),
        out_of=full(tokens, states, 128),
        into_wide=full(tokens, states, 128),
        out_wide=full(tokens, states, 128),
        hist=full(2, tokens, states, 128),
        step_sum=full(8, channels),
        starts=full(states, channels),
        rate_sum=full(states, channels),
        step_low_grad=low(tokens, channels),
        **handing(count, states, channels),
        part=low(2, 2, quarter, width),
        total=low(2, 2, quarter, width),
        first_land=low(2, quarter, width),
        second_land=low(quarter, width),
        second_move=low(quarter, width),
        raw_move=full(2, tokens, narrow),
        raw_land=full(2, tokens, narrow),
        raw_low=low(tokens, narrow),
        step_low=low(tokens, rank),
        grad_pre=full(tokens + 8, channels),
        extended=full(tokens + 16, channels),
        flat_move=full(2 + len(bits), 8, width),
        flat_land=full(2 + len(bits), 8, width),
        small_work=[full(size, 2, rows_out, tokens) for size in halves],
        small_away=[low(size, rows_out, tokens) for size in halves],
        small_land=[low(size, rows_out, tokens) for size in halves],
        down=unit(rows_down, width // 2),
        late=unit(rows_down, width // 2),
        gate0=unit(rows_in, hid // 2),
        gate1=unit(rows_in, hid // 2),
        up0=unit(rows_in, hid // 2),
        up1=unit(rows_in, hid // 2),
        out0=unit(rows_out, width // 2),
        out1=unit(rows_out, width // 2),
        gin=unit(rows_in, channels),
        cin0=unit(rows_in, channels // 2),
        cin1=unit(rows_in, channels // 2),
        load_sems=sems(32),
        write_sems=sems(11),
        pair_sends=sems(8),
        pair_receives=sems(8),
        shared_sends=sems(4),
        shared_receives=sems(4),
        unit_sends=sems(11 * n_bits),
        unit_receives=sems(11 * n_bits),
        sum_sends=sems(16),
        sum_receives=sems(16),
        raw_sends=sems(3),
        raw_receives=sems(3),
        last_sends=sems(len(bits)),
        last_receives=sems(len(bits)),
        flat_sends=sems(2 + len(bits)),
        flat_receives=sems(2 + len(bits)),
    )
    names, shapes = [(name, 0) for name in [*ins, *hbm_ins, *outs]], []
    for name, held in scratch.items():
        listed = isinstance(held, list)
        names.append((name, len(held) if listed else 0))
        shapes += held if listed else [held]
    places = [VMEM for _ in ins]
    places[0] = pl.BlockSpec(memory_space=pltpu.SMEM)
    made = pl.pallas_call(
        functools.partial(backward_kernel, bits, names),
        out_shape=[shape for shape, _ in outs.values()],
        in_specs=places + [ANY] * len(hbm_ins),
        out_specs=[spec for _, spec in outs.values()],
        scratch_shapes=shapes,
        compiler_params=pltpu.CompilerParams(
            collective_id=ident, has_side_effects=True, vmem_limit_bytes=63 * 2**20
        ),
        name="block_backward",
    )(*ins.values(), *hbm_ins.values())
    return types.SimpleNamespace(**dict(zip(outs, made)))


def finish_kernel(cells, names, *refs):
    r = named(names, refs)
    me = lax.axis_index("seq")
    moves = [
        (r.out_rows, r.out), (r.stream_grad, r.stream), (r.out_out, r.w_out),
        (r.down_out, r.w_down), (r.gate_out, r.w_gate_up.at[:, 0]),
        (r.up_out, r.w_gate_up.at[:, 1]), (r.cin_out, r.w_in.at[:, 0]),
        (r.gin_out, r.w_in.at[:, 1]),
    ]
    little = [(r.small_out, r.small_here), (r.flat_out, r.flat_here)]
    loads = [
        pltpu.make_async_copy(source, here, r.sems.at[k])
        for k, (source, here) in enumerate(
            [*little, *((source, here) for (source, _), here in zip(moves, r.here))]
        )
    ]
    for copy in loads:
        copy.start()
    copies = []
    for k, (_, target) in enumerate(moves):
        loads[k + 2].wait()
        copy = pltpu.make_async_copy(r.here[k], target, r.out_sems.at[k])
        copy.start()
        copies.append(copy)
    for copy in loads[:2]:
        copy.wait()
    narrow, rank, states = r.x.shape[1], r.dt.shape[0], r.decay.shape[0]
    small = r.small_here[...]
    r.x[...] = small[:, :narrow]
    turned = small[:, narrow:].T
    r.dt[...] = turned[:rank]
    r.decay[...] = turned[rank : rank + states]
    r.chan[...] = turned[rank + states : rank + states + 7]
    flat = r.flat_here[...]
    width = flat.shape[1]
    count = width // r.gains.shape[1]
    gains, tail = jnp.zeros(r.gains.shape, f32), jnp.zeros(r.small.shape, f32)
    for k in range(count):
        gain_at, tail_at = k * r.gains.shape[1], k * r.small.shape[1]
        mine = me == k
        gains = gains + jnp.where(mine, flat[0:2, gain_at : gain_at + r.gains.shape[1]], 0.0)
        tail = tail + jnp.where(mine, flat[2:3, tail_at : tail_at + r.small.shape[1]], 0.0)
    r.gains[...] = gains
    r.small[...] = tail
    totals = [jnp.sum(flat[3 + k : 4 + k], axis=1, keepdims=True) for k in range(3)]
    r.rms[...] = jnp.sqrt(jnp.concatenate(totals, 1) / cells)
    for copy in copies:
        copy.wait()


def finish(made, cells, narrow, rank, states, count):
    rows_out = made.small_out.shape[0]
    width = made.flat_out.shape[1]
    rows_in, hid = made.gate_out.shape
    channels = made.cin_out.shape[1]
    outs = dict(
        out=shape_of(*made.out_rows.shape, dtype=bf16),
        stream=shape_of(*made.stream_grad.shape),
        gains=shape_of(2, width // count),
        w_in=shape_of(rows_in, 2, channels),
        chan=shape_of(7, rows_out),
        decay=shape_of(states, rows_out),
        x=shape_of(rows_out, narrow),
        small=shape_of(1, narrow // count),
        dt=shape_of(rank, rows_out),
        w_out=shape_of(*made.out_out.shape),
        w_gate_up=shape_of(rows_in, 2, hid),
        w_down=shape_of(*made.down_out.shape),
        rms=shape_of(1, 3),
    )
    ins = vars(made)
    held = [
        made.out_rows, made.stream_grad, made.out_out, made.down_out, made.gate_out, made.up_out,
        made.cin_out, made.gin_out, made.small_out, made.flat_out,
    ]
    places = [pltpu.VMEM(item.shape, item.dtype) for item in held]
    names = [(name, 0) for name in [*ins, *outs]]
    rest = dict(here=8, small_here=0, flat_here=0, sems=0, out_sems=0)
    names += list(rest.items())
    big = {id(outs[name]) for name in ("out", "stream", "w_in", "w_out", "w_gate_up", "w_down")}
    done = pl.pallas_call(
        functools.partial(finish_kernel, cells, names),
        out_shape=list(outs.values()),
        in_specs=[ANY for _ in ins],
        out_specs=[ANY if id(item) in big else VMEM for item in outs.values()],
        scratch_shapes=[*places, pltpu.SemaphoreType.DMA((10,)), pltpu.SemaphoreType.DMA((8,))],
        compiler_params=pltpu.CompilerParams(vmem_limit_bytes=62 * 2**20),
        name="finish",
    )(*ins.values())
    out, stream, gains, w_in, chan, decay, x, small, dt, w_out, w_gate_up, w_down, rms = done
    return (
        out, stream, gains, w_in, chan, decay, x, small.reshape(-1), dt, w_out, w_gate_up, w_down,
        rms.reshape(-1),
    )


def local(
    seq_count,
    stream,
    doc_bounds,
    norm_gains,
    w_in,
    chan_vectors,
    decay_logs,
    w_x,
    small_gains,
    w_dt,
    w_out,
    w_gate_up,
    w_down,
    cotangent,
):
    tokens, width = stream.shape
    rank, (states, channels) = w_dt.shape[0], decay_logs.shape

    w_in_flat = w_in.reshape(width, 2 * channels)
    (
        in_proj, one_in, halo, pre_conv, conv_low, raw_proj, step_pre, into, out_of, scan_out, gated_low,
        last_state, mixer_low, gated_in, before, one_came, cot_came, w_gate_up_flat,
    ) = mixer_forward(
        doc_bounds, stream, norm_gains, chan_vectors, decay_logs, w_x, small_gains[None], w_dt,
        w_out, w_in_flat, cotangent, w_gate_up, seq_count, 1,
    )
    mid = feed_forward(
        dict(stream=stream, mixer=mixer_low, gains=norm_gains),
        dict(
            cot=cotangent, cot_came=cot_came, w_gate_up_in=w_gate_up_flat,
            w_down_in=w_down,
        ),
        seq_count,
        3,
    )
    made = backward(
        dict(
            bounds=doc_bounds, stream=stream, gains=norm_gains, two_total=mid.total,
            proj=in_proj, halo=halo,
            pre=pre_conv, low=conv_low, raw=raw_proj, step_pre=step_pre, last_state=last_state,
            chan=chan_vectors, logs=decay_logs, w_x=w_x, w_dt=w_dt, small_gains=small_gains[None],
        ),
        dict(
            feed_part=mid.feed_part, left_two_in=mid.left_two, right_two_in=mid.right_two,
            down_away_in=mid.down_away, down_kept_in=mid.down_kept,
            late_away_in=mid.late_away, late_kept_in=mid.late_kept, mixer_in=mixer_low,
            cot=cotangent, gated_in=gated_in, one_in=one_in,
            one_came=one_came, w_out=w_out, w_in=w_in_flat, scan_in=scan_out, into_in=into,
            out_of_in=out_of, hist_in=before,
        ),
        seq_count,
        2,
    )
    return finish(
        made, tokens * seq_count * width, w_x.shape[1], rank, states, seq_count
    )


def solution(mesh):
    in_specs = (
        P("seq", None),
        P(),
        P(),
        P(None, None, "ch"),
        P(None, "ch"),
        P(None, "ch"),
        P("ch", None),
        P(),
        P(None, "ch"),
        P("ch", None),
        P(None, None, "ch"),
        P("ch", None),
        P("seq", None),
    )
    out_specs = (
        P("seq", None),
        P("seq", None),
        P(None, "seq"),
        P("seq", None, "ch"),
        P(None, ("ch", "seq")),
        P(None, ("ch", "seq")),
        P(("ch", "seq"), None),
        P("seq"),
        P(None, ("ch", "seq")),
        P(("ch", "seq"), None),
        P("seq", None, "ch"),
        P(("ch", "seq"), None),
        P(),
    )
    return jax.shard_map(
        functools.partial(local, mesh.shape["seq"]),
        mesh=mesh,
        in_specs=in_specs,
        out_specs=out_specs,
        check_vma=False,
    )
```

```python
import functools
import math
import types

import jax
import jax.numpy as jnp
from jax import lax
from jax.experimental import pallas as pl
from jax.experimental.pallas import tpu as pltpu
from jax.sharding import PartitionSpec as P

f32 = jnp.float32
bf16 = jnp.bfloat16
LOG2E = math.log2(math.e)
LN2 = math.log(2.0)
RESET = 1e30
UNROLL = 8
LANES = 256
VMEM = pl.BlockSpec(memory_space=pltpu.VMEM)


def shape_of(*dims, dtype=f32):
    return jax.ShapeDtypeStruct(dims, dtype)


def cost(us):
    return pl.CostEstimate(flops=int(us * 1e9), bytes_accessed=int(us * 1e6), transcendentals=0)


def widened(column, width):
    return jnp.concatenate([column] * (width // 128), 1)


ANY = pl.BlockSpec(memory_space=pl.ANY)


def sent(source, target, sends, receives, slot, axis, partner):
    copy = pltpu.make_async_remote_copy(
        src_ref=source,
        dst_ref=target,
        send_sem=sends.at[slot],
        recv_sem=receives.at[slot],
        device_id={axis: partner},
        device_id_type=pl.DeviceIdType.MESH,
    )
    copy.start()
    return copy


def bits_of(count):
    return [1 << k for k in range(count.bit_length() - 1)]


def flipped(me, bit):
    mine = lax.rem(me // bit, 2)
    return mine, me + bit - 2 * bit * mine


CHUNK = 32


def sigmoid(values):
    return 1.0 / (1.0 + jnp.exp(-values))


def softplus(values):
    return jnp.maximum(values, 0.0) + jnp.log1p(jnp.exp(-jnp.abs(values)))


def row_doc(places, bounds):
    return (places >= bounds[0]).astype(jnp.int32) + (places >= bounds[1]).astype(jnp.int32)


def tap_mask(places, bounds, offset):
    source = places - offset
    same = row_doc(source, bounds) == row_doc(places, bounds)
    return jnp.where((source >= 0) & same, 1.0, 0.0)


def mean_square(values):
    return jnp.mean(values * values, axis=-1, keepdims=True)


def three_norms(raw, gains, rank, states):
    low, mid, high = raw[:, :rank], raw[:, rank : rank + states], raw[:, rank + states :]
    low_scale = lax.rsqrt(mean_square(low) + 1e-06)
    mid_scale = lax.rsqrt(jnp.maximum(mean_square(mid), 0.1))
    high_scale = lax.rsqrt(jnp.maximum(mean_square(high), 0.1))
    return (
        low * low_scale * gains[:, :rank],
        mid * mid_scale * gains[:, rank : rank + states],
        high * high_scale * gains[:, rank + states :],
    )


def widen(values, wide, first, count):
    states = values.shape[1]
    eye = (
        lax.broadcasted_iota(jnp.int32, (states, states), 0)
        == lax.broadcasted_iota(jnp.int32, (states, states), 1)
    ).astype(f32)
    spread = jnp.sum(values[:, None, :] * eye[None], axis=-1, keepdims=True)
    wide[pl.ds(first, count)] = jnp.broadcast_to(spread, (count, states, 128))


def greeted(axis_partners):
    barrier = pltpu.get_barrier_semaphore()
    for axis, partner in axis_partners:
        pl.semaphore_signal(
            barrier, inc=1, device_id={axis: partner}, device_id_type=pl.DeviceIdType.MESH
        )
    pl.semaphore_wait(barrier, len(axis_partners))


def handed_on(forward, state, steps, rates, r):
    me, count = lax.axis_index("seq"), r.state_land.shape[0] + 1
    r.state_move[...] = state.astype(bf16)
    r.steps_move[...] = steps
    copies = []
    for k in range(1, count):
        to = lax.rem(me + k, count)
        for source, land, sends, receives in (
            (r.state_move, r.state_land, r.state_sends, r.state_receives),
            (r.steps_move, r.steps_land, r.steps_sends, r.steps_receives),
        ):
            copies.append(sent(source, land.at[k - 1], sends, receives, k - 1, "seq", to))
    yield
    for copy in copies:
        copy.wait()
    total = jnp.zeros_like(state)
    passed = jnp.zeros_like(steps)
    for k in range(1, count):
        slot = k - 1 if forward else count - k - 1
        valid = (me >= k) if forward else (me + k < count)
        term = jnp.exp2(rates * passed) * r.state_land[slot].astype(f32)
        total = total + jnp.where(valid, term, 0.0)
        passed = passed + jnp.where(valid, r.steps_land[slot], 0.0)
    yield total


def handing(count, states, channels):
    sems = pltpu.SemaphoreType.DMA((count - 1,))
    return dict(
        state_move=pltpu.VMEM((states, channels), bf16),
        steps_move=pltpu.VMEM((1, channels), f32),
        state_land=pltpu.VMEM((count - 1, states, channels), bf16),
        steps_land=pltpu.VMEM((count - 1, 1, channels), f32),
        state_sends=sems,
        state_receives=sems,
        steps_sends=sems,
        steps_receives=sems,
    )


def turn(values, first, turned):
    rows = turned.shape[3]
    across_rows = values.T
    for k in range(values.shape[1] // rows):
        owner = first // rows + k
        turned[owner // 4, (owner // 2) % 2, owner % 2] = across_rows[k * rows : (k + 1) * rows]


def forward_kernel(
    bits, bounds, stream, norm_gains, chan, logs, w_x, gains, w_dt, w_out, w_in, cot, w_pairs,
    proj, one_in, halo, pre_out, low_out, raw_out, step_pre_out, into, out_of, scan_out, gated_out, last_state,
    mixer, turned_gate, hist_out, one_came, cot_came, w_flat,
    extended, raw_move, raw_land, step, drive, starts, part, first_land,
    second_move, second_land, hist, sends, receives, hist_sem, shared_sends, shared_receives,
    sum_sends, sum_receives, weights, normed, weight_sem, pairs, flat, pair_sems, *handed,
):
    tokens, channels = low_out.shape
    rank, states = w_dt.shape[0], logs.shape[0]
    chunks = tokens // CHUNK
    width = stream.shape[1]
    loads = []
    for k in range(width // 512):
        cols = pl.ds(k * 512, 512)
        copy = pltpu.make_async_copy(w_in.at[:, cols], weights.at[:, cols], weight_sem.at[k])
        copy.start()
        loads.append(copy)
    pair_copies = [pltpu.make_async_copy(w_pairs, pairs, pair_sems.at[0])]
    pair_copies[0].start()
    ahead = [0]

    def relay(count):
        first = ahead[0]
        ahead[0] = last = min(first + count, width // CHUNK)
        if first == 0:
            pair_copies.pop().wait()
        hid = pairs.shape[2]

        def laid(index, _):
            rows = pl.ds(pl.multiple_of(index * CHUNK, CHUNK), CHUNK)
            flat[rows, 0:hid] = pairs[rows, 0, :]
            flat[rows, hid:] = pairs[rows, 1, :]
            return 0

        lax.fori_loop(first, last, laid, 0)
        rows = pl.ds(first * CHUNK, (last - first) * CHUNK)
        copy = pltpu.make_async_copy(
            flat.at[rows], w_flat.at[rows], pair_sems.at[1 + len(pair_copies)]
        )
        copy.start()
        pair_copies.append(copy)

    ch_me, me = lax.axis_index("ch"), lax.axis_index("seq")
    seq_count = 1 << len(bits)
    low, across = flipped(ch_me, 1)
    high, along = flipped(ch_me, 2)
    following = lax.rem(me + 1, seq_count)
    greeted(
        [("ch", across), ("ch", along)]
        + [("seq", lax.rem(me + k, seq_count)) for k in range(1, seq_count)]
    )
    def norm_one(index, _):
        rows = pl.ds(pl.multiple_of(index * CHUNK, CHUNK), CHUNK)
        value = stream[rows].astype(f32)
        scale = lax.rsqrt(mean_square(value) + 1e-06)
        normed[rows] = (value * scale * norm_gains[0:1]).astype(bf16)
        return 0

    lax.fori_loop(0, chunks, norm_one, 0)

    def project(index, _):
        cols = pl.ds(pl.multiple_of(index * 256, 256), 256)
        proj[:, cols] = jnp.dot(
            normed[...], weights[:, cols], preferred_element_type=f32
        ).astype(bf16)
        return 0

    for copy in loads:
        copy.wait()
    lax.fori_loop(0, channels // 256, project, 0)
    halo_copy = sent(
        proj.at[pl.ds(tokens - 16, 16), pl.ds(0, channels)], halo, sends, receives, 0, "seq",
        following,
    )
    for at in range(0, width, 384):
        turn(normed[:, at : at + 384], at, one_in)
    mine, pair = flipped(me, bits[1])
    half = one_in.shape[0] // 2
    some = pl.ds(low * half, half)
    at = pl.ds(pl.multiple_of(low * (tokens // 2), tokens // 2), tokens // 2)
    shared = [
        (one_in.at[some, 1 - mine], one_came.at[some]),
        (cot.at[at], cot_came.at[at]),
    ]
    shared_copies = [
        sent(source, target, shared_sends, shared_receives, k, "seq", pair)
        for k, (source, target) in enumerate(shared)
    ]
    lax.fori_loop(channels // 256, 2 * channels // 256, project, 0)
    rates = -jnp.exp(logs[...]) * LOG2E

    def spread(index, _):
        first = pl.multiple_of(index * CHUNK, CHUNK)
        extended[pl.ds(first + 16, CHUNK)] = proj[pl.ds(first, CHUNK), :channels].astype(f32)
        return 0

    lax.fori_loop(0, chunks, spread, 0)

    def convolved(index, _):
        first = pl.multiple_of(index * CHUNK, CHUNK)
        places = me * tokens + first + lax.broadcasted_iota(jnp.int32, (CHUNK, 128), 0)
        window = extended[pl.ds(first, CHUNK + 16)]
        summed = chan[4:5]
        for k in range(4):
            mask = widened(tap_mask(places, bounds, 3 - k), channels)
            summed = summed + chan[k : k + 1] * window[13 + k : 13 + k + CHUNK] * mask
        pre_out[pl.ds(first, CHUNK)] = summed
        low_out[pl.ds(first, CHUNK)] = (summed * sigmoid(summed)).astype(bf16)
        return 0

    lax.fori_loop(1, chunks, convolved, 0)
    halo_copy.wait()
    extended[0:16] = halo[...].astype(f32)
    convolved(0, 0)
    raw_move[0] = jnp.dot(low_out[...], w_x[...], preferred_element_type=f32)
    copy = sent(raw_move.at[0], raw_land.at[0], sends, receives, 1, "ch", across)
    relay(4)
    copy.wait()
    raw_move[1] = raw_move[0] + raw_land[0]
    copy = sent(raw_move.at[1], raw_land.at[1], sends, receives, 2, "ch", along)
    relay(9)
    copy.wait()

    def stepped(index, total):
        first = pl.multiple_of(index * CHUNK, CHUNK)
        rows = pl.ds(first, CHUNK)
        raw = raw_move[1, rows] + raw_land[1, rows]
        raw_out[rows] = raw
        step_norm, input_norm, output_norm = three_norms(raw, gains[...], rank, states)
        widen(input_norm, into, first, CHUNK)
        widen(output_norm, out_of, first, CHUNK)
        pre = (
            jnp.dot(step_norm.astype(bf16), w_dt[...], preferred_element_type=f32) + chan[5:6]
        )
        step_pre_out[rows] = pre
        size = softplus(pre)
        drive[rows] = size * low_out[rows].astype(f32)
        places = me * tokens + first + lax.broadcasted_iota(jnp.int32, (CHUNK, 128), 0)
        resets = jnp.where((places == bounds[0]) | (places == bounds[1]), RESET, 0.0)
        size = size + widened(resets, channels)
        step[rows] = size
        return total + jnp.sum(size, axis=0, keepdims=True)

    total = lax.fori_loop(0, chunks, stepped, jnp.zeros((1, channels), f32))
    blocks = [slice(j, j + LANES) for j in range(0, channels, LANES)]
    for lanes in blocks:
        block_rates = rates[:, lanes]

        def ended(index, state, lanes=lanes, block_rates=block_rates):
            first = pl.multiple_of(index * UNROLL, UNROLL)
            steps, drives = step[pl.ds(first, UNROLL), lanes], drive[pl.ds(first, UNROLL), lanes]
            for k in range(UNROLL):
                decay = jnp.exp2(steps[k : k + 1] * block_rates)
                state = decay * state + widened(into[first + k], LANES) * drives[k : k + 1]
            return state

        starts[:, lanes] = lax.fori_loop(
            0, tokens // UNROLL, ended, jnp.zeros((states, LANES), f32)
        )
    hand = types.SimpleNamespace(**dict(zip(handing(2, 8, 128), handed)))
    handed_in = handed_on(True, starts[...], total, rates, hand)
    next(handed_in)
    relay(14)
    starts[...] = next(handed_in)
    hist_copies = []
    for number, lanes in enumerate(blocks):
        block_rates = rates[:, lanes]
        skip = chan[6:7, lanes]

        def walked(index, state, lanes=lanes, block_rates=block_rates, skip=skip):
            first = pl.multiple_of(index * UNROLL, UNROLL)
            steps, drives = step[pl.ds(first, UNROLL), lanes], drive[pl.ds(first, UNROLL), lanes]
            rows = []
            for k in range(UNROLL):
                hist[first + k, :, lanes] = state
                decay = jnp.exp2(steps[k : k + 1] * block_rates)
                state = decay * state + widened(into[first + k], LANES) * drives[k : k + 1]
                rows.append(
                    jnp.sum(widened(out_of[first + k], LANES) * state, axis=0, keepdims=True)
                )
            scan_out[pl.ds(first, UNROLL), lanes] = jnp.concatenate(rows, 0)
            return state

        last_state[:, lanes] = lax.fori_loop(0, tokens // UNROLL, walked, starts[:, lanes])
        copy = pltpu.make_async_copy(
            hist.at[:, :, lanes], hist_out.at[:, :, lanes], hist_sem.at[number]
        )
        copy.start()
        hist_copies.append(copy)

    def gate(index, _):
        first = pl.multiple_of(index * CHUNK, CHUNK)
        rows = pl.ds(first, CHUNK)
        scanned = scan_out[rows] + chan[6:7] * low_out[rows].astype(f32)
        scan_out[rows] = scanned
        gate_pre = proj[rows, channels:].astype(f32)
        gated_out[rows] = (scanned * gate_pre * sigmoid(gate_pre)).astype(bf16)
        return 0

    lax.fori_loop(0, chunks, gate, 0)
    quarter = tokens // 4
    for k, (_, target) in enumerate(shared):
        shared_copies[k].wait()
        shared_copies[k] = sent(
            target, target, shared_sends, shared_receives, 2 + k, "ch", across
        )

    def mixed(index, _):
        first = pl.multiple_of(index * 256, 256)
        product = jnp.dot(
            gated_out[...], w_out[:, pl.ds(first, 256)], preferred_element_type=f32
        ).astype(bf16)
        for k in range(4):
            part[k // 2, k % 2, :, pl.ds(first, 256)] = product[k * quarter : (k + 1) * quarter]
        return 0

    held = types.SimpleNamespace(
        first_land=first_land, second_land=second_land, second_move=second_move, total=mixer,
        sum_sends=sum_sends, sum_receives=sum_receives,
    )
    sums = [four_summed(held, (low, across, high, along), part, 0, k) for k in range(2)]
    for k, item in enumerate(sums):
        lax.fori_loop(k * width // 512, (k + 1) * width // 512, mixed, 0)
        next(item)
    turns = in_turn(*sums)
    for at in range(0, channels, 384):
        turn(gated_out[:, at : at + 384], at, turned_gate)
    for count in (3, 8, 8, width):
        next(turns)
        if ahead[0] < width // CHUNK:
            relay(count)
    next(turns)
    for copy in hist_copies + shared_copies + pair_copies:
        copy.wait()


def mixer_forward(
    bounds, stream, norm_gains, chan, logs, w_x, gains, w_dt, w_out, w_in, cot, w_pairs, count,
    ident,
):
    bits = bits_of(count)
    tokens, channels = stream.shape[0], w_out.shape[0]
    states, rank, width = logs.shape[0], w_dt.shape[0], w_out.shape[1]
    quarter, narrow = tokens // 4, w_x.shape[1]
    rows = shape_of(tokens, channels)
    low_rows = shape_of(tokens, channels, dtype=bf16)
    wide = shape_of(tokens, states, 128)
    raws = pltpu.VMEM((2, tokens, narrow), f32)
    out = pl.pallas_call(
        functools.partial(forward_kernel, bits),
        out_shape=[
            shape_of(tokens, 2 * channels, dtype=bf16),
            shape_of(count // 4, 2, 2, width // count, tokens, dtype=bf16),
            shape_of(16, channels, dtype=bf16), rows, low_rows, shape_of(tokens, narrow), rows,
            wide, wide, rows, low_rows, shape_of(states, channels),
            shape_of(2, 2, quarter, width, dtype=bf16),
            shape_of(count // 4, 2, 2, channels // count, tokens, dtype=bf16),
            shape_of(tokens, states, channels),
            shape_of(count // 4, 2, width // count, tokens, dtype=bf16),
            shape_of(tokens, width, dtype=bf16),
            shape_of(width, 2 * w_pairs.shape[2], dtype=bf16),
        ],
        in_specs=[pl.BlockSpec(memory_space=pltpu.SMEM)] + [VMEM] * 8 + [ANY] * 3,
        out_specs=[VMEM] * 14 + [ANY] * 4,
        scratch_shapes=[
            pltpu.VMEM((tokens + 16, channels), f32), raws, raws,
            pltpu.VMEM((tokens, channels), f32), pltpu.VMEM((tokens, channels), f32),
            pltpu.VMEM((states, channels), f32),
            pltpu.VMEM((2, 2, quarter, width), bf16), pltpu.VMEM((2, quarter, width), bf16),
            pltpu.VMEM((quarter, width), bf16), pltpu.VMEM((quarter, width), bf16),
            pltpu.VMEM((tokens, states, channels), f32),
            pltpu.SemaphoreType.DMA((3,)), pltpu.SemaphoreType.DMA((3,)),
            pltpu.SemaphoreType.DMA((channels // LANES,)),
            pltpu.SemaphoreType.DMA((4,)), pltpu.SemaphoreType.DMA((4,)),
            pltpu.SemaphoreType.DMA((8,)), pltpu.SemaphoreType.DMA((8,)),
            pltpu.VMEM(w_in.shape, bf16), pltpu.VMEM((tokens, width), bf16),
            pltpu.SemaphoreType.DMA((width // 512,)),
            pltpu.VMEM(w_pairs.shape, bf16), pltpu.VMEM((width, 2 * w_pairs.shape[2]), bf16),
            pltpu.SemaphoreType.DMA((9,)),
            *handing(count, states, channels).values(),
        ],
        compiler_params=pltpu.CompilerParams(
            collective_id=ident, has_side_effects=True, vmem_limit_bytes=56 * 2**20
        ),
        cost_estimate=cost(6),
        name="mixer_forward",
    )(bounds, stream, norm_gains, chan, logs, w_x, gains, w_dt, w_out, w_in, cot, w_pairs)
    return out


class Unit:
    def __init__(self, left, right, columns, refs, sends, receives, slot, bits, result):
        self.left, self.right, self.columns = left, right, columns
        away, *self.land, self.kept = refs
        self.away = [away.at[pl.ds(0, land.shape[0])] for land in self.land]
        self.sends, self.receives, self.slot, self.bits = sends, receives, slot, bits
        self.result = result
        self.stage = 0
        self.copy = None

    def made(self, *needed):
        for item in needed:
            item.wait()
        mine, partner = flipped(lax.axis_index("seq"), self.bits[0])
        self.make(1 - mine, self.away[0])
        self.stage = 1
        self.go = lambda: self.begin(partner, mine)
        return self

    def begin(self, partner, mine):
        self.copy = self.start(0, partner)
        self.make(mine, self.kept)

    def begun(self):
        _, partner = flipped(lax.axis_index("seq"), self.bits[0])
        self.stage = 1
        self.copy = self.start(0, partner)

    def resume(self):
        self.stage = 2
        if len(self.bits) > 1:
            _, partner = flipped(lax.axis_index("seq"), self.bits[1])
            self.copy = self.start(1, partner)

    def next(self, send_on=True):
        stage, me = self.stage, lax.axis_index("seq")
        if stage > len(self.bits):
            return
        self.stage += 1
        left_over = stage == len(self.bits)
        self.copy.wait()
        count = self.land[stage - 1].shape[0]
        rows = self.kept.shape[1]
        part = 32 if rows % 32 == 0 else rows
        parts = rows // part

        def total(index, at):
            return self.kept[index, at] + self.land[stage - 1][index, at].astype(f32)

        if left_over:

            def finish(step, _):
                at = pl.ds(pl.multiple_of(step * part, part), part)
                self.kept[0, at] = total(0, at)
                return 0

            lax.fori_loop(0, parts, finish, 0)
            self.written = self.result(self.kept.at[0])
            return
        mine, partner = flipped(me, self.bits[stage])

        def send(step, _):
            index = lax.div(step, parts)
            at = pl.ds(pl.multiple_of(lax.rem(step, parts) * part, part), part)
            self.away[stage][index, at] = total(2 * index + 1 - mine, at).astype(bf16)
            return 0

        lax.fori_loop(0, (count // 2) * parts, send, 0)
        if send_on:
            self.copy = self.start(stage, partner)

        def keep(step, _):
            index = lax.div(step, parts)
            at = pl.ds(pl.multiple_of(lax.rem(step, parts) * part, part), part)
            self.kept[index, at] = total(2 * index + mine, at)
            return 0

        lax.fori_loop(0, (count // 2) * parts, keep, 0)

    def start(self, stage, partner):
        return sent(
            self.away[stage], self.land[stage], self.sends, self.receives, self.slot + stage,
            "seq", partner,
        )

    def make(self, side, target):
        first, width = self.columns
        tile = width if width <= 512 else 512 if width % 512 == 0 else 384
        tiles = width // tile
        count, rows = target.shape[:2]
        together = count if rows % 16 == 0 else 1

        def block(step, _):
            index = lax.div(step, tiles)
            column = pl.multiple_of(lax.rem(step, tiles) * tile, tile)
            left = self.left[:, side] if together > 1 else self.left[pl.ds(index, 1), side]
            product = jnp.dot(
                left.reshape(together * rows, left.shape[2]),
                self.right[:, pl.ds(first + column, tile)],
                preferred_element_type=f32,
            ).astype(target.dtype)
            at = pl.ds(0, count) if together > 1 else pl.ds(index, 1)
            target[at, :, pl.ds(column, tile)] = product.reshape(together, rows, tile)
            return 0

        lax.fori_loop(0, count // together * tiles, block, 0)


def norm_back(values, scale, gains, grad, free=True):
    weighted = gains * grad
    result = scale * weighted
    inner = jnp.mean(values * weighted, axis=-1, keepdims=True)
    return result - jnp.where(free, 1.0, 0.0) * values * (scale * scale * scale) * inner, (
        grad * values * scale
    )


def silu_slope(values):
    part = sigmoid(values)
    return part * (1.0 + values * (1.0 - part))


def narrowed(wide, first, count):
    states = wide.shape[1]
    eye = (
        lax.broadcasted_iota(jnp.int32, (states, states), 0)
        == lax.broadcasted_iota(jnp.int32, (states, states), 1)
    ).astype(f32)
    sums = jnp.sum(wide[pl.ds(first, count)], axis=-1, keepdims=True)
    return jnp.sum(sums * eye[None], axis=1)


def dot_rows(left, right):
    return lax.dot_general(left, right, (((1,), (1,)), ((), ())), preferred_element_type=f32)


class Once:
    def __init__(self, *copies, then=None):
        self.copies, self.then = copies, then

    def wait(self):
        for copy in self.copies:
            copy.wait()
        self.copies = ()
        if self.then is not None:
            after, self.then = self.then, None
            after().wait()


def named(names, refs):
    refs, found = list(refs), {}
    for name, count in names:
        taken, refs = refs[: count or 1], refs[count or 1 :]
        found[name] = taken if count else taken[0]
    return types.SimpleNamespace(**found)


def four_summed(r, place, value, base, part):
    low, across, high, along = place
    half = value.shape[3] // 2
    cols = pl.ds(part * half, half)
    first, second, moving = (
        r.first_land.at[:, :, cols], r.second_land.at[:, cols], r.second_move.at[:, cols]
    )
    total, value = r.total.at[:, :, :, cols], value.at[:, :, :, cols]
    sends, receives, base = r.sum_sends, r.sum_receives, base + 4 * part
    copy = sent(value.at[:, 1 - low], first, sends, receives, base, "ch", across)
    yield
    copy.wait()
    moving[...] = (
        value[1 - high, low].astype(f32) + first[1 - high].astype(f32)
    ).astype(bf16)
    copy = sent(moving, second, sends, receives, base + 1, "ch", along)
    yield
    copy.wait()
    total[high, low] = (
        value[high, low].astype(f32) + first[high].astype(f32) + second[...].astype(f32)
    ).astype(bf16)
    own = total.at[high, low]
    copy = sent(own, own, sends, receives, base + 2, "ch", along)
    yield
    copy.wait()
    both = total.at[:, low]
    copy = sent(both, both, sends, receives, base + 3, "ch", across)
    yield
    copy.wait()
    yield


def in_turn(*steps):
    for _ in range(4):
        yield
        for item in steps:
            next(item)
    yield


def feed_forward_kernel(bits, names, *refs):
    r = named(names, refs)
    tokens, width = r.stream.shape
    quarter, chunks, seq_count = tokens // 4, tokens // CHUNK, 1 << len(bits)
    ch_me, me = lax.axis_index("ch"), lax.axis_index("seq")
    low, across = flipped(ch_me, 1)
    high, along = flipped(ch_me, 2)
    pair_bit, rest_bits = bits[1], [bits[0], *bits[2:]]
    mine, pair = flipped(me, pair_bit)
    hid = r.w_down_in.shape[0]
    tile = 256
    tiles = range(0, hid, tile)
    own, other = pl.ds(0, tokens), pl.ds(tokens, tokens)
    slots = []

    def load(source, target):
        copy = pltpu.make_async_copy(source, target, r.load_sems.at[len(slots)])
        copy.start()
        slots.append(0)
        return Once(copy)

    cot_own = load(r.cot, r.right_down.at[own])
    loads = []
    for at in tiles:
        loads.append(
            [
                load(r.w_gate_up_in.at[:, pl.ds(at, tile)], r.w_gate_up.at[:, pl.ds(at, tile)]),
                load(
                    r.w_gate_up_in.at[:, pl.ds(hid + at, tile)],
                    r.w_gate_up.at[:, pl.ds(hid + at, tile)],
                ),
                load(r.w_down_in.at[pl.ds(at, tile)], r.w_down.at[pl.ds(at, tile)]),
            ]
        )
    cot_other = load(r.cot_came, r.right_down.at[other])
    greeted(
        [("ch", across), ("ch", along), ("seq", pair), ("seq", flipped(me, rest_bits[0])[1])]
    )

    def norm_two(index, _):
        rows = pl.ds(pl.multiple_of(index * CHUNK, CHUNK), CHUNK)
        per = quarter // CHUNK
        part = lax.div(index, per)
        at = pl.ds(pl.multiple_of(lax.rem(index, per) * CHUNK, CHUNK), CHUNK)
        mixed = r.mixer[lax.div(part, 2), lax.rem(part, 2), at].astype(f32)
        middle = r.stream[rows].astype(f32) + mixed
        scale = lax.rsqrt(mean_square(middle) + 1e-06)
        r.normed[rows] = (middle * scale * r.gains[1:2]).astype(bf16)
        return 0

    lax.fori_loop(0, chunks, norm_two, 0)

    group = 384
    for at in range(0, width, group):
        turn(r.normed[:, at : at + group], at, r.two_turned)
    half = r.two_turned.shape[0] // 2
    some = pl.ds(low * half, half)
    target = r.left_two.at[some, :, :, other]
    two_copy = sent(
        r.two_turned.at[some, 1 - mine], target, r.pair_sends, r.pair_receives, 0, "seq", pair
    )
    r.left_two[:, :, :, own] = r.two_turned[:, mine]
    cot_own.wait()
    hidden_copies, quads_sent = [], 0
    for number, at in enumerate(tiles):
        for item in loads[number]:
            item.wait()
        gate = jnp.dot(
            r.normed[...], r.w_gate_up[:, pl.ds(at, tile)], preferred_element_type=f32
        )
        up = jnp.dot(
            r.normed[...], r.w_gate_up[:, pl.ds(hid + at, tile)], preferred_element_type=f32
        )
        part = sigmoid(gate)
        act = gate * part
        hidden = (act * up).astype(bf16)
        r.hidden[:, pl.ds(at, tile)] = hidden
        turn(hidden, at, r.hidden_turned)
        grad = dot_rows(r.right_down[own], r.w_down[pl.ds(at, tile)])
        r.right_two[own, pl.ds(at, tile)] = (
            grad * up * (part * (1.0 + gate * (1.0 - part)))
        ).astype(bf16)
        r.right_two[own, pl.ds(hid + at, tile)] = (grad * act).astype(bf16)
        quads = (at + tile) // r.hidden_turned.shape[3] // 4
        if quads > quads_sent:
            some = pl.ds(quads_sent, quads - quads_sent)
            hidden_copies.append(
                sent(
                    r.hidden_turned.at[some, 1 - mine], r.left_hidden.at[some, :, :, other],
                    r.pair_sends, r.pair_receives, 3 + len(hidden_copies), "seq", pair,
                )
            )
            quads_sent = quads
    gate_copy = sent(
        r.right_two.at[own, pl.ds(0, hid)], r.right_two.at[other, pl.ds(0, hid)], r.pair_sends,
        r.pair_receives, 1, "seq", pair,
    )
    r.left_hidden[:, :, :, own] = r.hidden_turned[:, mine]

    def store(values, target, at):
        for k in range(4):
            target[k // 2, k % 2, :, pl.ds(at, tile)] = values[k * quarter : (k + 1) * quarter]

    def two_part(index, _):
        at = pl.multiple_of(index * tile, tile)
        store(dot_rows(r.right_two[own], r.w_gate_up[pl.ds(at, tile)]).astype(bf16), r.part, at)
        return 0

    sums = [four_summed(r, (low, across, high, along), r.part, 0, k) for k in range(2)]
    for k, item in enumerate(sums):
        lax.fori_loop(k * width // (2 * tile), (k + 1) * width // (2 * tile), two_part, 0)
        next(item)
    total = in_turn(*sums)
    next(total)

    def feed_part(index, _):
        at = pl.multiple_of(index * tile, tile)
        product = jnp.dot(
            r.hidden[...], r.w_down[:, pl.ds(at, tile)], preferred_element_type=f32
        )
        store(product.astype(bf16), r.feed_part, at)
        return 0

    n_bits = len(rest_bits)
    part = width // 2
    down, down_late = (
        Unit(r.left_hidden, r.right_down, (k * part, part), r.down, r.unit_sends,
             r.unit_receives, 0, rest_bits, None)
        for k in range(2)
    )
    next(total)
    cot_other.wait()
    down.made(*hidden_copies).go()
    next(total)
    lax.fori_loop(0, width // tile, feed_part, 0)
    next(total)
    side, _ = flipped(me, rest_bits[0])
    down_late.make(1 - side, r.late_away)
    down_late.make(side, r.late_kept)
    two_copy.wait()
    two_copy = sent(target, target, r.pair_sends, r.pair_receives, 2, "ch", across)
    next(total)
    two_copy.wait()
    gate_copy.wait()
    if n_bits > 1:
        down.next(send_on=False)
    r.down_away[...] = down.away[1][...]
    kept = r.down_kept.shape[0]
    r.down_kept[...] = down.kept[0:kept]


def feed_forward(ins, hbm_ins, count, ident):
    bits = bits_of(count)
    n_bits = len(bits) - 1
    tokens, width = ins["stream"].shape
    hid = hbm_ins["w_down_in"].shape[0]
    half, quarter = count // 2, tokens // 4
    rows_in, rows_down = width // count, hid // count

    def low(*dims):
        return pltpu.VMEM(dims, bf16)

    def sems(size):
        return pltpu.SemaphoreType.DMA((size,))

    lands = [low(half >> (k + 1), rows_down, width // 2) for k in range(n_bits)]
    outs = dict(
        total=shape_of(2, 2, quarter, width, dtype=bf16),
        feed_part=shape_of(2, 2, quarter, width, dtype=bf16),
        left_two=shape_of(count // 4, 2, rows_in, 2 * tokens, dtype=bf16),
        right_two=shape_of(2 * tokens, 2 * hid, dtype=bf16),
        down_away=shape_of(half >> 2, rows_down, width // 2, dtype=bf16),
        down_kept=shape_of(half >> 2, rows_down, width // 2),
        late_away=shape_of(half >> 1, rows_down, width // 2, dtype=bf16),
        late_kept=shape_of(half >> 1, rows_down, width // 2),
    )
    scratch = dict(
        w_gate_up=low(width, 2 * hid),
        w_down=low(hid, width),
        normed=low(tokens, width),
        hidden=low(tokens, hid),
        two_turned=low(count // 4, 2, 2, rows_in, tokens),
        hidden_turned=low(count // 4, 2, 2, rows_down, tokens),
        left_hidden=low(count // 4, 2, rows_down, 2 * tokens),
        right_down=low(2 * tokens, width),
        part=low(2, 2, quarter, width),
        first_land=low(2, quarter, width),
        second_land=low(quarter, width),
        second_move=low(quarter, width),
        down=[low(half // 2, rows_down, width // 2), *lands, pltpu.VMEM((half // 2, rows_down, width // 2), f32)],
        load_sems=sems(2 + 3 * (hid // 256)),
        pair_sends=sems(7),
        pair_receives=sems(7),
        sum_sends=sems(8),
        sum_receives=sems(8),
        unit_sends=sems(n_bits),
        unit_receives=sems(n_bits),
    )
    names, shapes = [(name, 0) for name in [*ins, *hbm_ins, *outs]], []
    for name, held in scratch.items():
        listed = isinstance(held, list)
        names.append((name, len(held) if listed else 0))
        shapes += held if listed else [held]
    made = pl.pallas_call(
        functools.partial(feed_forward_kernel, bits, names),
        out_shape=list(outs.values()),
        in_specs=[VMEM] * len(ins) + [ANY] * len(hbm_ins),
        out_specs=[VMEM] * len(outs),
        scratch_shapes=shapes,
        compiler_params=pltpu.CompilerParams(
            collective_id=ident, has_side_effects=True, vmem_limit_bytes=56 * 2**20
        ),
        name="feed_forward",
    )(*ins.values(), *hbm_ins.values())
    return types.SimpleNamespace(**dict(zip(outs, made)))


def backward_kernel(bits, names, *refs):
    r = named(names, refs)
    tokens, width = r.stream.shape
    channels, rank, states = r.low.shape[1], r.w_dt.shape[0], r.logs.shape[0]
    quarter, chunks = tokens // 4, tokens // CHUNK
    ch_me, me = lax.axis_index("ch"), lax.axis_index("seq")
    seq_count = 1 << len(bits)
    low, across = flipped(ch_me, 1)
    high, along = flipped(ch_me, 2)
    pair_bit, rest_bits = bits[1], [bits[0], *bits[2:]]
    mine, pair = flipped(me, pair_bit)
    previous = lax.rem(me + seq_count - 1, seq_count)
    load_slots, pair_slots, shared_slots, write_slots = ([] for _ in range(4))

    def slot_of(slots):
        slots.append(0)
        return len(slots) - 1

    def load(source, target):
        copy = pltpu.make_async_copy(source, target, r.load_sems.at[slot_of(load_slots)])
        copy.start()
        return Once(copy)

    own, other = pl.ds(0, tokens), pl.ds(tokens, tokens)
    mixer_own = load(r.mixer_in, r.mixer)
    cot_own = load(r.cot, r.cot_rows)
    weights = load(r.w_out, r.weights)
    scan_own = load(r.scan_in, r.scan)
    out_of_own = load(r.out_of_in, r.out_of)
    into_own = load(r.into_in, r.into)
    hid = r.right_two_in.shape[1] // 2
    down_away = load(r.down_away_in, r.down[0].at[pl.ds(0, r.down_away_in.shape[0])])
    late_away = load(r.late_away_in, r.late[0])
    two_own = load(r.left_two_in, r.left_two)
    gate_up_own = load(r.right_two_in.at[own], r.right_two.at[own])
    gate_other = load(
        r.right_two_in.at[other, pl.ds(0, hid)], r.right_two.at[other, pl.ds(0, hid)]
    )
    down_kept = load(r.down_kept_in, r.down[-1].at[pl.ds(0, r.down_kept_in.shape[0])])
    late_kept = load(r.late_kept_in, r.late[-1])
    part_in = load(r.feed_part, r.part)
    one_own = load(r.one_in.at[:, mine], r.left_one.at[:, :, :, own])
    one_other = load(r.one_came, r.left_one.at[:, :, :, other])
    gated_own = load(r.gated_in.at[:, mine], r.left_gated.at[:, :, :, own])
    blocks = [slice(j, j + 128) for j in range(0, channels, 128)]
    hists = [load(r.hist_in.at[:, :, blocks[k]], r.hist.at[k]) for k in range(2)]

    greeted(
        [("ch", across), ("ch", along)]
        + [("seq", lax.rem(me + k, seq_count)) for k in range(1, seq_count)]
    )

    def swap(source, target):
        slot = slot_of(pair_slots)
        return Once(sent(source, target, r.pair_sends, r.pair_receives, slot, "seq", pair))

    def swap_shared(source, target):
        slot = 2 * slot_of(shared_slots)
        copy = sent(source, target, r.shared_sends, r.shared_receives, slot, "seq", pair)
        return Once(
            copy,
            then=lambda: sent(
                target, target, r.shared_sends, r.shared_receives, slot + 1, "ch", across
            ),
        )

    n_bits = len(rest_bits)

    def writer(target):
        def write(source):
            copy = pltpu.make_async_copy(source, target, r.write_sems.at[slot_of(write_slots)])
            copy.start()
            return copy

        return write

    def unit(left, right, columns, refs, slot, target):
        return Unit(
            left, right, columns, refs, r.unit_sends, r.unit_receives, slot * n_bits, rest_bits,
            writer(target),
        )

    part = width // 2
    down, late = (
        unit(None, None, None, refs, k, r.down_out.at[:, pl.ds(k * part, part)])
        for k, refs in enumerate((r.down, r.late))
    )
    part = hid // 2
    quarters = [
        unit(
            r.left_two, r.right_two, (k * part, part), refs, 2 + k,
            (r.gate_out, r.up_out)[k // 2].at[:, pl.ds(k % 2 * part, part)],
        )
        for k, refs in enumerate((r.gate0, r.gate1, r.up0, r.up1))
    ]
    gate0, gate1, up0, up1 = quarters
    part = width // 2
    outs = [
        unit(
            r.left_gated, r.right_out, (k * part, part), refs, 6 + 4 * k,
            r.out_out.at[:, pl.ds(k * part, part)],
        )
        for k, refs in enumerate((r.out0, r.out1))
    ]
    part = channels // 2
    gins = [
        unit(
            r.left_one, r.right_in, (channels + k * part, part), refs, 7 + 4 * k,
            r.gin_out.at[:, pl.ds(k * part, part)],
        )
        for k, refs in enumerate((r.gin0, r.gin1))
    ]
    cins = [
        unit(
            r.left_one, r.right_in, (k * part, part), refs, 8 + k,
            r.cin_out.at[:, pl.ds(k * part, part)],
        )
        for k, refs in enumerate((r.cin0, r.cin1))
    ]

    up_other = swap(
        r.right_two_in.at[own, pl.ds(hid, hid)], r.right_two.at[other, pl.ds(hid, hid)]
    )
    down_away.wait()
    down.resume()
    late_away.wait()
    late.begun()

    summed = functools.partial(four_summed, r, (low, across, high, along))


    rates = -jnp.exp(r.logs[...]) * LOG2E

    def places_of(first, count):
        return me * tokens + first + lax.broadcasted_iota(jnp.int32, (count, 128), 0)

    def resteps():
        def body(index, total):
            first = pl.multiple_of(index * CHUNK, CHUNK)
            rows = pl.ds(first, CHUNK)
            size = softplus(r.step_pre[rows])
            r.drive[rows] = size * r.low[rows].astype(f32)
            places = places_of(first, CHUNK)
            resets = jnp.where((places == r.bounds[0]) | (places == r.bounds[1]), RESET, 0.0)
            size = size + widened(resets, channels)
            r.step[rows] = size
            return total + jnp.sum(size, axis=0, keepdims=True)

        r.step_sum[...] = jnp.broadcast_to(
            lax.fori_loop(0, chunks, body, jnp.zeros((1, channels), f32)), (8, channels)
        )

    resteps()
    mixer_own.wait()
    cot_own.wait()

    def quarter_rows(index):
        per = quarter // CHUNK
        part = lax.div(index, per)
        at = pl.ds(pl.multiple_of(lax.rem(index, per) * CHUNK, CHUNK), CHUNK)
        return lax.div(part, 2), lax.rem(part, 2), at

    def norm_two(index, total):
        first = pl.multiple_of(index * CHUNK, CHUNK)
        rows = pl.ds(first, CHUNK)
        a, b, at = quarter_rows(index)
        middle = r.stream[rows].astype(f32) + r.mixer[a, b, at].astype(f32)
        scale = lax.rsqrt(mean_square(middle) + 1e-06)
        back, gain = norm_back(middle, scale, r.gains[1:2], r.two_total[a, b, at].astype(f32))
        grad = r.cot_rows[rows].astype(f32) + back
        r.stream_grad[rows] = grad
        r.right_out[rows] = grad.astype(bf16)
        return total + jnp.sum(gain, axis=0, keepdims=True)

    gain_two = lax.fori_loop(0, chunks, norm_two, jnp.zeros((1, width), f32))
    r.flat_move[0] = jnp.zeros_like(r.flat_move[0])
    r.flat_move[0, 1:2] = gain_two
    weights.wait()
    scan_own.wait()
    skips = []
    for j in range(0, channels, 256):
        lanes = slice(j, j + 256)
        gated_grad = dot_rows(r.right_out[own], r.weights[pl.ds(j, 256)])
        gate_pre = r.proj[:, channels + j : channels + j + 256].astype(f32)
        part = sigmoid(gate_pre)
        slope = part * (1.0 + gate_pre * (1.0 - part))
        r.right_in[own, channels + j : channels + j + 256] = (
            gated_grad * r.scan[:, lanes] * slope
        ).astype(bf16)
        grad = gated_grad * gate_pre * part
        r.scan[:, lanes] = grad
        skips.append(jnp.sum(grad * r.low[:, lanes].astype(f32), axis=0, keepdims=True))
    skip_grad = jnp.concatenate(skips, 1)
    weights = load(r.w_in.at[pl.ds(0, channels)], r.weights)
    out_of_own.wait()
    for j in range(0, channels, LANES):
        lanes = slice(j, j + LANES)

        def ended(index, carried, lanes=lanes, block_rates=rates[:, j : j + LANES]):
            first = pl.multiple_of(tokens - UNROLL - index * UNROLL, UNROLL)
            steps, grads = r.step[pl.ds(first, UNROLL), lanes], r.scan[pl.ds(first, UNROLL), lanes]
            for k in reversed(range(UNROLL)):
                decay = jnp.exp2(steps[k : k + 1] * block_rates)
                carried = decay * (widened(r.out_of[first + k], LANES) * grads[k : k + 1] + carried)
            return carried

        r.starts[:, lanes] = lax.fori_loop(
            0, tokens // UNROLL, ended, jnp.zeros((states, LANES), f32)
        )

    chain = handed_on(False, r.starts[...], r.step_sum[0:1], rates, r)
    next(chain)
    gate0.made(two_own, gate_up_own, gate_other)
    gate1.made()
    r.starts[...] = next(chain)
    gate0.go()
    late_kept.wait()
    late.next()
    gate1.go()
    up0.made(up_other)
    first = pl.multiple_of(low * (tokens // 2), tokens // 2)
    mixer_other = swap_shared(
        r.right_out.at[pl.ds(first, tokens // 2)],
        r.right_out.at[pl.ds(tokens + first, tokens // 2)],
    )
    gated_other = swap(r.gated_in.at[:, 1 - mine], r.left_gated.at[:, :, :, other])
    gin_other = swap(
        r.right_in.at[own, pl.ds(channels, channels)],
        r.right_in.at[other, pl.ds(channels, channels)],
    )
    up0.go()
    up1.made().go()

    part_in.wait()
    feed_sums = [summed(r.part, 0, k) for k in range(2)]
    into_own.wait()

    def results():
        totals = lax.fori_loop(
            0, chunks, results_of, tuple(jnp.zeros((1, width), f32) for _ in range(3))
        )
        for number, total in enumerate(totals):
            r.flat_move[0, 3 + number : 4 + number] = total

    def feed_start():
        for item in feed_sums:
            next(item)
        return in_turn(*feed_sums)

    feed = []
    between = [
        lambda: (feed.append(feed_start()), next(feed[0]), gate0.next()),
        lambda: next(feed[0]),
        lambda: (next(feed[0]), gate1.next()),
        lambda: next(feed[0]),
        lambda: (next(feed[0]), up0.next()),
        lambda: (
            results(), outs[0].made(gated_own, mixer_other, gated_other).go(), outs[1].made(),
        ),
    ]

    def results_of(index, totals):
        rows = pl.ds(pl.multiple_of(index * CHUNK, CHUNK), CHUNK)
        a, b, at = quarter_rows(index)
        mixed, feed = r.mixer[a, b, at].astype(f32), r.total[a, b, at].astype(f32)
        result = r.stream[rows].astype(f32) + mixed + feed
        r.out_rows[rows] = result.astype(bf16)
        return tuple(
            total + jnp.sum(v * v, axis=0, keepdims=True)
            for total, v in zip(totals, (result, mixed, feed))
        )

    r.into_wide[...] = jnp.zeros_like(r.into_wide)
    r.out_wide[...] = jnp.zeros_like(r.out_wide)
    for number, lanes in enumerate(blocks):
        hists[number].wait()
        hist = r.hist.at[number % 2]
        block_rates = rates[:, lanes]

        def walked(index, carry, lanes=lanes, block_rates=block_rates, hist=hist):
            carried, state, total = carry
            first = pl.multiple_of(tokens - UNROLL - index * UNROLL, UNROLL)
            some = pl.ds(first, UNROLL)
            steps, drives, grads = r.step[some, lanes], r.drive[some, lanes], r.scan[some, lanes]
            decay_list, push_list = [None] * UNROLL, [None] * UNROLL
            for k in reversed(range(UNROLL)):
                place = first + k
                grad_row = grads[k : k + 1]
                decay = jnp.exp2(steps[k : k + 1] * block_rates)
                adjoint = r.out_of[place] * grad_row + carried
                carried = decay * adjoint
                r.out_wide[place] = r.out_wide[place] + state * grad_row
                r.into_wide[place] = r.into_wide[place] + adjoint * drives[k : k + 1]
                state = hist[place]
                share = carried * state
                total = total + share * steps[k : k + 1]
                decay_list[k] = jnp.sum(share * block_rates, axis=0, keepdims=True)
                push_list[k] = jnp.sum(r.into[place] * adjoint, axis=0, keepdims=True)
            r.decay_rows[some, :] = jnp.concatenate(decay_list, 0)
            r.push[some, lanes] = jnp.concatenate(push_list, 0)
            return (carried, state, total)

        _, _, total = lax.fori_loop(
            0,
            tokens // UNROLL,
            walked,
            (r.starts[:, lanes], r.last_state[:, lanes], jnp.zeros((states, 128), f32)),
        )
        r.rate_sum[:, lanes] = total * (rates[:, lanes] * LN2)

        def gathered(index, _, lanes=lanes):
            rows = pl.ds(pl.multiple_of(index * CHUNK, CHUNK), CHUNK)
            used, pushed = r.low[rows, lanes].astype(f32), r.push[rows, lanes]
            pre = r.step_pre[rows, lanes]
            grad = (LN2 * r.decay_rows[rows] + pushed * used) * sigmoid(pre)
            r.step_low_grad[rows, lanes] = grad.astype(bf16)
            r.push[rows, lanes] = pushed * softplus(pre) + r.chan[6:7, lanes] * r.scan[rows, lanes]
            return 0

        lax.fori_loop(0, chunks, gathered, 0)
        if number + 2 < len(blocks):
            hists.append(load(r.hist_in.at[:, :, blocks[number + 2]], r.hist.at[number % 2]))
        if number < len(between):
            between[number]()
    for later in between[len(blocks) :]:
        later()

    def norm_grads(index, _):
        first = pl.multiple_of(index * CHUNK, CHUNK)
        rows = pl.ds(first, CHUNK)
        low_part = dot_rows(r.step_low_grad[rows], r.w_dt[...])
        r.raw_move[0, rows] = jnp.concatenate(
            [low_part, narrowed(r.into_wide, first, CHUNK), narrowed(r.out_wide, first, CHUNK)], 1
        )
        return 0

    lax.fori_loop(0, chunks, norm_grads, 0)
    copy = sent(r.raw_move.at[0], r.raw_land.at[0], r.raw_sends, r.raw_receives, 0, "ch", across)
    gins[0].made(one_own, one_other, gin_other)
    gins[1].made()
    copy.wait()
    r.raw_move[1] = r.raw_move[0] + r.raw_land[0]
    copy = sent(r.raw_move.at[1], r.raw_land.at[1], r.raw_sends, r.raw_receives, 1, "ch", along)
    up1.next()
    copy.wait()

    def raw_back(index, total):
        rows = pl.ds(pl.multiple_of(index * CHUNK, CHUNK), CHUNK)
        grads, raw = r.raw_move[1, rows] + r.raw_land[1, rows], r.raw[rows]
        gains = r.small_gains[...]
        values, sums_to = [], []
        for start, stop, floor in ((0, rank, None), (rank, rank + states, 0.1),
                                   (rank + states, rank + 2 * states, 0.1)):
            value = raw[:, start:stop]
            square = mean_square(value)
            if floor is None:
                scale, free = lax.rsqrt(square + 1e-06), True
            else:
                scale, free = lax.rsqrt(jnp.maximum(square, floor)), square > floor
            back, gain = norm_back(value, scale, gains[:, start:stop], grads[:, start:stop], free)
            values.append(back)
            sums_to.append(jnp.sum(gain, axis=0, keepdims=True))
        norm = raw[:, :rank] * lax.rsqrt(mean_square(raw[:, :rank]) + 1e-06) * gains[:, :rank]
        r.raw_low[rows] = jnp.concatenate(values, 1).astype(bf16)
        r.step_low[rows] = norm.astype(bf16)
        return total + jnp.concatenate(sums_to, 1)

    small = lax.fori_loop(0, chunks, raw_back, jnp.zeros((1, rank + 2 * states), f32))
    r.flat_move[0, 2:3, : rank + 2 * states] = small

    def conv_back(index, total):
        first = pl.multiple_of(index * CHUNK, CHUNK)
        rows = pl.ds(first, CHUNK)
        grad = r.push[rows] + dot_rows(r.raw_low[rows], r.w_x[...])
        grad = grad * silu_slope(r.pre[rows])
        r.grad_pre[rows] = grad
        return total + jnp.sum(grad, axis=0, keepdims=True)

    tap_bias = lax.fori_loop(0, chunks, conv_back, jnp.zeros((1, channels), f32))
    copy = sent(r.grad_pre.at[pl.ds(0, 8)], r.grad_pre.at[pl.ds(tokens, 8)], r.raw_sends,
                r.raw_receives, 2, "seq", previous)
    outs[1].go()
    gins[0].go()
    gins[1].go()
    r.extended[0:16] = r.halo[...].astype(f32)

    def extend(index, _):
        first = pl.multiple_of(index * CHUNK, CHUNK)
        r.extended[pl.ds(first + 16, CHUNK)] = r.proj[pl.ds(first, CHUNK), :channels].astype(f32)
        return 0

    lax.fori_loop(0, chunks, extend, 0)

    def taps(index, totals):
        first = pl.multiple_of(index * CHUNK, CHUNK)
        places = places_of(first, CHUNK)
        window = r.extended[pl.ds(first, CHUNK + 16)]
        grad = r.grad_pre[pl.ds(first, CHUNK)]
        return tuple(
            totals[k]
            + jnp.sum(
                grad
                * widened(tap_mask(places, r.bounds, 3 - k), channels)
                * window[13 + k : 13 + k + CHUNK],
                axis=0,
                keepdims=True,
            )
            for k in range(4)
        )

    tap_grads = lax.fori_loop(
        0, chunks, taps, tuple(jnp.zeros((1, channels), f32) for _ in range(4))
    )
    copy.wait()

    def conv_in_back(index, _):
        first = pl.multiple_of(index * CHUNK, CHUNK)
        window = r.grad_pre[pl.ds(first, CHUNK + 8)]
        grad = jnp.zeros((CHUNK, channels), f32)
        for k in range(4):
            places = places_of(first + 3 - k, CHUNK)
            mask = jnp.where(
                places < seq_count * tokens, tap_mask(places, r.bounds, 3 - k), 0.0
            )
            grad = grad + r.chan[k : k + 1] * widened(mask, channels) * window[3 - k : 3 - k + CHUNK]
        r.right_in[pl.ds(first, CHUNK), :channels] = grad.astype(bf16)
        return 0

    lax.fori_loop(0, chunks, conv_in_back, 0)
    cin_others = [
        swap(
            r.right_in.at[own, pl.ds(*item.columns)], r.right_in.at[other, pl.ds(*item.columns)]
        )
        for item in cins
    ]

    def small_columns():
        narrow = r.w_x.shape[1]
        pack = r.step
        pack[0:narrow] = lax.dot_general(
            r.raw_low[...], r.low[...], (((0,), (0,)), ((), ())), preferred_element_type=f32
        )
        pack[narrow : narrow + rank] = lax.dot_general(
            r.step_low[...], r.step_low_grad[...], (((0,), (0,)), ((), ())),
            preferred_element_type=f32,
        )
        at = narrow + rank
        pack[at : at + states] = r.rate_sum[...]
        at += states
        bias = jnp.sum(r.step_low_grad[...].astype(f32), axis=0, keepdims=True)
        pack[at : at + 8] = jnp.concatenate(
            [*tap_grads, tap_bias, bias, skip_grad, jnp.zeros((1, channels), f32)], 0
        )
        at += 8
        pack[at:] = jnp.zeros((pack.shape[0] - at, channels), f32)
        turned = pack[...].T
        r.small_work[0][...] = turned.reshape(r.small_work[0].shape)

    def small_summed():
        for k, bit in enumerate(bits):
            side, partner = flipped(me, bit)
            work, away, land = r.small_work[k], r.small_away[k], r.small_land[k]
            away[...] = work[:, 1 - side].astype(bf16)
            copy = sent(away, land, r.last_sends, r.last_receives, k, "seq", partner)
            yield
            copy.wait()
            total = work[:, side] + land[...].astype(f32)
            target = r.small_work[k + 1] if k + 1 < len(bits) else r.small_out
            target[...] = total.reshape(target.shape)
        yield

    one_sums = [summed(r.part, 8, k) for k in range(2)]
    for number in range(width // channels):
        weights.wait()

        def one_part(index, _, first=number * channels):
            at = pl.multiple_of(index * 256, 256)
            product = dot_rows(r.right_in[own], r.weights[pl.ds(at, 256)]).astype(bf16)
            for k in range(4):
                r.part[k // 2, k % 2, :, pl.ds(first + at, 256)] = product[
                    k * quarter : (k + 1) * quarter
                ]
            return 0

        lax.fori_loop(0, channels // 256, one_part, 0)
        next(one_sums[number])
        if (number + 1) * channels < width:
            weights = load(r.w_in.at[pl.ds((number + 1) * channels, channels)], r.weights)
    one_sum = in_turn(*one_sums)
    next(one_sum)

    def gain_part(index, total):
        rows = pl.ds(pl.multiple_of(index * CHUNK, CHUNK), CHUNK)
        a, b, at = quarter_rows(index)
        value = r.stream[rows].astype(f32)
        scale = lax.rsqrt(mean_square(value) + 1e-06)
        return total + jnp.sum(r.part[a, b, at].astype(f32) * value * scale, axis=0, keepdims=True)

    r.flat_move[0] = r.flat_move[0] * 0.25
    r.flat_move[0, 0:1] = lax.fori_loop(0, chunks, gain_part, jnp.zeros((1, width), f32))
    ways = [("ch", across), ("ch", along)] + [("seq", flipped(me, bit)[1]) for bit in bits]

    def flat_summed():
        for k, (axis, partner) in enumerate(ways):
            copy = sent(r.flat_move.at[k], r.flat_land.at[k], r.flat_sends, r.flat_receives, k,
                        axis, partner)
            yield
            copy.wait()
            target = r.flat_move.at[k + 1] if k + 1 < len(ways) else r.flat_out
            target[...] = r.flat_move[k] + r.flat_land[k]
        yield

    flat_sum = flat_summed()
    next(flat_sum)

    outs[0].next()
    cins[0].made(cin_others[0]).go()
    next(one_sum)
    next(flat_sum)
    outs[1].next()
    cins[1].made(cin_others[1]).go()
    next(one_sum)
    next(flat_sum)
    small_columns()
    small_sum = small_summed()
    next(small_sum)
    gins[0].next()
    down_kept.wait()
    down.next()
    late.next()
    next(one_sum)
    gins[1].next()
    gate0.next()
    next(flat_sum)
    gate1.next()
    next(one_sum)

    def norm_one(index, _):
        rows = pl.ds(pl.multiple_of(index * CHUNK, CHUNK), CHUNK)
        a, b, at = quarter_rows(index)
        value = r.stream[rows].astype(f32)
        scale = lax.rsqrt(mean_square(value) + 1e-06)
        back, _ = norm_back(value, scale, r.gains[0:1], r.total[a, b, at].astype(f32))
        r.stream_grad[rows] = r.stream_grad[rows] + back
        return 0

    lax.fori_loop(0, chunks, norm_one, 0)
    cins[0].next()
    next(small_sum)
    next(flat_sum)
    cins[1].next()
    for item in (up0, up1):
        item.next()
    next(small_sum)
    for waiting in (flat_sum, small_sum):
        for _ in waiting:
            pass
    pending = [*outs, *gins, *cins, down, late, *quarters]
    for _ in range(len(bits)):
        for item in pending:
            item.next()
    for item in pending:
        item.written.wait()


def backward(ins, hbm_ins, count, ident):
    bits = bits_of(count)
    n_bits = len(bits) - 1
    tokens, width = ins["stream"].shape
    channels, rank, states = ins["low"].shape[1], ins["w_dt"].shape[0], ins["logs"].shape[0]
    hid = hbm_ins["right_two_in"].shape[1] // 2
    narrow = ins["w_x"].shape[1]
    half, quarter = count // 2, tokens // 4
    rows_in, rows_out, rows_down = width // count, channels // count, hid // count
    rows = pltpu.VMEM((tokens, channels), f32)

    def low(*dims):
        return pltpu.VMEM(dims, bf16)

    def full(*dims):
        return pltpu.VMEM(dims, f32)

    outs = dict(
        stream_grad=(shape_of(tokens, width), VMEM),
        out_rows=(shape_of(tokens, width, dtype=bf16), VMEM),
        small_out=(shape_of(rows_out, tokens), VMEM),
        flat_out=(shape_of(8, width), VMEM),
        down_out=(shape_of(rows_down, width), ANY),
        gate_out=(shape_of(rows_in, hid), ANY),
        up_out=(shape_of(rows_in, hid), ANY),
        out_out=(shape_of(rows_out, width), ANY),
        gin_out=(shape_of(rows_in, channels), ANY),
        cin_out=(shape_of(rows_in, channels), ANY),
    )
    quads = count // 4

    def unit(part, columns):
        lands = [low(half >> (k + 1), part, columns) for k in range(n_bits)]
        return [low(half // 2, part, columns), *lands, full(half // 2, part, columns)]

    def sems(size):
        return pltpu.SemaphoreType.DMA((size,))

    halves = [count >> (k + 1) for k in range(len(bits))]
    scratch = dict(
        left_two=low(quads, 2, rows_in, 2 * tokens),
        left_one=low(quads, 2, rows_in, 2 * tokens),
        left_gated=low(quads, 2, rows_out, 2 * tokens),
        cot_rows=low(tokens, width),
        right_two=low(2 * tokens, 2 * hid),
        right_out=low(2 * tokens, width),
        right_in=low(2 * tokens, 2 * channels),
        mixer=low(2, 2, quarter, width),
        weights=low(channels, width),
        scan=rows,
        step=rows,
        drive=rows,
        push=rows,
        decay_rows=full(tokens, 128),
        into=full(tokens, states, 128),
        out_of=full(tokens, states, 128),
        into_wide=full(tokens, states, 128),
        out_wide=full(tokens, states, 128),
        hist=full(2, tokens, states, 128),
        step_sum=full(8, channels),
        starts=full(states, channels),
        rate_sum=full(states, channels),
        step_low_grad=low(tokens, channels),
        **handing(count, states, channels),
        part=low(2, 2, quarter, width),
        total=low(2, 2, quarter, width),
        first_land=low(2, quarter, width),
        second_land=low(quarter, width),
        second_move=low(quarter, width),
        raw_move=full(2, tokens, narrow),
        raw_land=full(2, tokens, narrow),
        raw_low=low(tokens, narrow),
        step_low=low(tokens, rank),
        grad_pre=full(tokens + 8, channels),
        extended=full(tokens + 16, channels),
        flat_move=full(2 + len(bits), 8, width),
        flat_land=full(2 + len(bits), 8, width),
        small_work=[full(size, 2, rows_out, tokens) for size in halves],
        small_away=[low(size, rows_out, tokens) for size in halves],
        small_land=[low(size, rows_out, tokens) for size in halves],
        down=unit(rows_down, width // 2),
        late=unit(rows_down, width // 2),
        gate0=unit(rows_in, hid // 2),
        gate1=unit(rows_in, hid // 2),
        up0=unit(rows_in, hid // 2),
        up1=unit(rows_in, hid // 2),
        out0=unit(rows_out, width // 2),
        out1=unit(rows_out, width // 2),
        gin0=unit(rows_in, channels // 2),
        gin1=unit(rows_in, channels // 2),
        cin0=unit(rows_in, channels // 2),
        cin1=unit(rows_in, channels // 2),
        load_sems=sems(32),
        write_sems=sems(12),
        pair_sends=sems(8),
        pair_receives=sems(8),
        shared_sends=sems(4),
        shared_receives=sems(4),
        unit_sends=sems(12 * n_bits),
        unit_receives=sems(12 * n_bits),
        sum_sends=sems(16),
        sum_receives=sems(16),
        raw_sends=sems(3),
        raw_receives=sems(3),
        last_sends=sems(len(bits)),
        last_receives=sems(len(bits)),
        flat_sends=sems(2 + len(bits)),
        flat_receives=sems(2 + len(bits)),
    )
    names, shapes = [(name, 0) for name in [*ins, *hbm_ins, *outs]], []
    for name, held in scratch.items():
        listed = isinstance(held, list)
        names.append((name, len(held) if listed else 0))
        shapes += held if listed else [held]
    places = [VMEM for _ in ins]
    places[0] = pl.BlockSpec(memory_space=pltpu.SMEM)
    made = pl.pallas_call(
        functools.partial(backward_kernel, bits, names),
        out_shape=[shape for shape, _ in outs.values()],
        in_specs=places + [ANY] * len(hbm_ins),
        out_specs=[spec for _, spec in outs.values()],
        scratch_shapes=shapes,
        compiler_params=pltpu.CompilerParams(
            collective_id=ident, has_side_effects=True, vmem_limit_bytes=63 * 2**20
        ),
        name="block_backward",
    )(*ins.values(), *hbm_ins.values())
    return types.SimpleNamespace(**dict(zip(outs, made)))


def finish_kernel(cells, names, *refs):
    r = named(names, refs)
    me = lax.axis_index("seq")
    moves = [
        (r.out_rows, r.out), (r.stream_grad, r.stream), (r.out_out, r.w_out),
        (r.down_out, r.w_down), (r.gate_out, r.w_gate_up.at[:, 0]),
        (r.up_out, r.w_gate_up.at[:, 1]), (r.cin_out, r.w_in.at[:, 0]),
        (r.gin_out, r.w_in.at[:, 1]),
    ]
    little = [(r.small_out, r.small_here), (r.flat_out, r.flat_here)]
    loads = [
        pltpu.make_async_copy(source, here, r.sems.at[k])
        for k, (source, here) in enumerate(
            [*little, *((source, here) for (source, _), here in zip(moves, r.here))]
        )
    ]
    for copy in loads:
        copy.start()
    copies = []
    for k, (_, target) in enumerate(moves):
        loads[k + 2].wait()
        copy = pltpu.make_async_copy(r.here[k], target, r.out_sems.at[k])
        copy.start()
        copies.append(copy)
    for copy in loads[:2]:
        copy.wait()
    narrow, rank, states = r.x.shape[1], r.dt.shape[0], r.decay.shape[0]
    small = r.small_here[...]
    r.x[...] = small[:, :narrow]
    turned = small[:, narrow:].T
    r.dt[...] = turned[:rank]
    r.decay[...] = turned[rank : rank + states]
    r.chan[...] = turned[rank + states : rank + states + 7]
    flat = r.flat_here[...]
    width = flat.shape[1]
    count = width // r.gains.shape[1]
    gains, tail = jnp.zeros(r.gains.shape, f32), jnp.zeros(r.small.shape, f32)
    for k in range(count):
        gain_at, tail_at = k * r.gains.shape[1], k * r.small.shape[1]
        mine = me == k
        gains = gains + jnp.where(mine, flat[0:2, gain_at : gain_at + r.gains.shape[1]], 0.0)
        tail = tail + jnp.where(mine, flat[2:3, tail_at : tail_at + r.small.shape[1]], 0.0)
    r.gains[...] = gains
    r.small[...] = tail
    totals = [jnp.sum(flat[3 + k : 4 + k], axis=1, keepdims=True) for k in range(3)]
    r.rms[...] = jnp.sqrt(jnp.concatenate(totals, 1) / cells)
    for copy in copies:
        copy.wait()


def finish(made, cells, narrow, rank, states, count):
    rows_out = made.small_out.shape[0]
    width = made.flat_out.shape[1]
    rows_in, hid = made.gate_out.shape
    channels = made.cin_out.shape[1]
    outs = dict(
        out=shape_of(*made.out_rows.shape, dtype=bf16),
        stream=shape_of(*made.stream_grad.shape),
        gains=shape_of(2, width // count),
        w_in=shape_of(rows_in, 2, channels),
        chan=shape_of(7, rows_out),
        decay=shape_of(states, rows_out),
        x=shape_of(rows_out, narrow),
        small=shape_of(1, narrow // count),
        dt=shape_of(rank, rows_out),
        w_out=shape_of(*made.out_out.shape),
        w_gate_up=shape_of(rows_in, 2, hid),
        w_down=shape_of(*made.down_out.shape),
        rms=shape_of(1, 3),
    )
    ins = vars(made)
    held = [
        made.out_rows, made.stream_grad, made.out_out, made.down_out, made.gate_out, made.up_out,
        made.cin_out, made.gin_out, made.small_out, made.flat_out,
    ]
    places = [pltpu.VMEM(item.shape, item.dtype) for item in held]
    names = [(name, 0) for name in [*ins, *outs]]
    rest = dict(here=8, small_here=0, flat_here=0, sems=0, out_sems=0)
    names += list(rest.items())
    big = {id(outs[name]) for name in ("out", "stream", "w_in", "w_out", "w_gate_up", "w_down")}
    done = pl.pallas_call(
        functools.partial(finish_kernel, cells, names),
        out_shape=list(outs.values()),
        in_specs=[ANY for _ in ins],
        out_specs=[ANY if id(item) in big else VMEM for item in outs.values()],
        scratch_shapes=[*places, pltpu.SemaphoreType.DMA((10,)), pltpu.SemaphoreType.DMA((8,))],
        compiler_params=pltpu.CompilerParams(vmem_limit_bytes=62 * 2**20),
        name="finish",
    )(*ins.values())
    out, stream, gains, w_in, chan, decay, x, small, dt, w_out, w_gate_up, w_down, rms = done
    return (
        out, stream, gains, w_in, chan, decay, x, small.reshape(-1), dt, w_out, w_gate_up, w_down,
        rms.reshape(-1),
    )


def local(
    seq_count,
    stream,
    doc_bounds,
    norm_gains,
    w_in,
    chan_vectors,
    decay_logs,
    w_x,
    small_gains,
    w_dt,
    w_out,
    w_gate_up,
    w_down,
    cotangent,
):
    tokens, width = stream.shape
    rank, (states, channels) = w_dt.shape[0], decay_logs.shape

    w_in_flat = w_in.reshape(width, 2 * channels)
    (
        in_proj, one_in, halo, pre_conv, conv_low, raw_proj, step_pre, into, out_of, scan_out, gated_low,
        last_state, mixer_low, gated_in, before, one_came, cot_came, w_gate_up_flat,
    ) = mixer_forward(
        doc_bounds, stream, norm_gains, chan_vectors, decay_logs, w_x, small_gains[None], w_dt,
        w_out, w_in_flat, cotangent, w_gate_up, seq_count, 1,
    )
    mid = feed_forward(
        dict(stream=stream, mixer=mixer_low, gains=norm_gains),
        dict(
            cot=cotangent, cot_came=cot_came, w_gate_up_in=w_gate_up_flat,
            w_down_in=w_down,
        ),
        seq_count,
        3,
    )
    made = backward(
        dict(
            bounds=doc_bounds, stream=stream, gains=norm_gains, two_total=mid.total,
            proj=in_proj, halo=halo,
            pre=pre_conv, low=conv_low, raw=raw_proj, step_pre=step_pre, last_state=last_state,
            chan=chan_vectors, logs=decay_logs, w_x=w_x, w_dt=w_dt, small_gains=small_gains[None],
        ),
        dict(
            feed_part=mid.feed_part, left_two_in=mid.left_two, right_two_in=mid.right_two,
            down_away_in=mid.down_away, down_kept_in=mid.down_kept,
            late_away_in=mid.late_away, late_kept_in=mid.late_kept, mixer_in=mixer_low,
            cot=cotangent, gated_in=gated_in, one_in=one_in,
            one_came=one_came, w_out=w_out, w_in=w_in_flat, scan_in=scan_out, into_in=into,
            out_of_in=out_of, hist_in=before,
        ),
        seq_count,
        2,
    )
    return finish(
        made, tokens * seq_count * width, w_x.shape[1], rank, states, seq_count
    )


def solution(mesh):
    in_specs = (
        P("seq", None),
        P(),
        P(),
        P(None, None, "ch"),
        P(None, "ch"),
        P(None, "ch"),
        P("ch", None),
        P(),
        P(None, "ch"),
        P("ch", None),
        P(None, None, "ch"),
        P("ch", None),
        P("seq", None),
    )
    out_specs = (
        P("seq", None),
        P("seq", None),
        P(None, "seq"),
        P("seq", None, "ch"),
        P(None, ("ch", "seq")),
        P(None, ("ch", "seq")),
        P(("ch", "seq"), None),
        P("seq"),
        P(None, ("ch", "seq")),
        P(("ch", "seq"), None),
        P("seq", None, "ch"),
        P(("ch", "seq"), None),
        P(),
    )
    return jax.shard_map(
        functools.partial(local, mesh.shape["seq"]),
        mesh=mesh,
        in_specs=in_specs,
        out_specs=out_specs,
        check_vma=False,
    )
```
